128 devices in a mesh: seq: 32 (over y, x, core), fsdp: 4 (over z).
Axes of the slice: x: 4, y: 4, z: 4, core: 2. Of those that a mesh axis runs over, the one named last changes fastest.
Arguments:
- hidden: bfloat16 [16, 4096, 768], P('fsdp', 'seq'), may hold values from -6 to 6
- segments: int32 [16, 4096], P('fsdp', 'seq'), may hold values from 0 to 4095, as said below
- norm_gain: bfloat16 [768], P('fsdp'), may hold values from 0.5 to 1.5
- in_weight: bfloat16 [768, 3352], P('fsdp'), may hold values from -0.21875 to 0.21875
- conv_weight: bfloat16 [4, 1792], P(None, 'fsdp'), may hold values from -3 to 3
- conv_bias: bfloat16 [1792], P('fsdp'), may hold values from -0.5 to 0.5
- dt_bias: bfloat16 [24], P('fsdp'), may hold values from -1.5 to 0.5
- a_log: bfloat16 [24], P('fsdp')
- skip: bfloat16 [24], P('fsdp'), may hold values from 0.5 to 1.5
- gate_gain: bfloat16 [1536], P('fsdp'), may hold values from 0.5 to 1.5
- out_weight: bfloat16 [1536, 768], P('fsdp'), may hold values from -0.15625 to 0.15625
- cotangent: bfloat16 [16, 4096, 768], P('fsdp', 'seq'), may hold values from -6 to 6
Outputs:
- output: bfloat16 [16, 4096, 768], P('fsdp', 'seq')
- grad_hidden: bfloat16 [16, 4096, 768], P('fsdp', 'seq')
- grad_norm_gain: float32 [768], P('fsdp')
- grad_in_weight: float32 [768, 3352], P('fsdp')
- grad_conv_weight: float32 [4, 1792], P(None, 'fsdp')
- grad_conv_bias: float32 [1792], P('fsdp')
- grad_dt_bias: float32 [24], P('fsdp')
- grad_a_log: float32 [24], P('fsdp')
- grad_skip: float32 [24], P('fsdp')
- grad_gate_gain: float32 [1536], P('fsdp')
- grad_out_weight: float32 [1536, 768], P('fsdp')
The draws below stay inside these ranges and needn't reach their ends.
Inputs may be any that keep to these rules, and one draw needn't show every extreme that they name: `segments`: each token's number is the position within its sequence of the first token of its document, so numbers never fall along a sequence; every sequence's last token starts a document; among sequences 4i to 4i+3, for each i, one holds a document from a position within its first 128 tokens to its next-to-last token.
All inputs are finite; a program needn't handle non-finite values.
Results may differ from the reference program's by a relative error of at most 0.025.
Values may be sent and summed in bfloat16 or wider, within the bound.
No kernel may reach another device: no remote copies, remote signals or barrier semaphores. Data moves between devices by JAX's collectives and lax.ppermute only.
A program may use at most 320 MiB of HBM per device.

```python
import math
import jax
import jax.numpy as jnp
from jax import lax

D = 768
INNER = 1536
HEADS = 24
HEADDIM = 64
STATE = 128
CONV = 4
SHARD = 128
SEQS = 4
XBC = 1792
PROJ = 3352
LENGTH = 4096
SEQS_ALL = 16


def draw_segments(key, part):
    key = jax.random.fold_in(key, 5)
    rate_key, start_key, whole_key, begin_key = jax.random.split(key, 4)
    levels = jax.random.randint(rate_key, (SEQS_ALL, 1), 0, 3)
    period = 64 * jnp.power(4, levels).astype(jnp.int32)
    tosses = jax.random.randint(start_key, (SEQS_ALL, LENGTH), 0, 1 << 20) % period
    groups = SEQS_ALL // SEQS
    picked = jax.random.randint(whole_key, (groups,), 0, SEQS)
    begins = jax.random.randint(begin_key, (SEQS_ALL, 1), 1, SHARD)
    rows = jnp.arange(SEQS_ALL)
    single = rows % SEQS == picked[rows // SEQS]
    position = jnp.arange(LENGTH)
    random_starts = (tosses == 0) & (position[None, :] > 0)
    long_starts = position[None, :] == begins
    starts = jnp.where(single[:, None], long_starts, random_starts)
    starts = starts | (position[None, :] == LENGTH - 1)
    marked = jnp.where(starts, position[None, :], 0).astype(jnp.int32)
    return lax.cummax(marked, axis=1).astype(jnp.int32)


def draw_a_log(key, part):
    key = jax.random.fold_in(key, 7)
    order_key, slow_key, fast_key = jax.random.split(key, 3)
    slow_count = HEADS // 2
    shuffled = jax.random.permutation(order_key, HEADS)
    slow_heads = shuffled < slow_count
    slow_rate = jnp.exp(jax.random.uniform(slow_key, (HEADS,), jnp.float32, math.log(0.4), math.log(2.4))) / LENGTH
    fast_rate = jnp.exp(jax.random.uniform(fast_key, (HEADS,), jnp.float32, math.log(0.04), math.log(0.15)))
    return jnp.log(jnp.where(slow_heads, slow_rate, fast_rate)).astype(jnp.bfloat16)


def shard_levels(own_key, extent, pieces, least, top_value):
    def one(axis_at, blocks):
        draws = jax.random.uniform(jax.random.fold_in(jax.random.fold_in(own_key, 6), axis_at), (blocks,), jnp.float32, least / len(pieces), top_value / len(pieces))
        return jnp.repeat(jnp.exp(draws), extent[axis_at] // blocks).reshape((-1,) + (1,) * (len(extent) - axis_at - 1))

    loudness = one(*pieces[0])
    for cut in pieces[1:]:
        loudness = loudness * one(*cut)
    return loudness


def normal_values(rng, shape, width, most, cuts=(), held_as=jnp.bfloat16):
    gain = shard_levels(rng, shape, cuts, -0.22, 0.18) if cuts else 1.0
    values = jax.random.normal(rng, shape, jnp.float32) * width * gain
    return jnp.minimum(jnp.maximum(values, -most), most).astype(held_as)


def setup_inputs(seed: int = 0) -> dict:
    key_list = jax.random.split(jax.random.key(seed), 13)
    return {
        "hidden": normal_values(key_list[0], (SEQS_ALL, LENGTH, D), 1.0, 6.0, ((0, 4), (1, 32))),
        "segments": draw_segments(jax.random.fold_in(key_list[12], 71), 0),
        "norm_gain": jnp.clip(1.0 + 0.1 * jax.random.normal(key_list[2], (D,), jnp.float32), 0.5, 1.5).astype(jnp.bfloat16),
        "in_weight": normal_values(key_list[3], (D, PROJ), D ** -0.5, 0.21875, ((0, 4),)),
        "conv_weight": normal_values(key_list[4], (CONV, XBC), CONV ** -0.5, 3.0, ((1, 4),)),
        "conv_bias": jnp.clip(jax.random.uniform(key_list[5], (XBC,), jnp.float32, -0.5, 0.5) * shard_levels(key_list[5], (XBC,), ((0, 4),), -0.4, 0.0), -0.5, 0.5).astype(jnp.bfloat16),
        "dt_bias": jnp.clip(-1.5 + 2.0 * jax.random.uniform(key_list[6], (HEADS,), jnp.float32) ** shard_levels(key_list[6], (HEADS,), ((0, 4),), -0.2, 0.2), -1.5, 0.5).astype(jnp.bfloat16),
        "a_log": draw_a_log(jax.random.fold_in(key_list[12], 71), 0),
        "skip": jnp.clip(0.5 + 1.0 * jax.random.uniform(key_list[8], (HEADS,), jnp.float32) ** shard_levels(key_list[8], (HEADS,), ((0, 4),), -0.2, 0.2), 0.5, 1.5).astype(jnp.bfloat16),
        "gate_gain": jnp.clip(1.0 + 0.1 * jax.random.normal(key_list[9], (INNER,), jnp.float32), 0.5, 1.5).astype(jnp.bfloat16),
        "out_weight": normal_values(key_list[10], (INNER, D), INNER ** -0.5, 0.15625, ((0, 4),)),
        "cotangent": normal_values(key_list[11], (SEQS_ALL, LENGTH, D), 1.0, 6.0, ((0, 4), (1, 32))),
    }


@jax.custom_vjp
def low(v):
    return lax.optimization_barrier(v.astype(jnp.bfloat16)).astype(jnp.float32)

@jax.custom_vjp
def low_back(v):
    return v

def low_keep(v):
    return (low(v), None)

def low_pass(kept, grad):
    return (grad,)

def back_keep(v):
    return (v, None)

def back_low(kept, grad):
    return (low(grad),)
low.defvjp(low_keep, low_pass)
low_back.defvjp(back_keep, back_low)
epsilon = 1e-05
highest = lax.Precision.HIGHEST

def block_step(state, block):
    x_block, b_block, c_block, dt_block, da_block, same_block, keep_block, end_block = block
    cumul = jnp.cumsum(da_block, axis=0)
    differ = cumul[:, None, :] - cumul[None, :, :]
    masked = same_block[:, :, None]
    decay = jnp.exp(jnp.where(masked > 0, differ, -60.0)) * masked
    scores = jnp.dot(c_block, b_block.T, precision=highest)
    weights = scores[:, :, None] * decay * dt_block[None, :, :]
    mixed = jnp.einsum('tsh,shp->thp', weights, x_block, precision=highest)
    carried = jnp.einsum('tn,hpn->thp', c_block, state, precision=highest)
    mixed = mixed + (jnp.exp(cumul) * keep_block[:, None])[:, :, None] * carried
    final = cumul[-1]
    weight_end = jnp.exp(final[None, :] - cumul) * end_block[:, None] * dt_block
    update = jnp.einsum('sh,shp,sn->hpn', weight_end, x_block, b_block, precision=highest)
    state = (jnp.exp(final) * keep_block[-1])[:, None, None] * state + update
    return (state, mixed)

def sequence_forward(values, seg_row, weights):
    norm_gain, in_weight, conv_weight, conv_bias, dt_bias, a_log, skip, gate_gain, out_weight = weights
    scale = lax.rsqrt(lax.optimization_barrier(jnp.mean(values * values, axis=-1, keepdims=True)) + epsilon)
    normed = low(values * scale * norm_gain)
    proj = low_back(jnp.dot(normed, in_weight, precision=highest))
    gates = proj[:, :INNER]
    mixin = low(proj[:, INNER:INNER + XBC])
    dt_raw = proj[:, INNER + XBC:]
    padded = jnp.concatenate([jnp.zeros((CONV - 1, XBC), jnp.float32), mixin], 0)
    total = conv_weight[0] * padded[0:LENGTH]
    for offset in range(1, CONV):
        total = total + conv_weight[offset] * padded[offset:offset + LENGTH]
    active = jax.nn.silu(total + conv_bias)
    x_heads = active[:, :INNER].reshape(LENGTH, HEADS, HEADDIM)
    b_proj = active[:, INNER:INNER + STATE]
    c_proj = active[:, INNER + STATE:]
    steps = jax.nn.softplus(dt_raw + dt_bias)
    rates = -steps * jnp.exp(a_log)
    block_rows = math.gcd(LENGTH, 256)
    block_count = LENGTH // block_rows
    seg_blocks = seg_row.reshape(block_count, block_rows).astype(jnp.int32)
    before = jnp.concatenate([jnp.full((1,), -1, jnp.int32), seg_blocks[:-1, -1].astype(jnp.int32)])
    lower = jnp.arange(block_rows)[:, None] >= jnp.arange(block_rows)[None, :]
    same = ((seg_blocks[:, :, None] == seg_blocks[:, None, :]) & lower[None]).astype(jnp.float32)
    keep = (seg_blocks == before[:, None]).astype(jnp.float32)
    ending = (seg_blocks == seg_blocks[:, -1:]).astype(jnp.float32)
    inputs = (x_heads.reshape(block_count, block_rows, HEADS, HEADDIM), b_proj.reshape(block_count, block_rows, STATE), c_proj.reshape(block_count, block_rows, STATE), steps.reshape(block_count, block_rows, HEADS), rates.reshape(block_count, block_rows, HEADS), same, keep, ending)
    start_state = jnp.zeros((HEADS, HEADDIM, STATE), jnp.float32)
    final_state, mixed = lax.scan(jax.checkpoint(block_step), start_state, inputs)
    mixed = mixed.reshape(LENGTH, HEADS, HEADDIM) + skip[:, None] * x_heads
    gated = mixed.reshape(LENGTH, INNER) * jax.nn.silu(gates)
    gscale = lax.rsqrt(lax.optimization_barrier(jnp.mean(gated * gated, axis=-1, keepdims=True)) + epsilon)
    normed_out = low(gated * gscale * gate_gain)
    return values + jnp.dot(normed_out, out_weight, precision=highest)

def reference(hidden, segments, norm_gain, in_weight, conv_weight, conv_bias, dt_bias, a_log, skip, gate_gain, out_weight, cotangent):
    params = tuple((param.astype(jnp.float32) for param in (norm_gain, in_weight, conv_weight, conv_bias, dt_bias, a_log, skip, gate_gain, out_weight)))

    def forward(values, *weights):

        def one_sequence(pair_item):
            return sequence_forward(pair_item[0], pair_item[1], weights)
        return lax.map(jax.checkpoint(one_sequence), (values, segments))
    output, pullback = jax.vjp(forward, hidden.astype(jnp.float32), *params)
    grads = pullback(cotangent.astype(jnp.float32))
    return (output.astype(jnp.bfloat16), grads[0].astype(jnp.bfloat16), grads[1], grads[2], grads[3], grads[4], grads[5], grads[6], grads[7], grads[8], grads[9])
```

```python
import functools

import jax
import jax.numpy as jnp
import numpy as np
from jax import lax
from jax.experimental import pallas as pl
from jax.experimental.pallas import tpu as pltpu
from jax.sharding import Mesh
from jax.sharding import PartitionSpec as P

INNER = 1536
HEADS = 24
HEADDIM = 64
STATE = 128
XBC = 1792
MIX = 1816
MIX_PAD = 1920
MIX_WIDE = 2048
EDGE = 8
TOKENS = 128
LANES = 128
PAIRS = 12
SEQ = ("seq_0", "seq_1", "seq_2")
CHIPS = ("seq_0", "seq_1")
COLUMNS = ("seq_0", "seq_1", "fsdp")

epsilon = 1e-05
bf16 = jnp.bfloat16
f32 = jnp.float32
VMEM_MIB = 24
LARGE = 60
COST = 1.1e9

CONV_W, CONV_B, GATE_GAIN, GAIN, DT_BIAS, DECAY, SKIP, SKIP_WIDE = 0, 4, 5, 6, 7, 8, 9, 10


def ring(value, axis, steps):
    count = lax.axis_size(axis)
    pairs = [(source, (source + steps) % count) for source in range(count)]
    return lax.ppermute(value, axis, pairs)


def line(value, axis, steps):
    count = lax.axis_size(axis)
    initial, last = (max(0, -steps), min(count, count - steps))
    return lax.ppermute(value, axis, [(source, source + steps) for source in range(initial, last)])


def swap(value):
    return ring(value, "seq_2", 1)


def dot(pattern, left, right):
    return jnp.einsum(pattern, left, right, preferred_element_type=f32)


def exchange(blocks, axes):
    return lax.all_to_all(blocks, axes, 0, 0, tiled=False)


def split_three(value):
    high = value.astype(bf16)
    rest = value - high.astype(f32)
    middle = rest.astype(bf16)
    low = (rest - middle.astype(f32)).astype(bf16)
    return high, middle, low


def mm(left, right):
    return lax.dot_general(left, right, (((1,), (0,)), ((), ())), preferred_element_type=f32)


def mm_nt(left, right):
    return lax.dot_general(left, right, (((1,), (1,)), ((), ())), preferred_element_type=f32)


def mm_tn(left, right):
    return lax.dot_general(left, right, (((0,), (0,)), ((), ())), preferred_element_type=f32)


def exact_mm(ones, value):
    high, middle, low = split_three(value)
    return mm(ones, high) + mm(ones, middle) + mm(ones, low)


def halves(value):
    high = value.astype(bf16)
    return high, (value - high.astype(f32)).astype(bf16)


def widen(pieces, spread):
    return mm(pieces[0], spread) + mm(pieces[1], spread)


def sum_heads(value, gather):
    high, low = halves(value)
    return mm(high, gather) + mm(low, gather)


def sigmoid(value):
    return 1.0 / (1.0 + jnp.exp(-value))


def call(
    kernel, outs, ins, operands, grid=None, scratch=(), micros=1, after=(), mib=VMEM_MIB, scalars=None
):
    whole = pl.BlockSpec(memory_space=pltpu.VMEM)
    lead = [] if scalars is None else [scalars]
    count = len(operands) + len(lead)

    def body(*refs):
        kernel(*refs[:count], *refs[count + len(after) :])

    return pl.pallas_call(
        body,
        grid_spec=pltpu.PrefetchScalarGridSpec(
            num_scalar_prefetch=len(lead),
            grid=grid or (),
            in_specs=[spec or whole for spec in ins]
            + [pl.BlockSpec(memory_space=pl.ANY)] * len(after),
            out_specs=[spec or whole for spec, _ in outs],
            scratch_shapes=list(scratch),
        ),
        out_shape=[shape for _, shape in outs],
        compiler_params=pltpu.CompilerParams(vmem_limit_bytes=mib * 1024 * 1024),
        cost_estimate=pl.CostEstimate(
            flops=int(micros * COST), bytes_accessed=0, transcendentals=0
        ),
    )(*lead, *operands, *after)


def shaped(shape, dtype=f32):
    return jax.ShapeDtypeStruct(shape, dtype)


def by_seq(*shape):
    return pl.BlockSpec((1,) + shape, lambda a, *_: (a,) + (0,) * len(shape))


def constant(*shape):
    return pl.BlockSpec(shape, lambda a, *_: (0,) * len(shape))


def own_half(*shape):
    return pl.BlockSpec(
        (1,) + shape,
        lambda a, where: (jnp.clip(a - 2 * where[1], 0, 1),) + (0,) * len(shape),
    )


def other_half(*shape):
    return pl.BlockSpec(
        (1,) + shape,
        lambda a, where: (jnp.clip(a - 2 + 2 * where[1], 0, 1),) + (0,) * len(shape),
    )


ANYWHERE = pl.BlockSpec(memory_space=pl.ANY)
SCALARS = pl.BlockSpec(memory_space=pltpu.SMEM)


def columns(index, width=LANES):
    return slice(index * width, (index + 1) * width)


def message_kernel(
    where, in_weight, norm_gain, conv_weight, conv_bias, dt_bias, a_log, skip, gate_gain,
    message, mix_shard, held, narrow,
):
    place, core = where[0], where[1]
    narrow[...] = jnp.zeros_like(narrow)
    narrow[:, 0 : MIX - XBC] = in_weight[:, INNER + XBC :].astype(f32)
    mix_shard[:, 0:XBC] = in_weight[:, INNER : INNER + XBC]
    mix_shard[:, XBC:] = narrow[...].astype(bf16)
    half = pl.ds(pl.multiple_of(core * 96, 96), 96)
    message[0:96, 0:XBC] = in_weight[half, INNER : INNER + XBC]
    message[0:96, XBC:] = narrow[half].astype(bf16)
    message[96:112, XBC:] = jnp.zeros((16, LANES), bf16)
    held[...] = jnp.zeros_like(held)
    held[CONV_W : CONV_W + 4, 0:448] = conv_weight[...].astype(f32)
    for target, source in (
        (CONV_B, conv_bias), (GATE_GAIN, gate_gain), (GAIN, norm_gain), (DT_BIAS, dt_bias),
        (DECAY, a_log), (SKIP, skip),
    ):
        size = source.shape[0]
        held[target : target + 1, 0:size] = source[...].astype(f32).reshape(1, size)
    row = lax.broadcasted_iota(jnp.int32, (16, 1), 0)
    for z in range(4):

        @pl.when(place == z)
        def _(z=z):
            value = held[...]
            if z:
                moved = pltpu.roll(value, 448 * z, 1)
                moved = jnp.where(row == GATE_GAIN, pltpu.roll(value, 384 * z, 1), moved)
                moved = jnp.where(row == GAIN, pltpu.roll(value, 192 * z, 1), moved)
                value = jnp.where(row >= DT_BIAS, pltpu.roll(value, 6 * z, 1), moved)
            message[96:112, 0:XBC] = value.astype(bf16)


def tables_kernel(where, segments, halo, same, keep, ending, passing, halo_held):
    start = where[2].astype(f32)
    below = lax.broadcasted_iota(jnp.int32, (TOKENS, TOKENS), 0) >= lax.broadcasted_iota(
        jnp.int32, (TOKENS, TOKENS), 1
    )
    for a in range(4):
        row = jnp.broadcast_to(segments[a : a + 1].astype(f32), (TOKENS, TOKENS))
        column = row.T
        first, last = column[0:1], column[TOKENS - 1 :]
        same[a] = jnp.where((column == row) & below, 1.0, 0.0)
        keep[a] = jnp.where((column == first) & (first < start), 1.0, 0.0)
        ending[a] = jnp.where(column == last, 1.0, 0.0)
        passing[a : a + 1] = jnp.where(last < start, 1.0, 0.0)
        halo_held[a] = halo[a].astype(f32)


def assemble_kernel(width, where, shard, m_1, m_2, m_3, o_1, o_2, o_3, full, sems):
    copies = weight_copies(
        where[0], where[1], shard.at[:, pl.ds(0, width)], (m_1, m_2, m_3), (o_1, o_2, o_3), full, sems
    )
    for copy in copies:
        copy.start()
    for copy in copies:
        copy.wait()


def halves_kernel(where, in_weight, out_weight, gate_half, out_half, sems):
    core = where[1]
    first = pltpu.make_async_copy(
        in_weight.at[pl.ds(pl.multiple_of(core * 96, 96), 96), pl.ds(0, INNER)],
        gate_half,
        sems.at[0],
    )
    second = pltpu.make_async_copy(
        out_weight.at[pl.ds(pl.multiple_of(core * 192, 192), 192)], out_half, sems.at[1]
    )
    first.start()
    second.start()
    first.wait()
    second.wait()


def fetch(half):
    return [ring(half, "fsdp", steps) for steps in (3, 2, 1)]


def assemble(fetched, shard, width, where, after=()):
    other = [swap(part) for part in fetched]
    anywhere = pl.BlockSpec(memory_space=pl.ANY)
    rows = shard.shape[0]
    return call(
        functools.partial(assemble_kernel, width),
        [(None, shaped((4 * rows, width), bf16))],
        [SCALARS] + [anywhere] * 7,
        [where, shard] + fetched + other,
        scratch=[pltpu.SemaphoreType.DMA((7,))],
        micros=2,
        after=after,
    )[0]


def weight_copies(place, core, shard, mine, others, full, sems):
    rows = shard.shape[0]
    half = rows // 2
    copies = [
        pltpu.make_async_copy(
            shard, full.at[pl.ds(pl.multiple_of(place * rows, rows), rows)], sems.at[0]
        )
    ]
    for k in range(3):
        owner = lax.rem(place + (1 + k), 4) * rows
        low = pl.multiple_of(owner + core * half, half)
        high = pl.multiple_of(owner + (1 - core) * half, half)
        for slot, part, begin in ((1 + 2 * k, mine[k], low), (2 + 2 * k, others[k], high)):
            copies.append(
                pltpu.make_async_copy(
                    part.at[pl.ds(0, half)], full.at[pl.ds(begin, half)], sems.at[slot]
                )
            )
    return copies


def front_kernel(
    where, hidden, halo, ending, passing, spread, lower, own, shard, m_1, m_2, m_3, o_1, o_2, o_3,
    params, mixin, mixin_halo, active, dt_arg, dt, cumul, through, local_mine, local_send,
    normed, normed_t, halo_t, full,
    weight, packed, x_low, x_turned, mix_held, act_held, mine_held, send_held,
    extended, state_b, scaled, in_sems, out_sems,
):
    place, core = where[0], where[1]
    incoming = weight_copies(
        place, core, shard, (m_1, m_2, m_3), (o_1, o_2, o_3), weight, in_sems
    )
    rows_in = [
        pltpu.make_async_copy(part.at[pl.ds(96, 16)], packed.at[k], in_sems.at[7 + k])
        for k, part in enumerate((own, m_1, m_2, m_3))
    ]
    for copy in rows_in + incoming:
        copy.start()
    outgoing = []

    def send(source, target):
        copy = pltpu.make_async_copy(source, target, out_sems.at[len(outgoing)])
        copy.start()
        outgoing.append(copy)

    for copy in rows_in:
        copy.wait()
    whole = packed[0].astype(f32) + packed[1].astype(f32)
    whole = (whole + packed[2].astype(f32) + packed[3].astype(f32))[:, 0:XBC]
    params[...] = whole
    decay_rate = jnp.exp(whole[DECAY : DECAY + 1, 0:LANES])
    params[DECAY : DECAY + 1, 0:LANES] = decay_rate
    params[SKIP_WIDE : SKIP_WIDE + 1, 0:INNER] = mm(
        whole[SKIP : SKIP + 1, 0:LANES].astype(bf16), spread[...]
    )
    gain = whole[GAIN : GAIN + 1, 0:768]

    def normalised(value):
        scale = lax.rsqrt(jnp.mean(value * value, axis=1, keepdims=True) + epsilon)
        return value * scale * gain

    edges = []
    for a in range(4):
        value = normalised(hidden[a].astype(f32))
        x_low[a * TOKENS : (a + 1) * TOKENS] = value.astype(bf16)
        x_turned[:, a * TOKENS : (a + 1) * TOKENS] = value.T.astype(bf16)
        edges.append(normalised(halo[a]))
    send(x_low, normed)
    send(x_turned, normed_t)
    edges = jnp.concatenate(edges, 0)
    edge_low = edges.astype(bf16)
    edges = jnp.concatenate([edges, jnp.zeros((LANES - 32, 768), f32)], 0)
    halo_t[...] = edges.T.astype(bf16)

    for copy in incoming:
        copy.wait()
    send(weight, full)
    argument = mm(x_low[...], weight[:, XBC:]) + whole[DT_BIAS : DT_BIAS + 1, 0:LANES]
    steps = jnp.maximum(argument, 0.0) + jnp.log1p(jnp.exp(-jnp.abs(argument)))
    for a in range(4):
        rows = slice(a * TOKENS, (a + 1) * TOKENS)
        dt_arg[a] = argument[rows]
        dt[a] = steps[rows]
        total = exact_mm(lower[...], -steps[rows] * decay_rate)
        cumul[a] = total
        final = total[TOKENS - 1 :]
        through[a : a + 1] = jnp.exp(final) * passing[a : a + 1]
        scaled[a] = (jnp.exp(final - total) * ending[a] * steps[rows]).astype(bf16)
    for turn, chunk in enumerate((6, 0, 1, 2, 3, 4, 5)):
        lanes = columns(chunk, 256)
        span = pl.ds(chunk * 256, 256)
        slot = turn % 2
        part = mm(x_low[...], weight[:, lanes]).astype(bf16)
        edge = mm(edge_low, weight[:, lanes]).astype(bf16).astype(f32)
        for a in range(4):
            rows = slice(a * TOKENS, (a + 1) * TOKENS)
            mix_held[a, :, lanes] = part[rows]
            mixin_halo[a, :, lanes] = edge[a * EDGE : (a + 1) * EDGE]
            extended[slot, a, 0:EDGE] = edge[a * EDGE : (a + 1) * EDGE]
            extended[slot, a, EDGE:] = part[rows].astype(f32)
        send(mix_held.at[:, :, span], mixin.at[:, :, span])
        for i in range(4):
            a = lax.rem(i + 2 * core, 4)
            value = params[CONV_B : CONV_B + 1, lanes] + params[0:1, lanes] * extended[
                slot, a, EDGE - 3 : EDGE + 125
            ]
            for k in range(1, 4):
                value = value + params[k : k + 1, lanes] * extended[
                    slot, a, EDGE - 3 + k : EDGE + 125 + k
                ]
            value = (value * sigmoid(value)).astype(bf16)
            act_held[a, :, lanes] = value
            if chunk == 6:
                state_b[a] = value[:, :STATE].astype(f32).T.astype(bf16)
            else:
                wide = mm(scaled[a], spread[:, lanes])
                weighted = (wide * value.astype(f32)).astype(bf16)
                local = mm(state_b[a], weighted).astype(bf16)
                if i < 2:
                    mine_held[i, :, lanes] = local
                else:
                    send_held[i - 2, :, lanes] = local
        send(act_held.at[:, :, span], active.at[:, :, span])
        if chunk < 6:
            send(send_held.at[:, :, span], local_send.at[:, :, span])
            send(mine_held.at[:, :, span], local_mine.at[:, :, span])
    for copy in outgoing:
        copy.wait()


def pair_weights(p, scores, cumul, turned, same):
    made = []
    for h in (2 * p, 2 * p + 1):
        differ = cumul[:, h : h + 1] - turned[h : h + 1, :]
        decay = jnp.exp(jnp.where(same, differ, -1e30))
        made.append((decay, (scores * decay).astype(bf16)))
    return made


def inner_kernel(active, dt, cumul, same, spread, low_lanes, high_lanes, inner):
    b_low = active[0, :, INNER : INNER + STATE]
    c_low = active[0, :, INNER + STATE :]
    scores = mm_nt(c_low, b_low)
    total = cumul[0]
    turned = total.T
    allowed = same[0] > 0
    dt_low = dt[0].astype(bf16)
    for p in range(PAIRS):
        lanes = columns(p)
        (_, first), (_, second) = pair_weights(p, scores, total, turned, allowed)
        xdt = (mm(dt_low, spread[:, lanes]) * active[0, :, lanes].astype(f32)).astype(bf16)
        stacked = jnp.concatenate([xdt * low_lanes[...], xdt * high_lanes[...]], 0)
        inner[0, :, lanes] = mm(jnp.concatenate([first, second], 1), stacked)


def pick(where, kept, given, lanes):
    own = where[1] == pl.program_id(0) // 2
    return jnp.where(own, kept[0, :, lanes].astype(f32), given[0, :, lanes].astype(f32)).astype(bf16)


def middle_kernel(
    where, inner, active, kept, given, gates, g_mixed, cumul, keep, params, spread, gather,
    mixed, g_y, g_gates, row_part, skip_part, g_mine, g_send,
    y_held, recur_held, act_held, slope_held, enter_held, entered,
):
    a = pl.program_id(0)
    enter = (jnp.exp(cumul[0]) * keep[0]).astype(bf16)
    c_low = active[0, :, INNER + STATE :]
    squares = jnp.zeros((TOKENS, LANES), f32)
    products = jnp.zeros((TOKENS, LANES), f32)
    for p in range(PAIRS):
        lanes = columns(p)
        carried = mm(c_low, pick(where, kept, given, lanes))
        wide = mm(enter, spread[:, lanes])
        enter_held[:, lanes] = wide
        recur = inner[0, :, lanes] + wide * carried
        y = recur + params[SKIP_WIDE : SKIP_WIDE + 1, lanes] * active[0, :, lanes].astype(f32)
        gate = gates[0, :, lanes].astype(f32)
        unit_grad = g_mixed[0, :, lanes].astype(f32) * params[GATE_GAIN : GATE_GAIN + 1, lanes]
        sig = sigmoid(gate)
        act = gate * sig
        gated = y * act
        squares = squares + gated * gated
        products = products + unit_grad * gated
        y_held[:, lanes] = y
        recur_held[:, lanes] = recur
        act_held[:, lanes] = act
        slope_held[:, lanes] = sig + act * (1.0 - sig)
    scale = lax.rsqrt(jnp.sum(squares, 1, keepdims=True) * (1.0 / INNER) + epsilon)
    slant = scale * jnp.sum(products, 1, keepdims=True) * (1.0 / INNER)
    rows = jnp.zeros((TOKENS, LANES), f32)

    @pl.when(a == 0)
    def _():
        skip_part[...] = jnp.zeros_like(skip_part)

    for p in range(PAIRS):
        lanes = columns(p)
        y, act = y_held[:, lanes], act_held[:, lanes]
        unit = y * act * scale
        mixed[0, :, lanes] = (unit * params[GATE_GAIN : GATE_GAIN + 1, lanes]).astype(bf16)
        unit_grad = g_mixed[0, :, lanes].astype(f32) * params[GATE_GAIN : GATE_GAIN + 1, lanes]
        g_gated = scale * (unit_grad - unit * slant)
        grad = g_gated * act
        g_gates[0, :, lanes] = (g_gated * y * slope_held[:, lanes]).astype(bf16)
        low = grad.astype(bf16)
        g_y[0, :, lanes] = low
        low = low.astype(f32)
        rows = rows + sum_heads(low * recur_held[:, lanes], gather[lanes])
        share = grad * active[0, :, lanes].astype(f32)
        skip_part[:, lanes] += jnp.sum(share.reshape(16, 8, LANES), 0)
        entered[:, lanes] = (enter_held[:, lanes] * low).astype(bf16)
    row_part[0] = rows
    g_state = mm_tn(c_low, entered[...]).astype(bf16)

    here = where[1] == a // 2

    @pl.when(here)
    def _():
        g_mine[lax.rem(a, 2)] = g_state

    @pl.when(jnp.logical_not(here))
    def _():
        g_send[lax.rem(a, 2)] = g_state


def inner_back_kernel(
    where, active, g_y, kept, given, dt, cumul, keep, same, spread, gather, low_lanes, high_lanes,
    g_inner, g_b, g_c, direct, column, entered, state,
):
    b_low = active[0, :, INNER : INNER + STATE]
    c_low = active[0, :, INNER + STATE :]
    scores = mm_nt(c_low, b_low)
    total = cumul[0]
    turned = total.T
    allowed = same[0] > 0
    dt_low = dt[0].astype(bf16)
    enter = (jnp.exp(total) * keep[0]).astype(bf16)
    g_scores = jnp.zeros((TOKENS, TOKENS), f32)
    by_x = jnp.zeros((TOKENS, LANES), f32)
    by_xdt = jnp.zeros((TOKENS, LANES), f32)
    for p in range(PAIRS):
        lanes = columns(p)
        (decay_1, first), (decay_2, second) = pair_weights(p, scores, total, turned, allowed)
        x = active[0, :, lanes].astype(f32)
        xdt = (mm(dt_low, spread[:, lanes]) * x).astype(bf16)
        grad = g_y[0, :, lanes]
        entered[:, lanes] = (mm(enter, spread[:, lanes]) * grad.astype(f32)).astype(bf16)
        state[:, lanes] = pick(where, kept, given, lanes)
        stacked = jnp.concatenate([grad * low_lanes[...], grad * high_lanes[...]], 0)
        g_weights = mm_nt(stacked, xdt)
        g_scores = g_scores + g_weights[:TOKENS] * decay_1 + g_weights[TOKENS:] * decay_2
        own = mm_tn(jnp.concatenate([first, second], 0), stacked)
        g_inner[0, :, lanes] = own.astype(bf16)
        by_x = by_x + mm((x * own).astype(bf16), gather[lanes])
        by_xdt = by_xdt + sum_heads(xdt.astype(f32) * own, gather[lanes])
    direct[0] = by_x
    column[0] = by_xdt
    g_scores = g_scores.astype(bf16)
    g_c[0] = mm(g_scores, b_low) + mm_nt(entered[...], state[...])
    g_b[0] = mm_tn(g_scores, c_low)


def late_kernel(
    where, kept_end, given_end, kept, given, active, mixin, mixin_halo, g_y, g_inner, g_b, g_c,
    dt, dt_arg, cumul, ending, row_part, direct, column, through, params, spread, gather, upper,
    g_mix, g_halo, taps, head_sums,
    weighted, state, extended, padded, inner_row,
):
    a = pl.program_id(0)

    @pl.when(a == 0)
    def _():
        taps[...] = jnp.zeros_like(taps)
        head_sums[...] = jnp.zeros_like(head_sums)

    b_low = active[0, :, 0:STATE]
    decay_rate = params[DECAY : DECAY + 1, 0:LANES]
    total = cumul[0]
    steps = dt[0]
    to_end = jnp.exp(total[TOKENS - 1 :] - total) * ending[0]
    scaled = to_end * steps
    to_end_low = to_end.astype(bf16)
    scaled_low = scaled.astype(bf16)
    dt_low = steps.astype(bf16)
    through_state = jnp.zeros((TOKENS, LANES), f32)
    padded[:, 0:8] = jnp.zeros((2, 8, LANES), f32)
    padded[:, 136:144] = jnp.zeros((2, 8, LANES), f32)

    def convolved(chunk):
        lanes = columns(chunk)
        slot = chunk % 2
        extended[slot, 0:EDGE] = mixin_halo[0, :, lanes]
        extended[slot, EDGE:] = mixin[0, :, lanes].astype(f32)
        shifted = [extended[slot, EDGE - 3 + k : EDGE + 125 + k] for k in range(4)]
        value = params[CONV_B : CONV_B + 1, lanes]
        for k in range(4):
            value = value + params[k : k + 1, lanes] * shifted[k]
        return value, sigmoid(value), shifted

    def back(chunk, grad, value, sig, shifted):
        lanes = columns(chunk)
        slot = chunk % 2
        grad = grad * (sig * (1.0 + value * (1.0 - sig)))
        padded[slot, 8:136] = grad
        main = jnp.zeros((TOKENS, LANES), f32)
        edge = jnp.zeros((EDGE, LANES), f32)
        for k in range(4):
            tap = params[k : k + 1, lanes]
            main = main + tap * padded[slot, 11 - k : 139 - k]
            edge = edge + tap * padded[slot, 3 - k : 11 - k]
            taps[k : k + 1, lanes] += jnp.sum(grad * shifted[k], 0, keepdims=True)
        taps[4:5, lanes] += jnp.sum(grad, 0, keepdims=True)
        g_mix[0, :, lanes] = main.astype(bf16)
        g_halo[0, :, lanes] = edge

    for p in range(PAIRS):
        lanes = columns(p)
        end = pick(where, kept_end, given_end, lanes)
        begin = pick(where, kept, given, lanes)
        inner_row[0:1, lanes] = jnp.sum(begin.astype(f32) * end.astype(f32), 0, keepdims=True)
        state[:, lanes] = end
        from_state = mm(b_low, end)
        value, sig, shifted = convolved(p)
        x = (value * sig).astype(bf16).astype(f32)
        weighted[:, lanes] = (mm(scaled_low, spread[:, lanes]) * x).astype(bf16)
        grad = mm(dt_low, spread[:, lanes]) * (
            g_inner[0, :, lanes].astype(f32) + mm(to_end_low, spread[:, lanes]) * from_state
        ) + params[SKIP_WIDE : SKIP_WIDE + 1, lanes] * g_y[0, :, lanes].astype(f32)
        through_state = through_state + mm((x * from_state).astype(bf16), gather[lanes])
        back(p, grad, value, sig, shifted)
    state_part = scaled * through_state
    inner_sum = jnp.zeros((8, LANES), f32)
    for p in range(PAIRS):
        lanes = columns(p)
        inner_sum = inner_sum + sum_heads(inner_row[:, lanes], gather[lanes])
    mask = lax.broadcasted_iota(jnp.int32, (4, LANES), 0) == a
    flow = jnp.sum(jnp.where(mask, through[...], 0.0), 0, keepdims=True)
    at_end = jnp.sum(state_part, 0, keepdims=True) + flow * inner_sum[0:1]
    g_rate = exact_mm(upper[...], row_part[0] - column[0] - state_part) + at_end
    g_raw = direct[0] + to_end * through_state - decay_rate * g_rate
    g_raw = g_raw * sigmoid(dt_arg[0])
    head_sums[0:1] += jnp.sum(g_raw, 0, keepdims=True)
    head_sums[1:2] -= decay_rate * jnp.sum(steps * g_rate, 0, keepdims=True)
    g_mix[0, :, XBC:MIX_PAD] = g_raw.astype(bf16)
    g_mix[0, :, MIX_PAD:] = jnp.zeros((TOKENS, MIX_WIDE - MIX_PAD), bf16)
    back(PAIRS, g_b[0] + mm_nt(weighted[...], state[...]), *convolved(PAIRS))
    back(PAIRS + 1, g_c[0], *convolved(PAIRS + 1))


def early_grads_kernel(where, mixed, cotangent, normed_t, g_gates, mine, send):
    core = where[1]
    rows = pl.ds(pl.multiple_of(pl.program_id(0) * 192, 192), 192)
    of_gate = mm(normed_t[rows], g_gates[...])
    of_out = mm_tn(mixed[...], cotangent[...])
    gate_blocks, out_blocks = [], []
    for j in range(16):
        high, low = divmod(j, 4)
        span = slice(high * 48, (high + 1) * 48)
        gate_blocks.append(of_gate[span, columns(low, 384)].astype(bf16))
        part, side = divmod(low, 2)
        span = slice(part * 192 + high * 48, part * 192 + (high + 1) * 48)
        out_blocks.append(of_out[span, columns(side, 384)].astype(bf16))

    @pl.when(core == 0)
    def _():
        for j in range(16):
            mine[j, 0] = gate_blocks[j]
            send[j, 0] = out_blocks[j]

    @pl.when(core == 1)
    def _():
        for j in range(16):
            mine[j, 0] = out_blocks[j]
            send[j, 0] = gate_blocks[j]


def late_grads_kernel(where, normed_t, halo_t, g_mix, g_halo, taps, head_sums, skip_part, gather, mine, send):
    core = where[1]
    step = pl.program_id(0)
    g_edge = jnp.concatenate([g_halo[...], jnp.zeros((LANES - 32, 256), f32)], 0).astype(bf16)
    g_edge = jnp.where(step < 7, g_edge, jnp.zeros_like(g_edge))
    grad = mm(normed_t[...], g_mix[...]) + mm(halo_t[...], g_edge)
    nothing = jnp.zeros((16, LANES), bf16)

    def put(first, second):
        for jj in range(2):
            for z in range(4):
                for c, target in ((0, first), (1, second)):
                    top = 192 * z + 96 * c
                    target[jj, z, 0:96] = grad[top : top + 96, columns(jj)].astype(bf16)
                    target[jj, z, 96:112] = nothing

    @pl.when(core == 0)
    def _():
        put(mine, send)

    @pl.when(core == 1)
    def _():
        put(send, mine)

    def put_extra(target):
        lane = lax.broadcasted_iota(jnp.int32, (8, LANES), 1)
        for at in range(2):

            @pl.when(step == at)
            def _(at=at):
                for jj in range(2):
                    for z in range(4):
                        begin = 448 * z + LANES * (2 * at + jj)
                        tile = taps[:, begin // LANES * LANES : begin // LANES * LANES + LANES]
                        if begin % LANES:
                            after = min(begin // LANES + 1, XBC // LANES - 1) * LANES
                            tile = jnp.where(lane < 64, taps[:, after : after + LANES], tile)
                            tile = pltpu.roll(tile, 64, 1)
                        tile = jnp.concatenate([tile, jnp.zeros((8, LANES), f32)], 0)
                        target[jj, z, 96:112] = tile.astype(bf16)

        @pl.when(step == 2)
        def _():
            skips = sum_heads(skip_part[...], gather[...])
            row = lax.broadcasted_iota(jnp.int32, (8, LANES), 0)
            head_rows = jnp.where(row == 2, jnp.sum(skips, 0, keepdims=True), head_sums[...])
            tile = jnp.concatenate([head_rows, jnp.zeros((8, LANES), f32)], 0)
            for z in range(4):
                target[0, z, 96:112] = tile.astype(bf16)

    @pl.when(core == 0)
    def _():
        put_extra(mine)

    @pl.when(core == 1)
    def _():
        put_extra(send)


def both_cores(where, mine, other):
    first = where[1] == 0
    return jnp.where(first, mine, other), jnp.where(first, other, mine)


def join_kernel(where, mine, other, through, through_other, spread, total, wide):
    first = where[1] == 0
    own = jnp.where(first, through[0:2], through[2:4])
    theirs = jnp.where(first, through_other[0:2], through_other[2:4])
    through_0, through_1 = both_cores(where, own, theirs)
    high, middle, low = split_three(through_0 * through_1)
    rows = jnp.concatenate([through_0, through_1, jnp.zeros((4, LANES), f32)], 0)
    wide[...] = widen(halves(rows), spread[...])
    row = lax.broadcasted_iota(jnp.int32, (16, LANES), 0)
    for a in range(2):
        piece = jnp.where(row == 0, high[a : a + 1].astype(f32), 0.0)
        piece = jnp.where(row == 1, middle[a : a + 1].astype(f32), piece)
        piece = jnp.where(row == 2, low[a : a + 1].astype(f32), piece).astype(bf16)
        for part in range(8):
            span = slice(part * 16, (part + 1) * 16)
            state_0, state_1 = both_cores(
                where, mine[a, span].astype(f32), other[a, span].astype(f32)
            )
            value = wide[2 + a : 3 + a] * state_0 + state_1
            total[8 * a + part, :, 0:INNER] = value.astype(bf16)
            total[8 * a + part, :, INNER:] = piece


def split_kernel(where, back, mine, other, wide, kept, given):
    for a in range(2):
        for part in range(8):
            span = slice(part * 16, (part + 1) * 16)
            state_0, _ = both_cores(where, mine[a, span].astype(f32), other[a, span].astype(f32))
            in_0 = back[8 * a + part].astype(f32)
            in_1 = wide[a : a + 1] * in_0 + state_0
            keeps, gives = both_cores(where, in_0, in_1)
            kept[a, span] = keeps.astype(bf16)
            given[a, span] = gives.astype(bf16)


def join_back_kernel(where, mine, other, wide, total):
    for a in range(2):
        for part in range(8):
            span = slice(part * 16, (part + 1) * 16)
            g_0, g_1 = both_cores(where, mine[a, span].astype(f32), other[a, span].astype(f32))
            total[8 * a + part] = (g_0 + wide[a : a + 1] * g_1).astype(bf16)


def split_back_kernel(where, back, mine, other, wide, kept, given):
    for a in range(2):
        for part in range(8):
            span = slice(part * 16, (part + 1) * 16)
            _, g_1 = both_cores(where, mine[a, span].astype(f32), other[a, span].astype(f32))
            end_1 = back[8 * a + part].astype(f32)
            end_0 = g_1 + wide[2 + a : 3 + a] * end_1
            keeps, gives = both_cores(where, end_0, end_1)
            kept[a, span] = keeps.astype(bf16)
            given[a, span] = gives.astype(bf16)


def scan_kernel(arrived, spread, before, factors):
    for i in range(16):
        wide = mm(arrived[i, :, INNER:], spread[...])
        factors[i : i + 1] = wide[0:1] + wide[1:2] + wide[2:3]
    so_far = jnp.zeros((16, INNER), f32)
    for i in range(16):
        before[i] = so_far.astype(bf16)
        so_far = factors[i : i + 1] * so_far + arrived[i, :, :INNER].astype(f32)


def scan_back_kernel(arrived, factors, after):
    so_far = jnp.zeros((16, INNER), f32)
    for i in reversed(range(16)):
        after[i] = so_far.astype(bf16)
        so_far = factors[i : i + 1] * so_far + arrived[i].astype(f32)


def pair_kernel(mine, other, pair):
    pair[...] = (mine[...].astype(f32) + other[...].astype(f32)).astype(bf16)


def reduce_kernel(early, late, owned):
    total = early[0].astype(f32)
    for k in range(1, 64):
        total = total + early[k].astype(f32)
    held = [total[:, columns(k)].astype(bf16) for k in range(3)]
    total = late[0].astype(f32)
    for k in range(1, 64):
        total = total + late[k].astype(f32)
    total = total.astype(bf16)
    for copy in range(16):
        for k in range(3):
            owned[copy, 48 * k : 48 * (k + 1)] = held[k]
        owned[copy, 144:256] = total


def last_kernel(
    hidden, cotangent, mixed, g_gates, g_mix, spill, mix_weight, gate_weight, out_full, params,
    output, grad_hidden, held,
):
    x = hidden[0].astype(f32)
    output[0] = (x + mm(mixed[0], out_full[...])).astype(bf16)
    held[...] = g_mix[0, :, 0:MIX_PAD]
    end = g_mix[0, TOKENS - 16 :, 0:XBC].astype(f32)
    shift = jnp.concatenate([jnp.zeros((8, XBC), f32), spill[0].astype(f32)], 0)
    held[TOKENS - 16 :, 0:XBC] = (end + shift).astype(bf16)
    grad = mm_nt(held[...], mix_weight[...]) + mm_nt(g_gates[0], gate_weight[...])
    grad = grad * params[GAIN : GAIN + 1, 0:768]
    scale = lax.rsqrt(jnp.mean(x * x, axis=1, keepdims=True) + epsilon)
    pull = jnp.mean(grad * x, axis=1, keepdims=True)
    value = cotangent[0].astype(f32) + scale * grad - x * (scale * scale * scale * pull)
    grad_hidden[0] = value.astype(bf16)


def finish_kernel(
    where, shared, other, weight, gain, out_weight, gate_gain,
    grad, by_gain, conv_w, conv_b, by_head, grad_out, by_gate_gain,
):
    first = where[1] == 0
    for j in range(16):
        a, b = shared[j].astype(f32), other[j].astype(f32)
        low = jnp.where(first, a, b)
        high = jnp.where(first, b, a)
        up, right = divmod(j, 4)
        half, side = divmod(right, 2)
        for k in range(3):
            piece = slice(48 * k, 48 * (k + 1))
            grad[up * 48 : (up + 1) * 48, columns(3 * right + k)] = low[piece]
            grad_out[
                half * 192 + up * 48 : half * 192 + (up + 1) * 48, columns(3 * side + k)
            ] = high[piece]
        begin = INNER + LANES * j
        width = min(LANES, INNER + MIX - begin)
        if width > 0:
            grad[0:96, begin : begin + width] = low[144:240, 0:width]
            grad[96:192, begin : begin + width] = high[144:240, 0:width]
        if j < 4:
            span = min(LANES, 448 - LANES * j)
            conv_w[:, LANES * j : LANES * j + span] = low[240:244, 0:span]
            conv_b[:, LANES * j : LANES * j + span] = low[244:245, 0:span]
        if j == 4:
            by_head[...] = low[240:248]
    total = jnp.sum(grad[...] * weight[...].astype(f32), axis=1, keepdims=True)
    by_gain[...] = jnp.broadcast_to(total, (192, LANES)).T[0:8] / gain[...]
    total = jnp.sum(grad_out[...] * out_weight[...].astype(f32), axis=1, keepdims=True)
    by_gate_gain[...] = jnp.broadcast_to(total, (384, LANES)).T[0:8] / gate_gain[...]


def per_device(
    hidden,
    segments,
    norm_gain,
    in_weight,
    conv_weight,
    conv_bias,
    dt_bias,
    a_log,
    skip,
    gate_gain,
    out_weight,
    cotangent,
):
    core = lax.axis_index("seq_2")
    place = lax.axis_index("fsdp")
    chip = lax.axis_index("seq_0") * 4 + lax.axis_index("seq_1")
    where = jnp.stack([place, core, (chip * 2 + core) * TOKENS]).astype(jnp.int32)

    message, mix_shard = call(
        message_kernel,
        [(None, shaped((112, MIX_PAD), bf16)), (None, shaped((192, MIX_PAD), bf16))],
        [SCALARS] + [None] * 8,
        [
            where, in_weight, norm_gain, conv_weight, conv_bias, dt_bias, a_log, skip, gate_gain,
        ],
        scratch=[pltpu.VMEM((16, XBC), f32), pltpu.VMEM((192, LANES), f32)],
    )
    mix_fetched = fetch(message)
    halo = line(hidden[:, TOKENS - EDGE :], SEQ, 1)

    head_of = np.arange(INNER) // HEADDIM
    spread = jnp.asarray((np.arange(LANES)[:, None] == head_of[None]), bf16)
    gather = jnp.asarray((head_of[:, None] == np.arange(LANES)[None]), bf16)
    lower = jnp.asarray(np.tril(np.ones((TOKENS, TOKENS))), bf16)
    upper = jnp.asarray(np.triu(np.ones((TOKENS, TOKENS))), bf16)
    low_lanes = jnp.asarray(np.ones((TOKENS, 1)) * (np.arange(LANES) < 64), bf16)
    high_lanes = jnp.asarray(np.ones((TOKENS, 1)) * (np.arange(LANES) >= 64), bf16)

    tokens = shaped((4, TOKENS, LANES))
    same, keep, ending, passing, halo = call(
        tables_kernel,
        [
            (None, tokens), (None, tokens), (None, tokens), (None, shaped((4, LANES))),
            (None, shaped((4, EDGE, 768))),
        ],
        [SCALARS, None, None],
        [where, segments, halo],
        micros=2,
    )
    half = shaped((2, STATE, INNER), bf16)
    (
        params, mixin, mixin_halo, active, dt_arg, dt, cumul, through, local_mine, local_send,
        normed, normed_t, halo_t, mix_weight,
    ) = call(
        front_kernel,
        [
            (None, shaped((16, XBC))),
            (ANYWHERE, shaped((4, TOKENS, XBC), bf16)),
            (None, shaped((4, EDGE, XBC))),
            (ANYWHERE, shaped((4, TOKENS, XBC), bf16)),
            (None, tokens),
            (None, tokens),
            (None, tokens),
            (None, shaped((4, LANES))),
            (ANYWHERE, half),
            (ANYWHERE, half),
            (ANYWHERE, shaped((512, 768), bf16)),
            (ANYWHERE, shaped((768, 512), bf16)),
            (None, shaped((768, LANES), bf16)),
            (ANYWHERE, shaped((768, MIX_PAD), bf16)),
        ],
        [SCALARS] + [None] * 6 + [ANYWHERE] * 8,
        [where, hidden, halo, ending, passing, spread, lower, message, mix_shard]
        + mix_fetched
        + [swap(part) for part in mix_fetched],
        scratch=[
            pltpu.VMEM((768, MIX_PAD), bf16),
            pltpu.VMEM((4, 16, MIX_PAD), bf16),
            pltpu.VMEM((512, 768), bf16),
            pltpu.VMEM((768, 512), bf16),
            pltpu.VMEM((4, TOKENS, XBC), bf16),
            pltpu.VMEM((4, TOKENS, XBC), bf16),
            pltpu.VMEM((2, STATE, INNER), bf16),
            pltpu.VMEM((2, STATE, INNER), bf16),
            pltpu.VMEM((2, 4, EDGE + TOKENS, 256), f32),
            pltpu.VMEM((4, STATE, TOKENS), bf16),
            pltpu.VMEM((4, TOKENS, LANES), bf16),
            pltpu.SemaphoreType.DMA((11,)),
            pltpu.SemaphoreType.DMA((29,)),
        ],
        micros=10,
        mib=32,
    )

    blocks = shaped((16, 16, INNER), bf16)
    local_other = swap(local_send)
    through_other = swap(through)
    total, wide = call(
        join_kernel,
        [(None, shaped((16, 16, INNER + LANES), bf16)), (None, shaped((8, INNER)))],
        [SCALARS] + [None] * 5,
        [where, local_mine, local_other, through, through_other, spread],
        micros=2,
    )
    gate_half, out_half = call(
        halves_kernel,
        [(None, shaped((96, INNER), bf16)), (None, shaped((192, 768), bf16))],
        [SCALARS, ANYWHERE, ANYWHERE],
        [where, in_weight, out_weight],
        scratch=[pltpu.SemaphoreType.DMA((2,))],
        after=[total],
    )
    gate_fetched = fetch(gate_half)
    out_fetched = fetch(out_half)
    (inner,) = call(
        inner_kernel,
        [(by_seq(TOKENS, INNER), shaped((4, TOKENS, INNER)))],
        [
            by_seq(TOKENS, XBC), by_seq(TOKENS, LANES), by_seq(TOKENS, LANES),
            by_seq(TOKENS, TOKENS), constant(LANES, INNER), constant(TOKENS, LANES),
            constant(TOKENS, LANES),
        ],
        [active, dt, cumul, same, spread, low_lanes, high_lanes],
        grid=(4,),
        mib=LARGE,
        micros=4,
        after=[total],
    )
    before, factors = call(
        scan_kernel,
        [(None, blocks), (None, shaped((16, INNER)))],
        [None] * 2,
        [exchange(total, CHIPS), spread],
        micros=2,
        after=[inner] + gate_fetched + out_fetched,
    )
    gate_weight = assemble(gate_fetched, in_weight, INNER, where)
    out_full = assemble(out_fetched, out_weight, 768, where)
    gates = dot("sd,dk->sk", normed, gate_weight).astype(bf16).reshape(4, TOKENS, INNER)
    g_mixed = dot("asd,id->asi", cotangent, out_full).astype(bf16)
    kept, given = call(
        split_kernel,
        [(None, half), (None, half)],
        [SCALARS] + [None] * 4,
        [where, exchange(before, CHIPS), local_mine, local_other, wide],
        micros=2,
        after=[gates, g_mixed],
    )
    given = swap(given)

    mixed, g_y, g_gates, row_part, skip_part, g_mine, g_send = call(
        middle_kernel,
        [
            (by_seq(TOKENS, INNER), shaped((4, TOKENS, INNER), bf16)),
            (by_seq(TOKENS, INNER), shaped((4, TOKENS, INNER), bf16)),
            (by_seq(TOKENS, INNER), shaped((4, TOKENS, INNER), bf16)),
            (by_seq(TOKENS, LANES), tokens),
            (constant(8, INNER), shaped((8, INNER))),
            (constant(2, STATE, INNER), half),
            (constant(2, STATE, INNER), half),
        ],
        [
            by_seq(TOKENS, INNER), by_seq(TOKENS, XBC), own_half(STATE, INNER),
            other_half(STATE, INNER), by_seq(TOKENS, INNER), by_seq(TOKENS, INNER),
            by_seq(TOKENS, LANES), by_seq(TOKENS, LANES), constant(16, XBC),
            constant(LANES, INNER), constant(INNER, LANES),
        ],
        [inner, active, kept, given, gates, g_mixed, cumul, keep, params, spread, gather],
        scalars=where,
        grid=(4,),
        scratch=[pltpu.VMEM((TOKENS, INNER), f32)] * 5 + [pltpu.VMEM((TOKENS, INNER), bf16)],
        mib=LARGE,
        micros=11,
    )

    g_other = swap(g_send)
    (g_total,) = call(
        join_back_kernel,
        [(None, blocks)],
        [SCALARS] + [None] * 3,
        [where, g_mine, g_other, wide],
        micros=2,
    )
    g_inner, g_b, g_c, direct, column = call(
        inner_back_kernel,
        [
            (by_seq(TOKENS, INNER), shaped((4, TOKENS, INNER), bf16)),
            (by_seq(TOKENS, STATE), tokens),
            (by_seq(TOKENS, STATE), tokens),
            (by_seq(TOKENS, LANES), tokens),
            (by_seq(TOKENS, LANES), tokens),
        ],
        [
            by_seq(TOKENS, XBC), by_seq(TOKENS, INNER), own_half(STATE, INNER),
            other_half(STATE, INNER), by_seq(TOKENS, LANES), by_seq(TOKENS, LANES),
            by_seq(TOKENS, LANES), by_seq(TOKENS, TOKENS), constant(LANES, INNER),
            constant(INNER, LANES), constant(TOKENS, LANES), constant(TOKENS, LANES),
        ],
        [
            active, g_y, kept, given, dt, cumul, keep, same, spread, gather, low_lanes, high_lanes,
        ],
        scalars=where,
        grid=(4,),
        scratch=[pltpu.VMEM((TOKENS, INNER), bf16), pltpu.VMEM((STATE, INNER), bf16)],
        mib=LARGE,
        micros=11,
        after=[g_total],
    )
    (after,) = call(
        scan_back_kernel,
        [(None, blocks)],
        [None] * 2,
        [exchange(g_total, CHIPS), factors],
        micros=2,
        after=[g_inner],
    )

    early_spec = pl.BlockSpec((16, 1, 48, 384), lambda z: (0, z, 0, 0))
    early_shape = shaped((16, 4, 48, 384), bf16)
    early_mine, early_send = call(
        early_grads_kernel,
        [(early_spec, early_shape), (early_spec, early_shape)],
        [
            SCALARS, pl.BlockSpec((512, 384), lambda z: (0, z)), constant(512, 768),
            constant(768, 512), constant(512, INNER),
        ],
        [
            where, mixed.reshape(512, INNER), cotangent.reshape(512, 768), normed_t,
            g_gates.reshape(512, INNER),
        ],
        grid=(4,),
        mib=LARGE,
        micros=6,
        after=[after],
    )
    (early_pair,) = call(
        pair_kernel,
        [(pl.BlockSpec((4, 4, 48, 384), lambda i: (i, 0, 0, 0)), early_shape)],
        [pl.BlockSpec((4, 4, 48, 384), lambda i: (i, 0, 0, 0))] * 2,
        [early_mine, swap(early_send)],
        grid=(4,),
        micros=3,
    )
    kept_end, given_end = call(
        split_back_kernel,
        [(None, half), (None, half)],
        [SCALARS] + [None] * 4,
        [where, exchange(after, CHIPS), g_mine, g_other, wide],
        micros=2,
        after=[early_pair],
    )
    given_end = swap(given_end)
    early_parts = exchange(early_pair.reshape(64, 48, 384), COLUMNS)

    g_mix, g_halo, taps, head_sums = call(
        late_kernel,
        [
            (by_seq(TOKENS, MIX_WIDE), shaped((4, TOKENS, MIX_WIDE), bf16)),
            (by_seq(EDGE, XBC), shaped((4, EDGE, XBC))),
            (constant(8, XBC), shaped((8, XBC))),
            (constant(8, LANES), shaped((8, LANES))),
        ],
        [own_half(STATE, INNER), other_half(STATE, INNER)] * 2
        + [
            pl.BlockSpec((1, TOKENS, 256), lambda a, *_: (a, 0, 6)), by_seq(TOKENS, XBC),
            by_seq(EDGE, XBC), by_seq(TOKENS, INNER), by_seq(TOKENS, INNER),
            by_seq(TOKENS, STATE), by_seq(TOKENS, STATE),
        ]
        + [by_seq(TOKENS, LANES)] * 7
        + [
            constant(4, LANES), constant(16, XBC), constant(LANES, INNER), constant(INNER, LANES),
            constant(TOKENS, TOKENS),
        ],
        [
            kept_end, given_end, kept, given, active, mixin, mixin_halo, g_y, g_inner, g_b, g_c, dt,
            dt_arg, cumul, ending, row_part, direct, column, through, params, spread, gather, upper,
        ],
        scalars=where,
        grid=(4,),
        scratch=[
            pltpu.VMEM((TOKENS, INNER), bf16),
            pltpu.VMEM((STATE, INNER), bf16),
            pltpu.VMEM((2, EDGE + TOKENS, LANES), f32),
            pltpu.VMEM((2, 144, LANES), f32),
            pltpu.VMEM((8, INNER), f32),
        ],
        mib=LARGE,
        micros=16,
    )
    late_spec = pl.BlockSpec((2, 4, 112, LANES), lambda s: (s, 0, 0, 0))
    late_shape = shaped((16, 4, 112, LANES), bf16)
    late_mine, late_send = call(
        late_grads_kernel,
        [(late_spec, late_shape), (late_spec, late_shape)],
        [
            SCALARS, constant(768, 512), constant(768, LANES),
            pl.BlockSpec((512, 256), lambda s: (0, s)),
            pl.BlockSpec((32, 256), lambda s: (0, jnp.minimum(s, 6))),
            constant(8, XBC), constant(8, LANES), constant(8, INNER), constant(INNER, LANES),
        ],
        [
            where, normed_t, halo_t, g_mix.reshape(512, MIX_WIDE), g_halo.reshape(32, XBC), taps,
            head_sums, skip_part, gather,
        ],
        grid=(8,),
        mib=LARGE,
        micros=8,
    )
    spill = line(g_halo.astype(bf16), SEQ, -1)
    late_block = pl.BlockSpec((4, 4, 112, LANES), lambda i: (i, 0, 0, 0))
    (late_pair,) = call(
        pair_kernel,
        [(late_block, late_shape)],
        [late_block] * 2,
        [late_mine, swap(late_send)],
        grid=(4,),
        micros=2,
        after=[spill],
    )
    late_parts = exchange(late_pair.reshape(64, 112, LANES), COLUMNS)

    rows = by_seq(TOKENS, 768)
    output, grad_hidden = call(
        last_kernel,
        [(rows, shaped((4, TOKENS, 768), bf16)), (rows, shaped((4, TOKENS, 768), bf16))],
        [
            rows, rows, by_seq(TOKENS, INNER), by_seq(TOKENS, INNER), by_seq(TOKENS, MIX_WIDE),
            by_seq(EDGE, XBC), constant(768, MIX_PAD), constant(768, INNER), constant(INNER, 768),
            constant(16, XBC),
        ],
        [
            hidden, cotangent, mixed, g_gates, g_mix, spill, mix_weight, gate_weight, out_full,
            params,
        ],
        grid=(4,),
        scratch=[pltpu.VMEM((TOKENS, MIX_PAD), bf16)],
        mib=LARGE,
        micros=8,
        after=[late_pair],
    )

    (owned,) = call(
        reduce_kernel,
        [(None, shaped((16, 256, LANES), bf16))],
        [None, None],
        [early_parts, late_parts],
        micros=2,
        after=[output],
    )
    shared = exchange(owned, CHIPS)
    sum_in, by_gain, sum_conv_w, sum_conv_b, by_head, sum_out, by_gate_gain = call(
        finish_kernel,
        [
            (None, shaped((192, INNER + MIX))),
            (None, shaped((8, 192))),
            (None, shaped((4, 448))),
            (None, shaped((1, 448))),
            (None, shaped((8, LANES))),
            (None, shaped((384, 768))),
            (None, shaped((8, 384))),
        ],
        [SCALARS] + [None] * 6,
        [
            where, shared, swap(shared), in_weight, norm_gain.astype(f32).reshape(1, 192),
            out_weight, gate_gain.astype(f32).reshape(1, 384),
        ],
        micros=4,
    )
    by_head = lax.dynamic_slice(by_head, (0, place * 6), (3, 6))

    return (
        output,
        grad_hidden,
        by_gain[0],
        sum_in,
        sum_conv_w,
        sum_conv_b[0],
        by_head[0],
        by_head[1],
        by_head[2],
        by_gate_gain[0],
        sum_out,
    )


def solution(mesh):
    finer = Mesh(
        mesh.devices.reshape(4, 4, 2, mesh.shape["fsdp"]), ("seq_0", "seq_1", "seq_2", "fsdp")
    )
    in_specs = (
        P("fsdp", SEQ, None),
        P("fsdp", SEQ),
        P("fsdp"),
        P("fsdp", None),
        P(None, "fsdp"),
        P("fsdp"),
        P("fsdp"),
        P("fsdp"),
        P("fsdp"),
        P("fsdp"),
        P("fsdp", None),
        P("fsdp", SEQ, None),
    )
    out_specs = (
        P("fsdp", SEQ, None),
        P("fsdp", SEQ, None),
        P("fsdp"),
        P("fsdp", None),
        P(None, "fsdp"),
        P("fsdp"),
        P("fsdp"),
        P("fsdp"),
        P("fsdp"),
        P("fsdp"),
        P("fsdp", None),
    )
    return jax.shard_map(
        per_device, mesh=finer, in_specs=in_specs, out_specs=out_specs, check_vma=False
    )
```

```python
import functools

import jax
import jax.numpy as jnp
import numpy as np
from jax import lax
from jax.experimental import pallas as pl
from jax.experimental.pallas import tpu as pltpu
from jax.sharding import Mesh
from jax.sharding import PartitionSpec as P

INNER = 1536
HEADS = 24
HEADDIM = 64
STATE = 128
XBC = 1792
MIX = 1816
MIX_PAD = 1920
MIX_WIDE = 2048
EDGE = 8
TOKENS = 128
LANES = 128
PAIRS = 12
SEQ = ("seq_0", "seq_1", "seq_2")
CHIPS = ("seq_0", "seq_1")
COLUMNS = ("seq_0", "seq_1", "fsdp")

epsilon = 1e-05
bf16 = jnp.bfloat16
f32 = jnp.float32
VMEM_MIB = 24
LARGE = 60
LATE_PIECES = 4
COST = 1.1e9

CONV_W, CONV_B, GATE_GAIN, GAIN, DT_BIAS, DECAY, SKIP, SKIP_WIDE = 0, 4, 5, 6, 7, 8, 9, 10


def ring(value, axis, steps):
    count = lax.axis_size(axis)
    pairs = [(source, (source + steps) % count) for source in range(count)]
    return lax.ppermute(value, axis, pairs)


def line(value, axis, steps):
    count = lax.axis_size(axis)
    initial, last = (max(0, -steps), min(count, count - steps))
    return lax.ppermute(value, axis, [(source, source + steps) for source in range(initial, last)])


def swap(value):
    return ring(value, "seq_2", 1)


def dot(pattern, left, right):
    return jnp.einsum(pattern, left, right, preferred_element_type=f32)


def exchange(blocks, axes):
    return lax.all_to_all(blocks, axes, 0, 0, tiled=False)


def split_three(value):
    high = value.astype(bf16)
    rest = value - high.astype(f32)
    middle = rest.astype(bf16)
    low = (rest - middle.astype(f32)).astype(bf16)
    return high, middle, low


def mm(left, right):
    return lax.dot_general(left, right, (((1,), (0,)), ((), ())), preferred_element_type=f32)


def mm_nt(left, right):
    return lax.dot_general(left, right, (((1,), (1,)), ((), ())), preferred_element_type=f32)


def mm_tn(left, right):
    return lax.dot_general(left, right, (((0,), (0,)), ((), ())), preferred_element_type=f32)


def exact_mm(ones, value):
    high, middle, low = split_three(value)
    return mm(ones, high) + mm(ones, middle) + mm(ones, low)


def halves(value):
    high = value.astype(bf16)
    return high, (value - high.astype(f32)).astype(bf16)


def widen(pieces, spread):
    return mm(pieces[0], spread) + mm(pieces[1], spread)


def sum_heads(value, gather):
    high, low = halves(value)
    return mm(high, gather) + mm(low, gather)


def sigmoid(value):
    return 0.5 * jnp.tanh(0.5 * value) + 0.5


def call(
    kernel, outs, ins, operands, grid=None, scratch=(), micros=1, after=(), mib=VMEM_MIB, scalars=None,
    marked=False,
):
    whole = pl.BlockSpec(memory_space=pltpu.VMEM)
    lead = [] if scalars is None else [scalars]
    count = len(operands) + len(lead)
    if marked:
        outs = list(outs) + [(constant(8, LANES) if grid else None, shaped((8, LANES)))]
    first = count + len(after)
    last = first + len(outs) - marked

    def body(*refs):
        kernel(*refs[:count], *refs[first:last], *refs[last + marked :])
        if marked:
            refs[last][...] = jnp.zeros((8, LANES), f32)

    return pl.pallas_call(
        body,
        grid_spec=pltpu.PrefetchScalarGridSpec(
            num_scalar_prefetch=len(lead),
            grid=grid or (),
            in_specs=[spec or whole for spec in ins]
            + [pl.BlockSpec(memory_space=pl.ANY)] * len(after),
            out_specs=[spec or whole for spec, _ in outs],
            scratch_shapes=list(scratch),
        ),
        out_shape=[shape for _, shape in outs],
        compiler_params=pltpu.CompilerParams(vmem_limit_bytes=mib * 1024 * 1024),
        cost_estimate=pl.CostEstimate(
            flops=int(micros * COST), bytes_accessed=0, transcendentals=0
        ),
    )(*lead, *operands, *after)


def shaped(shape, dtype=f32):
    return jax.ShapeDtypeStruct(shape, dtype)


def by_seq(*shape):
    return pl.BlockSpec((1,) + shape, lambda a, *_: (a,) + (0,) * len(shape))


def constant(*shape):
    return pl.BlockSpec(shape, lambda a, *_: (0,) * len(shape))


def seq_first(*shape):
    return pl.BlockSpec(
        (1,) + shape, lambda a, *_: (jnp.minimum(a, 3),) + (0,) * len(shape)
    )


def own_half(*shape):
    return pl.BlockSpec(
        (1,) + shape,
        lambda a, where: (jnp.clip(a - 2 * where[1], 0, 1),) + (0,) * len(shape),
    )


def other_half(*shape):
    return pl.BlockSpec(
        (1,) + shape,
        lambda a, where: (jnp.clip(a - 2 + 2 * where[1], 0, 1),) + (0,) * len(shape),
    )


ANYWHERE = pl.BlockSpec(memory_space=pl.ANY)
SCALARS = pl.BlockSpec(memory_space=pltpu.SMEM)


def columns(index, width=LANES):
    return slice(index * width, (index + 1) * width)


def message_kernel(
    where, in_weight, norm_gain, conv_weight, conv_bias, dt_bias, a_log, skip, gate_gain,
    message, mix_shard, held, narrow,
):
    place, core = where[0], where[1]
    narrow[...] = jnp.zeros_like(narrow)
    narrow[:, 0 : MIX - XBC] = in_weight[:, INNER + XBC :].astype(f32)
    mix_shard[:, 0:XBC] = in_weight[:, INNER : INNER + XBC]
    mix_shard[:, XBC:] = narrow[...].astype(bf16)
    half = pl.ds(pl.multiple_of(core * 96, 96), 96)
    message[0:96, 0:XBC] = in_weight[half, INNER : INNER + XBC]
    message[0:96, XBC:] = narrow[half].astype(bf16)
    message[96:112, XBC:] = jnp.zeros((16, LANES), bf16)
    held[...] = jnp.zeros_like(held)
    held[CONV_W : CONV_W + 4, 0:448] = conv_weight[...].astype(f32)
    for target, source in (
        (CONV_B, conv_bias), (GATE_GAIN, gate_gain), (GAIN, norm_gain), (DT_BIAS, dt_bias),
        (DECAY, a_log), (SKIP, skip),
    ):
        size = source.shape[0]
        held[target : target + 1, 0:size] = source[...].astype(f32).reshape(1, size)
    row = lax.broadcasted_iota(jnp.int32, (16, 1), 0)
    for z in range(4):

        @pl.when(place == z)
        def _(z=z):
            value = held[...]
            if z:
                moved = pltpu.roll(value, 448 * z, 1)
                moved = jnp.where(row == GATE_GAIN, pltpu.roll(value, 384 * z, 1), moved)
                moved = jnp.where(row == GAIN, pltpu.roll(value, 192 * z, 1), moved)
                value = jnp.where(row >= DT_BIAS, pltpu.roll(value, 6 * z, 1), moved)
            message[96:112, 0:XBC] = value.astype(bf16)


def tables_kernel(where, segments, halo, same, keep, ending, passing, halo_held):
    start = where[2].astype(f32)
    below = lax.broadcasted_iota(jnp.int32, (TOKENS, TOKENS), 0) >= lax.broadcasted_iota(
        jnp.int32, (TOKENS, TOKENS), 1
    )
    for a in range(4):
        row = jnp.broadcast_to(segments[a : a + 1].astype(f32), (TOKENS, TOKENS))
        column = row.T
        first, last = column[0:1], column[TOKENS - 1 :]
        same[a] = jnp.where((column == row) & below, 1.0, 0.0)
        keep[a] = jnp.where((column == first) & (first < start), 1.0, 0.0)
        ending[a] = jnp.where(column == last, 1.0, 0.0)
        passing[a : a + 1] = jnp.where(last < start, 1.0, 0.0)
        halo_held[a] = halo[a].astype(f32)


def second_message_kernel(where, in_weight, out_weight, message, sems):
    core = where[1]
    low = pl.multiple_of(core * 192, 192)
    copies = [
        pltpu.make_async_copy(
            in_weight.at[pl.ds(pl.multiple_of(core * 96, 96), 96), pl.ds(0, INNER)],
            message.at[pl.ds(0, 96)],
            sems.at[0],
        )
    ]
    for k in range(2):
        copies.append(
            pltpu.make_async_copy(
                out_weight.at[pl.ds(low + 96 * k, 96)],
                message.at[pl.ds(96, 96), pl.ds(768 * k, 768)],
                sems.at[1 + k],
            )
        )
    for copy in copies:
        copy.start()
    for copy in copies:
        copy.wait()


def weights_kernel(
    where, normed, cotangent, in_weight, out_weight, m_1, m_2, m_3, o_1, o_2, o_3,
    gate_full, out_full, gates, g_mixed,
    gate_held, out_held, gates_held, g_held, in_sems, out_sems,
):
    place, core = where[0], where[1]
    gate_copies = weight_copies(
        place, core, in_weight.at[:, pl.ds(0, INNER)], (m_1, m_2, m_3), (o_1, o_2, o_3), gate_held,
        in_sems,
    )
    out_copies = [
        pltpu.make_async_copy(
            out_weight, out_held.at[pl.ds(pl.multiple_of(place * 384, 384), 384)], in_sems.at[7]
        )
    ]
    for k, (mine, other) in enumerate(((m_1, o_1), (m_2, o_2), (m_3, o_3))):
        owner = lax.rem(place + (1 + k), 4) * 384
        for which, part in ((core, mine), (1 - core, other)):
            for side in range(2):
                begin = pl.multiple_of(owner + which * 192 + 96 * side, 96)
                out_copies.append(
                    pltpu.make_async_copy(
                        part.at[pl.ds(96, 96), pl.ds(768 * side, 768)],
                        out_held.at[pl.ds(begin, 96)],
                        in_sems.at[7 + len(out_copies)],
                    )
                )
    for copy in gate_copies + out_copies:
        copy.start()
    outgoing = []

    def send(source, target):
        copy = pltpu.make_async_copy(source, target, out_sems.at[len(outgoing)])
        copy.start()
        outgoing.append(copy)

    for copy in gate_copies:
        copy.wait()
    for chunk in range(6):
        lanes, span = columns(chunk, 256), pl.ds(chunk * 256, 256)
        gates_held[:, lanes] = mm(normed[...], gate_held[:, lanes]).astype(bf16)
        send(gates_held.at[:, span], gates.at[:, span])
    send(gate_held, gate_full)
    for copy in out_copies:
        copy.wait()
    for chunk in range(6):
        lanes, span = columns(chunk, 256), pl.ds(chunk * 256, 256)
        g_held[:, lanes] = mm_nt(cotangent[...], out_held[lanes]).astype(bf16)
        send(g_held.at[:, span], g_mixed.at[:, span])
    send(out_held, out_full)
    for copy in outgoing:
        copy.wait()


def fetch(half):
    return [ring(half, "fsdp", steps) for steps in (3, 2, 1)]


def weight_copies(place, core, shard, mine, others, full, sems):
    rows = shard.shape[0]
    half = rows // 2
    copies = [
        pltpu.make_async_copy(
            shard, full.at[pl.ds(pl.multiple_of(place * rows, rows), rows)], sems.at[0]
        )
    ]
    for k in range(3):
        owner = lax.rem(place + (1 + k), 4) * rows
        low = pl.multiple_of(owner + core * half, half)
        high = pl.multiple_of(owner + (1 - core) * half, half)
        for slot, part, begin in ((1 + 2 * k, mine[k], low), (2 + 2 * k, others[k], high)):
            copies.append(
                pltpu.make_async_copy(
                    part.at[pl.ds(0, half)], full.at[pl.ds(begin, half)], sems.at[slot]
                )
            )
    return copies


def front_kernel(
    where, hidden, halo, ending, passing, spread, lower, own, shard, m_1, m_2, m_3, o_1, o_2, o_3,
    params, mixin, mixin_halo, active, dt_arg, dt, cumul, through, local_mine, local_send,
    normed, normed_t, halo_t, full,
    weight, packed, x_low, x_turned, mix_held, act_held, local_held,
    extended, state_b, scaled, wide_held, in_sems, out_sems,
):
    place, core = where[0], where[1]
    incoming = weight_copies(
        place, core, shard, (m_1, m_2, m_3), (o_1, o_2, o_3), weight, in_sems
    )
    rows_in = [
        pltpu.make_async_copy(part.at[pl.ds(96, 16)], packed.at[k], in_sems.at[7 + k])
        for k, part in enumerate((own, m_1, m_2, m_3))
    ]
    for copy in rows_in + incoming:
        copy.start()
    outgoing = []

    def send(source, target):
        copy = pltpu.make_async_copy(source, target, out_sems.at[len(outgoing)])
        copy.start()
        outgoing.append(copy)

    for copy in rows_in:
        copy.wait()
    whole = packed[0].astype(f32) + packed[1].astype(f32)
    whole = (whole + packed[2].astype(f32) + packed[3].astype(f32))[:, 0:XBC]
    params[...] = whole
    decay_rate = jnp.exp(whole[DECAY : DECAY + 1, 0:LANES])
    params[DECAY : DECAY + 1, 0:LANES] = decay_rate
    params[SKIP_WIDE : SKIP_WIDE + 1, 0:INNER] = mm(
        whole[SKIP : SKIP + 1, 0:LANES].astype(bf16), spread[...]
    )
    gain = whole[GAIN : GAIN + 1, 0:768]

    def normalised(value):
        scale = lax.rsqrt(jnp.mean(value * value, axis=1, keepdims=True) + epsilon)
        return value * scale * gain

    edges = []
    for a in range(4):
        value = normalised(hidden[a].astype(f32))
        x_low[a * TOKENS : (a + 1) * TOKENS] = value.astype(bf16)
        x_turned[:, a * TOKENS : (a + 1) * TOKENS] = value.T.astype(bf16)
        edges.append(normalised(halo[a]))
    send(x_low, normed)
    send(x_turned, normed_t)
    edges = jnp.concatenate(edges, 0)
    edge_low = edges.astype(bf16)
    edges = jnp.concatenate([edges, jnp.zeros((LANES - 32, 768), f32)], 0)
    halo_t[...] = edges.T.astype(bf16)

    for copy in incoming:
        copy.wait()
    send(weight, full)
    argument = mm(x_low[...], weight[:, XBC:]) + whole[DT_BIAS : DT_BIAS + 1, 0:LANES]
    steps = jnp.maximum(argument, 0.0) + jnp.log1p(jnp.exp(-jnp.abs(argument)))
    for a in range(4):
        rows = slice(a * TOKENS, (a + 1) * TOKENS)
        dt_arg[a] = argument[rows]
        dt[a] = steps[rows]
        total = exact_mm(lower[...], -steps[rows] * decay_rate)
        cumul[a] = total
        final = total[TOKENS - 1 :]
        through[a : a + 1] = jnp.exp(final) * passing[a : a + 1]
        scaled[rows] = (jnp.exp(final - total) * ending[a] * steps[rows]).astype(bf16)
    order = (6, 0, 1, 2, 3, 4, 5)

    def project(turn, a):
        chunk, slot = order[turn], turn % 2
        lanes = columns(chunk, 256)
        rows = slice(a * TOKENS, (a + 1) * TOKENS)
        if a == 0:
            edge = mm(edge_low, weight[:, lanes]).astype(bf16).astype(f32)
            for b in range(4):
                mixin_halo[b, :, lanes] = edge[b * EDGE : (b + 1) * EDGE]
                for side in range(2):
                    extended[slot, 2 * b + side, 0:EDGE] = edge[
                        b * EDGE : (b + 1) * EDGE, columns(side)
                    ]
        part = mm(x_low[rows], weight[:, lanes]).astype(bf16)
        mix_held[a, :, lanes] = part
        part = part.astype(f32)
        for side in range(2):
            extended[slot, 2 * a + side, EDGE:] = part[:, columns(side)]
        if chunk < 6:
            wide_held[slot, rows] = mm(scaled[rows], spread[:, lanes])

    def convolve(turn, a):
        chunk, slot = order[turn], turn % 2
        for side in range(2):
            lanes = columns(2 * chunk + side)
            at = 2 * a + side
            value = params[CONV_B : CONV_B + 1, lanes]
            for k in range(4):
                value = value + params[k : k + 1, lanes] * extended[
                    slot, at, EDGE - 3 + k : EDGE + 125 + k
                ]
            value = (value * sigmoid(value)).astype(bf16)
            act_held[a, :, lanes] = value
            if chunk == 6:
                if side == 0:
                    state_b[a] = value.astype(f32).T.astype(bf16)
            else:
                wide = wide_held[slot, a * TOKENS : (a + 1) * TOKENS, columns(side)]
                weighted = (wide * value.astype(f32)).astype(bf16)
                local_held[a, :, lanes] = mm(state_b[a], weighted).astype(bf16)

    for a in range(4):
        project(0, a)
    for turn, chunk in enumerate(order):
        span = pl.ds(chunk * 256, 256)
        send(mix_held.at[:, :, span], mixin.at[:, :, span])
        for a in range(4):
            if turn < 6:
                project(turn + 1, a)
            convolve(turn, a)
        send(act_held.at[:, :, span], active.at[:, :, span])
        if chunk < 6:
            own, given = pl.ds(2 * core, 2), pl.ds(2 - 2 * core, 2)
            send(local_held.at[given, :, span], local_send.at[:, :, span])
            send(local_held.at[own, :, span], local_mine.at[:, :, span])
    for copy in outgoing:
        copy.wait()


def pair_weights(p, scores, cumul, turned, same):
    made = []
    for h in (2 * p, 2 * p + 1):
        differ = cumul[:, h : h + 1] - turned[h : h + 1, :]
        decay = jnp.exp(jnp.where(same, differ, -1e30))
        made.append((decay, (scores * decay).astype(bf16)))
    return made


def inner_kernel(active, dt, cumul, same, spread, low_lanes, high_lanes, inner, dt_wide):
    b_low = active[0, :, INNER : INNER + STATE]
    c_low = active[0, :, INNER + STATE :]
    scores = mm_nt(c_low, b_low)
    total = cumul[0]
    turned = total.T
    allowed = same[0] > 0
    dt_wide[...] = mm(dt[0].astype(bf16), spread[...])
    for p in range(PAIRS):
        lanes = columns(p)
        (_, first), (_, second) = pair_weights(p, scores, total, turned, allowed)
        xdt = (dt_wide[:, lanes] * active[0, :, lanes].astype(f32)).astype(bf16)
        stacked = jnp.concatenate([xdt * low_lanes[...], xdt * high_lanes[...]], 0)
        inner[0, :, lanes] = mm(jnp.concatenate([first, second], 1), stacked)


def pick(where, kept, given, use):
    own = where[1] == pl.program_id(0) // 2

    @pl.when(own)
    def _():
        use(kept)

    @pl.when(jnp.logical_not(own))
    def _():
        use(given)


def pick_lanes(where, kept, given, lanes):
    own = where[1] == pl.program_id(0) // 2
    return jnp.where(own, kept[0, :, lanes].astype(f32), given[0, :, lanes].astype(f32)).astype(bf16)


def middle_kernel(
    where, inner, active, kept, given, gates, g_mixed, cumul, keep, params, spread, gather,
    mixed, g_y, g_gates, row_part, skip_part, g_mine, g_send,
    y_held, recur_held, act_held, slope_held, enter_held, entered,
):
    a = pl.program_id(0)
    enter = (jnp.exp(cumul[0]) * keep[0]).astype(bf16)
    c_low = active[0, :, INNER + STATE :]
    squares = jnp.zeros((TOKENS, LANES), f32)
    products = jnp.zeros((TOKENS, LANES), f32)
    for p in range(PAIRS):
        lanes = columns(p)
        carried = mm(c_low, pick_lanes(where, kept, given, lanes))
        wide = mm(enter, spread[:, lanes])
        enter_held[:, lanes] = wide
        recur = inner[0, :, lanes] + wide * carried
        y = recur + params[SKIP_WIDE : SKIP_WIDE + 1, lanes] * active[0, :, lanes].astype(f32)
        gate = gates[0, :, lanes].astype(f32)
        unit_grad = g_mixed[0, :, lanes].astype(f32) * params[GATE_GAIN : GATE_GAIN + 1, lanes]
        sig = sigmoid(gate)
        act = gate * sig
        gated = y * act
        squares = squares + gated * gated
        products = products + unit_grad * gated
        y_held[:, lanes] = y
        recur_held[:, lanes] = recur
        act_held[:, lanes] = act
        slope_held[:, lanes] = sig + act * (1.0 - sig)
    scale = lax.rsqrt(jnp.sum(squares, 1, keepdims=True) * (1.0 / INNER) + epsilon)
    slant = scale * jnp.sum(products, 1, keepdims=True) * (1.0 / INNER)
    rows = jnp.zeros((TOKENS, LANES), f32)

    @pl.when(a == 0)
    def _():
        skip_part[...] = jnp.zeros_like(skip_part)

    for p in range(PAIRS):
        lanes = columns(p)
        y, act = y_held[:, lanes], act_held[:, lanes]
        unit = y * act * scale
        mixed[0, :, lanes] = (unit * params[GATE_GAIN : GATE_GAIN + 1, lanes]).astype(bf16)
        unit_grad = g_mixed[0, :, lanes].astype(f32) * params[GATE_GAIN : GATE_GAIN + 1, lanes]
        g_gated = scale * (unit_grad - unit * slant)
        grad = g_gated * act
        g_gates[0, :, lanes] = (g_gated * y * slope_held[:, lanes]).astype(bf16)
        low = grad.astype(bf16)
        g_y[0, :, lanes] = low
        low = low.astype(f32)
        rows = rows + sum_heads(low * recur_held[:, lanes], gather[lanes])
        share = grad * active[0, :, lanes].astype(f32)
        skip_part[:, lanes] += jnp.sum(share.reshape(16, 8, LANES), 0)
        entered[:, lanes] = (enter_held[:, lanes] * low).astype(bf16)
    row_part[0] = rows
    g_state = mm_tn(c_low, entered[...]).astype(bf16)

    here = where[1] == a // 2

    @pl.when(here)
    def _():
        g_mine[0] = g_state

    @pl.when(jnp.logical_not(here))
    def _():
        g_send[0] = g_state


def inner_back_kernel(
    where, active, g_y, kept, given, dt, cumul, keep, same, spread, gather, low_lanes, high_lanes,
    g_inner, g_b, g_c, direct, column,
    dt_wide, enter_wide, entered, by_x, column_high, column_low,
):
    b_low = active[0, :, INNER : INNER + STATE]
    c_low = active[0, :, INNER + STATE :]
    scores = mm_nt(c_low, b_low)
    total = cumul[0]
    turned = total.T
    allowed = same[0] > 0
    dt_wide[...] = mm(dt[0].astype(bf16), spread[...])
    enter_wide[...] = mm((jnp.exp(total) * keep[0]).astype(bf16), spread[...])
    g_scores = jnp.zeros((TOKENS, TOKENS), f32)
    for p in range(PAIRS):
        lanes = columns(p)
        (decay_1, first), (decay_2, second) = pair_weights(p, scores, total, turned, allowed)
        x = active[0, :, lanes].astype(f32)
        xdt = (dt_wide[:, lanes] * x).astype(bf16)
        grad = g_y[0, :, lanes]
        entered[:, lanes] = (enter_wide[:, lanes] * grad.astype(f32)).astype(bf16)
        stacked = jnp.concatenate([grad * low_lanes[...], grad * high_lanes[...]], 0)
        g_weights = mm_nt(stacked, xdt)
        g_scores = g_scores + g_weights[:TOKENS] * decay_1 + g_weights[TOKENS:] * decay_2
        own = mm_tn(jnp.concatenate([first, second], 0), stacked)
        g_inner[0, :, lanes] = own.astype(bf16)
        by_x[:, lanes] = (x * own).astype(bf16)
        column_high[:, lanes], column_low[:, lanes] = halves(xdt.astype(f32) * own)
    direct[0] = mm(by_x[...], gather[...])
    column[0] = mm(column_high[...], gather[...]) + mm(column_low[...], gather[...])
    g_scores = g_scores.astype(bf16)
    from_scores = mm(g_scores, b_low)

    def add_state(state):
        g_c[0] = from_scores + mm_nt(entered[...], state[0])

    pick(where, kept, given, add_state)
    g_b[0] = mm_tn(g_scores, c_low)


def late_rows(
    where, kept_end, given_end, kept, given, active, mixin, mixin_halo, g_y, g_inner, g_b, g_c,
    dt, dt_arg, cumul, ending, row_part, direct, column, through, params, spread, gather, upper,
    g_mix, g_halo, taps, head_sums,
    weighted, state, extended, padded, inner_row,
):
    a = pl.program_id(0)

    @pl.when(a == 0)
    def _():
        taps[...] = jnp.zeros_like(taps)
        head_sums[...] = jnp.zeros_like(head_sums)

    b_low = active[0, :, 0:STATE]
    decay_rate = params[DECAY : DECAY + 1, 0:LANES]
    total = cumul[0]
    steps = dt[0]
    to_end = jnp.exp(total[TOKENS - 1 :] - total) * ending[0]
    scaled = to_end * steps
    to_end_low = to_end.astype(bf16)
    scaled_low = scaled.astype(bf16)
    dt_low = steps.astype(bf16)
    through_state = jnp.zeros((TOKENS, LANES), f32)
    padded[:, 0:8] = jnp.zeros((2, 8, LANES), f32)
    padded[:, 136:144] = jnp.zeros((2, 8, LANES), f32)

    def convolved(chunk):
        lanes = columns(chunk)
        slot = chunk % 2
        extended[slot, 0:EDGE] = mixin_halo[0, :, lanes]
        extended[slot, EDGE:] = mixin[0, :, lanes].astype(f32)
        shifted = [extended[slot, EDGE - 3 + k : EDGE + 125 + k] for k in range(4)]
        value = params[CONV_B : CONV_B + 1, lanes]
        for k in range(4):
            value = value + params[k : k + 1, lanes] * shifted[k]
        return value, sigmoid(value), shifted

    def back(chunk, grad, value, sig, shifted):
        lanes = columns(chunk)
        slot = chunk % 2
        grad = grad * (sig * (1.0 + value * (1.0 - sig)))
        padded[slot, 8:136] = grad
        main = jnp.zeros((TOKENS, LANES), f32)
        edge = jnp.zeros((EDGE, LANES), f32)
        for k in range(4):
            tap = params[k : k + 1, lanes]
            main = main + tap * padded[slot, 11 - k : 139 - k]
            edge = edge + tap * padded[slot, 3 - k : 11 - k]
            taps[k : k + 1, lanes] += jnp.sum(grad * shifted[k], 0, keepdims=True)
        taps[4:5, lanes] += jnp.sum(grad, 0, keepdims=True)
        g_mix[0, :, lanes] = main.astype(bf16)
        g_halo[0, :, lanes] = edge

    for p in range(PAIRS):
        lanes = columns(p)
        end = pick_lanes(where, kept_end, given_end, lanes)
        begin = pick_lanes(where, kept, given, lanes)
        inner_row[0:1, lanes] = jnp.sum(begin.astype(f32) * end.astype(f32), 0, keepdims=True)
        state[:, lanes] = end
        from_state = mm(b_low, end)
        value, sig, shifted = convolved(p)
        x = (value * sig).astype(bf16).astype(f32)
        weighted[:, lanes] = (mm(scaled_low, spread[:, lanes]) * x).astype(bf16)
        grad = mm(dt_low, spread[:, lanes]) * (
            g_inner[0, :, lanes].astype(f32) + mm(to_end_low, spread[:, lanes]) * from_state
        ) + params[SKIP_WIDE : SKIP_WIDE + 1, lanes] * g_y[0, :, lanes].astype(f32)
        through_state = through_state + mm((x * from_state).astype(bf16), gather[lanes])
        back(p, grad, value, sig, shifted)
    state_part = scaled * through_state
    inner_sum = jnp.zeros((8, LANES), f32)
    for p in range(PAIRS):
        lanes = columns(p)
        inner_sum = inner_sum + sum_heads(inner_row[:, lanes], gather[lanes])
    mask = lax.broadcasted_iota(jnp.int32, (4, LANES), 0) == a
    flow = jnp.sum(jnp.where(mask, through[...], 0.0), 0, keepdims=True)
    at_end = jnp.sum(state_part, 0, keepdims=True) + flow * inner_sum[0:1]
    g_rate = exact_mm(upper[...], row_part[0] - column[0] - state_part) + at_end
    g_raw = direct[0] + to_end * through_state - decay_rate * g_rate
    g_raw = g_raw * sigmoid(dt_arg[0])
    head_sums[0:1] += jnp.sum(g_raw, 0, keepdims=True)
    head_sums[1:2] -= decay_rate * jnp.sum(steps * g_rate, 0, keepdims=True)
    g_mix[0, :, XBC:MIX_PAD] = g_raw.astype(bf16)
    g_mix[0, :, MIX_PAD:] = jnp.zeros((TOKENS, MIX_WIDE - MIX_PAD), bf16)
    back(PAIRS, g_b[0] + mm_nt(weighted[...], state[...]), *convolved(PAIRS))
    back(PAIRS + 1, g_c[0], *convolved(PAIRS + 1))


def early_rows(kind, step, where, mixed, cotangent, normed_t, g_gates, use):
    @pl.when(kind == 0)
    def _():
        rows = pl.ds(pl.multiple_of(lax.rem(where[0] + step, 4) * 192, 192), 192)
        use(mm(normed_t[rows], g_gates[...]).astype(bf16))

    @pl.when(kind == 1)
    def _():
        grad = mm_tn(mixed[...], cotangent[...])
        use(jnp.concatenate([grad[0:192], grad[192:384]], 1).astype(bf16))


def early_send_kernel(
    where, mixed, cotangent, normed_t, g_gates, send_0, send_1, send_2, send_3, held, sems
):
    step = pl.program_id(0)

    def use(value):
        held[step] = value

    early_rows(1 - where[1], step, where, mixed, cotangent, normed_t, g_gates, use)
    copies = [
        pltpu.make_async_copy(held.at[k], target, sems.at[k])
        for k, target in enumerate((send_0, send_1, send_2, send_3))
    ]
    for k in range(4):

        @pl.when(step == k)
        def _(k=k):
            copies[k].start()

    @pl.when(step == 3)
    def _():
        for copy in copies:
            copy.wait()


def early_own_kernel(where, mixed, cotangent, normed_t, g_gates, mine):
    def use(value):
        mine[...] = value

    early_rows(where[1], pl.program_id(0), where, mixed, cotangent, normed_t, g_gates, use)


def early_pair_kernel(mine, *rest):
    for k in range(4):
        rows = slice(192 * k, 192 * (k + 1))
        rest[4 + k][...] = (mine[rows].astype(f32) + rest[k][...].astype(f32)).astype(bf16)


def sum_blocks_kernel(a, b, c, d, total):
    for high in range(4):
        rows = slice(48 * high, 48 * (high + 1))
        value = a[rows].astype(f32) + b[rows].astype(f32) + c[rows].astype(f32) + d[rows].astype(f32)
        for low in range(4):
            total[4 * high + low] = value[:, columns(low, 384)].astype(bf16)


def late_columns(
    core, step, normed_t, halo_t, g_held, g_halo, taps, head_sums, skip_part, gather, mine, sends,
    held, sent, sems,
):
    lanes = pl.ds(pl.multiple_of(step * 256, 256), 256)
    g_mix = g_held[:, lanes]
    g_edge = jnp.concatenate([g_halo[:, lanes], jnp.zeros((LANES - 32, 256), f32)], 0).astype(bf16)
    for z in range(4):
        rows = slice(192 * z, 192 * (z + 1))
        grad = (mm(normed_t[rows], g_mix) + mm(halo_t[rows], g_edge)).astype(bf16)
        for c in range(2):
            for jj in range(2):
                held[c, jj, z] = grad[96 * c : 96 * (c + 1), columns(jj)]

    @pl.when(step == 7)
    def _():
        lane = lax.broadcasted_iota(jnp.int32, (8, LANES), 1)
        row = lax.broadcasted_iota(jnp.int32, (8, LANES), 0)
        nothing = jnp.zeros((8, LANES), f32)
        skips = sum_heads(skip_part[...], gather[...])
        head_rows = jnp.where(row == 2, jnp.sum(skips, 0, keepdims=True), head_sums[...])
        for z in range(4):
            for part in range(5):
                tile = head_rows
                if part < 4:
                    begin = 448 * z + LANES * part
                    tile = taps[:, begin // LANES * LANES : begin // LANES * LANES + LANES]
                    if begin % LANES:
                        after = min(begin // LANES + 1, XBC // LANES - 1) * LANES
                        tile = jnp.where(lane < 64, taps[:, after : after + LANES], tile)
                        tile = pltpu.roll(tile, 64, 1)
                tile = jnp.concatenate([tile, nothing], 0)
                held[0, 1, z, 16 * part : 16 * (part + 1)] = tile.astype(bf16)

    mine[...] = held[core]
    sent[pl.ds(2 * step, 2)] = held[1 - core]
    count = 16 // LATE_PIECES
    copies = [
        pltpu.make_async_copy(sent.at[pl.ds(count * k, count)], target, sems.at[k])
        for k, target in enumerate(sends)
    ]
    for k in range(LATE_PIECES):

        @pl.when(step == (k + 1) * (8 // LATE_PIECES) - 1)
        def _(k=k):
            copies[k].start()

    @pl.when(step == 7)
    def _():
        for copy in copies:
            copy.wait()


def late_kernel(
    where, kept_end, given_end, kept, given, active, mixin, mixin_halo, g_y, g_inner, g_b, g_c,
    dt, dt_arg, cumul, ending, row_part, direct, column, through, params, spread, gather, upper,
    normed_t, halo_t, skip_part,
    g_mix, g_halo, mine, send_0, send_1, send_2, send_3,
    weighted, state, extended, padded, inner_row, g_held, halo_held, taps, head_sums, held, sent,
    sems,
):
    step = pl.program_id(0)

    @pl.when(step < 4)
    def _():
        late_rows(
            where, kept_end, given_end, kept, given, active, mixin, mixin_halo, g_y, g_inner, g_b,
            g_c, dt, dt_arg, cumul, ending, row_part, direct, column, through, params, spread,
            gather, upper, g_mix, g_halo, taps, head_sums,
            weighted, state, extended, padded, inner_row,
        )
        g_held[pl.ds(pl.multiple_of(step * TOKENS, TOKENS), TOKENS)] = g_mix[0]
        halo_held[pl.ds(pl.multiple_of(step * EDGE, EDGE), EDGE), 0:XBC] = g_halo[0]
        halo_held[pl.ds(pl.multiple_of(step * EDGE, EDGE), EDGE), XBC:] = jnp.zeros(
            (EDGE, MIX_WIDE - XBC), f32
        )

    @pl.when(step >= 4)
    def _():
        late_columns(
            where[1], step - 4, normed_t, halo_t, g_held, halo_held, taps, head_sums, skip_part,
            gather, mine, (send_0, send_1, send_2, send_3), held, sent, sems,
        )


def both_cores(where, mine, other):
    first = where[1] == 0
    return jnp.where(first, mine, other), jnp.where(first, other, mine)


def join_kernel(where, mine, other, through, through_other, spread, total, wide):
    first = where[1] == 0
    own = jnp.where(first, through[0:2], through[2:4])
    theirs = jnp.where(first, through_other[0:2], through_other[2:4])
    through_0, through_1 = both_cores(where, own, theirs)
    high, middle, low = split_three(through_0 * through_1)
    rows = jnp.concatenate([through_0, through_1, jnp.zeros((4, LANES), f32)], 0)
    wide[...] = widen(halves(rows), spread[...])
    row = lax.broadcasted_iota(jnp.int32, (16, LANES), 0)
    for a in range(2):
        piece = jnp.where(row == 0, high[a : a + 1].astype(f32), 0.0)
        piece = jnp.where(row == 1, middle[a : a + 1].astype(f32), piece)
        piece = jnp.where(row == 2, low[a : a + 1].astype(f32), piece).astype(bf16)
        for part in range(8):
            span = slice(part * 16, (part + 1) * 16)
            state_0, state_1 = both_cores(
                where, mine[a, span].astype(f32), other[a, span].astype(f32)
            )
            value = wide[2 + a : 3 + a] * state_0 + state_1
            total[8 * a + part, :, 0:INNER] = value.astype(bf16)
            total[8 * a + part, :, INNER:] = piece


def split_kernel(where, back, mine, other, wide, kept, given):
    for a in range(2):
        for part in range(8):
            span = slice(part * 16, (part + 1) * 16)
            state_0, _ = both_cores(where, mine[a, span].astype(f32), other[a, span].astype(f32))
            in_0 = back[8 * a + part].astype(f32)
            in_1 = wide[a : a + 1] * in_0 + state_0
            keeps, gives = both_cores(where, in_0, in_1)
            kept[a, span] = keeps.astype(bf16)
            given[a, span] = gives.astype(bf16)


def join_back_kernel(where, mine, other, wide, total):
    for a in range(2):
        for part in range(8):
            span = slice(part * 16, (part + 1) * 16)
            g_0, g_1 = both_cores(where, mine[a, span].astype(f32), other[a, span].astype(f32))
            total[8 * a + part] = (g_0 + wide[a : a + 1] * g_1).astype(bf16)


def split_back_kernel(where, back, mine, other, wide, kept, given):
    for a in range(2):
        for part in range(8):
            span = slice(part * 16, (part + 1) * 16)
            _, g_1 = both_cores(where, mine[a, span].astype(f32), other[a, span].astype(f32))
            end_1 = back[8 * a + part].astype(f32)
            end_0 = g_1 + wide[2 + a : 3 + a] * end_1
            keeps, gives = both_cores(where, end_0, end_1)
            kept[a, span] = keeps.astype(bf16)
            given[a, span] = gives.astype(bf16)


def scan_kernel(arrived, spread, before, factors):
    for i in range(16):
        wide = mm(arrived[i, :, INNER:], spread[...])
        factors[i : i + 1] = wide[0:1] + wide[1:2] + wide[2:3]
    so_far = jnp.zeros((16, INNER), f32)
    for i in range(16):
        before[i] = so_far.astype(bf16)
        so_far = factors[i : i + 1] * so_far + arrived[i, :, :INNER].astype(f32)


def scan_back_kernel(arrived, factors, after):
    so_far = jnp.zeros((16, INNER), f32)
    for i in reversed(range(16)):
        after[i] = so_far.astype(bf16)
        so_far = factors[i : i + 1] * so_far + arrived[i].astype(f32)


def pair_kernel(mine, *rest):
    pair = rest[-1]
    count = rest[0].shape[0]
    for k, other in enumerate(rest[:-1]):
        rows = slice(count * k, count * (k + 1))
        pair[rows] = (mine[rows].astype(f32) + other[...].astype(f32)).astype(bf16)


def reduce_early_kernel(parts, owned):
    total = parts[0].astype(f32)
    for k in range(1, 16):
        total = total + parts[k].astype(f32)
    owned[...] = total.astype(bf16)


def reduce_kernel(early, late, owned):
    held = [early[:, columns(k)] for k in range(3)]
    total = late[0].astype(f32)
    for k in range(1, 64):
        total = total + late[k].astype(f32)
    total = total.astype(bf16)
    for copy in range(16):
        for k in range(3):
            owned[copy, 48 * k : 48 * (k + 1)] = held[k]
        owned[copy, 144:240] = total


def last_kernel(
    hidden, cotangent, mixed, g_gates, g_mix, spill, mix_weight, gate_weight, out_full, params,
    output, grad_hidden, held,
):
    x = hidden[0].astype(f32)
    output[0] = (x + mm(mixed[0], out_full[...])).astype(bf16)
    held[...] = g_mix[0, :, 0:MIX_PAD]
    end = g_mix[0, TOKENS - 16 :, 0:XBC].astype(f32)
    shift = jnp.concatenate([jnp.zeros((8, XBC), f32), spill[0].astype(f32)], 0)
    held[TOKENS - 16 :, 0:XBC] = (end + shift).astype(bf16)
    grad = mm_nt(held[...], mix_weight[...]) + mm_nt(g_gates[0], gate_weight[...])
    grad = grad * params[GAIN : GAIN + 1, 0:768]
    scale = lax.rsqrt(jnp.mean(x * x, axis=1, keepdims=True) + epsilon)
    pull = jnp.mean(grad * x, axis=1, keepdims=True)
    value = cotangent[0].astype(f32) + scale * grad - x * (scale * scale * scale * pull)
    grad_hidden[0] = value.astype(bf16)


def finish_kernel(
    where, shared, other, weight, gain, out_weight, gate_gain,
    grad, by_gain, conv_w, conv_b, by_head, grad_out, by_gate_gain,
):
    first = where[1] == 0
    for j in range(16):
        a, b = shared[j].astype(f32), other[j].astype(f32)
        low = jnp.where(first, a, b)
        high = jnp.where(first, b, a)
        up, right = divmod(j, 4)
        half, side = divmod(right, 2)
        for k in range(3):
            piece = slice(48 * k, 48 * (k + 1))
            grad[up * 48 : (up + 1) * 48, columns(3 * right + k)] = low[piece]
            grad_out[
                half * 192 + up * 48 : half * 192 + (up + 1) * 48, columns(3 * side + k)
            ] = high[piece]
        begin = INNER + LANES * j
        width = min(LANES, INNER + MIX - begin)
        if width > 0:
            grad[0:96, begin : begin + width] = low[144:240, 0:width]
            grad[96:192, begin : begin + width] = high[144:240, 0:width]
    rest = jnp.where(first, shared[15].astype(f32), other[15].astype(f32))[144:240]
    for part in range(4):
        span = min(LANES, 448 - LANES * part)
        lanes = slice(LANES * part, LANES * part + span)
        conv_w[:, lanes] = rest[16 * part : 16 * part + 4, 0:span]
        conv_b[:, lanes] = rest[16 * part + 4 : 16 * part + 5, 0:span]
    by_head[...] = rest[64:72]
    total = jnp.sum(grad[...] * weight[...].astype(f32), axis=1, keepdims=True)
    by_gain[...] = jnp.broadcast_to(total, (192, LANES)).T[0:8] / gain[...]
    total = jnp.sum(grad_out[...] * out_weight[...].astype(f32), axis=1, keepdims=True)
    by_gate_gain[...] = jnp.broadcast_to(total, (384, LANES)).T[0:8] / gate_gain[...]


def per_device(
    hidden,
    segments,
    norm_gain,
    in_weight,
    conv_weight,
    conv_bias,
    dt_bias,
    a_log,
    skip,
    gate_gain,
    out_weight,
    cotangent,
):
    core = lax.axis_index("seq_2")
    place = lax.axis_index("fsdp")
    chip = lax.axis_index("seq_0") * 4 + lax.axis_index("seq_1")
    where = jnp.stack(
        [
            place, core, (chip * 2 + core) * TOKENS, lax.axis_index("seq_0"),
            lax.axis_index("seq_1"),
        ]
    ).astype(jnp.int32)

    message, mix_shard = call(
        message_kernel,
        [(None, shaped((112, MIX_PAD), bf16)), (None, shaped((192, MIX_PAD), bf16))],
        [SCALARS] + [None] * 8,
        [
            where, in_weight, norm_gain, conv_weight, conv_bias, dt_bias, a_log, skip, gate_gain,
        ],
        scratch=[pltpu.VMEM((16, XBC), f32), pltpu.VMEM((192, LANES), f32)],
        mib=LARGE,
    )
    mix_fetched = fetch(message)
    halo = line(hidden[:, TOKENS - EDGE :], SEQ, 1)

    head_of = np.arange(INNER) // HEADDIM
    spread = jnp.asarray((np.arange(LANES)[:, None] == head_of[None]), bf16)
    gather = jnp.asarray((head_of[:, None] == np.arange(LANES)[None]), bf16)
    lower = jnp.asarray(np.tril(np.ones((TOKENS, TOKENS))), bf16)
    upper = jnp.asarray(np.triu(np.ones((TOKENS, TOKENS))), bf16)
    low_lanes = jnp.asarray(np.ones((TOKENS, 1)) * (np.arange(LANES) < 64), bf16)
    high_lanes = jnp.asarray(np.ones((TOKENS, 1)) * (np.arange(LANES) >= 64), bf16)

    tokens = shaped((4, TOKENS, LANES))
    second, second_done = call(
        second_message_kernel,
        [(None, shaped((192, INNER), bf16))],
        [SCALARS, ANYWHERE, ANYWHERE],
        [where, in_weight, out_weight],
        scratch=[pltpu.SemaphoreType.DMA((3,))],
        marked=True,
        mib=LARGE,
    )
    same, keep, ending, passing, halo = call(
        tables_kernel,
        [
            (None, tokens), (None, tokens), (None, tokens), (None, shaped((4, LANES))),
            (None, shaped((4, EDGE, 768))),
        ],
        [SCALARS, None, None],
        [where, segments, halo],
        micros=60,
        after=[second_done],
    )
    half = shaped((2, STATE, INNER), bf16)
    (
        params, mixin, mixin_halo, active, dt_arg, dt, cumul, through, local_mine, local_send,
        normed, normed_t, halo_t, mix_weight,
    ) = call(
        front_kernel,
        [
            (None, shaped((16, XBC))),
            (ANYWHERE, shaped((4, TOKENS, XBC), bf16)),
            (None, shaped((4, EDGE, XBC))),
            (ANYWHERE, shaped((4, TOKENS, XBC), bf16)),
            (None, tokens),
            (None, tokens),
            (None, tokens),
            (None, shaped((4, LANES))),
            (ANYWHERE, half),
            (ANYWHERE, half),
            (ANYWHERE, shaped((512, 768), bf16)),
            (ANYWHERE, shaped((768, 512), bf16)),
            (None, shaped((768, LANES), bf16)),
            (ANYWHERE, shaped((768, MIX_PAD), bf16)),
        ],
        [SCALARS] + [None] * 6 + [ANYWHERE] * 8,
        [where, hidden, halo, ending, passing, spread, lower, message, mix_shard]
        + mix_fetched
        + [swap(part) for part in mix_fetched],
        scratch=[
            pltpu.VMEM((768, MIX_PAD), bf16),
            pltpu.VMEM((4, 16, MIX_PAD), bf16),
            pltpu.VMEM((512, 768), bf16),
            pltpu.VMEM((768, 512), bf16),
            pltpu.VMEM((4, TOKENS, XBC), bf16),
            pltpu.VMEM((4, TOKENS, XBC), bf16),
            pltpu.VMEM((4, STATE, INNER), bf16),
            pltpu.VMEM((2, 8, EDGE + TOKENS, LANES), f32),
            pltpu.VMEM((4, STATE, TOKENS), bf16),
            pltpu.VMEM((512, LANES), bf16),
            pltpu.VMEM((2, 512, 256), f32),
            pltpu.SemaphoreType.DMA((11,)),
            pltpu.SemaphoreType.DMA((29,)),
        ],
        mib=LARGE,
        micros=10,
    )

    blocks = shaped((16, 16, INNER), bf16)
    local_other = swap(local_send)
    through_other = swap(through)
    total, wide, joined = call(
        join_kernel,
        [(None, shaped((16, 16, INNER + LANES), bf16)), (None, shaped((8, INNER)))],
        [SCALARS] + [None] * 5,
        [where, local_mine, local_other, through, through_other, spread],
        marked=True,
        micros=0,
    )
    fetched = fetch(second)
    inner, inner_done = call(
        inner_kernel,
        [(by_seq(TOKENS, INNER), shaped((4, TOKENS, INNER)))],
        [
            by_seq(TOKENS, XBC), by_seq(TOKENS, LANES), by_seq(TOKENS, LANES),
            by_seq(TOKENS, TOKENS), constant(LANES, INNER), constant(TOKENS, LANES),
            constant(TOKENS, LANES),
        ],
        [active, dt, cumul, same, spread, low_lanes, high_lanes],
        grid=(4,),
        scratch=[pltpu.VMEM((TOKENS, INNER), f32)],
        mib=LARGE,
        marked=True,
        micros=60,
        after=[joined],
    )
    before, factors, scanned = call(
        scan_kernel,
        [(None, blocks), (None, shaped((16, INNER)))],
        [None] * 2,
        [exchange(total, CHIPS), spread],
        marked=True,
        micros=0,
        after=[inner_done],
    )
    gate_weight, out_full, gates, g_mixed, projected = call(
        weights_kernel,
        [
            (ANYWHERE, shaped((768, INNER), bf16)),
            (ANYWHERE, shaped((INNER, 768), bf16)),
            (ANYWHERE, shaped((512, INNER), bf16)),
            (ANYWHERE, shaped((512, INNER), bf16)),
        ],
        [SCALARS, None, None] + [ANYWHERE] * 8,
        [where, normed, cotangent.reshape(512, 768), in_weight, out_weight]
        + fetched
        + [swap(part) for part in fetched],
        scratch=[
            pltpu.VMEM((768, INNER), bf16),
            pltpu.VMEM((INNER, 768), bf16),
            pltpu.VMEM((512, INNER), bf16),
            pltpu.VMEM((512, INNER), bf16),
            pltpu.SemaphoreType.DMA((20,)),
            pltpu.SemaphoreType.DMA((14,)),
        ],
        marked=True,
        micros=0,
        mib=LARGE,
        after=[scanned],
    )
    gates = gates.reshape(4, TOKENS, INNER)
    g_mixed = g_mixed.reshape(4, TOKENS, INNER)
    kept, given = call(
        split_kernel,
        [(None, half), (None, half)],
        [SCALARS] + [None] * 4,
        [where, exchange(before, CHIPS), local_mine, local_other, wide],
        micros=0,
        after=[projected],
    )
    given = swap(given)

    mixed, g_y, g_gates, row_part, skip_part, g_mine, g_send = call(
        middle_kernel,
        [
            (by_seq(TOKENS, INNER), shaped((4, TOKENS, INNER), bf16)),
            (by_seq(TOKENS, INNER), shaped((4, TOKENS, INNER), bf16)),
            (by_seq(TOKENS, INNER), shaped((4, TOKENS, INNER), bf16)),
            (by_seq(TOKENS, LANES), tokens),
            (constant(8, INNER), shaped((8, INNER))),
            (own_half(STATE, INNER), half),
            (other_half(STATE, INNER), half),
        ],
        [
            by_seq(TOKENS, INNER), by_seq(TOKENS, XBC), own_half(STATE, INNER),
            other_half(STATE, INNER), by_seq(TOKENS, INNER), by_seq(TOKENS, INNER),
            by_seq(TOKENS, LANES), by_seq(TOKENS, LANES), constant(16, XBC),
            constant(LANES, INNER), constant(INNER, LANES),
        ],
        [inner, active, kept, given, gates, g_mixed, cumul, keep, params, spread, gather],
        scalars=where,
        grid=(4,),
        scratch=[pltpu.VMEM((TOKENS, INNER), f32)] * 5 + [pltpu.VMEM((TOKENS, INNER), bf16)],
        mib=LARGE,
        micros=11,
    )

    g_other = swap(g_send)
    g_total, joined_back = call(
        join_back_kernel,
        [(None, blocks)],
        [SCALARS] + [None] * 3,
        [where, g_mine, g_other, wide],
        marked=True,
        micros=2,
    )
    early_spec = pl.BlockSpec((192, INNER), lambda k, *_: (k, 0))
    early_shape = shaped((768, INNER), bf16)
    early_specs = [
        pl.BlockSpec((512, 384), lambda k, where: (0, lax.rem(where[0] + k, 4))),
        constant(512, 768), constant(768, 512), constant(512, INNER),
    ]
    early_operands = [
        mixed.reshape(512, INNER), cotangent.reshape(512, 768), normed_t,
        g_gates.reshape(512, INNER),
    ]
    *early_send, early_sent = call(
        early_send_kernel,
        [(ANYWHERE, shaped((192, INNER), bf16))] * 4,
        early_specs,
        early_operands,
        scalars=where,
        grid=(4,),
        scratch=[pltpu.VMEM((4, 192, INNER), bf16), pltpu.SemaphoreType.DMA((4,))],
        mib=LARGE,
        marked=True,
        micros=60,
        after=[joined_back],
    )
    early_mine, early_done = call(
        early_own_kernel,
        [(early_spec, early_shape)],
        early_specs,
        early_operands,
        scalars=where,
        grid=(4,),
        mib=LARGE,
        marked=True,
        micros=0,
        after=[early_sent],
    )
    parts = call(
        early_pair_kernel,
        [(None, shaped((192, INNER), bf16))] * 4,
        [None] * 5,
        [early_mine] + [swap(part) for part in early_send],
        micros=0,
    )
    early_blocks, early_summed = call(
        sum_blocks_kernel,
        [(None, shaped((16, 48, 384), bf16))],
        [None] * 4,
        [parts[0]] + [ring(parts[k], "fsdp", k) for k in (1, 2, 3)],
        marked=True,
        micros=0,
    )

    after, scanned_back = call(
        scan_back_kernel,
        [(None, blocks)],
        [None] * 2,
        [exchange(g_total, CHIPS), factors],
        marked=True,
        micros=2,
        after=[early_done],
    )

    g_inner, g_b, g_c, direct, column, inner_back_done = call(
        inner_back_kernel,
        [
            (by_seq(TOKENS, INNER), shaped((4, TOKENS, INNER), bf16)),
            (by_seq(TOKENS, STATE), tokens),
            (by_seq(TOKENS, STATE), tokens),
            (by_seq(TOKENS, LANES), tokens),
            (by_seq(TOKENS, LANES), tokens),
        ],
        [
            by_seq(TOKENS, XBC), by_seq(TOKENS, INNER), own_half(STATE, INNER),
            other_half(STATE, INNER), by_seq(TOKENS, LANES), by_seq(TOKENS, LANES),
            by_seq(TOKENS, LANES), by_seq(TOKENS, TOKENS), constant(LANES, INNER),
            constant(INNER, LANES), constant(TOKENS, LANES), constant(TOKENS, LANES),
        ],
        [
            active, g_y, kept, given, dt, cumul, keep, same, spread, gather, low_lanes, high_lanes,
        ],
        scalars=where,
        grid=(4,),
        scratch=[pltpu.VMEM((TOKENS, INNER), f32)] * 2 + [pltpu.VMEM((TOKENS, INNER), bf16)] * 4,
        mib=LARGE,
        marked=True,
        micros=60,
        after=[scanned_back],
    )
    kept_end, given_end = call(
        split_back_kernel,
        [(None, half), (None, half)],
        [SCALARS] + [None] * 4,
        [where, exchange(after, CHIPS), g_mine, g_other, wide],
        micros=2,
        after=[inner_back_done, early_summed],
    )
    given_end = swap(given_end)
    late_spec = pl.BlockSpec((2, 4, 96, LANES), lambda s, *_: (jnp.maximum(s - 4, 0), 0, 0, 0))
    late_shape = shaped((16, 4, 96, LANES), bf16)
    piece = shaped((16 // LATE_PIECES, 4, 96, LANES), bf16)
    g_mix, g_halo, late_mine, *late_send, late_done = call(
        late_kernel,
        [
            (seq_first(TOKENS, MIX_WIDE), shaped((4, TOKENS, MIX_WIDE), bf16)),
            (seq_first(EDGE, XBC), shaped((4, EDGE, XBC))),
            (late_spec, late_shape),
        ]
        + [(ANYWHERE, piece)] * LATE_PIECES,
        [own_half(STATE, INNER), other_half(STATE, INNER)] * 2
        + [
            pl.BlockSpec((1, TOKENS, 256), lambda a, *_: (jnp.minimum(a, 3), 0, 6)),
            seq_first(TOKENS, XBC), seq_first(EDGE, XBC), seq_first(TOKENS, INNER),
            seq_first(TOKENS, INNER), seq_first(TOKENS, STATE), seq_first(TOKENS, STATE),
        ]
        + [seq_first(TOKENS, LANES)] * 7
        + [
            constant(4, LANES), constant(16, XBC), constant(LANES, INNER), constant(INNER, LANES),
            constant(TOKENS, TOKENS), constant(768, 512), constant(768, LANES), constant(8, INNER),
        ],
        [
            kept_end, given_end, kept, given, active, mixin, mixin_halo, g_y, g_inner, g_b, g_c, dt,
            dt_arg, cumul, ending, row_part, direct, column, through, params, spread, gather, upper,
            normed_t, halo_t, skip_part,
        ],
        scalars=where,
        grid=(12,),
        scratch=[
            pltpu.VMEM((TOKENS, INNER), bf16),
            pltpu.VMEM((STATE, INNER), bf16),
            pltpu.VMEM((2, EDGE + TOKENS, LANES), f32),
            pltpu.VMEM((2, 144, LANES), f32),
            pltpu.VMEM((8, INNER), f32),
            pltpu.VMEM((512, MIX_WIDE), bf16),
            pltpu.VMEM((32, MIX_WIDE), f32),
            pltpu.VMEM((8, XBC), f32),
            pltpu.VMEM((8, LANES), f32),
            pltpu.VMEM((2, 2, 4, 96, LANES), bf16),
            pltpu.VMEM((16, 4, 96, LANES), bf16),
            pltpu.SemaphoreType.DMA((LATE_PIECES,)),
        ],
        marked=True,
        mib=LARGE,
        micros=60,
    )
    early_owned, early_reduced = call(
        reduce_early_kernel,
        [(None, shaped((48, 384), bf16))],
        [None],
        [exchange(early_blocks, CHIPS)],
        marked=True,
        micros=0,
        after=[late_done],
    )
    spill = line(g_halo.astype(bf16), SEQ, -1)
    late_pair, paired = call(
        pair_kernel,
        [(None, late_shape)],
        [None] * (1 + LATE_PIECES),
        [late_mine] + [swap(part) for part in late_send],
        marked=True,
        micros=0,
        after=[spill, early_reduced],
    )
    late_parts = exchange(late_pair.reshape(64, 96, LANES), COLUMNS)

    rows = by_seq(TOKENS, 768)
    output, grad_hidden, last_done = call(
        last_kernel,
        [(rows, shaped((4, TOKENS, 768), bf16)), (rows, shaped((4, TOKENS, 768), bf16))],
        [
            rows, rows, by_seq(TOKENS, INNER), by_seq(TOKENS, INNER), by_seq(TOKENS, MIX_WIDE),
            by_seq(EDGE, XBC), constant(768, MIX_PAD), constant(768, INNER), constant(INNER, 768),
            constant(16, XBC),
        ],
        [
            hidden, cotangent, mixed, g_gates, g_mix, spill, mix_weight, gate_weight, out_full,
            params,
        ],
        grid=(4,),
        scratch=[pltpu.VMEM((TOKENS, MIX_PAD), bf16)],
        mib=LARGE,
        marked=True,
        micros=60,
        after=[paired],
    )
    (owned,) = call(
        reduce_kernel,
        [(None, shaped((16, 240, LANES), bf16))],
        [None] * 2,
        [early_owned, late_parts],
        micros=2,
        after=[last_done],
    )
    shared = exchange(owned, CHIPS)
    sum_in, by_gain, sum_conv_w, sum_conv_b, by_head, sum_out, by_gate_gain = call(
        finish_kernel,
        [
            (None, shaped((192, INNER + MIX))),
            (None, shaped((8, 192))),
            (None, shaped((4, 448))),
            (None, shaped((1, 448))),
            (None, shaped((8, LANES))),
            (None, shaped((384, 768))),
            (None, shaped((8, 384))),
        ],
        [SCALARS] + [None] * 6,
        [
            where, shared, swap(shared), in_weight, norm_gain.astype(f32).reshape(1, 192),
            out_weight, gate_gain.astype(f32).reshape(1, 384),
        ],
        micros=4,
    )
    by_head = lax.dynamic_slice(by_head, (0, place * 6), (3, 6))

    return (
        output,
        grad_hidden,
        by_gain[0],
        sum_in,
        sum_conv_w,
        sum_conv_b[0],
        by_head[0],
        by_head[1],
        by_head[2],
        by_gate_gain[0],
        sum_out,
    )


def solution(mesh):
    finer = Mesh(
        mesh.devices.reshape(4, 4, 2, mesh.shape["fsdp"]), ("seq_0", "seq_1", "seq_2", "fsdp")
    )
    in_specs = (
        P("fsdp", SEQ, None),
        P("fsdp", SEQ),
        P("fsdp"),
        P("fsdp", None),
        P(None, "fsdp"),
        P("fsdp"),
        P("fsdp"),
        P("fsdp"),
        P("fsdp"),
        P("fsdp"),
        P("fsdp", None),
        P("fsdp", SEQ, None),
    )
    out_specs = (
        P("fsdp", SEQ, None),
        P("fsdp", SEQ, None),
        P("fsdp"),
        P("fsdp", None),
        P(None, "fsdp"),
        P("fsdp"),
        P("fsdp"),
        P("fsdp"),
        P("fsdp"),
        P("fsdp"),
        P("fsdp", None),
    )
    return jax.shard_map(
        per_device, mesh=finer, in_specs=in_specs, out_specs=out_specs, check_vma=False
    )
```

```python
import functools

import jax
import jax.numpy as jnp
import numpy as np
from jax import lax
from jax.experimental import pallas as pl
from jax.experimental.pallas import tpu as pltpu
from jax.sharding import Mesh
from jax.sharding import PartitionSpec as P

INNER = 1536
HEADS = 24
HEADDIM = 64
STATE = 128
XBC = 1792
MIX = 1816
MIX_PAD = 1920
MIX_WIDE = 2048
EDGE = 8
TOKENS = 128
LANES = 128
PAIRS = 12
SEQ = ("seq_0", "seq_1", "seq_2")
CHIPS = ("seq_0", "seq_1")
COLUMNS = ("seq_0", "seq_1", "fsdp")

epsilon = 1e-05
bf16 = jnp.bfloat16
f32 = jnp.float32
VMEM_MIB = 24
LARGE = 60
LATE_PIECES = 4
COST = 1.1e9

CONV_W, CONV_B, GATE_GAIN, GAIN, DT_BIAS, DECAY, SKIP, SKIP_WIDE = 0, 4, 5, 6, 7, 8, 9, 10


def ring(value, axis, steps):
    count = lax.axis_size(axis)
    pairs = [(source, (source + steps) % count) for source in range(count)]
    return lax.ppermute(value, axis, pairs)


def line(value, axis, steps):
    count = lax.axis_size(axis)
    initial, last = (max(0, -steps), min(count, count - steps))
    return lax.ppermute(value, axis, [(source, source + steps) for source in range(initial, last)])


def swap(value):
    return ring(value, "seq_2", 1)


def dot(pattern, left, right):
    return jnp.einsum(pattern, left, right, preferred_element_type=f32)


def exchange(blocks, axes):
    return lax.all_to_all(blocks, axes, 0, 0, tiled=False)


def split_three(value):
    high = value.astype(bf16)
    rest = value - high.astype(f32)
    middle = rest.astype(bf16)
    low = (rest - middle.astype(f32)).astype(bf16)
    return high, middle, low


def mm(left, right):
    return lax.dot_general(left, right, (((1,), (0,)), ((), ())), preferred_element_type=f32)


def mm_nt(left, right):
    return lax.dot_general(left, right, (((1,), (1,)), ((), ())), preferred_element_type=f32)


def mm_tn(left, right):
    return lax.dot_general(left, right, (((0,), (0,)), ((), ())), preferred_element_type=f32)


def exact_mm(ones, value):
    high, middle, low = split_three(value)
    return mm(ones, high) + mm(ones, middle) + mm(ones, low)


def halves(value):
    high = value.astype(bf16)
    return high, (value - high.astype(f32)).astype(bf16)


def widen(pieces, spread):
    return mm(pieces[0], spread) + mm(pieces[1], spread)


def sum_heads(value, gather):
    high, low = halves(value)
    return mm(high, gather) + mm(low, gather)


def sigmoid(value):
    return 0.5 * jnp.tanh(0.5 * value) + 0.5


def call(
    kernel, outs, ins, operands, grid=None, scratch=(), micros=1, after=(), mib=VMEM_MIB, scalars=None,
    marked=False,
):
    whole = pl.BlockSpec(memory_space=pltpu.VMEM)
    lead = [] if scalars is None else [scalars]
    count = len(operands) + len(lead)
    if marked:
        outs = list(outs) + [(constant(8, LANES) if grid else None, shaped((8, LANES)))]
    first = count + len(after)
    last = first + len(outs) - marked

    def body(*refs):
        kernel(*refs[:count], *refs[first:last], *refs[last + marked :])
        if marked:
            refs[last][...] = jnp.zeros((8, LANES), f32)

    return pl.pallas_call(
        body,
        grid_spec=pltpu.PrefetchScalarGridSpec(
            num_scalar_prefetch=len(lead),
            grid=grid or (),
            in_specs=[spec or whole for spec in ins]
            + [pl.BlockSpec(memory_space=pl.ANY)] * len(after),
            out_specs=[spec or whole for spec, _ in outs],
            scratch_shapes=list(scratch),
        ),
        out_shape=[shape for _, shape in outs],
        compiler_params=pltpu.CompilerParams(vmem_limit_bytes=mib * 1024 * 1024),
        cost_estimate=pl.CostEstimate(
            flops=int(micros * COST), bytes_accessed=0, transcendentals=0
        ),
    )(*lead, *operands, *after)


def shaped(shape, dtype=f32):
    return jax.ShapeDtypeStruct(shape, dtype)


def by_seq(*shape):
    return pl.BlockSpec((1,) + shape, lambda a, *_: (a,) + (0,) * len(shape))


def constant(*shape):
    return pl.BlockSpec(shape, lambda a, *_: (0,) * len(shape))


def seq_first(*shape):
    return pl.BlockSpec(
        (1,) + shape, lambda a, *_: (jnp.minimum(a, 3),) + (0,) * len(shape)
    )


def own_half(*shape):
    return pl.BlockSpec(
        (1,) + shape,
        lambda a, where: (jnp.clip(a - 2 * where[1], 0, 1),) + (0,) * len(shape),
    )


def other_half(*shape):
    return pl.BlockSpec(
        (1,) + shape,
        lambda a, where: (jnp.clip(a - 2 + 2 * where[1], 0, 1),) + (0,) * len(shape),
    )


ANYWHERE = pl.BlockSpec(memory_space=pl.ANY)
SCALARS = pl.BlockSpec(memory_space=pltpu.SMEM)


def columns(index, width=LANES):
    return slice(index * width, (index + 1) * width)


def groups():
    listed = []
    for row, count in (
        (CONV_W, 7), (CONV_W + 1, 7), (CONV_W + 2, 7), (CONV_W + 3, 7), (CONV_B, 7), (GATE_GAIN, 6),
        (GAIN, 3),
    ):
        for j in range(count):
            listed.append((row, j, len(listed)))
    return listed


SPANS = {CONV_B: 448, GATE_GAIN: 384, GAIN: 192}
HEAD_LINE = 44


def message_kernel(
    where, in_weight, norm_gain, conv_weight, conv_bias, dt_bias, a_log, skip, gate_gain,
    message, tail, held, narrow, lines,
):
    core = where[1]
    narrow[...] = jnp.zeros_like(narrow)
    narrow[:, 0 : MIX - XBC] = in_weight[:, INNER + XBC :].astype(f32)
    tail[...] = narrow[...].astype(bf16)
    half = pl.ds(pl.multiple_of(core * 96, 96), 96)
    message[:, 0:XBC] = in_weight[half, INNER : INNER + XBC]
    held[...] = jnp.zeros_like(held)
    held[CONV_W : CONV_W + 4, 0:448] = conv_weight[...].astype(f32)
    for target, source in (
        (CONV_B, conv_bias), (GATE_GAIN, gate_gain), (GAIN, norm_gain), (DT_BIAS, dt_bias),
        (DECAY, a_log), (SKIP, skip),
    ):
        size = source.shape[0]
        held[target : target + 1, 0:size] = source[...].astype(f32).reshape(1, size)
    lane = lax.broadcasted_iota(jnp.int32, (1, LANES), 1)
    lines[...] = jnp.zeros_like(lines)
    for row, j, line in groups():
        tile = held[row : row + 1, columns(j // 2)]
        tile = tile if j % 2 else pltpu.roll(tile, 64, 1)
        lines[line : line + 1] = jnp.where(lane < 64, 0.0, tile)
    heads = pltpu.roll(held[DT_BIAS : DT_BIAS + 1, 0:LANES], 64, 1)
    heads = heads + pltpu.roll(held[DECAY : DECAY + 1, 0:LANES], 70, 1)
    lines[HEAD_LINE : HEAD_LINE + 1] = heads + pltpu.roll(held[SKIP : SKIP + 1, 0:LANES], 76, 1)
    message[:, XBC:] = (narrow[half] + lines[...]).astype(bf16)


def tables_kernel(where, segments, halo, same, keep, ending, passing, halo_held):
    start = where[2].astype(f32)
    below = lax.broadcasted_iota(jnp.int32, (TOKENS, TOKENS), 0) >= lax.broadcasted_iota(
        jnp.int32, (TOKENS, TOKENS), 1
    )
    for a in range(4):
        row = jnp.broadcast_to(segments[a : a + 1].astype(f32), (TOKENS, TOKENS))
        column = row.T
        first, last = column[0:1], column[TOKENS - 1 :]
        same[a] = jnp.where((column == row) & below, 1.0, 0.0)
        keep[a] = jnp.where((column == first) & (first < start), 1.0, 0.0)
        ending[a] = jnp.where(column == last, 1.0, 0.0)
        passing[a : a + 1] = jnp.where(last < start, 1.0, 0.0)
        halo_held[a] = halo[a].astype(f32)


def second_message_kernel(where, in_weight, out_weight, message, sems):
    core = where[1]
    low = pl.multiple_of(core * 192, 192)
    copies = [
        pltpu.make_async_copy(
            in_weight.at[pl.ds(pl.multiple_of(core * 96, 96), 96), pl.ds(0, INNER)],
            message.at[pl.ds(0, 96)],
            sems.at[0],
        )
    ]
    for k in range(2):
        copies.append(
            pltpu.make_async_copy(
                out_weight.at[pl.ds(low + 96 * k, 96)],
                message.at[pl.ds(96, 96), pl.ds(768 * k, 768)],
                sems.at[1 + k],
            )
        )
    for copy in copies:
        copy.start()
    for copy in copies:
        copy.wait()


def weights_kernel(
    where, normed, cotangent, in_weight, out_weight, m_1, m_2, m_3, o_1, o_2, o_3,
    gate_full, out_full, gates, g_mixed,
    gate_held, out_held, gates_held, g_held, in_sems, out_sems,
):
    place, core = where[0], where[1]
    gate_copies = weight_copies(
        place, core, in_weight.at[:, pl.ds(0, INNER)], (m_1, m_2, m_3), (o_1, o_2, o_3), gate_held,
        in_sems,
    )
    out_copies = [
        pltpu.make_async_copy(
            out_weight, out_held.at[pl.ds(pl.multiple_of(place * 384, 384), 384)], in_sems.at[7]
        )
    ]
    for k, (mine, other) in enumerate(((m_1, o_1), (m_2, o_2), (m_3, o_3))):
        owner = lax.rem(place + (1 + k), 4) * 384
        for which, part in ((core, mine), (1 - core, other)):
            for side in range(2):
                begin = pl.multiple_of(owner + which * 192 + 96 * side, 96)
                out_copies.append(
                    pltpu.make_async_copy(
                        part.at[pl.ds(96, 96), pl.ds(768 * side, 768)],
                        out_held.at[pl.ds(begin, 96)],
                        in_sems.at[7 + len(out_copies)],
                    )
                )
    for copy in gate_copies + out_copies:
        copy.start()
    outgoing = []

    def send(source, target):
        copy = pltpu.make_async_copy(source, target, out_sems.at[len(outgoing)])
        copy.start()
        outgoing.append(copy)

    for copy in gate_copies:
        copy.wait()
    for chunk in range(6):
        lanes, span = columns(chunk, 256), pl.ds(chunk * 256, 256)
        gates_held[:, lanes] = mm(normed[...], gate_held[:, lanes]).astype(bf16)
        send(gates_held.at[:, span], gates.at[:, span])
    send(gate_held, gate_full)
    for copy in out_copies:
        copy.wait()
    for chunk in range(6):
        lanes, span = columns(chunk, 256), pl.ds(chunk * 256, 256)
        g_held[:, lanes] = mm_nt(cotangent[...], out_held[lanes]).astype(bf16)
        send(g_held.at[:, span], g_mixed.at[:, span])
    send(out_held, out_full)
    for copy in outgoing:
        copy.wait()


def fetch(half):
    return [ring(half, "fsdp", steps) for steps in (3, 2, 1)]


def weight_copies(place, core, shard, mine, others, full, sems, own_width=None):
    rows = shard.shape[0]
    half = rows // 2
    copies = [
        pltpu.make_async_copy(
            shard,
            full.at[pl.ds(pl.multiple_of(place * rows, rows), rows), pl.ds(0, own_width or full.shape[1])],
            sems.at[0],
        )
    ]
    for k in range(3):
        owner = lax.rem(place + (1 + k), 4) * rows
        low = pl.multiple_of(owner + core * half, half)
        high = pl.multiple_of(owner + (1 - core) * half, half)
        for slot, part, begin in ((1 + 2 * k, mine[k], low), (2 + 2 * k, others[k], high)):
            copies.append(
                pltpu.make_async_copy(
                    part.at[pl.ds(0, half)], full.at[pl.ds(begin, half)], sems.at[slot]
                )
            )
    return copies


def front_kernel(
    where, hidden, halo, ending, passing, spread, lower, own, in_weight, tail,
    m_1, m_2, m_3, o_1, o_2, o_3,
    params, mixin, mixin_halo, active, dt_arg, dt, cumul, through, local_mine, local_send,
    normed, normed_t, halo_t, full,
    weight, packed, x_low, x_turned, mix_held, act_held, local_held,
    extended, state_b, scaled, wide_held, in_sems, out_sems,
):
    place, core = where[0], where[1]
    incoming = weight_copies(
        place, core, in_weight.at[:, pl.ds(INNER, XBC)], (m_1, m_2, m_3), (o_1, o_2, o_3), weight,
        in_sems, XBC,
    )
    incoming.append(
        pltpu.make_async_copy(
            tail,
            weight.at[pl.ds(pl.multiple_of(place * 192, 192), 192), pl.ds(XBC, LANES)],
            in_sems.at[11],
        )
    )
    rows_in = [
        pltpu.make_async_copy(part.at[:, pl.ds(XBC, LANES)], packed.at[k], in_sems.at[7 + k])
        for k, part in enumerate((own, m_1, m_2, m_3))
    ]
    for copy in rows_in + incoming:
        copy.start()
    outgoing = []

    def send(source, target):
        copy = pltpu.make_async_copy(source, target, out_sems.at[len(outgoing)])
        copy.start()
        outgoing.append(copy)

    for copy in rows_in:
        copy.wait()
    params[...] = jnp.zeros_like(params)
    lane = lax.broadcasted_iota(jnp.int32, (1, LANES), 1)
    for at in range(4):

        @pl.when(place == at)
        def _(at=at):
            for slot in range(4):
                z = (at + slot) % 4
                lines = packed[slot].astype(f32)
                turned = pltpu.roll(lines, 64, 1)
                for row, j, line in groups():
                    begin = SPANS.get(row, 448) * z + 64 * j
                    if begin % LANES:
                        params[row : row + 1, begin : begin + 64] = lines[line : line + 1, 64:LANES]
                    else:
                        params[row : row + 1, begin : begin + 64] = turned[line : line + 1, 0:64]
                heads = lines[HEAD_LINE : HEAD_LINE + 1]
                here = (lane >= 6 * z) & (lane < 6 * z + 6)
                for row, begin in ((DT_BIAS, 64), (DECAY, 70), (SKIP, 76)):
                    moved = pltpu.roll(heads, (LANES - begin + 6 * z) % LANES, 1)
                    params[row : row + 1, 0:LANES] += jnp.where(here, moved, 0.0)

    decay_rate = jnp.exp(params[DECAY : DECAY + 1, 0:LANES])
    params[DECAY : DECAY + 1, 0:LANES] = decay_rate
    params[SKIP_WIDE : SKIP_WIDE + 1, 0:INNER] = mm(
        params[SKIP : SKIP + 1, 0:LANES].astype(bf16), spread[...]
    )
    gain = params[GAIN : GAIN + 1, 0:768]

    def normalised(value):
        scale = lax.rsqrt(jnp.mean(value * value, axis=1, keepdims=True) + epsilon)
        return value * scale * gain

    edges = []
    for a in range(4):
        value = normalised(hidden[a].astype(f32))
        x_low[a * TOKENS : (a + 1) * TOKENS] = value.astype(bf16)
        x_turned[:, a * TOKENS : (a + 1) * TOKENS] = value.T.astype(bf16)
        edges.append(normalised(halo[a]))
    send(x_low, normed)
    send(x_turned, normed_t)
    edges = jnp.concatenate(edges, 0)
    edge_low = edges.astype(bf16)
    edges = jnp.concatenate([edges, jnp.zeros((LANES - 32, 768), f32)], 0)
    halo_t[...] = edges.T.astype(bf16)

    for copy in incoming:
        copy.wait()
    last = weight[:, XBC:].astype(f32)
    weight[:, XBC:] = jnp.where(lane < MIX - XBC, last, 0.0).astype(bf16)
    send(weight, full)
    argument = mm(x_low[...], weight[:, XBC:]) + params[DT_BIAS : DT_BIAS + 1, 0:LANES]
    steps = jnp.maximum(argument, 0.0) + jnp.log1p(jnp.exp(-jnp.abs(argument)))
    for a in range(4):
        rows = slice(a * TOKENS, (a + 1) * TOKENS)
        dt_arg[a] = argument[rows]
        dt[a] = steps[rows]
        total = exact_mm(lower[...], -steps[rows] * decay_rate)
        cumul[a] = total
        final = total[TOKENS - 1 :]
        through[a : a + 1] = jnp.exp(final) * passing[a : a + 1]
        scaled[rows] = (jnp.exp(final - total) * ending[a] * steps[rows]).astype(bf16)
    order = (6, 0, 1, 2, 3, 4, 5)

    def project(turn, a):
        chunk, slot = order[turn], turn % 2
        lanes = columns(chunk, 256)
        rows = slice(a * TOKENS, (a + 1) * TOKENS)
        if a == 0:
            edge = mm(edge_low, weight[:, lanes]).astype(bf16).astype(f32)
            for b in range(4):
                mixin_halo[b, :, lanes] = edge[b * EDGE : (b + 1) * EDGE]
                for side in range(2):
                    extended[slot, 2 * b + side, 0:EDGE] = edge[
                        b * EDGE : (b + 1) * EDGE, columns(side)
                    ]
        part = mm(x_low[rows], weight[:, lanes]).astype(bf16)
        mix_held[a, :, lanes] = part
        part = part.astype(f32)
        for side in range(2):
            extended[slot, 2 * a + side, EDGE:] = part[:, columns(side)]
        if chunk < 6:
            wide_held[slot, rows] = mm(scaled[rows], spread[:, lanes])

    def convolve(turn, a):
        chunk, slot = order[turn], turn % 2
        for side in range(2):
            lanes = columns(2 * chunk + side)
            at = 2 * a + side
            value = params[CONV_B : CONV_B + 1, lanes]
            for k in range(4):
                value = value + params[k : k + 1, lanes] * extended[
                    slot, at, EDGE - 3 + k : EDGE + 125 + k
                ]
            value = (value * sigmoid(value)).astype(bf16)
            act_held[a, :, lanes] = value
            if chunk == 6:
                if side == 0:
                    state_b[a] = value.astype(f32).T.astype(bf16)
            else:
                wide = wide_held[slot, a * TOKENS : (a + 1) * TOKENS, columns(side)]
                weighted = (wide * value.astype(f32)).astype(bf16)
                local_held[a, :, lanes] = mm(state_b[a], weighted).astype(bf16)

    for a in range(4):
        project(0, a)
    for turn, chunk in enumerate(order):
        span = pl.ds(chunk * 256, 256)
        send(mix_held.at[:, :, span], mixin.at[:, :, span])
        for a in range(4):
            if turn < 6:
                project(turn + 1, a)
            convolve(turn, a)
        send(act_held.at[:, :, span], active.at[:, :, span])
        if chunk < 6:
            own, given = pl.ds(2 * core, 2), pl.ds(2 - 2 * core, 2)
            send(local_held.at[given, :, span], local_send.at[:, :, span])
            send(local_held.at[own, :, span], local_mine.at[:, :, span])
    for copy in outgoing:
        copy.wait()


def pair_weights(p, scores, cumul, turned, same):
    made = []
    for h in (2 * p, 2 * p + 1):
        differ = cumul[:, h : h + 1] - turned[h : h + 1, :]
        decay = jnp.exp(jnp.where(same, differ, -1e30))
        made.append((decay, (scores * decay).astype(bf16)))
    return made


def inner_kernel(active, dt, cumul, same, spread, low_lanes, high_lanes, inner, dt_wide):
    b_low = active[0, :, INNER : INNER + STATE]
    c_low = active[0, :, INNER + STATE :]
    scores = mm_nt(c_low, b_low)
    total = cumul[0]
    turned = total.T
    allowed = same[0] > 0
    dt_wide[...] = mm(dt[0].astype(bf16), spread[...])
    for p in range(PAIRS):
        lanes = columns(p)
        (_, first), (_, second) = pair_weights(p, scores, total, turned, allowed)
        xdt = (dt_wide[:, lanes] * active[0, :, lanes].astype(f32)).astype(bf16)
        stacked = jnp.concatenate([xdt * low_lanes[...], xdt * high_lanes[...]], 0)
        inner[0, :, lanes] = mm(jnp.concatenate([first, second], 1), stacked)


def pick(where, kept, given, use):
    own = where[1] == pl.program_id(0) // 2

    @pl.when(own)
    def _():
        use(kept)

    @pl.when(jnp.logical_not(own))
    def _():
        use(given)


def pick_lanes(where, kept, given, lanes):
    own = where[1] == pl.program_id(0) // 2
    return jnp.where(own, kept[0, :, lanes].astype(f32), given[0, :, lanes].astype(f32)).astype(bf16)


def middle_kernel(
    where, inner, active, kept, given, gates, g_mixed, cumul, keep, params, spread, gather,
    mixed, g_y, g_gates, row_part, skip_part, g_state,
    y_held, recur_held, act_held, slope_held, enter_held, entered,
):
    a = pl.program_id(0)
    enter = (jnp.exp(cumul[0]) * keep[0]).astype(bf16)
    c_low = active[0, :, INNER + STATE :]
    squares = jnp.zeros((TOKENS, LANES), f32)
    products = jnp.zeros((TOKENS, LANES), f32)
    for p in range(PAIRS):
        lanes = columns(p)
        carried = mm(c_low, pick_lanes(where, kept, given, lanes))
        wide = mm(enter, spread[:, lanes])
        enter_held[:, lanes] = wide
        recur = inner[0, :, lanes] + wide * carried
        y = recur + params[SKIP_WIDE : SKIP_WIDE + 1, lanes] * active[0, :, lanes].astype(f32)
        gate = gates[0, :, lanes].astype(f32)
        unit_grad = g_mixed[0, :, lanes].astype(f32) * params[GATE_GAIN : GATE_GAIN + 1, lanes]
        sig = sigmoid(gate)
        act = gate * sig
        gated = y * act
        squares = squares + gated * gated
        products = products + unit_grad * gated
        y_held[:, lanes] = y
        recur_held[:, lanes] = recur
        act_held[:, lanes] = act
        slope_held[:, lanes] = sig + act * (1.0 - sig)
    scale = lax.rsqrt(jnp.sum(squares, 1, keepdims=True) * (1.0 / INNER) + epsilon)
    slant = scale * jnp.sum(products, 1, keepdims=True) * (1.0 / INNER)
    rows = jnp.zeros((TOKENS, LANES), f32)

    @pl.when(a == 0)
    def _():
        skip_part[...] = jnp.zeros_like(skip_part)

    for p in range(PAIRS):
        lanes = columns(p)
        y, act = y_held[:, lanes], act_held[:, lanes]
        unit = y * act * scale
        mixed[0, :, lanes] = (unit * params[GATE_GAIN : GATE_GAIN + 1, lanes]).astype(bf16)
        unit_grad = g_mixed[0, :, lanes].astype(f32) * params[GATE_GAIN : GATE_GAIN + 1, lanes]
        g_gated = scale * (unit_grad - unit * slant)
        grad = g_gated * act
        g_gates[0, :, lanes] = (g_gated * y * slope_held[:, lanes]).astype(bf16)
        low = grad.astype(bf16)
        g_y[0, :, lanes] = low
        low = low.astype(f32)
        rows = rows + sum_heads(low * recur_held[:, lanes], gather[lanes])
        share = grad * active[0, :, lanes].astype(f32)
        skip_part[:, lanes] += jnp.sum(share.reshape(16, 8, LANES), 0)
        entered[:, lanes] = (enter_held[:, lanes] * low).astype(bf16)
    row_part[0] = rows
    g_state[0] = mm_tn(c_low, entered[...]).astype(bf16)


def inner_back_kernel(
    where, active, g_y, kept, given, dt, cumul, keep, same, spread, gather, low_lanes, high_lanes,
    g_inner, g_b, g_c, direct, column,
    dt_wide, enter_wide, entered, by_x, column_high, column_low,
):
    b_low = active[0, :, INNER : INNER + STATE]
    c_low = active[0, :, INNER + STATE :]
    scores = mm_nt(c_low, b_low)
    total = cumul[0]
    turned = total.T
    allowed = same[0] > 0
    dt_wide[...] = mm(dt[0].astype(bf16), spread[...])
    enter_wide[...] = mm((jnp.exp(total) * keep[0]).astype(bf16), spread[...])
    g_scores = jnp.zeros((TOKENS, TOKENS), f32)
    for p in range(PAIRS):
        lanes = columns(p)
        (decay_1, first), (decay_2, second) = pair_weights(p, scores, total, turned, allowed)
        x = active[0, :, lanes].astype(f32)
        xdt = (dt_wide[:, lanes] * x).astype(bf16)
        grad = g_y[0, :, lanes]
        entered[:, lanes] = (enter_wide[:, lanes] * grad.astype(f32)).astype(bf16)
        stacked = jnp.concatenate([grad * low_lanes[...], grad * high_lanes[...]], 0)
        g_weights = mm_nt(stacked, xdt)
        g_scores = g_scores + g_weights[:TOKENS] * decay_1 + g_weights[TOKENS:] * decay_2
        own = mm_tn(jnp.concatenate([first, second], 0), stacked)
        g_inner[0, :, lanes] = own.astype(bf16)
        by_x[:, lanes] = (x * own).astype(bf16)
        column_high[:, lanes], column_low[:, lanes] = halves(xdt.astype(f32) * own)
    direct[0] = mm(by_x[...], gather[...])
    column[0] = mm(column_high[...], gather[...]) + mm(column_low[...], gather[...])
    g_scores = g_scores.astype(bf16)
    from_scores = mm(g_scores, b_low)

    def add_state(state):
        g_c[0] = from_scores + mm_nt(entered[...], state[0])

    pick(where, kept, given, add_state)
    g_b[0] = mm_tn(g_scores, c_low)


def late_rows(
    where, g_end, kept, given, active, mixin, mixin_halo, g_y, g_inner, g_b, g_c,
    dt, dt_arg, cumul, ending, row_part, direct, column, through, params, spread, gather, upper,
    g_mix, taps, head_sums,
    weighted, state, extended, padded, inner_row, halo_held,
):
    a = pl.program_id(0)

    @pl.when(a == 0)
    def _():
        taps[...] = jnp.zeros_like(taps)
        head_sums[...] = jnp.zeros_like(head_sums)

    b_low = active[0, :, 0:STATE]
    decay_rate = params[DECAY : DECAY + 1, 0:LANES]
    total = cumul[0]
    steps = dt[0]
    to_end = jnp.exp(total[TOKENS - 1 :] - total) * ending[0]
    scaled = to_end * steps
    to_end_low = to_end.astype(bf16)
    scaled_low = scaled.astype(bf16)
    dt_low = steps.astype(bf16)
    through_state = jnp.zeros((TOKENS, LANES), f32)
    padded[:, 0:8] = jnp.zeros((2, 8, LANES), f32)
    padded[:, 136:144] = jnp.zeros((2, 8, LANES), f32)

    def convolved(chunk):
        lanes = columns(chunk)
        slot = chunk % 2
        extended[slot, 0:EDGE] = mixin_halo[0, :, lanes]
        extended[slot, EDGE:] = mixin[0, :, lanes].astype(f32)
        shifted = [extended[slot, EDGE - 3 + k : EDGE + 125 + k] for k in range(4)]
        value = params[CONV_B : CONV_B + 1, lanes]
        for k in range(4):
            value = value + params[k : k + 1, lanes] * shifted[k]
        return value, sigmoid(value), shifted

    def back(chunk, grad, value, sig, shifted):
        lanes = columns(chunk)
        slot = chunk % 2
        grad = grad * (sig * (1.0 + value * (1.0 - sig)))
        padded[slot, 8:136] = grad
        main = jnp.zeros((TOKENS, LANES), f32)
        edge = jnp.zeros((EDGE, LANES), f32)
        for k in range(4):
            tap = params[k : k + 1, lanes]
            main = main + tap * padded[slot, 11 - k : 139 - k]
            edge = edge + tap * padded[slot, 3 - k : 11 - k]
            taps[k : k + 1, lanes] += jnp.sum(grad * shifted[k], 0, keepdims=True)
        taps[4:5, lanes] += jnp.sum(grad, 0, keepdims=True)
        g_mix[0, :, lanes] = main.astype(bf16)
        halo_held[:, lanes] = edge

    for p in range(PAIRS):
        lanes = columns(p)
        end = g_end[0, :, lanes]
        begin = pick_lanes(where, kept, given, lanes)
        inner_row[0:1, lanes] = jnp.sum(begin.astype(f32) * end.astype(f32), 0, keepdims=True)
        state[:, lanes] = end
        from_state = mm(b_low, end)
        value, sig, shifted = convolved(p)
        x = (value * sig).astype(bf16).astype(f32)
        weighted[:, lanes] = (mm(scaled_low, spread[:, lanes]) * x).astype(bf16)
        grad = mm(dt_low, spread[:, lanes]) * (
            g_inner[0, :, lanes].astype(f32) + mm(to_end_low, spread[:, lanes]) * from_state
        ) + params[SKIP_WIDE : SKIP_WIDE + 1, lanes] * g_y[0, :, lanes].astype(f32)
        through_state = through_state + mm((x * from_state).astype(bf16), gather[lanes])
        back(p, grad, value, sig, shifted)
    state_part = scaled * through_state
    inner_sum = jnp.zeros((8, LANES), f32)
    for p in range(PAIRS):
        lanes = columns(p)
        inner_sum = inner_sum + sum_heads(inner_row[:, lanes], gather[lanes])
    mask = lax.broadcasted_iota(jnp.int32, (4, LANES), 0) == a
    flow = jnp.sum(jnp.where(mask, through[...], 0.0), 0, keepdims=True)
    at_end = jnp.sum(state_part, 0, keepdims=True) + flow * inner_sum[0:1]
    g_rate = exact_mm(upper[...], row_part[0] - column[0] - state_part) + at_end
    g_raw = direct[0] + to_end * through_state - decay_rate * g_rate
    g_raw = g_raw * sigmoid(dt_arg[0])
    head_sums[0:1] += jnp.sum(g_raw, 0, keepdims=True)
    head_sums[1:2] -= decay_rate * jnp.sum(steps * g_rate, 0, keepdims=True)
    g_mix[0, :, XBC:MIX_PAD] = g_raw.astype(bf16)
    g_mix[0, :, MIX_PAD:] = jnp.zeros((TOKENS, MIX_WIDE - MIX_PAD), bf16)
    back(PAIRS, g_b[0] + mm_nt(weighted[...], state[...]), *convolved(PAIRS))
    back(PAIRS + 1, g_c[0], *convolved(PAIRS + 1))


def early_grads_kernel(
    where, mixed, cotangent, normed_t, g_gates, mine, send_0, send_1, send_2, send_3,
    mixed_held, cot_held, normed_held, gates_held, mine_held, send_held, in_sems, out_sems,
):
    place, core = where[0], where[1]
    for_out = [
        pltpu.make_async_copy(mixed, mixed_held, in_sems.at[0]),
        pltpu.make_async_copy(cotangent, cot_held, in_sems.at[1]),
    ]
    for_gate = [
        pltpu.make_async_copy(normed_t, normed_held, in_sems.at[2]),
        pltpu.make_async_copy(g_gates, gates_held, in_sems.at[3]),
    ]
    to_mine = [
        pltpu.make_async_copy(
            mine_held.at[pl.ds(192 * k, 192)], mine.at[pl.ds(192 * k, 192)], out_sems.at[k]
        )
        for k in range(4)
    ]
    to_send = [
        pltpu.make_async_copy(send_held.at[pl.ds(192 * k, 192)], target, out_sems.at[4 + k])
        for k, target in enumerate((send_0, send_1, send_2, send_3))
    ]

    def gate_rows(target, copies):
        for copy in for_gate:
            copy.wait()
        for k in range(4):
            rows = pl.ds(pl.multiple_of(lax.rem(place + k, 4) * 192, 192), 192)
            target[192 * k : 192 * (k + 1)] = mm(normed_held[rows], gates_held[...]).astype(bf16)
            copies[k].start()

    def out_rows(target, copies):
        for copy in for_out:
            copy.wait()
        for k in range(4):
            lanes = pl.ds(pl.multiple_of(lax.rem(place + k, 4) * 384, 384), 384)
            grad = mm_tn(mixed_held[:, lanes], cot_held[...]).astype(bf16)
            target[192 * k : 192 * (k + 1), 0:768] = grad[0:192]
            target[192 * k : 192 * (k + 1), 768:] = grad[192:384]
            copies[k].start()

    @pl.when(core == 0)
    def _():
        for copy in for_out + for_gate:
            copy.start()
        out_rows(send_held, to_send)
        gate_rows(mine_held, to_mine)

    @pl.when(core == 1)
    def _():
        for copy in for_gate + for_out:
            copy.start()
        gate_rows(send_held, to_send)
        out_rows(mine_held, to_mine)

    for copy in to_mine + to_send:
        copy.wait()


def early_pair_kernel(mine, *rest):
    for k in range(4):
        rows = slice(192 * k, 192 * (k + 1))
        rest[4 + k][...] = (mine[rows].astype(f32) + rest[k][...].astype(f32)).astype(bf16)


def sum_blocks_kernel(a, b, c, d, total):
    for high in range(4):
        rows = slice(48 * high, 48 * (high + 1))
        value = a[rows].astype(f32) + b[rows].astype(f32) + c[rows].astype(f32) + d[rows].astype(f32)
        for low in range(4):
            total[4 * high + low] = value[:, columns(low, 384)].astype(bf16)


def late_columns(
    core, step, normed_t, halo_t, g_held, g_halo, taps, head_sums, skip_part, gather, mine, sends,
    held, sent, sems,
):
    lanes = pl.ds(pl.multiple_of(step * 512, 512), 512)
    g_mix = g_held[:, lanes]
    g_edge = jnp.concatenate([g_halo[:, lanes], jnp.zeros((LANES - 32, 512), f32)], 0).astype(bf16)
    for z in range(4):
        rows = slice(192 * z, 192 * (z + 1))
        grad = (mm(normed_t[rows], g_mix) + mm(halo_t[rows], g_edge)).astype(bf16)
        for c in range(2):
            for jj in range(4):
                held[c, jj, z] = grad[96 * c : 96 * (c + 1), columns(jj)]

    @pl.when(step == 3)
    def _():
        lane = lax.broadcasted_iota(jnp.int32, (8, LANES), 1)
        row = lax.broadcasted_iota(jnp.int32, (8, LANES), 0)
        nothing = jnp.zeros((8, LANES), f32)
        skips = sum_heads(skip_part[...], gather[...])
        head_rows = jnp.where(row == 2, jnp.sum(skips, 0, keepdims=True), head_sums[...])
        for z in range(4):
            for part in range(5):
                tile = head_rows
                if part < 4:
                    begin = 448 * z + LANES * part
                    tile = taps[:, begin // LANES * LANES : begin // LANES * LANES + LANES]
                    if begin % LANES:
                        after = min(begin // LANES + 1, XBC // LANES - 1) * LANES
                        tile = jnp.where(lane < 64, taps[:, after : after + LANES], tile)
                        tile = pltpu.roll(tile, 64, 1)
                tile = jnp.concatenate([tile, nothing], 0)
                held[0, 3, z, 16 * part : 16 * (part + 1)] = tile.astype(bf16)

    mine[...] = held[core]
    sent[pl.ds(4 * step, 4)] = held[1 - core]
    copies = [
        pltpu.make_async_copy(sent.at[pl.ds(4 * k, 4)], target, sems.at[k])
        for k, target in enumerate(sends)
    ]
    for k in range(4):

        @pl.when(step == k)
        def _(k=k):
            copies[k].start()

    @pl.when(step == 3)
    def _():
        for copy in copies:
            copy.wait()


def late_kernel(
    where, g_end, kept, given, active, mixin, mixin_halo, g_y, g_inner, g_b, g_c,
    dt, dt_arg, cumul, ending, row_part, direct, column, through, params, spread, gather, upper,
    normed_t, halo_t, skip_part,
    g_mix, g_halo, mine, send_0, send_1, send_2, send_3,
    weighted, state, extended, padded, inner_row, g_held, halo_held, taps, head_sums, held, sent,
    edge_held, sems,
):
    step = pl.program_id(0)

    @pl.when(step < 4)
    def _():
        late_rows(
            where, g_end, kept, given, active, mixin, mixin_halo, g_y, g_inner, g_b, g_c,
            dt, dt_arg, cumul, ending, row_part, direct, column, through, params, spread,
            gather, upper, g_mix, taps, head_sums,
            weighted, state, extended, padded, inner_row, edge_held,
        )
        g_held[pl.ds(pl.multiple_of(step * TOKENS, TOKENS), TOKENS)] = g_mix[0]
        rows = pl.ds(pl.multiple_of(step * EDGE, EDGE), EDGE)
        halo_held[rows, 0:XBC] = edge_held[...]
        halo_held[rows, XBC:] = jnp.zeros((EDGE, MIX_WIDE - XBC), f32)
        g_halo[0] = edge_held[...].astype(bf16)

    @pl.when(step >= 4)
    def _():
        late_columns(
            where[1], step - 4, normed_t, halo_t, g_held, halo_held, taps, head_sums, skip_part,
            gather, mine, (send_0, send_1, send_2, send_3), held, sent, sems,
        )


def both_cores(where, mine, other):
    first = where[1] == 0
    return jnp.where(first, mine, other), jnp.where(first, other, mine)


def join_kernel(where, mine, other, through, through_other, spread, total, wide):
    first = where[1] == 0
    own = jnp.where(first, through[0:2], through[2:4])
    theirs = jnp.where(first, through_other[0:2], through_other[2:4])
    through_0, through_1 = both_cores(where, own, theirs)
    everything_0, everything_1 = both_cores(where, through[...], through_other[...])
    rows = jnp.concatenate([through_0, through_1, jnp.zeros((4, LANES), f32)], 0)
    wide[...] = widen(halves(rows), spread[...])
    row = lax.broadcasted_iota(jnp.int32, (16, LANES), 0)
    piece = jnp.zeros((16, LANES), f32)
    for c, source in enumerate((everything_0, everything_1)):
        for p, value in enumerate(halves(source)):
            for a in range(4):
                piece = jnp.where(row == 4 * a + 2 * c + p, value[a : a + 1].astype(f32), piece)
    piece = piece.astype(bf16)
    for a in range(2):
        for part in range(8):
            span = slice(part * 16, (part + 1) * 16)
            state_0, state_1 = both_cores(
                where, mine[a, span].astype(f32), other[a, span].astype(f32)
            )
            value = wide[2 + a : 3 + a] * state_0 + state_1
            total[8 * a + part, :, 0:INNER] = value.astype(bf16)
            total[8 * a + part, :, INNER:] = piece


def split_kernel(where, back, mine, other, wide, kept, given):
    for a in range(2):
        for part in range(8):
            span = slice(part * 16, (part + 1) * 16)
            state_0, _ = both_cores(where, mine[a, span].astype(f32), other[a, span].astype(f32))
            in_0 = back[8 * a + part].astype(f32)
            in_1 = wide[a : a + 1] * in_0 + state_0
            keeps, gives = both_cores(where, in_0, in_1)
            kept[a, span] = keeps.astype(bf16)
            given[a, span] = gives.astype(bf16)


def scan_kernel(where, arrived, spread, before, factors, picked):
    chip = where[3] * 4 + where[4]
    forward = 2 * where[1] + chip // 8
    backward = (2 * chip + where[1]) // 8
    row = lax.broadcasted_iota(jnp.int32, (8, 16), 0)
    column = lax.broadcasted_iota(jnp.int32, (8, 16), 1)
    wanted = jnp.where(row < 2, 4 * forward + 2 * row, 4 * backward + 2 * (row - 2))
    chosen = (column >= wanted) & (column < wanted + 2) & (row < 4)
    chosen = jnp.where(chosen, 1.0, 0.0).astype(bf16)
    for i in range(16):
        picked[8 * i : 8 * (i + 1)] = mm(chosen, arrived[i, :, INNER:])
    factors[...] = widen(halves(picked[...]), spread[...])
    so_far = jnp.zeros((16, INNER), f32)
    for i in range(16):
        before[i] = so_far.astype(bf16)
        factor = factors[8 * i : 8 * i + 1] * factors[8 * i + 1 : 8 * i + 2]
        so_far = factor * so_far + arrived[i, :, :INNER].astype(f32)


def scan_back_kernel(arrived, factors, after):
    so_far = jnp.zeros((16, INNER), f32)
    for i in reversed(range(32)):
        after[i] = so_far.astype(bf16)
        at = 8 * (i // 2) + 2 + i % 2
        so_far = factors[at : at + 1] * so_far + arrived[i].astype(f32)


def pair_kernel(mine, *rest):
    pair = rest[-1]
    count = rest[0].shape[0]
    for k, other in enumerate(rest[:-1]):
        rows = slice(count * k, count * (k + 1))
        pair[rows] = (mine[rows].astype(f32) + other[...].astype(f32)).astype(bf16)


def reduce_early_kernel(parts, owned):
    total = parts[0].astype(f32)
    for k in range(1, 16):
        total = total + parts[k].astype(f32)
    owned[...] = total.astype(bf16)


def reduce_kernel(early, late, owned):
    held = [early[:, columns(k)] for k in range(3)]
    total = late[0].astype(f32)
    for k in range(1, 64):
        total = total + late[k].astype(f32)
    total = total.astype(bf16)
    for copy in range(16):
        for k in range(3):
            owned[copy, 48 * k : 48 * (k + 1)] = held[k]
        owned[copy, 144:240] = total


def last_kernel(
    hidden, cotangent, mixed, g_gates, g_mix, spill, mix_weight, gate_weight, out_full, params,
    output, grad_hidden, held,
):
    x = hidden[0].astype(f32)
    output[0] = (x + mm(mixed[0], out_full[...])).astype(bf16)
    held[...] = g_mix[0, :, 0:MIX_PAD]
    end = g_mix[0, TOKENS - 16 :, 0:XBC].astype(f32)
    shift = jnp.concatenate([jnp.zeros((8, XBC), f32), spill[0].astype(f32)], 0)
    held[TOKENS - 16 :, 0:XBC] = (end + shift).astype(bf16)
    grad = mm_nt(held[...], mix_weight[...]) + mm_nt(g_gates[0], gate_weight[...])
    grad = grad * params[GAIN : GAIN + 1, 0:768]
    scale = lax.rsqrt(jnp.mean(x * x, axis=1, keepdims=True) + epsilon)
    pull = jnp.mean(grad * x, axis=1, keepdims=True)
    value = cotangent[0].astype(f32) + scale * grad - x * (scale * scale * scale * pull)
    grad_hidden[0] = value.astype(bf16)


def finish_kernel(
    where, shared, other, weight, gain, out_weight, gate_gain,
    grad, by_gain, conv_w, conv_b, grad_dt, grad_a, grad_skip, grad_out, by_gate_gain,
    sums, out_sums,
):
    up = pl.program_id(0)
    first = where[1] == 0

    def both(j, rows):
        a, b = shared[j, rows].astype(f32), other[j, rows].astype(f32)
        return jnp.where(first, a, b), jnp.where(first, b, a)

    for right in range(4):
        half, side = divmod(right, 2)
        for k in range(3):
            low, high = both(4 * up + right, slice(48 * k, 48 * (k + 1)))
            grad[:, columns(3 * right + k)] = low
            grad_out[half, :, columns(3 * side + k)] = high
    from_core = up // 2
    rows = pl.ds(pl.multiple_of(144 + 48 * lax.rem(up, 2), 16), 48)
    for j in range(15):
        begin = INNER + LANES * j
        width = min(LANES, INNER + MIX - begin)
        low, high = both(j, rows)
        grad[:, begin : begin + width] = jnp.where(from_core == 0, low, high)[:, 0:width]
    total = jnp.sum(grad[...] * weight[...].astype(f32), axis=1, keepdims=True)
    sums[pl.ds(pl.multiple_of(48 * up, 48), 48)] = jnp.broadcast_to(total, (48, LANES))
    for half in range(2):
        total = jnp.sum(grad_out[half] * out_weight[half].astype(f32), axis=1, keepdims=True)
        begin = pl.multiple_of(192 * half + 48 * up, 48)
        out_sums[pl.ds(begin, 48)] = jnp.broadcast_to(total, (48, LANES))

    @pl.when(up == 3)
    def _():
        by_gain[...] = sums[...].T[0:1].reshape(192) / gain[...]
        by_gate_gain[...] = out_sums[...].T[0:1].reshape(384) / gate_gain[...]
        rest, _ = both(15, slice(144, 240))
        for part in range(4):
            span = min(LANES, 448 - LANES * part)
            lanes = slice(LANES * part, LANES * part + span)
            conv_w[:, lanes] = rest[16 * part : 16 * part + 4, 0:span]
            conv_b[lanes] = rest[16 * part + 4 : 16 * part + 5, 0:span].reshape(span)
        for z in range(4):

            @pl.when(where[0] == z)
            def _(z=z):
                heads = pltpu.roll(rest[64:72], (LANES - 6 * z) % LANES, 1)
                for k, target in enumerate((grad_dt, grad_a, grad_skip)):
                    target[...] = heads[k : k + 1, 0:6].reshape(6)


def per_device(
    hidden,
    segments,
    norm_gain,
    in_weight,
    conv_weight,
    conv_bias,
    dt_bias,
    a_log,
    skip,
    gate_gain,
    out_weight,
    cotangent,
):
    core = lax.axis_index("seq_2")
    place = lax.axis_index("fsdp")
    chip = lax.axis_index("seq_0") * 4 + lax.axis_index("seq_1")
    where = jnp.stack(
        [
            place, core, (chip * 2 + core) * TOKENS, lax.axis_index("seq_0"),
            lax.axis_index("seq_1"),
        ]
    ).astype(jnp.int32)

    message, mix_tail = call(
        message_kernel,
        [(None, shaped((96, MIX_PAD), bf16)), (None, shaped((192, LANES), bf16))],
        [SCALARS] + [None] * 8,
        [
            where, in_weight, norm_gain, conv_weight, conv_bias, dt_bias, a_log, skip, gate_gain,
        ],
        scratch=[
            pltpu.VMEM((16, 512), f32), pltpu.VMEM((192, LANES), f32), pltpu.VMEM((96, LANES), f32)
        ],
        mib=LARGE,
    )
    mix_fetched = fetch(message)
    halo = line(hidden[:, TOKENS - EDGE :], SEQ, 1)

    head_of = np.arange(INNER) // HEADDIM
    spread = jnp.asarray((np.arange(LANES)[:, None] == head_of[None]), bf16)
    gather = jnp.asarray((head_of[:, None] == np.arange(LANES)[None]), bf16)
    lower = jnp.asarray(np.tril(np.ones((TOKENS, TOKENS))), bf16)
    upper = jnp.asarray(np.triu(np.ones((TOKENS, TOKENS))), bf16)
    low_lanes = jnp.asarray(np.ones((TOKENS, 1)) * (np.arange(LANES) < 64), bf16)
    high_lanes = jnp.asarray(np.ones((TOKENS, 1)) * (np.arange(LANES) >= 64), bf16)

    tokens = shaped((4, TOKENS, LANES))
    second, second_done = call(
        second_message_kernel,
        [(None, shaped((192, INNER), bf16))],
        [SCALARS, ANYWHERE, ANYWHERE],
        [where, in_weight, out_weight],
        scratch=[pltpu.SemaphoreType.DMA((3,))],
        marked=True,
        mib=LARGE,
    )
    same, keep, ending, passing, halo = call(
        tables_kernel,
        [
            (None, tokens), (None, tokens), (None, tokens), (None, shaped((4, LANES))),
            (None, shaped((4, EDGE, 768))),
        ],
        [SCALARS, None, None],
        [where, segments, halo],
        micros=60,
        after=[second_done],
    )
    half = shaped((2, STATE, INNER), bf16)
    (
        params, mixin, mixin_halo, active, dt_arg, dt, cumul, through, local_mine, local_send,
        normed, normed_t, halo_t, mix_weight,
    ) = call(
        front_kernel,
        [
            (None, shaped((16, XBC))),
            (ANYWHERE, shaped((4, TOKENS, XBC), bf16)),
            (None, shaped((4, EDGE, XBC))),
            (ANYWHERE, shaped((4, TOKENS, XBC), bf16)),
            (None, tokens),
            (None, tokens),
            (None, tokens),
            (None, shaped((4, LANES))),
            (ANYWHERE, half),
            (ANYWHERE, half),
            (ANYWHERE, shaped((512, 768), bf16)),
            (ANYWHERE, shaped((768, 512), bf16)),
            (None, shaped((768, LANES), bf16)),
            (ANYWHERE, shaped((768, MIX_PAD), bf16)),
        ],
        [SCALARS] + [None] * 6 + [ANYWHERE] * 9,
        [where, hidden, halo, ending, passing, spread, lower, message, in_weight, mix_tail]
        + mix_fetched
        + [swap(part) for part in mix_fetched],
        scratch=[
            pltpu.VMEM((768, MIX_PAD), bf16),
            pltpu.VMEM((4, 96, LANES), bf16),
            pltpu.VMEM((512, 768), bf16),
            pltpu.VMEM((768, 512), bf16),
            pltpu.VMEM((4, TOKENS, XBC), bf16),
            pltpu.VMEM((4, TOKENS, XBC), bf16),
            pltpu.VMEM((4, STATE, INNER), bf16),
            pltpu.VMEM((2, 8, EDGE + TOKENS, LANES), f32),
            pltpu.VMEM((4, STATE, TOKENS), bf16),
            pltpu.VMEM((512, LANES), bf16),
            pltpu.VMEM((2, 512, 256), f32),
            pltpu.SemaphoreType.DMA((12,)),
            pltpu.SemaphoreType.DMA((29,)),
        ],
        mib=LARGE,
        micros=10,
    )

    blocks = shaped((16, 16, INNER), bf16)
    local_other = swap(local_send)
    through_other = swap(through)
    total, wide, joined = call(
        join_kernel,
        [(None, shaped((16, 16, INNER + LANES), bf16)), (None, shaped((8, INNER)))],
        [SCALARS] + [None] * 5,
        [where, local_mine, local_other, through, through_other, spread],
        marked=True,
        micros=0,
    )
    fetched = fetch(second)
    inner, inner_done = call(
        inner_kernel,
        [(by_seq(TOKENS, INNER), shaped((4, TOKENS, INNER)))],
        [
            by_seq(TOKENS, XBC), by_seq(TOKENS, LANES), by_seq(TOKENS, LANES),
            by_seq(TOKENS, TOKENS), constant(LANES, INNER), constant(TOKENS, LANES),
            constant(TOKENS, LANES),
        ],
        [active, dt, cumul, same, spread, low_lanes, high_lanes],
        grid=(4,),
        scratch=[pltpu.VMEM((TOKENS, INNER), f32)],
        mib=LARGE,
        marked=True,
        micros=60,
        after=[joined],
    )
    before, factors, scanned = call(
        scan_kernel,
        [(None, blocks), (None, shaped((128, INNER)))],
        [SCALARS, None, None],
        [where, exchange(total, CHIPS), spread],
        scratch=[pltpu.VMEM((128, LANES), f32)],
        marked=True,
        micros=0,
        after=[inner_done],
    )
    gate_weight, out_full, gates, g_mixed, projected = call(
        weights_kernel,
        [
            (ANYWHERE, shaped((768, INNER), bf16)),
            (ANYWHERE, shaped((INNER, 768), bf16)),
            (ANYWHERE, shaped((512, INNER), bf16)),
            (ANYWHERE, shaped((512, INNER), bf16)),
        ],
        [SCALARS, None, None] + [ANYWHERE] * 8,
        [where, normed, cotangent.reshape(512, 768), in_weight, out_weight]
        + fetched
        + [swap(part) for part in fetched],
        scratch=[
            pltpu.VMEM((768, INNER), bf16),
            pltpu.VMEM((INNER, 768), bf16),
            pltpu.VMEM((512, INNER), bf16),
            pltpu.VMEM((512, INNER), bf16),
            pltpu.SemaphoreType.DMA((20,)),
            pltpu.SemaphoreType.DMA((14,)),
        ],
        marked=True,
        micros=0,
        mib=LARGE,
        after=[scanned],
    )
    gates = gates.reshape(4, TOKENS, INNER)
    g_mixed = g_mixed.reshape(4, TOKENS, INNER)
    kept, given = call(
        split_kernel,
        [(None, half), (None, half)],
        [SCALARS] + [None] * 4,
        [where, exchange(before, CHIPS), local_mine, local_other, wide],
        micros=0,
        after=[projected],
    )
    given = swap(given)

    mixed, g_y, g_gates, row_part, skip_part, g_state, middle_done = call(
        middle_kernel,
        [
            (by_seq(TOKENS, INNER), shaped((4, TOKENS, INNER), bf16)),
            (by_seq(TOKENS, INNER), shaped((4, TOKENS, INNER), bf16)),
            (by_seq(TOKENS, INNER), shaped((4, TOKENS, INNER), bf16)),
            (by_seq(TOKENS, LANES), tokens),
            (constant(8, INNER), shaped((8, INNER))),
            (by_seq(STATE, INNER), shaped((4, STATE, INNER), bf16)),
        ],
        [
            by_seq(TOKENS, INNER), by_seq(TOKENS, XBC), own_half(STATE, INNER),
            other_half(STATE, INNER), by_seq(TOKENS, INNER), by_seq(TOKENS, INNER),
            by_seq(TOKENS, LANES), by_seq(TOKENS, LANES), constant(16, XBC),
            constant(LANES, INNER), constant(INNER, LANES),
        ],
        [inner, active, kept, given, gates, g_mixed, cumul, keep, params, spread, gather],
        scalars=where,
        grid=(4,),
        scratch=[pltpu.VMEM((TOKENS, INNER), f32)] * 5 + [pltpu.VMEM((TOKENS, INNER), bf16)],
        mib=LARGE,
        marked=True,
        micros=11,
    )

    blocks_back = shaped((32, 16, INNER), bf16)
    arrived_back = exchange(g_state.reshape(32, 16, INNER), SEQ)

    early_shape = shaped((768, INNER), bf16)
    early_mine, *early_send, early_done = call(
        early_grads_kernel,
        [(ANYWHERE, early_shape)] + [(ANYWHERE, shaped((192, INNER), bf16))] * 4,
        [SCALARS] + [ANYWHERE] * 4,
        [
            where, mixed.reshape(512, INNER), cotangent.reshape(512, 768), normed_t,
            g_gates.reshape(512, INNER),
        ],
        scratch=[
            pltpu.VMEM((512, INNER), bf16),
            pltpu.VMEM((512, 768), bf16),
            pltpu.VMEM((768, 512), bf16),
            pltpu.VMEM((512, INNER), bf16),
            pltpu.VMEM((768, INNER), bf16),
            pltpu.VMEM((768, INNER), bf16),
            pltpu.SemaphoreType.DMA((4,)),
            pltpu.SemaphoreType.DMA((8,)),
        ],
        marked=True,
        mib=LARGE,
        micros=60,
        after=[middle_done],
    )
    parts = call(
        early_pair_kernel,
        [(None, shaped((192, INNER), bf16))] * 4,
        [None] * 5,
        [early_mine] + [swap(part) for part in early_send],
        micros=0,
    )
    early_parts = [parts[0]] + [ring(parts[k], "fsdp", k) for k in (1, 2, 3)]

    after, scanned_back = call(
        scan_back_kernel,
        [(None, blocks_back)],
        [None] * 2,
        [arrived_back, factors],
        marked=True,
        micros=2,
        after=[early_done],
    )

    g_inner, g_b, g_c, direct, column, inner_back_done = call(
        inner_back_kernel,
        [
            (by_seq(TOKENS, INNER), shaped((4, TOKENS, INNER), bf16)),
            (by_seq(TOKENS, STATE), tokens),
            (by_seq(TOKENS, STATE), tokens),
            (by_seq(TOKENS, LANES), tokens),
            (by_seq(TOKENS, LANES), tokens),
        ],
        [
            by_seq(TOKENS, XBC), by_seq(TOKENS, INNER), own_half(STATE, INNER),
            other_half(STATE, INNER), by_seq(TOKENS, LANES), by_seq(TOKENS, LANES),
            by_seq(TOKENS, LANES), by_seq(TOKENS, TOKENS), constant(LANES, INNER),
            constant(INNER, LANES), constant(TOKENS, LANES), constant(TOKENS, LANES),
        ],
        [
            active, g_y, kept, given, dt, cumul, keep, same, spread, gather, low_lanes, high_lanes,
        ],
        scalars=where,
        grid=(4,),
        scratch=[pltpu.VMEM((TOKENS, INNER), f32)] * 2 + [pltpu.VMEM((TOKENS, INNER), bf16)] * 4,
        mib=LARGE,
        marked=True,
        micros=60,
        after=[scanned_back],
    )
    early_blocks, early_summed = call(
        sum_blocks_kernel,
        [(None, shaped((16, 48, 384), bf16))],
        [None] * 4,
        early_parts,
        marked=True,
        micros=0,
        after=[inner_back_done],
    )
    g_end = exchange(after, SEQ).reshape(4, STATE, INNER)
    late_spec = pl.BlockSpec((4, 4, 96, LANES), lambda s, *_: (jnp.maximum(s - 4, 0), 0, 0, 0))
    late_shape = shaped((16, 4, 96, LANES), bf16)
    piece = shaped((16 // LATE_PIECES, 4, 96, LANES), bf16)
    g_mix, g_halo, late_mine, *late_send, late_done = call(
        late_kernel,
        [
            (seq_first(TOKENS, MIX_WIDE), shaped((4, TOKENS, MIX_WIDE), bf16)),
            (seq_first(EDGE, XBC), shaped((4, EDGE, XBC), bf16)),
            (late_spec, late_shape),
        ]
        + [(ANYWHERE, piece)] * LATE_PIECES,
        [seq_first(STATE, INNER), own_half(STATE, INNER), other_half(STATE, INNER)]
        + [
            pl.BlockSpec((1, TOKENS, 256), lambda a, *_: (jnp.minimum(a, 3), 0, 6)),
            seq_first(TOKENS, XBC), seq_first(EDGE, XBC), seq_first(TOKENS, INNER),
            seq_first(TOKENS, INNER), seq_first(TOKENS, STATE), seq_first(TOKENS, STATE),
        ]
        + [seq_first(TOKENS, LANES)] * 7
        + [
            constant(4, LANES), constant(16, XBC), constant(LANES, INNER), constant(INNER, LANES),
            constant(TOKENS, TOKENS), constant(768, 512), constant(768, LANES), constant(8, INNER),
        ],
        [
            g_end, kept, given, active, mixin, mixin_halo, g_y, g_inner, g_b, g_c, dt,
            dt_arg, cumul, ending, row_part, direct, column, through, params, spread, gather, upper,
            normed_t, halo_t, skip_part,
        ],
        scalars=where,
        grid=(8,),
        scratch=[
            pltpu.VMEM((TOKENS, INNER), bf16),
            pltpu.VMEM((STATE, INNER), bf16),
            pltpu.VMEM((2, EDGE + TOKENS, LANES), f32),
            pltpu.VMEM((2, 144, LANES), f32),
            pltpu.VMEM((8, INNER), f32),
            pltpu.VMEM((512, MIX_WIDE), bf16),
            pltpu.VMEM((32, MIX_WIDE), f32),
            pltpu.VMEM((8, XBC), f32),
            pltpu.VMEM((8, LANES), f32),
            pltpu.VMEM((2, 4, 4, 96, LANES), bf16),
            pltpu.VMEM((16, 4, 96, LANES), bf16),
            pltpu.VMEM((EDGE, XBC), f32),
            pltpu.SemaphoreType.DMA((LATE_PIECES,)),
        ],
        marked=True,
        mib=LARGE,
        micros=60,
        after=[early_summed, inner_back_done],
    )
    early_owned, early_reduced = call(
        reduce_early_kernel,
        [(None, shaped((48, 384), bf16))],
        [None],
        [exchange(early_blocks, CHIPS)],
        marked=True,
        micros=0,
        after=[late_done],
    )
    spill = line(g_halo, SEQ, -1)
    late_pair, paired = call(
        pair_kernel,
        [(None, late_shape)],
        [None] * (1 + LATE_PIECES),
        [late_mine] + [swap(part) for part in late_send],
        marked=True,
        micros=0,
        after=[spill, early_reduced],
    )
    late_parts = exchange(late_pair.reshape(64, 96, LANES), COLUMNS)

    rows = by_seq(TOKENS, 768)
    output, grad_hidden, last_done = call(
        last_kernel,
        [(rows, shaped((4, TOKENS, 768), bf16)), (rows, shaped((4, TOKENS, 768), bf16))],
        [
            rows, rows, by_seq(TOKENS, INNER), by_seq(TOKENS, INNER), by_seq(TOKENS, MIX_WIDE),
            by_seq(EDGE, XBC), constant(768, MIX_PAD), constant(768, INNER), constant(INNER, 768),
            constant(16, XBC),
        ],
        [
            hidden, cotangent, mixed, g_gates, g_mix, spill, mix_weight, gate_weight, out_full,
            params,
        ],
        grid=(4,),
        scratch=[pltpu.VMEM((TOKENS, MIX_PAD), bf16)],
        mib=LARGE,
        marked=True,
        micros=60,
        after=[paired],
    )
    (owned,) = call(
        reduce_kernel,
        [(None, shaped((16, 240, LANES), bf16))],
        [None] * 2,
        [early_owned, late_parts],
        micros=2,
        after=[last_done],
    )
    shared = exchange(owned, CHIPS)
    sum_in, by_gain, sum_conv_w, sum_conv_b, sum_dt, sum_a, sum_skip, sum_out, by_gate_gain = call(
        finish_kernel,
        [
            (pl.BlockSpec((48, INNER + MIX), lambda i, *_: (i, 0)), shaped((192, INNER + MIX))),
            (constant(192), shaped((192,))),
            (constant(4, 448), shaped((4, 448))),
            (constant(448), shaped((448,))),
            (constant(6), shaped((6,))),
            (constant(6), shaped((6,))),
            (constant(6), shaped((6,))),
            (pl.BlockSpec((2, 48, 768), lambda i, *_: (0, i, 0)), shaped((2, 192, 768))),
            (constant(384), shaped((384,))),
        ],
        [
            constant(16, 240, LANES), constant(16, 240, LANES),
            pl.BlockSpec((48, INNER + MIX), lambda i, *_: (i, 0)), constant(192),
            pl.BlockSpec((2, 48, 768), lambda i, *_: (0, i, 0)), constant(384),
        ],
        [
            shared, swap(shared), in_weight, norm_gain.astype(f32),
            out_weight.reshape(2, 192, 768), gate_gain.astype(f32),
        ],
        scalars=where,
        grid=(4,),
        scratch=[pltpu.VMEM((192, LANES), f32), pltpu.VMEM((384, LANES), f32)],
        micros=4,
    )

    return (
        output,
        grad_hidden,
        by_gain,
        sum_in,
        sum_conv_w,
        sum_conv_b,
        sum_dt,
        sum_a,
        sum_skip,
        by_gate_gain,
        sum_out.reshape(384, 768),
    )


def solution(mesh):
    finer = Mesh(
        mesh.devices.reshape(4, 4, 2, mesh.shape["fsdp"]), ("seq_0", "seq_1", "seq_2", "fsdp")
    )
    in_specs = (
        P("fsdp", SEQ, None),
        P("fsdp", SEQ),
        P("fsdp"),
        P("fsdp", None),
        P(None, "fsdp"),
        P("fsdp"),
        P("fsdp"),
        P("fsdp"),
        P("fsdp"),
        P("fsdp"),
        P("fsdp", None),
        P("fsdp", SEQ, None),
    )
    out_specs = (
        P("fsdp", SEQ, None),
        P("fsdp", SEQ, None),
        P("fsdp"),
        P("fsdp", None),
        P(None, "fsdp"),
        P("fsdp"),
        P("fsdp"),
        P("fsdp"),
        P("fsdp"),
        P("fsdp"),
        P("fsdp", None),
    )
    return jax.shard_map(
        per_device, mesh=finer, in_specs=in_specs, out_specs=out_specs, check_vma=False
    )
```

```python
import functools

import jax
import jax.numpy as jnp
import numpy as np
from jax import lax
from jax.experimental import pallas as pl
from jax.experimental.pallas import tpu as pltpu
from jax.sharding import Mesh
from jax.sharding import PartitionSpec as P

INNER = 1536
HEADS = 24
HEADDIM = 64
STATE = 128
XBC = 1792
MIX = 1816
MIX_PAD = 1920
MIX_WIDE = 2048
EDGE = 8
TOKENS = 128
LANES = 128
PAIRS = 12
SEQ = ("seq_0", "seq_1", "seq_2")
CHIPS = ("seq_0", "seq_1")
COLUMNS = ("seq_0", "seq_1", "fsdp")

epsilon = 1e-05
bf16 = jnp.bfloat16
f32 = jnp.float32
VMEM_MIB = 24
LARGE = 60
LATE_PIECES = 4
COST = 1.1e9

CONV_W, CONV_B, GATE_GAIN, GAIN, DT_BIAS, DECAY, SKIP, SKIP_WIDE = 0, 4, 5, 6, 7, 8, 9, 10


def ring(value, axis, steps):
    count = lax.axis_size(axis)
    pairs = [(source, (source + steps) % count) for source in range(count)]
    return lax.ppermute(value, axis, pairs)


def line(value, axis, steps):
    count = lax.axis_size(axis)
    initial, last = (max(0, -steps), min(count, count - steps))
    return lax.ppermute(value, axis, [(source, source + steps) for source in range(initial, last)])


def swap(value):
    return ring(value, "seq_2", 1)


def dot(pattern, left, right):
    return jnp.einsum(pattern, left, right, preferred_element_type=f32)


def exchange(blocks, axes):
    return lax.all_to_all(blocks, axes, 0, 0, tiled=False)


def split_three(value):
    high = value.astype(bf16)
    rest = value - high.astype(f32)
    middle = rest.astype(bf16)
    low = (rest - middle.astype(f32)).astype(bf16)
    return high, middle, low


def mm(left, right):
    return lax.dot_general(left, right, (((1,), (0,)), ((), ())), preferred_element_type=f32)


def mm_nt(left, right):
    return lax.dot_general(left, right, (((1,), (1,)), ((), ())), preferred_element_type=f32)


def mm_tn(left, right):
    return lax.dot_general(left, right, (((0,), (0,)), ((), ())), preferred_element_type=f32)


def exact_mm(ones, value):
    high, middle, low = split_three(value)
    return mm(ones, high) + mm(ones, middle) + mm(ones, low)


def halves(value):
    high = value.astype(bf16)
    return high, (value - high.astype(f32)).astype(bf16)


def widen(pieces, spread):
    return mm(pieces[0], spread) + mm(pieces[1], spread)


def sum_heads(value, gather):
    high, low = halves(value)
    return mm(high, gather) + mm(low, gather)


def sigmoid(value):
    return 0.5 * jnp.tanh(0.5 * value) + 0.5


HBM = pl.BlockSpec(memory_space=pltpu.HBM)


def call(
    kernel, outs, ins, operands, grid=None, scratch=(), micros=1, after=(), mib=VMEM_MIB, scalars=None,
    marked=False,
):
    whole = pl.BlockSpec(memory_space=pltpu.VMEM)
    lead = [] if scalars is None else [scalars]
    count = len(operands) + len(lead)
    if marked:
        outs = list(outs) + [(HBM, shaped((8, LANES)))]
    first = count + len(after)
    last = first + len(outs) - marked

    def body(*refs):
        kernel(*refs[:count], *refs[first:last], *refs[last + marked :])

    return pl.pallas_call(
        body,
        grid_spec=pltpu.PrefetchScalarGridSpec(
            num_scalar_prefetch=len(lead),
            grid=grid or (),
            in_specs=[spec or whole for spec in ins]
            + [HBM] * len(after),
            out_specs=[spec or whole for spec, _ in outs],
            scratch_shapes=list(scratch),
        ),
        out_shape=[shape for _, shape in outs],
        compiler_params=pltpu.CompilerParams(vmem_limit_bytes=mib * 1024 * 1024),
        cost_estimate=pl.CostEstimate(
            flops=int(micros * COST), bytes_accessed=0, transcendentals=0
        ),
    )(*lead, *operands, *after)


def shaped(shape, dtype=f32):
    return jax.ShapeDtypeStruct(shape, dtype)


def by_seq(*shape):
    return pl.BlockSpec((1,) + shape, lambda a, *_: (a,) + (0,) * len(shape))


def constant(*shape):
    return pl.BlockSpec(shape, lambda a, *_: (0,) * len(shape))


def seq_first(*shape):
    return pl.BlockSpec(
        (1,) + shape, lambda a, *_: (jnp.minimum(a, 3),) + (0,) * len(shape)
    )


def own_half(*shape):
    return pl.BlockSpec(
        (1,) + shape,
        lambda a, where: (jnp.clip(a - 2 * where[1], 0, 1),) + (0,) * len(shape),
    )


def other_half(*shape):
    return pl.BlockSpec(
        (1,) + shape,
        lambda a, where: (jnp.clip(a - 2 + 2 * where[1], 0, 1),) + (0,) * len(shape),
    )


ANYWHERE = pl.BlockSpec(memory_space=pl.ANY)
SCALARS = pl.BlockSpec(memory_space=pltpu.SMEM)


def columns(index, width=LANES):
    return slice(index * width, (index + 1) * width)


def groups():
    listed = []
    for row, count in (
        (CONV_W, 7), (CONV_W + 1, 7), (CONV_W + 2, 7), (CONV_W + 3, 7), (CONV_B, 7), (GATE_GAIN, 6),
        (GAIN, 3),
    ):
        for j in range(count):
            listed.append((row, j, len(listed)))
    return listed


SPANS = {CONV_B: 448, GATE_GAIN: 384, GAIN: 192}
HEAD_LINE = 44


def message_kernel(
    where, in_weight, norm_gain, conv_weight, conv_bias, dt_bias, a_log, skip, gate_gain,
    message, tail, held, narrow, lines,
):
    core = where[1]
    narrow[...] = jnp.zeros_like(narrow)
    narrow[:, 0 : MIX - XBC] = in_weight[:, INNER + XBC :].astype(f32)
    tail[...] = narrow[...].astype(bf16)
    half = pl.ds(pl.multiple_of(core * 96, 96), 96)
    message[:, 0:XBC] = in_weight[half, INNER : INNER + XBC]
    held[...] = jnp.zeros_like(held)
    held[CONV_W : CONV_W + 4, 0:448] = conv_weight[...].astype(f32)
    for target, source in (
        (CONV_B, conv_bias), (GATE_GAIN, gate_gain), (GAIN, norm_gain), (DT_BIAS, dt_bias),
        (DECAY, a_log), (SKIP, skip),
    ):
        size = source.shape[0]
        held[target : target + 1, 0:size] = source[...].astype(f32).reshape(1, size)
    lane = lax.broadcasted_iota(jnp.int32, (1, LANES), 1)
    lines[...] = jnp.zeros_like(lines)
    for row, j, line in groups():
        tile = held[row : row + 1, columns(j // 2)]
        tile = tile if j % 2 else pltpu.roll(tile, 64, 1)
        lines[line : line + 1] = jnp.where(lane < 64, 0.0, tile)
    heads = pltpu.roll(held[DT_BIAS : DT_BIAS + 1, 0:LANES], 64, 1)
    heads = heads + pltpu.roll(held[DECAY : DECAY + 1, 0:LANES], 70, 1)
    lines[HEAD_LINE : HEAD_LINE + 1] = heads + pltpu.roll(held[SKIP : SKIP + 1, 0:LANES], 76, 1)
    message[:, XBC:] = (narrow[half] + lines[...]).astype(bf16)


def tables_kernel(where, segments, halo, same, keep, ending, passing, halo_held):
    start = where[2].astype(f32)
    below = lax.broadcasted_iota(jnp.int32, (TOKENS, TOKENS), 0) >= lax.broadcasted_iota(
        jnp.int32, (TOKENS, TOKENS), 1
    )
    for a in range(4):
        row = jnp.broadcast_to(segments[a : a + 1].astype(f32), (TOKENS, TOKENS))
        column = row.T
        first, last = column[0:1], column[TOKENS - 1 :]
        same[a] = jnp.where((column == row) & below, 1.0, 0.0)
        keep[a] = jnp.where((column == first) & (first < start), 1.0, 0.0)
        ending[a] = jnp.where(column == last, 1.0, 0.0)
        passing[a : a + 1] = jnp.where(last < start, 1.0, 0.0)
        halo_held[a] = halo[a].astype(f32)


def second_message_kernel(where, in_weight, out_weight, message, sems):
    core = where[1]
    low = pl.multiple_of(core * 192, 192)
    copies = [
        pltpu.make_async_copy(
            in_weight.at[pl.ds(pl.multiple_of(core * 96, 96), 96), pl.ds(0, INNER)],
            message.at[pl.ds(0, 96)],
            sems.at[0],
        )
    ]
    for k in range(2):
        copies.append(
            pltpu.make_async_copy(
                out_weight.at[pl.ds(low + 96 * k, 96)],
                message.at[pl.ds(96, 96), pl.ds(768 * k, 768)],
                sems.at[1 + k],
            )
        )
    for copy in copies:
        copy.start()
    for copy in copies:
        copy.wait()


def weights_kernel(
    where, normed, cotangent, in_weight, out_weight, m_1, m_2, m_3, o_1, o_2, o_3,
    gate_full, out_full, gates, g_mixed,
    gate_held, out_held, gates_held, g_held, in_sems, out_sems,
):
    place, core = where[0], where[1]
    gate_copies = weight_copies(
        place, core, in_weight.at[:, pl.ds(0, INNER)], (m_1, m_2, m_3), (o_1, o_2, o_3), gate_held,
        in_sems,
    )
    out_copies = [
        pltpu.make_async_copy(
            out_weight, out_held.at[pl.ds(pl.multiple_of(place * 384, 384), 384)], in_sems.at[7]
        )
    ]
    for k, (mine, other) in enumerate(((m_1, o_1), (m_2, o_2), (m_3, o_3))):
        owner = lax.rem(place + (1 + k), 4) * 384
        for which, part in ((core, mine), (1 - core, other)):
            for side in range(2):
                begin = pl.multiple_of(owner + which * 192 + 96 * side, 96)
                out_copies.append(
                    pltpu.make_async_copy(
                        part.at[pl.ds(96, 96), pl.ds(768 * side, 768)],
                        out_held.at[pl.ds(begin, 96)],
                        in_sems.at[7 + len(out_copies)],
                    )
                )
    for copy in gate_copies + out_copies:
        copy.start()
    outgoing = []

    def send(source, target):
        copy = pltpu.make_async_copy(source, target, out_sems.at[len(outgoing)])
        copy.start()
        outgoing.append(copy)

    for copy in gate_copies:
        copy.wait()
    for chunk in range(6):
        lanes, span = columns(chunk, 256), pl.ds(chunk * 256, 256)
        gates_held[:, lanes] = mm(normed[...], gate_held[:, lanes]).astype(bf16)
        send(gates_held.at[:, span], gates.at[:, span])
    send(gate_held, gate_full)
    for copy in out_copies:
        copy.wait()
    for chunk in range(6):
        lanes, span = columns(chunk, 256), pl.ds(chunk * 256, 256)
        g_held[:, lanes] = mm_nt(cotangent[...], out_held[lanes]).astype(bf16)
        send(g_held.at[:, span], g_mixed.at[:, span])
    send(out_held, out_full)
    for copy in outgoing:
        copy.wait()


def fetch(half):
    return [ring(half, "fsdp", steps) for steps in (3, 2, 1)]


def weight_copies(place, core, shard, mine, others, full, sems, own_width=None):
    rows = shard.shape[0]
    half = rows // 2
    copies = [
        pltpu.make_async_copy(
            shard,
            full.at[pl.ds(pl.multiple_of(place * rows, rows), rows), pl.ds(0, own_width or full.shape[1])],
            sems.at[0],
        )
    ]
    for k in range(3):
        owner = lax.rem(place + (1 + k), 4) * rows
        low = pl.multiple_of(owner + core * half, half)
        high = pl.multiple_of(owner + (1 - core) * half, half)
        for slot, part, begin in ((1 + 2 * k, mine[k], low), (2 + 2 * k, others[k], high)):
            copies.append(
                pltpu.make_async_copy(
                    part.at[pl.ds(0, half)], full.at[pl.ds(begin, half)], sems.at[slot]
                )
            )
    return copies


def front_kernel(
    where, hidden, halo, ending, passing, spread, lower, own, in_weight, tail,
    m_1, m_2, m_3, o_1, o_2, o_3,
    params, mixin, mixin_halo, active, dt_arg, dt, cumul, through, local_mine, local_send,
    normed, normed_t, halo_t, full,
    weight, packed, x_low, x_turned, mix_held, act_held, local_held,
    extended, state_b, scaled, wide_held, in_sems, out_sems,
):
    place, core = where[0], where[1]
    incoming = weight_copies(
        place, core, in_weight.at[:, pl.ds(INNER, XBC)], (m_1, m_2, m_3), (o_1, o_2, o_3), weight,
        in_sems, XBC,
    )
    incoming.append(
        pltpu.make_async_copy(
            tail,
            weight.at[pl.ds(pl.multiple_of(place * 192, 192), 192), pl.ds(XBC, LANES)],
            in_sems.at[11],
        )
    )
    rows_in = [
        pltpu.make_async_copy(part.at[:, pl.ds(XBC, LANES)], packed.at[k], in_sems.at[7 + k])
        for k, part in enumerate((own, m_1, m_2, m_3))
    ]
    for copy in rows_in + incoming:
        copy.start()
    outgoing = []

    def send(source, target):
        copy = pltpu.make_async_copy(source, target, out_sems.at[len(outgoing)])
        copy.start()
        outgoing.append(copy)

    for copy in rows_in:
        copy.wait()
    params[...] = jnp.zeros_like(params)
    lane = lax.broadcasted_iota(jnp.int32, (1, LANES), 1)
    for at in range(4):

        @pl.when(place == at)
        def _(at=at):
            for slot in range(4):
                z = (at + slot) % 4
                lines = packed[slot].astype(f32)
                turned = pltpu.roll(lines, 64, 1)
                for row, j, line in groups():
                    begin = SPANS.get(row, 448) * z + 64 * j
                    if begin % LANES:
                        params[row : row + 1, begin : begin + 64] = lines[line : line + 1, 64:LANES]
                    else:
                        params[row : row + 1, begin : begin + 64] = turned[line : line + 1, 0:64]
                heads = lines[HEAD_LINE : HEAD_LINE + 1]
                here = (lane >= 6 * z) & (lane < 6 * z + 6)
                for row, begin in ((DT_BIAS, 64), (DECAY, 70), (SKIP, 76)):
                    moved = pltpu.roll(heads, (LANES - begin + 6 * z) % LANES, 1)
                    params[row : row + 1, 0:LANES] += jnp.where(here, moved, 0.0)

    decay_rate = jnp.exp(params[DECAY : DECAY + 1, 0:LANES])
    params[DECAY : DECAY + 1, 0:LANES] = decay_rate
    params[SKIP_WIDE : SKIP_WIDE + 1, 0:INNER] = mm(
        params[SKIP : SKIP + 1, 0:LANES].astype(bf16), spread[...]
    )
    gain = params[GAIN : GAIN + 1, 0:768]

    def normalised(value):
        scale = lax.rsqrt(jnp.mean(value * value, axis=1, keepdims=True) + epsilon)
        return value * scale * gain

    edges = []
    for a in range(4):
        value = normalised(hidden[a].astype(f32))
        x_low[a * TOKENS : (a + 1) * TOKENS] = value.astype(bf16)
        x_turned[:, a * TOKENS : (a + 1) * TOKENS] = value.T.astype(bf16)
        edges.append(normalised(halo[a]))
    send(x_low, normed)
    send(x_turned, normed_t)
    edges = jnp.concatenate(edges, 0)
    edge_low = edges.astype(bf16)
    edges = jnp.concatenate([edges, jnp.zeros((LANES - 32, 768), f32)], 0)
    halo_t[...] = edges.T.astype(bf16)

    for copy in incoming:
        copy.wait()
    last = weight[:, XBC:].astype(f32)
    weight[:, XBC:] = jnp.where(lane < MIX - XBC, last, 0.0).astype(bf16)
    send(weight, full)
    argument = mm(x_low[...], weight[:, XBC:]) + params[DT_BIAS : DT_BIAS + 1, 0:LANES]
    steps = jnp.maximum(argument, 0.0) + jnp.log1p(jnp.exp(-jnp.abs(argument)))
    for a in range(4):
        rows = slice(a * TOKENS, (a + 1) * TOKENS)
        dt_arg[a] = argument[rows]
        dt[a] = steps[rows]
        total = exact_mm(lower[...], -steps[rows] * decay_rate)
        cumul[a] = total
        final = total[TOKENS - 1 :]
        through[a : a + 1] = jnp.exp(final) * passing[a : a + 1]
        scaled[rows] = (jnp.exp(final - total) * ending[a] * steps[rows]).astype(bf16)
    order = (6, 0, 1, 2, 3, 4, 5)

    def project(turn, a):
        chunk, slot = order[turn], turn % 2
        lanes = columns(chunk, 256)
        rows = slice(a * TOKENS, (a + 1) * TOKENS)
        if a == 0:
            edge = mm(edge_low, weight[:, lanes]).astype(bf16).astype(f32)
            for b in range(4):
                mixin_halo[b, :, lanes] = edge[b * EDGE : (b + 1) * EDGE]
                for side in range(2):
                    extended[slot, 2 * b + side, 0:EDGE] = edge[
                        b * EDGE : (b + 1) * EDGE, columns(side)
                    ]
        part = mm(x_low[rows], weight[:, lanes]).astype(bf16)
        mix_held[a, :, lanes] = part
        part = part.astype(f32)
        for side in range(2):
            extended[slot, 2 * a + side, EDGE:] = part[:, columns(side)]
        if chunk < 6:
            wide_held[slot, rows] = mm(scaled[rows], spread[:, lanes])

    def convolve(turn, a):
        chunk, slot = order[turn], turn % 2
        for side in range(2):
            lanes = columns(2 * chunk + side)
            at = 2 * a + side
            value = params[CONV_B : CONV_B + 1, lanes]
            for k in range(4):
                value = value + params[k : k + 1, lanes] * extended[
                    slot, at, EDGE - 3 + k : EDGE + 125 + k
                ]
            value = (value * sigmoid(value)).astype(bf16)
            act_held[a, :, lanes] = value
            if chunk == 6:
                if side == 0:
                    state_b[a] = value.astype(f32).T.astype(bf16)
            else:
                wide = wide_held[slot, a * TOKENS : (a + 1) * TOKENS, columns(side)]
                weighted = (wide * value.astype(f32)).astype(bf16)
                local_held[a, :, lanes] = mm(state_b[a], weighted).astype(bf16)

    for a in range(4):
        project(0, a)
    for turn, chunk in enumerate(order):
        span = pl.ds(chunk * 256, 256)
        send(mix_held.at[:, :, span], mixin.at[:, :, span])
        for a in range(4):
            if turn < 6:
                project(turn + 1, a)
            convolve(turn, a)
        send(act_held.at[:, :, span], active.at[:, :, span])
        if chunk < 6:
            own, given = pl.ds(2 * core, 2), pl.ds(2 - 2 * core, 2)
            send(local_held.at[given, :, span], local_send.at[:, :, span])
            send(local_held.at[own, :, span], local_mine.at[:, :, span])
    for copy in outgoing:
        copy.wait()


def pair_weights(p, scores, cumul, turned, same):
    made = []
    for h in (2 * p, 2 * p + 1):
        differ = cumul[:, h : h + 1] - turned[h : h + 1, :]
        decay = jnp.exp(jnp.where(same, differ, -1e30))
        made.append((decay, (scores * decay).astype(bf16)))
    return made


def inner_kernel(active, dt, cumul, same, spread, low_lanes, high_lanes, inner, dt_wide):
    b_low = active[0, :, INNER : INNER + STATE]
    c_low = active[0, :, INNER + STATE :]
    scores = mm_nt(c_low, b_low)
    total = cumul[0]
    turned = total.T
    allowed = same[0] > 0
    dt_wide[...] = mm(dt[0].astype(bf16), spread[...])
    for p in range(PAIRS):
        lanes = columns(p)
        (_, first), (_, second) = pair_weights(p, scores, total, turned, allowed)
        xdt = (dt_wide[:, lanes] * active[0, :, lanes].astype(f32)).astype(bf16)
        stacked = jnp.concatenate([xdt * low_lanes[...], xdt * high_lanes[...]], 0)
        inner[0, :, lanes] = mm(jnp.concatenate([first, second], 1), stacked)


def pick(where, kept, given, use):
    own = where[1] == pl.program_id(0) // 2

    @pl.when(own)
    def _():
        use(kept)

    @pl.when(jnp.logical_not(own))
    def _():
        use(given)


def pick_lanes(where, kept, given, lanes):
    own = where[1] == pl.program_id(0) // 2
    return jnp.where(own, kept[0, :, lanes].astype(f32), given[0, :, lanes].astype(f32)).astype(bf16)


def middle_kernel(
    where, inner, active, kept, given, gates, g_mixed, cumul, keep, params, spread, gather,
    mixed, g_y, g_gates, row_part, g_state,
    gated_held, recur_held, act_held, slope_held, unit_held, enter_held, entered,
):
    enter = (jnp.exp(cumul[0]) * keep[0]).astype(bf16)
    c_low = active[0, :, INNER + STATE :]
    squares = jnp.zeros((TOKENS, LANES), f32)
    products = jnp.zeros((TOKENS, LANES), f32)
    for p in range(PAIRS):
        lanes = columns(p)
        carried = mm(c_low, pick_lanes(where, kept, given, lanes))
        wide = mm(enter, spread[:, lanes])
        enter_held[:, lanes] = wide
        recur = inner[0, :, lanes] + wide * carried
        y = recur + params[SKIP_WIDE : SKIP_WIDE + 1, lanes] * active[0, :, lanes].astype(f32)
        gate = gates[0, :, lanes].astype(f32)
        unit_grad = g_mixed[0, :, lanes].astype(f32) * params[GATE_GAIN : GATE_GAIN + 1, lanes]
        sig = sigmoid(gate)
        act = gate * sig
        gated = y * act
        squares = squares + gated * gated
        products = products + unit_grad * gated
        gated_held[:, lanes] = gated
        recur_held[:, lanes] = recur
        act_held[:, lanes] = act
        slope_held[:, lanes] = y * (sig + act * (1.0 - sig))
        unit_held[:, lanes] = unit_grad
    scale = lax.rsqrt(jnp.sum(squares, 1, keepdims=True) * (1.0 / INNER) + epsilon)
    slant = scale * jnp.sum(products, 1, keepdims=True) * (1.0 / INNER)
    rows = jnp.zeros((TOKENS, LANES), f32)
    for p in range(PAIRS):
        lanes = columns(p)
        unit = gated_held[:, lanes] * scale
        mixed[0, :, lanes] = (unit * params[GATE_GAIN : GATE_GAIN + 1, lanes]).astype(bf16)
        g_gated = scale * (unit_held[:, lanes] - unit * slant)
        grad = g_gated * act_held[:, lanes]
        g_gates[0, :, lanes] = (g_gated * slope_held[:, lanes]).astype(bf16)
        low = grad.astype(bf16)
        g_y[0, :, lanes] = low
        low = low.astype(f32)
        rows = rows + sum_heads(low * recur_held[:, lanes], gather[lanes])
        entered[:, lanes] = (enter_held[:, lanes] * low).astype(bf16)
    row_part[0] = rows
    g_state[0] = mm_tn(c_low, entered[...]).astype(bf16)


def inner_back_kernel(
    where, active, g_y, kept, given, dt, cumul, keep, same, spread, gather, low_lanes, high_lanes,
    g_inner, g_b, g_c, direct, column, skip_part,
    dt_wide, enter_wide, entered, by_x, column_high, column_low,
):
    b_low = active[0, :, INNER : INNER + STATE]
    c_low = active[0, :, INNER + STATE :]
    scores = mm_nt(c_low, b_low)
    total = cumul[0]
    turned = total.T
    allowed = same[0] > 0
    dt_wide[...] = mm(dt[0].astype(bf16), spread[...])
    enter_wide[...] = mm((jnp.exp(total) * keep[0]).astype(bf16), spread[...])
    g_scores = jnp.zeros((TOKENS, TOKENS), f32)

    @pl.when(pl.program_id(0) == 0)
    def _():
        skip_part[...] = jnp.zeros_like(skip_part)

    for p in range(PAIRS):
        lanes = columns(p)
        (decay_1, first), (decay_2, second) = pair_weights(p, scores, total, turned, allowed)
        x = active[0, :, lanes].astype(f32)
        xdt = (dt_wide[:, lanes] * x).astype(bf16)
        grad = g_y[0, :, lanes]
        wide = grad.astype(f32)
        entered[:, lanes] = (enter_wide[:, lanes] * wide).astype(bf16)
        skip_part[:, lanes] += jnp.sum((wide * x).reshape(16, 8, LANES), 0)
        stacked = jnp.concatenate([grad * low_lanes[...], grad * high_lanes[...]], 0)
        g_weights = mm_nt(stacked, xdt)
        g_scores = g_scores + g_weights[:TOKENS] * decay_1 + g_weights[TOKENS:] * decay_2
        own = mm_tn(jnp.concatenate([first, second], 0), stacked)
        g_inner[0, :, lanes] = own.astype(bf16)
        by_x[:, lanes] = (x * own).astype(bf16)
        column_high[:, lanes], column_low[:, lanes] = halves(xdt.astype(f32) * own)
    direct[0] = mm(by_x[...], gather[...])
    column[0] = mm(column_high[...], gather[...]) + mm(column_low[...], gather[...])
    g_scores = g_scores.astype(bf16)
    from_scores = mm(g_scores, b_low)

    def add_state(state):
        g_c[0] = from_scores + mm_nt(entered[...], state[0])

    pick(where, kept, given, add_state)
    g_b[0] = mm_tn(g_scores, c_low)


def late_rows(
    where, g_end, kept, given, active, mixin, mixin_halo, g_y, g_inner, g_b, g_c,
    dt, dt_arg, cumul, ending, row_part, direct, column, through, params, spread, gather, upper,
    g_mix, taps, head_sums,
    weighted, state, extended, padded, inner_row, halo_held,
):
    a = pl.program_id(0)

    @pl.when(a == 0)
    def _():
        taps[...] = jnp.zeros_like(taps)
        head_sums[...] = jnp.zeros_like(head_sums)

    b_low = active[0, :, 0:STATE]
    decay_rate = params[DECAY : DECAY + 1, 0:LANES]
    total = cumul[0]
    steps = dt[0]
    to_end = jnp.exp(total[TOKENS - 1 :] - total) * ending[0]
    scaled = to_end * steps
    to_end_low = to_end.astype(bf16)
    scaled_low = scaled.astype(bf16)
    dt_low = steps.astype(bf16)
    through_state = jnp.zeros((TOKENS, LANES), f32)
    padded[:, 0:8] = jnp.zeros((2, 8, LANES), f32)
    padded[:, 136:144] = jnp.zeros((2, 8, LANES), f32)

    def convolved(chunk):
        lanes = columns(chunk)
        slot = chunk % 2
        extended[slot, 0:EDGE] = mixin_halo[0, :, lanes]
        extended[slot, EDGE:] = mixin[0, :, lanes].astype(f32)
        shifted = [extended[slot, EDGE - 3 + k : EDGE + 125 + k] for k in range(4)]
        value = params[CONV_B : CONV_B + 1, lanes]
        for k in range(4):
            value = value + params[k : k + 1, lanes] * shifted[k]
        return value, sigmoid(value), shifted

    def back(chunk, grad, value, sig, shifted):
        lanes = columns(chunk)
        slot = chunk % 2
        grad = grad * (sig + value * sig * (1.0 - sig))
        padded[slot, 8:136] = grad
        main = params[0:1, lanes] * padded[slot, 11:139]
        edge = params[0:1, lanes] * padded[slot, 3:11]
        for k in range(4):
            if k:
                tap = params[k : k + 1, lanes]
                main = main + tap * padded[slot, 11 - k : 139 - k]
                edge = edge + tap * padded[slot, 3 - k : 11 - k]
            taps[k : k + 1, lanes] += jnp.sum(grad * shifted[k], 0, keepdims=True)
        taps[4:5, lanes] += jnp.sum(grad, 0, keepdims=True)
        g_mix[0, :, lanes] = main.astype(bf16)
        halo_held[:, lanes] = edge

    for p in range(PAIRS):
        lanes = columns(p)
        end = g_end[0, :, lanes]
        begin = pick_lanes(where, kept, given, lanes)
        inner_row[0:1, lanes] = jnp.sum(begin.astype(f32) * end.astype(f32), 0, keepdims=True)
        state[:, lanes] = end
        from_state = mm(b_low, end)
        value, sig, shifted = convolved(p)
        x = (value * sig).astype(bf16).astype(f32)
        weighted[:, lanes] = (mm(scaled_low, spread[:, lanes]) * x).astype(bf16)
        grad = mm(dt_low, spread[:, lanes]) * (
            g_inner[0, :, lanes].astype(f32) + mm(to_end_low, spread[:, lanes]) * from_state
        ) + params[SKIP_WIDE : SKIP_WIDE + 1, lanes] * g_y[0, :, lanes].astype(f32)
        through_state = through_state + mm((x * from_state).astype(bf16), gather[lanes])
        back(p, grad, value, sig, shifted)
    state_part = scaled * through_state
    inner_sum = jnp.zeros((8, LANES), f32)
    for p in range(PAIRS):
        lanes = columns(p)
        inner_sum = inner_sum + sum_heads(inner_row[:, lanes], gather[lanes])
    mask = lax.broadcasted_iota(jnp.int32, (4, LANES), 0) == a
    flow = jnp.sum(jnp.where(mask, through[...], 0.0), 0, keepdims=True)
    at_end = jnp.sum(state_part, 0, keepdims=True) + flow * inner_sum[0:1]
    g_rate = exact_mm(upper[...], row_part[0] - column[0] - state_part) + at_end
    g_raw = direct[0] + to_end * through_state - decay_rate * g_rate
    g_raw = g_raw * sigmoid(dt_arg[0])
    head_sums[0:1] += jnp.sum(g_raw, 0, keepdims=True)
    head_sums[1:2] -= decay_rate * jnp.sum(steps * g_rate, 0, keepdims=True)
    g_mix[0, :, XBC:MIX_PAD] = g_raw.astype(bf16)
    g_mix[0, :, MIX_PAD:] = jnp.zeros((TOKENS, MIX_WIDE - MIX_PAD), bf16)
    back(PAIRS, g_b[0] + mm_nt(weighted[...], state[...]), *convolved(PAIRS))
    back(PAIRS + 1, g_c[0], *convolved(PAIRS + 1))


def early_grads_kernel(
    where, mixed, cotangent, normed_t, g_gates, mine, send_0, send_1, send_2, send_3,
    mixed_held, cot_held, normed_held, gates_held, mine_held, send_held, in_sems, out_sems,
):
    place, core = where[0], where[1]
    for_out = [
        pltpu.make_async_copy(mixed, mixed_held, in_sems.at[0]),
        pltpu.make_async_copy(cotangent, cot_held, in_sems.at[1]),
    ]
    for_gate = [
        pltpu.make_async_copy(normed_t, normed_held, in_sems.at[2]),
        pltpu.make_async_copy(g_gates, gates_held, in_sems.at[3]),
    ]
    to_mine = [
        pltpu.make_async_copy(
            mine_held.at[pl.ds(192 * k, 192)], mine.at[pl.ds(192 * k, 192)], out_sems.at[k]
        )
        for k in range(4)
    ]
    to_send = [
        pltpu.make_async_copy(send_held.at[pl.ds(192 * k, 192)], target, out_sems.at[4 + k])
        for k, target in enumerate((send_0, send_1, send_2, send_3))
    ]

    def gate_rows(target, copies):
        for copy in for_gate:
            copy.wait()
        for k in range(4):
            rows = pl.ds(pl.multiple_of(lax.rem(place + k, 4) * 192, 192), 192)
            target[192 * k : 192 * (k + 1)] = mm(normed_held[rows], gates_held[...]).astype(bf16)
            copies[k].start()

    def out_rows(target, copies):
        for copy in for_out:
            copy.wait()
        for k in range(4):
            lanes = pl.ds(pl.multiple_of(lax.rem(place + k, 4) * 384, 384), 384)
            grad = mm_tn(mixed_held[:, lanes], cot_held[...]).astype(bf16)
            target[192 * k : 192 * (k + 1), 0:768] = grad[0:192]
            target[192 * k : 192 * (k + 1), 768:] = grad[192:384]
            copies[k].start()

    @pl.when(core == 0)
    def _():
        for copy in for_out + for_gate:
            copy.start()
        out_rows(send_held, to_send)
        gate_rows(mine_held, to_mine)

    @pl.when(core == 1)
    def _():
        for copy in for_gate + for_out:
            copy.start()
        gate_rows(send_held, to_send)
        out_rows(mine_held, to_mine)

    for copy in to_mine + to_send:
        copy.wait()


def early_pair_kernel(mine, *rest):
    for k in range(4):
        rows = slice(192 * k, 192 * (k + 1))
        rest[4 + k][...] = (mine[rows].astype(f32) + rest[k][...].astype(f32)).astype(bf16)


def sum_blocks_kernel(a, b, c, d, total):
    for high in range(4):
        rows = slice(48 * high, 48 * (high + 1))
        value = a[rows].astype(f32) + b[rows].astype(f32) + c[rows].astype(f32) + d[rows].astype(f32)
        for low in range(4):
            total[4 * high + low] = value[:, columns(low, 384)].astype(bf16)


def late_columns(
    core, step, normed_t, halo_t, g_held, g_halo, taps, head_sums, skip_part, gather, mine, sends,
    held, sent, sems,
):
    lanes = pl.ds(pl.multiple_of(step * 512, 512), 512)
    g_mix = g_held[:, lanes]
    g_edge = jnp.concatenate([g_halo[:, lanes], jnp.zeros((LANES - 32, 512), f32)], 0).astype(bf16)
    for z in range(4):
        rows = slice(192 * z, 192 * (z + 1))
        grad = (mm(normed_t[rows], g_mix) + mm(halo_t[rows], g_edge)).astype(bf16)
        for c in range(2):
            for jj in range(4):
                held[c, jj, z] = grad[96 * c : 96 * (c + 1), columns(jj)]

    @pl.when(step == 3)
    def _():
        lane = lax.broadcasted_iota(jnp.int32, (8, LANES), 1)
        row = lax.broadcasted_iota(jnp.int32, (8, LANES), 0)
        nothing = jnp.zeros((8, LANES), f32)
        skips = sum_heads(skip_part[...], gather[...])
        head_rows = jnp.where(row == 2, jnp.sum(skips, 0, keepdims=True), head_sums[...])
        for z in range(4):
            for part in range(5):
                tile = head_rows
                if part < 4:
                    begin = 448 * z + LANES * part
                    tile = taps[:, begin // LANES * LANES : begin // LANES * LANES + LANES]
                    if begin % LANES:
                        after = min(begin // LANES + 1, XBC // LANES - 1) * LANES
                        tile = jnp.where(lane < 64, taps[:, after : after + LANES], tile)
                        tile = pltpu.roll(tile, 64, 1)
                tile = jnp.concatenate([tile, nothing], 0)
                held[0, 3, z, 16 * part : 16 * (part + 1)] = tile.astype(bf16)

    mine[...] = held[core]
    sent[pl.ds(4 * step, 4)] = held[1 - core]
    copies = [
        pltpu.make_async_copy(sent.at[pl.ds(4 * k, 4)], target, sems.at[k])
        for k, target in enumerate(sends)
    ]
    for k in range(4):

        @pl.when(step == k)
        def _(k=k):
            copies[k].start()

    @pl.when(step == 3)
    def _():
        for copy in copies:
            copy.wait()


def late_kernel(
    where, g_end, kept, given, active, mixin, mixin_halo, g_y, g_inner, g_b, g_c,
    dt, dt_arg, cumul, ending, row_part, direct, column, through, params, spread, gather, upper,
    normed_t, halo_t, skip_part,
    g_mix, g_halo, mine, send_0, send_1, send_2, send_3,
    weighted, state, extended, padded, inner_row, g_held, halo_held, taps, head_sums, held, sent,
    edge_held, sems,
):
    step = pl.program_id(0)

    @pl.when(step < 4)
    def _():
        late_rows(
            where, g_end, kept, given, active, mixin, mixin_halo, g_y, g_inner, g_b, g_c,
            dt, dt_arg, cumul, ending, row_part, direct, column, through, params, spread,
            gather, upper, g_mix, taps, head_sums,
            weighted, state, extended, padded, inner_row, edge_held,
        )
        g_held[pl.ds(pl.multiple_of(step * TOKENS, TOKENS), TOKENS)] = g_mix[0]
        rows = pl.ds(pl.multiple_of(step * EDGE, EDGE), EDGE)
        halo_held[rows, 0:XBC] = edge_held[...]
        halo_held[rows, XBC:] = jnp.zeros((EDGE, MIX_WIDE - XBC), f32)
        g_halo[0] = edge_held[...].astype(bf16)

    @pl.when(step >= 4)
    def _():
        late_columns(
            where[1], step - 4, normed_t, halo_t, g_held, halo_held, taps, head_sums, skip_part,
            gather, mine, (send_0, send_1, send_2, send_3), held, sent, sems,
        )


def both_cores(where, mine, other):
    first = where[1] == 0
    return jnp.where(first, mine, other), jnp.where(first, other, mine)


def join_kernel(where, mine, other, through, through_other, spread, total, wide):
    first = where[1] == 0
    own = jnp.where(first, through[0:2], through[2:4])
    theirs = jnp.where(first, through_other[0:2], through_other[2:4])
    through_0, through_1 = both_cores(where, own, theirs)
    everything_0, everything_1 = both_cores(where, through[...], through_other[...])
    rows = jnp.concatenate([through_0, through_1, jnp.zeros((4, LANES), f32)], 0)
    wide[...] = widen(halves(rows), spread[...])
    row = lax.broadcasted_iota(jnp.int32, (16, LANES), 0)
    piece = jnp.zeros((16, LANES), f32)
    for c, source in enumerate((everything_0, everything_1)):
        for p, value in enumerate(halves(source)):
            for a in range(4):
                piece = jnp.where(row == 4 * a + 2 * c + p, value[a : a + 1].astype(f32), piece)
    piece = piece.astype(bf16)
    for a in range(2):
        for part in range(8):
            span = slice(part * 16, (part + 1) * 16)
            state_0, state_1 = both_cores(
                where, mine[a, span].astype(f32), other[a, span].astype(f32)
            )
            value = wide[2 + a : 3 + a] * state_0 + state_1
            total[8 * a + part, :, 0:INNER] = value.astype(bf16)
            total[8 * a + part, :, INNER:] = piece


def split_kernel(where, back, mine, other, wide, kept, given):
    for a in range(2):
        for part in range(8):
            span = slice(part * 16, (part + 1) * 16)
            state_0, _ = both_cores(where, mine[a, span].astype(f32), other[a, span].astype(f32))
            in_0 = back[8 * a + part].astype(f32)
            in_1 = wide[a : a + 1] * in_0 + state_0
            keeps, gives = both_cores(where, in_0, in_1)
            kept[a, span] = keeps.astype(bf16)
            given[a, span] = gives.astype(bf16)


def scan_kernel(where, arrived, spread, before, picked, factors):
    chip = where[3] * 4 + where[4]
    forward = 2 * where[1] + chip // 8
    backward = (2 * chip + where[1]) // 8
    row = lax.broadcasted_iota(jnp.int32, (8, 16), 0)
    column = lax.broadcasted_iota(jnp.int32, (8, 16), 1)
    wanted = jnp.where(row < 2, 4 * forward + 2 * row, 4 * backward + 2 * (row - 2))
    chosen = (column >= wanted) & (column < wanted + 2) & (row < 4)
    chosen = jnp.where(chosen, 1.0, 0.0).astype(bf16)
    for i in range(16):
        picked[8 * i : 8 * (i + 1)] = mm(chosen, arrived[i, :, INNER:])
    factors[...] = widen(halves(picked[...]), spread[...])
    so_far = jnp.zeros((16, INNER), f32)
    for i in range(16):
        before[i] = so_far.astype(bf16)
        factor = factors[8 * i : 8 * i + 1] * factors[8 * i + 1 : 8 * i + 2]
        so_far = factor * so_far + arrived[i, :, :INNER].astype(f32)


def scan_back_kernel(arrived, picked, spread, after, factors):
    factors[...] = widen(halves(picked[...]), spread[...])
    so_far = jnp.zeros((16, INNER), f32)
    for i in reversed(range(32)):
        after[i] = so_far.astype(bf16)
        at = 8 * (i // 2) + 2 + i % 2
        so_far = factors[at : at + 1] * so_far + arrived[i].astype(f32)


def pair_kernel(mine, *rest):
    pair = rest[-1]
    count = rest[0].shape[0]
    for k, other in enumerate(rest[:-1]):
        rows = slice(count * k, count * (k + 1))
        pair[rows] = (mine[rows].astype(f32) + other[...].astype(f32)).astype(bf16)


def reduce_early_kernel(parts, owned):
    total = parts[0].astype(f32)
    for k in range(1, 16):
        total = total + parts[k].astype(f32)
    owned[...] = total.astype(bf16)


def reduce_kernel(early, late, owned):
    held = [early[:, columns(k)] for k in range(3)]
    total = late[0].astype(f32)
    for k in range(1, 64):
        total = total + late[k].astype(f32)
    total = total.astype(bf16)
    for copy in range(16):
        for k in range(3):
            owned[copy, 48 * k : 48 * (k + 1)] = held[k]
        owned[copy, 144:240] = total


def last_kernel(
    hidden, cotangent, mixed, g_gates, g_mix, spill, mix_weight, gate_weight, out_full, params,
    output, grad_hidden, held,
):
    x = hidden[0].astype(f32)
    output[0] = (x + mm(mixed[0], out_full[...])).astype(bf16)
    held[...] = g_mix[0, :, 0:MIX_PAD]
    end = g_mix[0, TOKENS - 16 :, 0:XBC].astype(f32)
    shift = jnp.concatenate([jnp.zeros((8, XBC), f32), spill[0].astype(f32)], 0)
    held[TOKENS - 16 :, 0:XBC] = (end + shift).astype(bf16)
    grad = mm_nt(held[...], mix_weight[...]) + mm_nt(g_gates[0], gate_weight[...])
    grad = grad * params[GAIN : GAIN + 1, 0:768]
    scale = lax.rsqrt(jnp.mean(x * x, axis=1, keepdims=True) + epsilon)
    pull = jnp.mean(grad * x, axis=1, keepdims=True)
    value = cotangent[0].astype(f32) + scale * grad - x * (scale * scale * scale * pull)
    grad_hidden[0] = value.astype(bf16)


def finish_kernel(
    where, shared, other, weight, gain, out_weight, gate_gain,
    grad, by_gain, conv_w, conv_b, grad_dt, grad_a, grad_skip, grad_out, by_gate_gain,
    sums, out_sums,
):
    up = pl.program_id(0)
    first = where[1] == 0

    def both(j, rows):
        a, b = shared[j, rows].astype(f32), other[j, rows].astype(f32)
        return jnp.where(first, a, b), jnp.where(first, b, a)

    for right in range(4):
        half, side = divmod(right, 2)
        for k in range(3):
            low, high = both(4 * up + right, slice(48 * k, 48 * (k + 1)))
            grad[:, columns(3 * right + k)] = low
            grad_out[half, :, columns(3 * side + k)] = high
    from_core = up // 2
    rows = pl.ds(pl.multiple_of(144 + 48 * lax.rem(up, 2), 16), 48)
    for j in range(15):
        begin = INNER + LANES * j
        width = min(LANES, INNER + MIX - begin)
        low, high = both(j, rows)
        grad[:, begin : begin + width] = jnp.where(from_core == 0, low, high)[:, 0:width]
    total = jnp.sum(grad[...] * weight[...].astype(f32), axis=1, keepdims=True)
    sums[pl.ds(pl.multiple_of(48 * up, 48), 48)] = jnp.broadcast_to(total, (48, LANES))
    for half in range(2):
        total = jnp.sum(grad_out[half] * out_weight[half].astype(f32), axis=1, keepdims=True)
        begin = pl.multiple_of(192 * half + 48 * up, 48)
        out_sums[pl.ds(begin, 48)] = jnp.broadcast_to(total, (48, LANES))

    @pl.when(up == 3)
    def _():
        by_gain[...] = sums[...].T[0:1].reshape(192) / gain[...]
        by_gate_gain[...] = out_sums[...].T[0:1].reshape(384) / gate_gain[...]
        rest, _ = both(15, slice(144, 240))
        for part in range(4):
            span = min(LANES, 448 - LANES * part)
            lanes = slice(LANES * part, LANES * part + span)
            conv_w[:, lanes] = rest[16 * part : 16 * part + 4, 0:span]
            conv_b[lanes] = rest[16 * part + 4 : 16 * part + 5, 0:span].reshape(span)
        for z in range(4):

            @pl.when(where[0] == z)
            def _(z=z):
                heads = pltpu.roll(rest[64:72], (LANES - 6 * z) % LANES, 1)
                for k, target in enumerate((grad_dt, grad_a, grad_skip)):
                    target[...] = heads[k : k + 1, 0:6].reshape(6)


def per_device(
    hidden,
    segments,
    norm_gain,
    in_weight,
    conv_weight,
    conv_bias,
    dt_bias,
    a_log,
    skip,
    gate_gain,
    out_weight,
    cotangent,
):
    core = lax.axis_index("seq_2")
    place = lax.axis_index("fsdp")
    chip = lax.axis_index("seq_0") * 4 + lax.axis_index("seq_1")
    where = jnp.stack(
        [
            place, core, (chip * 2 + core) * TOKENS, lax.axis_index("seq_0"),
            lax.axis_index("seq_1"),
        ]
    ).astype(jnp.int32)

    message, mix_tail = call(
        message_kernel,
        [(None, shaped((96, MIX_PAD), bf16)), (None, shaped((192, LANES), bf16))],
        [SCALARS] + [None] * 8,
        [
            where, in_weight, norm_gain, conv_weight, conv_bias, dt_bias, a_log, skip, gate_gain,
        ],
        scratch=[
            pltpu.VMEM((16, 512), f32), pltpu.VMEM((192, LANES), f32), pltpu.VMEM((96, LANES), f32)
        ],
        mib=LARGE,
    )
    mix_fetched = fetch(message)
    halo = line(hidden[:, TOKENS - EDGE :], SEQ, 1)

    head_of = np.arange(INNER) // HEADDIM
    spread = jnp.asarray((np.arange(LANES)[:, None] == head_of[None]), bf16)
    gather = jnp.asarray((head_of[:, None] == np.arange(LANES)[None]), bf16)
    lower = jnp.asarray(np.tril(np.ones((TOKENS, TOKENS))), bf16)
    upper = jnp.asarray(np.triu(np.ones((TOKENS, TOKENS))), bf16)
    low_lanes = jnp.asarray(np.ones((TOKENS, 1)) * (np.arange(LANES) < 64), bf16)
    high_lanes = jnp.asarray(np.ones((TOKENS, 1)) * (np.arange(LANES) >= 64), bf16)

    tokens = shaped((4, TOKENS, LANES))
    second, second_done = call(
        second_message_kernel,
        [(None, shaped((192, INNER), bf16))],
        [SCALARS, ANYWHERE, ANYWHERE],
        [where, in_weight, out_weight],
        scratch=[pltpu.SemaphoreType.DMA((3,))],
        marked=True,
        mib=LARGE,
    )
    same, keep, ending, passing, halo = call(
        tables_kernel,
        [
            (None, tokens), (None, tokens), (None, tokens), (None, shaped((4, LANES))),
            (None, shaped((4, EDGE, 768))),
        ],
        [SCALARS, None, None],
        [where, segments, halo],
        micros=60,
        after=[second_done],
        mib=LARGE,
    )
    half = shaped((2, STATE, INNER), bf16)
    (
        params, mixin, mixin_halo, active, dt_arg, dt, cumul, through, local_mine, local_send,
        normed, normed_t, halo_t, mix_weight,
    ) = call(
        front_kernel,
        [
            (None, shaped((16, XBC))),
            (ANYWHERE, shaped((4, TOKENS, XBC), bf16)),
            (None, shaped((4, EDGE, XBC))),
            (ANYWHERE, shaped((4, TOKENS, XBC), bf16)),
            (None, tokens),
            (None, tokens),
            (None, tokens),
            (None, shaped((4, LANES))),
            (ANYWHERE, half),
            (ANYWHERE, half),
            (ANYWHERE, shaped((512, 768), bf16)),
            (ANYWHERE, shaped((768, 512), bf16)),
            (None, shaped((768, LANES), bf16)),
            (ANYWHERE, shaped((768, MIX_PAD), bf16)),
        ],
        [SCALARS] + [None] * 6 + [ANYWHERE] * 9,
        [where, hidden, halo, ending, passing, spread, lower, message, in_weight, mix_tail]
        + mix_fetched
        + [swap(part) for part in mix_fetched],
        scratch=[
            pltpu.VMEM((768, MIX_PAD), bf16),
            pltpu.VMEM((4, 96, LANES), bf16),
            pltpu.VMEM((512, 768), bf16),
            pltpu.VMEM((768, 512), bf16),
            pltpu.VMEM((4, TOKENS, XBC), bf16),
            pltpu.VMEM((4, TOKENS, XBC), bf16),
            pltpu.VMEM((4, STATE, INNER), bf16),
            pltpu.VMEM((2, 8, EDGE + TOKENS, LANES), f32),
            pltpu.VMEM((4, STATE, TOKENS), bf16),
            pltpu.VMEM((512, LANES), bf16),
            pltpu.VMEM((2, 512, 256), f32),
            pltpu.SemaphoreType.DMA((12,)),
            pltpu.SemaphoreType.DMA((29,)),
        ],
        mib=LARGE,
        micros=10,
    )

    blocks = shaped((16, 16, INNER), bf16)
    local_other = swap(local_send)
    through_other = swap(through)
    total, wide = call(
        join_kernel,
        [(None, shaped((16, 16, INNER + LANES), bf16)), (None, shaped((8, INNER)))],
        [SCALARS] + [None] * 5,
        [where, local_mine, local_other, through, through_other, spread],
        micros=0,
    )
    fetched = fetch(second)
    inner, inner_done = call(
        inner_kernel,
        [(by_seq(TOKENS, INNER), shaped((4, TOKENS, INNER)))],
        [
            by_seq(TOKENS, XBC), by_seq(TOKENS, LANES), by_seq(TOKENS, LANES),
            by_seq(TOKENS, TOKENS), constant(LANES, INNER), constant(TOKENS, LANES),
            constant(TOKENS, LANES),
        ],
        [active, dt, cumul, same, spread, low_lanes, high_lanes],
        grid=(4,),
        scratch=[pltpu.VMEM((TOKENS, INNER), f32)],
        mib=LARGE,
        marked=True,
        micros=60,
    )
    before, picked = call(
        scan_kernel,
        [(None, blocks), (None, shaped((128, LANES)))],
        [SCALARS, None, None],
        [where, exchange(total, CHIPS), spread],
        scratch=[pltpu.VMEM((128, INNER), f32)],
        micros=0,
        after=[inner_done],
    )
    gate_weight, out_full, gates, g_mixed, projected = call(
        weights_kernel,
        [
            (ANYWHERE, shaped((768, INNER), bf16)),
            (ANYWHERE, shaped((INNER, 768), bf16)),
            (ANYWHERE, shaped((512, INNER), bf16)),
            (ANYWHERE, shaped((512, INNER), bf16)),
        ],
        [SCALARS, None, None] + [ANYWHERE] * 8,
        [where, normed, cotangent.reshape(512, 768), in_weight, out_weight]
        + fetched
        + [swap(part) for part in fetched],
        scratch=[
            pltpu.VMEM((768, INNER), bf16),
            pltpu.VMEM((INNER, 768), bf16),
            pltpu.VMEM((512, INNER), bf16),
            pltpu.VMEM((512, INNER), bf16),
            pltpu.SemaphoreType.DMA((20,)),
            pltpu.SemaphoreType.DMA((14,)),
        ],
        marked=True,
        micros=0,
        mib=LARGE,
    )
    gates = gates.reshape(4, TOKENS, INNER)
    g_mixed = g_mixed.reshape(4, TOKENS, INNER)
    kept, given = call(
        split_kernel,
        [(None, half), (None, half)],
        [SCALARS] + [None] * 4,
        [where, exchange(before, CHIPS), local_mine, local_other, wide],
        micros=0,
        after=[projected],
    )
    given = swap(given)

    mixed, g_y, g_gates, row_part, g_state = call(
        middle_kernel,
        [
            (by_seq(TOKENS, INNER), shaped((4, TOKENS, INNER), bf16)),
            (by_seq(TOKENS, INNER), shaped((4, TOKENS, INNER), bf16)),
            (by_seq(TOKENS, INNER), shaped((4, TOKENS, INNER), bf16)),
            (by_seq(TOKENS, LANES), tokens),
            (by_seq(STATE, INNER), shaped((4, STATE, INNER), bf16)),
        ],
        [
            by_seq(TOKENS, INNER), by_seq(TOKENS, XBC), own_half(STATE, INNER),
            other_half(STATE, INNER), by_seq(TOKENS, INNER), by_seq(TOKENS, INNER),
            by_seq(TOKENS, LANES), by_seq(TOKENS, LANES), constant(16, XBC),
            constant(LANES, INNER), constant(INNER, LANES),
        ],
        [inner, active, kept, given, gates, g_mixed, cumul, keep, params, spread, gather],
        scalars=where,
        grid=(4,),
        scratch=[pltpu.VMEM((TOKENS, INNER), f32)] * 6 + [pltpu.VMEM((TOKENS, INNER), bf16)],
        mib=LARGE,
        micros=11,
    )

    blocks_back = shaped((32, 16, INNER), bf16)
    arrived_back = exchange(g_state.reshape(32, 16, INNER), SEQ)

    early_shape = shaped((768, INNER), bf16)
    early_mine, *early_send, early_done = call(
        early_grads_kernel,
        [(ANYWHERE, early_shape)] + [(ANYWHERE, shaped((192, INNER), bf16))] * 4,
        [SCALARS] + [ANYWHERE] * 4,
        [
            where, mixed.reshape(512, INNER), cotangent.reshape(512, 768), normed_t,
            g_gates.reshape(512, INNER),
        ],
        scratch=[
            pltpu.VMEM((512, INNER), bf16),
            pltpu.VMEM((512, 768), bf16),
            pltpu.VMEM((768, 512), bf16),
            pltpu.VMEM((512, INNER), bf16),
            pltpu.VMEM((768, INNER), bf16),
            pltpu.VMEM((768, INNER), bf16),
            pltpu.SemaphoreType.DMA((4,)),
            pltpu.SemaphoreType.DMA((8,)),
        ],
        marked=True,
        mib=LARGE,
        micros=60,
    )
    parts = call(
        early_pair_kernel,
        [(None, shaped((192, INNER), bf16))] * 4,
        [None] * 5,
        [early_mine] + [swap(part) for part in early_send],
        micros=0,
    )
    early_parts = [parts[0]] + [ring(parts[k], "fsdp", k) for k in (1, 2, 3)]

    (after,) = call(
        scan_back_kernel,
        [(None, blocks_back)],
        [None] * 3,
        [arrived_back, picked, spread],
        scratch=[pltpu.VMEM((128, INNER), f32)],
        micros=2,
        after=[early_done],
    )

    g_inner, g_b, g_c, direct, column, skip_part, inner_back_done = call(
        inner_back_kernel,
        [
            (by_seq(TOKENS, INNER), shaped((4, TOKENS, INNER), bf16)),
            (by_seq(TOKENS, STATE), tokens),
            (by_seq(TOKENS, STATE), tokens),
            (by_seq(TOKENS, LANES), tokens),
            (by_seq(TOKENS, LANES), tokens),
            (constant(8, INNER), shaped((8, INNER))),
        ],
        [
            by_seq(TOKENS, XBC), by_seq(TOKENS, INNER), own_half(STATE, INNER),
            other_half(STATE, INNER), by_seq(TOKENS, LANES), by_seq(TOKENS, LANES),
            by_seq(TOKENS, LANES), by_seq(TOKENS, TOKENS), constant(LANES, INNER),
            constant(INNER, LANES), constant(TOKENS, LANES), constant(TOKENS, LANES),
        ],
        [
            active, g_y, kept, given, dt, cumul, keep, same, spread, gather, low_lanes, high_lanes,
        ],
        scalars=where,
        grid=(4,),
        scratch=[pltpu.VMEM((TOKENS, INNER), f32)] * 2 + [pltpu.VMEM((TOKENS, INNER), bf16)] * 4,
        mib=LARGE,
        marked=True,
        micros=60,
    )
    early_blocks, early_summed = call(
        sum_blocks_kernel,
        [(None, shaped((16, 48, 384), bf16))],
        [None] * 4,
        early_parts,
        marked=True,
        micros=0,
        after=[inner_back_done],
    )
    g_end = exchange(after, SEQ).reshape(4, STATE, INNER)
    late_spec = pl.BlockSpec((4, 4, 96, LANES), lambda s, *_: (jnp.maximum(s - 4, 0), 0, 0, 0))
    late_shape = shaped((16, 4, 96, LANES), bf16)
    piece = shaped((16 // LATE_PIECES, 4, 96, LANES), bf16)
    g_mix, g_halo, late_mine, *late_send, late_done = call(
        late_kernel,
        [
            (seq_first(TOKENS, MIX_WIDE), shaped((4, TOKENS, MIX_WIDE), bf16)),
            (seq_first(EDGE, XBC), shaped((4, EDGE, XBC), bf16)),
            (late_spec, late_shape),
        ]
        + [(ANYWHERE, piece)] * LATE_PIECES,
        [seq_first(STATE, INNER), own_half(STATE, INNER), other_half(STATE, INNER)]
        + [
            pl.BlockSpec((1, TOKENS, 256), lambda a, *_: (jnp.minimum(a, 3), 0, 6)),
            seq_first(TOKENS, XBC), seq_first(EDGE, XBC), seq_first(TOKENS, INNER),
            seq_first(TOKENS, INNER), seq_first(TOKENS, STATE), seq_first(TOKENS, STATE),
        ]
        + [seq_first(TOKENS, LANES)] * 7
        + [
            constant(4, LANES), constant(16, XBC), constant(LANES, INNER), constant(INNER, LANES),
            constant(TOKENS, TOKENS), constant(768, 512), constant(768, LANES), constant(8, INNER),
        ],
        [
            g_end, kept, given, active, mixin, mixin_halo, g_y, g_inner, g_b, g_c, dt,
            dt_arg, cumul, ending, row_part, direct, column, through, params, spread, gather, upper,
            normed_t, halo_t, skip_part,
        ],
        scalars=where,
        grid=(8,),
        scratch=[
            pltpu.VMEM((TOKENS, INNER), bf16),
            pltpu.VMEM((STATE, INNER), bf16),
            pltpu.VMEM((2, EDGE + TOKENS, LANES), f32),
            pltpu.VMEM((2, 144, LANES), f32),
            pltpu.VMEM((8, INNER), f32),
            pltpu.VMEM((512, MIX_WIDE), bf16),
            pltpu.VMEM((32, MIX_WIDE), f32),
            pltpu.VMEM((8, XBC), f32),
            pltpu.VMEM((8, LANES), f32),
            pltpu.VMEM((2, 4, 4, 96, LANES), bf16),
            pltpu.VMEM((16, 4, 96, LANES), bf16),
            pltpu.VMEM((EDGE, XBC), f32),
            pltpu.SemaphoreType.DMA((LATE_PIECES,)),
        ],
        marked=True,
        mib=LARGE,
        micros=60,
        after=[early_summed, inner_back_done],
    )
    early_owned, early_reduced = call(
        reduce_early_kernel,
        [(None, shaped((48, 384), bf16))],
        [None],
        [exchange(early_blocks, CHIPS)],
        marked=True,
        micros=0,
        after=[late_done],
    )
    spill = line(g_halo, SEQ, -1)
    (late_pair,) = call(
        pair_kernel,
        [(None, late_shape)],
        [None] * (1 + LATE_PIECES),
        [late_mine] + [swap(part) for part in late_send],
        micros=0,
        after=[spill, early_reduced],
    )
    late_parts = exchange(late_pair.reshape(64, 96, LANES), COLUMNS)

    rows = by_seq(TOKENS, 768)
    output, grad_hidden, last_done = call(
        last_kernel,
        [(rows, shaped((4, TOKENS, 768), bf16)), (rows, shaped((4, TOKENS, 768), bf16))],
        [
            rows, rows, by_seq(TOKENS, INNER), by_seq(TOKENS, INNER), by_seq(TOKENS, MIX_WIDE),
            by_seq(EDGE, XBC), constant(768, MIX_PAD), constant(768, INNER), constant(INNER, 768),
            constant(16, XBC),
        ],
        [
            hidden, cotangent, mixed, g_gates, g_mix, spill, mix_weight, gate_weight, out_full,
            params,
        ],
        grid=(4,),
        scratch=[pltpu.VMEM((TOKENS, MIX_PAD), bf16)],
        mib=LARGE,
        marked=True,
        micros=60,
    )
    (owned,) = call(
        reduce_kernel,
        [(None, shaped((16, 240, LANES), bf16))],
        [None] * 2,
        [early_owned, late_parts],
        micros=2,
        after=[last_done],
    )
    shared = exchange(owned, CHIPS)
    sum_in, by_gain, sum_conv_w, sum_conv_b, sum_dt, sum_a, sum_skip, sum_out, by_gate_gain = call(
        finish_kernel,
        [
            (pl.BlockSpec((48, INNER + MIX), lambda i, *_: (i, 0)), shaped((192, INNER + MIX))),
            (constant(192), shaped((192,))),
            (constant(4, 448), shaped((4, 448))),
            (constant(448), shaped((448,))),
            (constant(6), shaped((6,))),
            (constant(6), shaped((6,))),
            (constant(6), shaped((6,))),
            (pl.BlockSpec((2, 48, 768), lambda i, *_: (0, i, 0)), shaped((2, 192, 768))),
            (constant(384), shaped((384,))),
        ],
        [
            constant(16, 240, LANES), constant(16, 240, LANES),
            pl.BlockSpec((48, INNER + MIX), lambda i, *_: (i, 0)), constant(192),
            pl.BlockSpec((2, 48, 768), lambda i, *_: (0, i, 0)), constant(384),
        ],
        [
            shared, swap(shared), in_weight, norm_gain.astype(f32),
            out_weight.reshape(2, 192, 768), gate_gain.astype(f32),
        ],
        scalars=where,
        grid=(4,),
        scratch=[pltpu.VMEM((192, LANES), f32), pltpu.VMEM((384, LANES), f32)],
        micros=4,
    )

    return (
        output,
        grad_hidden,
        by_gain,
        sum_in,
        sum_conv_w,
        sum_conv_b,
        sum_dt,
        sum_a,
        sum_skip,
        by_gate_gain,
        sum_out.reshape(384, 768),
    )


def solution(mesh):
    finer = Mesh(
        mesh.devices.reshape(4, 4, 2, mesh.shape["fsdp"]), ("seq_0", "seq_1", "seq_2", "fsdp")
    )
    in_specs = (
        P("fsdp", SEQ, None),
        P("fsdp", SEQ),
        P("fsdp"),
        P("fsdp", None),
        P(None, "fsdp"),
        P("fsdp"),
        P("fsdp"),
        P("fsdp"),
        P("fsdp"),
        P("fsdp"),
        P("fsdp", None),
        P("fsdp", SEQ, None),
    )
    out_specs = (
        P("fsdp", SEQ, None),
        P("fsdp", SEQ, None),
        P("fsdp"),
        P("fsdp", None),
        P(None, "fsdp"),
        P("fsdp"),
        P("fsdp"),
        P("fsdp"),
        P("fsdp"),
        P("fsdp"),
        P("fsdp", None),
    )
    return jax.shard_map(
        per_device, mesh=finer, in_specs=in_specs, out_specs=out_specs, check_vma=False
    )
```

```python
import functools

import jax
import jax.numpy as jnp
import numpy as np
from jax import lax
from jax.experimental import pallas as pl
from jax.experimental.pallas import tpu as pltpu
from jax.sharding import Mesh
from jax.sharding import PartitionSpec as P

INNER = 1536
HEADS = 24
HEADDIM = 64
STATE = 128
XBC = 1792
MIX = 1816
MIX_PAD = 1920
MIX_WIDE = 2048
EDGE = 8
TOKENS = 128
LANES = 128
PAIRS = 12
SEQ = ("seq_0", "seq_1", "seq_2")
CHIPS = ("seq_0", "seq_1")
COLUMNS = ("seq_0", "seq_1", "fsdp")

epsilon = 1e-05
bf16 = jnp.bfloat16
f32 = jnp.float32
VMEM_MIB = 24
LARGE = 60
LATE_PIECES = 4
COST = 1.1e9

CONV_W, CONV_B, GATE_GAIN, GAIN, DT_BIAS, DECAY, SKIP, SKIP_WIDE = 0, 4, 5, 6, 7, 8, 9, 10


def ring(value, axis, steps):
    count = lax.axis_size(axis)
    pairs = [(source, (source + steps) % count) for source in range(count)]
    return lax.ppermute(value, axis, pairs)


def line(value, axis, steps):
    count = lax.axis_size(axis)
    initial, last = (max(0, -steps), min(count, count - steps))
    return lax.ppermute(value, axis, [(source, source + steps) for source in range(initial, last)])


def swap(value):
    return ring(value, "seq_2", 1)


def dot(pattern, left, right):
    return jnp.einsum(pattern, left, right, preferred_element_type=f32)


def exchange(blocks, axes):
    return lax.all_to_all(blocks, axes, 0, 0, tiled=False)


def split_three(value):
    high = value.astype(bf16)
    rest = value - high.astype(f32)
    middle = rest.astype(bf16)
    low = (rest - middle.astype(f32)).astype(bf16)
    return high, middle, low


def mm(left, right):
    return lax.dot_general(left, right, (((1,), (0,)), ((), ())), preferred_element_type=f32)


def mm_nt(left, right):
    return lax.dot_general(left, right, (((1,), (1,)), ((), ())), preferred_element_type=f32)


def mm_tn(left, right):
    return lax.dot_general(left, right, (((0,), (0,)), ((), ())), preferred_element_type=f32)


def exact_mm(ones, value):
    high, middle, low = split_three(value)
    return mm(ones, high) + mm(ones, middle) + mm(ones, low)


def halves(value):
    high = value.astype(bf16)
    return high, (value - high.astype(f32)).astype(bf16)


def widen(pieces, spread):
    return mm(pieces[0], spread) + mm(pieces[1], spread)


def sum_heads(value, gather):
    high, low = halves(value)
    return mm(high, gather) + mm(low, gather)


def sigmoid(value):
    return 0.5 * jnp.tanh(0.5 * value) + 0.5


HBM = pl.BlockSpec(memory_space=pltpu.HBM)


def call(
    kernel, outs, ins, operands, grid=None, scratch=(), micros=1, after=(), mib=VMEM_MIB, scalars=None,
    marked=False,
):
    whole = pl.BlockSpec(memory_space=pltpu.VMEM)
    lead = [] if scalars is None else [scalars]
    count = len(operands) + len(lead)
    if marked:
        outs = list(outs) + [(HBM, shaped((8192, 1280)))]
    first = count + len(after)
    last = first + len(outs) - marked

    def body(*refs):
        kernel(*refs[:count], *refs[first:last], *refs[last + marked :])

    return pl.pallas_call(
        body,
        grid_spec=pltpu.PrefetchScalarGridSpec(
            num_scalar_prefetch=len(lead),
            grid=grid or (),
            in_specs=[spec or whole for spec in ins]
            + [HBM] * len(after),
            out_specs=[spec or whole for spec, _ in outs],
            scratch_shapes=list(scratch),
        ),
        out_shape=[shape for _, shape in outs],
        compiler_params=pltpu.CompilerParams(vmem_limit_bytes=mib * 1024 * 1024),
        cost_estimate=pl.CostEstimate(
            flops=int(micros * COST), bytes_accessed=0, transcendentals=0
        ),
    )(*lead, *operands, *after)


def shaped(shape, dtype=f32):
    return jax.ShapeDtypeStruct(shape, dtype)


def by_seq(*shape):
    return pl.BlockSpec((1,) + shape, lambda a, *_: (a,) + (0,) * len(shape))


def constant(*shape):
    return pl.BlockSpec(shape, lambda a, *_: (0,) * len(shape))


def seq_first(*shape):
    return pl.BlockSpec(
        (1,) + shape, lambda a, *_: (jnp.minimum(a, 3),) + (0,) * len(shape)
    )


def own_half(*shape):
    return pl.BlockSpec(
        (1,) + shape,
        lambda a, where: (jnp.clip(a - 2 * where[1], 0, 1),) + (0,) * len(shape),
    )


def other_half(*shape):
    return pl.BlockSpec(
        (1,) + shape,
        lambda a, where: (jnp.clip(a - 2 + 2 * where[1], 0, 1),) + (0,) * len(shape),
    )


ANYWHERE = pl.BlockSpec(memory_space=pl.ANY)
SCALARS = pl.BlockSpec(memory_space=pltpu.SMEM)


def columns(index, width=LANES):
    return slice(index * width, (index + 1) * width)


def groups():
    listed = []
    for row, count in (
        (CONV_W, 7), (CONV_W + 1, 7), (CONV_W + 2, 7), (CONV_W + 3, 7), (CONV_B, 7), (GATE_GAIN, 6),
        (GAIN, 3),
    ):
        for j in range(count):
            listed.append((row, j, len(listed)))
    return listed


SPANS = {CONV_B: 448, GATE_GAIN: 384, GAIN: 192}
HEAD_LINE = 44


def message_kernel(
    where, in_weight, norm_gain, conv_weight, conv_bias, dt_bias, a_log, skip, gate_gain,
    message, tail, held, narrow, lines,
):
    core = where[1]
    narrow[...] = jnp.zeros_like(narrow)
    narrow[:, 0 : MIX - XBC] = in_weight[:, INNER + XBC :].astype(f32)
    tail[...] = narrow[...].astype(bf16)
    half = pl.ds(pl.multiple_of(core * 96, 96), 96)
    message[:, 0:XBC] = in_weight[half, INNER : INNER + XBC]
    held[...] = jnp.zeros_like(held)
    held[CONV_W : CONV_W + 4, 0:448] = conv_weight[...].astype(f32)
    for target, source in (
        (CONV_B, conv_bias), (GATE_GAIN, gate_gain), (GAIN, norm_gain), (DT_BIAS, dt_bias),
        (DECAY, a_log), (SKIP, skip),
    ):
        size = source.shape[0]
        held[target : target + 1, 0:size] = source[...].astype(f32).reshape(1, size)
    lane = lax.broadcasted_iota(jnp.int32, (1, LANES), 1)
    lines[...] = jnp.zeros_like(lines)
    for row, j, line in groups():
        tile = held[row : row + 1, columns(j // 2)]
        tile = tile if j % 2 else pltpu.roll(tile, 64, 1)
        lines[line : line + 1] = jnp.where(lane < 64, 0.0, tile)
    heads = pltpu.roll(held[DT_BIAS : DT_BIAS + 1, 0:LANES], 64, 1)
    heads = heads + pltpu.roll(held[DECAY : DECAY + 1, 0:LANES], 70, 1)
    lines[HEAD_LINE : HEAD_LINE + 1] = heads + pltpu.roll(held[SKIP : SKIP + 1, 0:LANES], 76, 1)
    message[:, XBC:] = (narrow[half] + lines[...]).astype(bf16)


def tables_kernel(where, segments, halo, same, keep, ending, passing, halo_held):
    start = where[2].astype(f32)
    below = lax.broadcasted_iota(jnp.int32, (TOKENS, TOKENS), 0) >= lax.broadcasted_iota(
        jnp.int32, (TOKENS, TOKENS), 1
    )
    for a in range(4):
        row = jnp.broadcast_to(segments[a : a + 1].astype(f32), (TOKENS, TOKENS))
        column = row.T
        first, last = column[0:1], column[TOKENS - 1 :]
        same[a] = jnp.where((column == row) & below, 1.0, 0.0)
        keep[a] = jnp.where((column == first) & (first < start), 1.0, 0.0)
        ending[a] = jnp.where(column == last, 1.0, 0.0)
        passing[a : a + 1] = jnp.where(last < start, 1.0, 0.0)
        halo_held[a] = halo[a].astype(f32)


def second_message_kernel(where, in_weight, out_weight, message, sems):
    core = where[1]
    low = pl.multiple_of(core * 192, 192)
    copies = [
        pltpu.make_async_copy(
            in_weight.at[pl.ds(pl.multiple_of(core * 96, 96), 96), pl.ds(0, INNER)],
            message.at[pl.ds(0, 96)],
            sems.at[0],
        )
    ]
    for k in range(2):
        copies.append(
            pltpu.make_async_copy(
                out_weight.at[pl.ds(low + 96 * k, 96)],
                message.at[pl.ds(96, 96), pl.ds(768 * k, 768)],
                sems.at[1 + k],
            )
        )
    for copy in copies:
        copy.start()
    for copy in copies:
        copy.wait()


def weights_kernel(
    where, normed, cotangent, in_weight, out_weight, m_1, m_2, m_3, o_1, o_2, o_3,
    gate_full, out_full, gates, g_mixed,
    gate_held, out_held, gates_held, g_held, in_sems, out_sems,
):
    place, core = where[0], where[1]
    gate_copies = weight_copies(
        place, core, in_weight.at[:, pl.ds(0, INNER)], (m_1, m_2, m_3), (o_1, o_2, o_3), gate_held,
        in_sems,
    )
    out_copies = [
        pltpu.make_async_copy(
            out_weight, out_held.at[pl.ds(pl.multiple_of(place * 384, 384), 384)], in_sems.at[7]
        )
    ]
    for k, (mine, other) in enumerate(((m_1, o_1), (m_2, o_2), (m_3, o_3))):
        owner = lax.rem(place + (1 + k), 4) * 384
        for which, part in ((core, mine), (1 - core, other)):
            for side in range(2):
                begin = pl.multiple_of(owner + which * 192 + 96 * side, 96)
                out_copies.append(
                    pltpu.make_async_copy(
                        part.at[pl.ds(96, 96), pl.ds(768 * side, 768)],
                        out_held.at[pl.ds(begin, 96)],
                        in_sems.at[7 + len(out_copies)],
                    )
                )
    for copy in gate_copies + out_copies:
        copy.start()
    outgoing = []

    def send(source, target):
        copy = pltpu.make_async_copy(source, target, out_sems.at[len(outgoing)])
        copy.start()
        outgoing.append(copy)

    for copy in gate_copies:
        copy.wait()
    for chunk in range(6):
        lanes, span = columns(chunk, 256), pl.ds(chunk * 256, 256)
        gates_held[:, lanes] = mm(normed[...], gate_held[:, lanes]).astype(bf16)
        send(gates_held.at[:, span], gates.at[:, span])
    send(gate_held, gate_full)
    for copy in out_copies:
        copy.wait()
    for chunk in range(6):
        lanes, span = columns(chunk, 256), pl.ds(chunk * 256, 256)
        g_held[:, lanes] = mm_nt(cotangent[...], out_held[lanes]).astype(bf16)
        send(g_held.at[:, span], g_mixed.at[:, span])
    send(out_held, out_full)
    for copy in outgoing:
        copy.wait()


def fetch(half):
    return [ring(half, "fsdp", steps) for steps in (3, 2, 1)]


def weight_copies(place, core, shard, mine, others, full, sems, own_width=None):
    rows = shard.shape[0]
    half = rows // 2
    copies = [
        pltpu.make_async_copy(
            shard,
            full.at[pl.ds(pl.multiple_of(place * rows, rows), rows), pl.ds(0, own_width or full.shape[1])],
            sems.at[0],
        )
    ]
    for k in range(3):
        owner = lax.rem(place + (1 + k), 4) * rows
        low = pl.multiple_of(owner + core * half, half)
        high = pl.multiple_of(owner + (1 - core) * half, half)
        for slot, part, begin in ((1 + 2 * k, mine[k], low), (2 + 2 * k, others[k], high)):
            copies.append(
                pltpu.make_async_copy(
                    part.at[pl.ds(0, half)], full.at[pl.ds(begin, half)], sems.at[slot]
                )
            )
    return copies


def front_kernel(
    where, hidden, halo, ending, passing, spread, lower, own, in_weight, tail,
    m_1, m_2, m_3, o_1, o_2, o_3,
    params, mixin, mixin_halo, active, dt_arg, dt, cumul, through, local_mine, local_send,
    normed, normed_t, halo_t, full,
    weight, packed, x_low, x_turned, mix_held, act_held, local_held,
    extended, state_b, scaled, wide_held, in_sems, out_sems,
):
    place, core = where[0], where[1]
    incoming = weight_copies(
        place, core, in_weight.at[:, pl.ds(INNER, XBC)], (m_1, m_2, m_3), (o_1, o_2, o_3), weight,
        in_sems, XBC,
    )
    incoming.append(
        pltpu.make_async_copy(
            tail,
            weight.at[pl.ds(pl.multiple_of(place * 192, 192), 192), pl.ds(XBC, LANES)],
            in_sems.at[11],
        )
    )
    rows_in = [
        pltpu.make_async_copy(part.at[:, pl.ds(XBC, LANES)], packed.at[k], in_sems.at[7 + k])
        for k, part in enumerate((own, m_1, m_2, m_3))
    ]
    for copy in rows_in + incoming:
        copy.start()
    outgoing = []

    def send(source, target):
        copy = pltpu.make_async_copy(source, target, out_sems.at[len(outgoing)])
        copy.start()
        outgoing.append(copy)

    for copy in rows_in:
        copy.wait()
    params[...] = jnp.zeros_like(params)
    lane = lax.broadcasted_iota(jnp.int32, (1, LANES), 1)
    for at in range(4):

        @pl.when(place == at)
        def _(at=at):
            for slot in range(4):
                z = (at + slot) % 4
                lines = packed[slot].astype(f32)
                turned = pltpu.roll(lines, 64, 1)
                for row, j, line in groups():
                    begin = SPANS.get(row, 448) * z + 64 * j
                    if begin % LANES:
                        params[row : row + 1, begin : begin + 64] = lines[line : line + 1, 64:LANES]
                    else:
                        params[row : row + 1, begin : begin + 64] = turned[line : line + 1, 0:64]
                heads = lines[HEAD_LINE : HEAD_LINE + 1]
                here = (lane >= 6 * z) & (lane < 6 * z + 6)
                for row, begin in ((DT_BIAS, 64), (DECAY, 70), (SKIP, 76)):
                    moved = pltpu.roll(heads, (LANES - begin + 6 * z) % LANES, 1)
                    params[row : row + 1, 0:LANES] += jnp.where(here, moved, 0.0)

    decay_rate = jnp.exp(params[DECAY : DECAY + 1, 0:LANES])
    params[DECAY : DECAY + 1, 0:LANES] = decay_rate
    params[SKIP_WIDE : SKIP_WIDE + 1, 0:INNER] = mm(
        params[SKIP : SKIP + 1, 0:LANES].astype(bf16), spread[...]
    )
    gain = params[GAIN : GAIN + 1, 0:768]

    def normalised(value):
        scale = lax.rsqrt(jnp.mean(value * value, axis=1, keepdims=True) + epsilon)
        return value * scale * gain

    edges = []
    for a in range(4):
        value = normalised(hidden[a].astype(f32))
        x_low[a * TOKENS : (a + 1) * TOKENS] = value.astype(bf16)
        x_turned[:, a * TOKENS : (a + 1) * TOKENS] = value.T.astype(bf16)
        edges.append(normalised(halo[a]))
    send(x_low, normed)
    send(x_turned, normed_t)
    edges = jnp.concatenate(edges, 0)
    edge_low = edges.astype(bf16)
    edges = jnp.concatenate([edges, jnp.zeros((LANES - 32, 768), f32)], 0)
    halo_t[...] = edges.T.astype(bf16)

    for copy in incoming:
        copy.wait()
    last = weight[:, XBC:].astype(f32)
    weight[:, XBC:] = jnp.where(lane < MIX - XBC, last, 0.0).astype(bf16)
    send(weight, full)
    argument = mm(x_low[...], weight[:, XBC:]) + params[DT_BIAS : DT_BIAS + 1, 0:LANES]
    steps = jnp.maximum(argument, 0.0) + jnp.log1p(jnp.exp(-jnp.abs(argument)))
    for a in range(4):
        rows = slice(a * TOKENS, (a + 1) * TOKENS)
        dt_arg[a] = argument[rows]
        dt[a] = steps[rows]
        total = exact_mm(lower[...], -steps[rows] * decay_rate)
        cumul[a] = total
        final = total[TOKENS - 1 :]
        through[a : a + 1] = jnp.exp(final) * passing[a : a + 1]
        scaled[rows] = (jnp.exp(final - total) * ending[a] * steps[rows]).astype(bf16)
    order = (6, 0, 1, 2, 3, 4, 5)

    def project(turn, a):
        chunk, slot = order[turn], turn % 2
        lanes = columns(chunk, 256)
        rows = slice(a * TOKENS, (a + 1) * TOKENS)
        if a == 0:
            edge = mm(edge_low, weight[:, lanes]).astype(bf16).astype(f32)
            for b in range(4):
                mixin_halo[b, :, lanes] = edge[b * EDGE : (b + 1) * EDGE]
                for side in range(2):
                    extended[slot, 2 * b + side, 0:EDGE] = edge[
                        b * EDGE : (b + 1) * EDGE, columns(side)
                    ]
        part = mm(x_low[rows], weight[:, lanes]).astype(bf16)
        mix_held[a, :, lanes] = part
        part = part.astype(f32)
        for side in range(2):
            extended[slot, 2 * a + side, EDGE:] = part[:, columns(side)]
        if chunk < 6:
            wide_held[slot, rows] = mm(scaled[rows], spread[:, lanes])

    def convolve(turn, a):
        chunk, slot = order[turn], turn % 2
        for side in range(2):
            lanes = columns(2 * chunk + side)
            at = 2 * a + side
            value = params[CONV_B : CONV_B + 1, lanes]
            for k in range(4):
                value = value + params[k : k + 1, lanes] * extended[
                    slot, at, EDGE - 3 + k : EDGE + 125 + k
                ]
            value = (value * sigmoid(value)).astype(bf16)
            act_held[a, :, lanes] = value
            if chunk == 6:
                if side == 0:
                    state_b[a] = value.astype(f32).T.astype(bf16)
            else:
                wide = wide_held[slot, a * TOKENS : (a + 1) * TOKENS, columns(side)]
                weighted = (wide * value.astype(f32)).astype(bf16)
                local_held[a, :, lanes] = mm(state_b[a], weighted).astype(bf16)

    for a in range(4):
        project(0, a)
    for turn, chunk in enumerate(order):
        span = pl.ds(chunk * 256, 256)
        send(mix_held.at[:, :, span], mixin.at[:, :, span])
        for a in range(4):
            if turn < 6:
                project(turn + 1, a)
            convolve(turn, a)
        send(act_held.at[:, :, span], active.at[:, :, span])
        if chunk < 6:
            own, given = pl.ds(2 * core, 2), pl.ds(2 - 2 * core, 2)
            send(local_held.at[given, :, span], local_send.at[:, :, span])
            send(local_held.at[own, :, span], local_mine.at[:, :, span])
    for copy in outgoing:
        copy.wait()


def pair_weights(p, scores, cumul, turned, same):
    made = []
    for h in (2 * p, 2 * p + 1):
        differ = cumul[:, h : h + 1] - turned[h : h + 1, :]
        decay = jnp.exp(jnp.where(same, differ, -1e30))
        made.append((decay, (scores * decay).astype(bf16)))
    return made


def inner_kernel(active, dt, cumul, same, spread, low_lanes, high_lanes, inner, dt_wide):
    b_low = active[0, :, INNER : INNER + STATE]
    c_low = active[0, :, INNER + STATE :]
    scores = mm_nt(c_low, b_low)
    total = cumul[0]
    turned = total.T
    allowed = same[0] > 0
    dt_wide[...] = mm(dt[0].astype(bf16), spread[...])
    for p in range(PAIRS):
        lanes = columns(p)
        (_, first), (_, second) = pair_weights(p, scores, total, turned, allowed)
        xdt = (dt_wide[:, lanes] * active[0, :, lanes].astype(f32)).astype(bf16)
        stacked = jnp.concatenate([xdt * low_lanes[...], xdt * high_lanes[...]], 0)
        inner[0, :, lanes] = mm(jnp.concatenate([first, second], 1), stacked)


def pick(where, kept, given, use):
    own = where[1] == pl.program_id(0) // 2

    @pl.when(own)
    def _():
        use(kept)

    @pl.when(jnp.logical_not(own))
    def _():
        use(given)


def pick_lanes(where, kept, given, lanes):
    own = where[1] == pl.program_id(0) // 2
    return jnp.where(own, kept[0, :, lanes].astype(f32), given[0, :, lanes].astype(f32)).astype(bf16)


def middle_kernel(
    where, inner, active, kept, given, gates, g_mixed, cumul, keep, params, spread, gather,
    mixed, g_y, g_gates, row_part, g_state,
    gated_held, recur_held, act_held, slope_held, unit_held, enter_held, entered,
):
    enter = (jnp.exp(cumul[0]) * keep[0]).astype(bf16)
    c_low = active[0, :, INNER + STATE :]
    squares = jnp.zeros((TOKENS, LANES), f32)
    products = jnp.zeros((TOKENS, LANES), f32)
    for p in range(PAIRS):
        lanes = columns(p)
        carried = mm(c_low, pick_lanes(where, kept, given, lanes))
        wide = mm(enter, spread[:, lanes])
        enter_held[:, lanes] = wide
        recur = inner[0, :, lanes] + wide * carried
        y = recur + params[SKIP_WIDE : SKIP_WIDE + 1, lanes] * active[0, :, lanes].astype(f32)
        gate = gates[0, :, lanes].astype(f32)
        unit_grad = g_mixed[0, :, lanes].astype(f32) * params[GATE_GAIN : GATE_GAIN + 1, lanes]
        sig = sigmoid(gate)
        act = gate * sig
        gated = y * act
        squares = squares + gated * gated
        products = products + unit_grad * gated
        gated_held[:, lanes] = gated
        recur_held[:, lanes] = recur
        act_held[:, lanes] = act
        slope_held[:, lanes] = y * (sig + act * (1.0 - sig))
        unit_held[:, lanes] = unit_grad
    scale = lax.rsqrt(jnp.sum(squares, 1, keepdims=True) * (1.0 / INNER) + epsilon)
    slant = scale * jnp.sum(products, 1, keepdims=True) * (1.0 / INNER)
    rows = jnp.zeros((TOKENS, LANES), f32)
    for p in range(PAIRS):
        lanes = columns(p)
        unit = gated_held[:, lanes] * scale
        mixed[0, :, lanes] = (unit * params[GATE_GAIN : GATE_GAIN + 1, lanes]).astype(bf16)
        g_gated = scale * (unit_held[:, lanes] - unit * slant)
        grad = g_gated * act_held[:, lanes]
        g_gates[0, :, lanes] = (g_gated * slope_held[:, lanes]).astype(bf16)
        low = grad.astype(bf16)
        g_y[0, :, lanes] = low
        low = low.astype(f32)
        rows = rows + sum_heads(low * recur_held[:, lanes], gather[lanes])
        entered[:, lanes] = (enter_held[:, lanes] * low).astype(bf16)
    row_part[0] = rows
    g_state[0] = mm_tn(c_low, entered[...]).astype(bf16)


def inner_back_kernel(
    where, active, g_y, kept, given, dt, cumul, keep, same, spread, gather, low_lanes, high_lanes,
    g_inner, g_b, g_c, direct, column, skip_part,
    dt_wide, enter_wide, entered, by_x, column_high, column_low,
):
    b_low = active[0, :, INNER : INNER + STATE]
    c_low = active[0, :, INNER + STATE :]
    scores = mm_nt(c_low, b_low)
    total = cumul[0]
    turned = total.T
    allowed = same[0] > 0
    dt_wide[...] = mm(dt[0].astype(bf16), spread[...])
    enter_wide[...] = mm((jnp.exp(total) * keep[0]).astype(bf16), spread[...])
    g_scores = jnp.zeros((TOKENS, TOKENS), f32)

    @pl.when(pl.program_id(0) == 0)
    def _():
        skip_part[...] = jnp.zeros_like(skip_part)

    for p in range(PAIRS):
        lanes = columns(p)
        (decay_1, first), (decay_2, second) = pair_weights(p, scores, total, turned, allowed)
        x = active[0, :, lanes].astype(f32)
        xdt = (dt_wide[:, lanes] * x).astype(bf16)
        grad = g_y[0, :, lanes]
        wide = grad.astype(f32)
        entered[:, lanes] = (enter_wide[:, lanes] * wide).astype(bf16)
        skip_part[:, lanes] += jnp.sum((wide * x).reshape(16, 8, LANES), 0)
        stacked = jnp.concatenate([grad * low_lanes[...], grad * high_lanes[...]], 0)
        g_weights = mm_nt(stacked, xdt)
        g_scores = g_scores + g_weights[:TOKENS] * decay_1 + g_weights[TOKENS:] * decay_2
        own = mm_tn(jnp.concatenate([first, second], 0), stacked)
        g_inner[0, :, lanes] = own.astype(bf16)
        by_x[:, lanes] = (x * own).astype(bf16)
        column_high[:, lanes], column_low[:, lanes] = halves(xdt.astype(f32) * own)
    direct[0] = mm(by_x[...], gather[...])
    column[0] = mm(column_high[...], gather[...]) + mm(column_low[...], gather[...])
    g_scores = g_scores.astype(bf16)
    from_scores = mm(g_scores, b_low)

    def add_state(state):
        g_c[0] = from_scores + mm_nt(entered[...], state[0])

    pick(where, kept, given, add_state)
    g_b[0] = mm_tn(g_scores, c_low)


def late_rows(
    where, g_end, kept, given, active, mixin, mixin_halo, g_y, g_inner, g_b, g_c,
    dt, dt_arg, cumul, ending, row_part, direct, column, through, params, spread, gather, upper,
    g_mix, taps, head_sums,
    weighted, state, extended, padded, inner_row, halo_held,
):
    a = pl.program_id(0)

    @pl.when(a == 0)
    def _():
        taps[...] = jnp.zeros_like(taps)
        head_sums[...] = jnp.zeros_like(head_sums)

    b_low = active[0, :, 0:STATE]
    decay_rate = params[DECAY : DECAY + 1, 0:LANES]
    total = cumul[0]
    steps = dt[0]
    to_end = jnp.exp(total[TOKENS - 1 :] - total) * ending[0]
    scaled = to_end * steps
    to_end_low = to_end.astype(bf16)
    scaled_low = scaled.astype(bf16)
    dt_low = steps.astype(bf16)
    through_state = jnp.zeros((TOKENS, LANES), f32)
    padded[:, 0:8] = jnp.zeros((2, 8, LANES), f32)
    padded[:, 136:144] = jnp.zeros((2, 8, LANES), f32)

    def convolved(chunk):
        lanes = columns(chunk)
        slot = chunk % 2
        extended[slot, 0:EDGE] = mixin_halo[0, :, lanes]
        extended[slot, EDGE:] = mixin[0, :, lanes].astype(f32)
        shifted = [extended[slot, EDGE - 3 + k : EDGE + 125 + k] for k in range(4)]
        value = params[CONV_B : CONV_B + 1, lanes]
        for k in range(4):
            value = value + params[k : k + 1, lanes] * shifted[k]
        return value, sigmoid(value), shifted

    def back(chunk, grad, value, sig, shifted):
        lanes = columns(chunk)
        slot = chunk % 2
        grad = grad * (sig + value * sig * (1.0 - sig))
        padded[slot, 8:136] = grad
        main = params[0:1, lanes] * padded[slot, 11:139]
        edge = params[0:1, lanes] * padded[slot, 3:11]
        for k in range(4):
            if k:
                tap = params[k : k + 1, lanes]
                main = main + tap * padded[slot, 11 - k : 139 - k]
                edge = edge + tap * padded[slot, 3 - k : 11 - k]
            taps[k : k + 1, lanes] += jnp.sum(grad * shifted[k], 0, keepdims=True)
        taps[4:5, lanes] += jnp.sum(grad, 0, keepdims=True)
        g_mix[0, :, lanes] = main.astype(bf16)
        halo_held[:, lanes] = edge

    for p in range(PAIRS):
        lanes = columns(p)
        end = g_end[0, :, lanes]
        begin = pick_lanes(where, kept, given, lanes)
        inner_row[0:1, lanes] = jnp.sum(begin.astype(f32) * end.astype(f32), 0, keepdims=True)
        state[:, lanes] = end
        from_state = mm(b_low, end)
        value, sig, shifted = convolved(p)
        x = (value * sig).astype(bf16).astype(f32)
        weighted[:, lanes] = (mm(scaled_low, spread[:, lanes]) * x).astype(bf16)
        grad = mm(dt_low, spread[:, lanes]) * (
            g_inner[0, :, lanes].astype(f32) + mm(to_end_low, spread[:, lanes]) * from_state
        ) + params[SKIP_WIDE : SKIP_WIDE + 1, lanes] * g_y[0, :, lanes].astype(f32)
        through_state = through_state + mm((x * from_state).astype(bf16), gather[lanes])
        back(p, grad, value, sig, shifted)
    state_part = scaled * through_state
    inner_sum = jnp.zeros((8, LANES), f32)
    for p in range(PAIRS):
        lanes = columns(p)
        inner_sum = inner_sum + sum_heads(inner_row[:, lanes], gather[lanes])
    mask = lax.broadcasted_iota(jnp.int32, (4, LANES), 0) == a
    flow = jnp.sum(jnp.where(mask, through[...], 0.0), 0, keepdims=True)
    at_end = jnp.sum(state_part, 0, keepdims=True) + flow * inner_sum[0:1]
    g_rate = exact_mm(upper[...], row_part[0] - column[0] - state_part) + at_end
    g_raw = direct[0] + to_end * through_state - decay_rate * g_rate
    g_raw = g_raw * sigmoid(dt_arg[0])
    head_sums[0:1] += jnp.sum(g_raw, 0, keepdims=True)
    head_sums[1:2] -= decay_rate * jnp.sum(steps * g_rate, 0, keepdims=True)
    g_mix[0, :, XBC:MIX_PAD] = g_raw.astype(bf16)
    g_mix[0, :, MIX_PAD:] = jnp.zeros((TOKENS, MIX_WIDE - MIX_PAD), bf16)
    back(PAIRS, g_b[0] + mm_nt(weighted[...], state[...]), *convolved(PAIRS))
    back(PAIRS + 1, g_c[0], *convolved(PAIRS + 1))


def early_grads_kernel(
    where, mixed, cotangent, normed_t, g_gates, mine, send_0, send_1, send_2, send_3,
    mixed_held, cot_held, normed_held, gates_held, mine_held, send_held, in_sems, out_sems,
):
    place, core = where[0], where[1]
    for_out = [
        pltpu.make_async_copy(mixed, mixed_held, in_sems.at[0]),
        pltpu.make_async_copy(cotangent, cot_held, in_sems.at[1]),
    ]
    for_gate = [
        pltpu.make_async_copy(normed_t, normed_held, in_sems.at[2]),
        pltpu.make_async_copy(g_gates, gates_held, in_sems.at[3]),
    ]
    to_mine = [
        pltpu.make_async_copy(
            mine_held.at[pl.ds(192 * k, 192)], mine.at[pl.ds(192 * k, 192)], out_sems.at[k]
        )
        for k in range(4)
    ]
    to_send = [
        pltpu.make_async_copy(send_held.at[pl.ds(192 * k, 192)], target, out_sems.at[4 + k])
        for k, target in enumerate((send_0, send_1, send_2, send_3))
    ]

    def gate_rows(target, copies):
        for copy in for_gate:
            copy.wait()
        for k in range(4):
            rows = pl.ds(pl.multiple_of(lax.rem(place + k, 4) * 192, 192), 192)
            target[192 * k : 192 * (k + 1)] = mm(normed_held[rows], gates_held[...]).astype(bf16)
            copies[k].start()

    def out_rows(target, copies):
        for copy in for_out:
            copy.wait()
        for k in range(4):
            lanes = pl.ds(pl.multiple_of(lax.rem(place + k, 4) * 384, 384), 384)
            grad = mm_tn(mixed_held[:, lanes], cot_held[...]).astype(bf16)
            target[192 * k : 192 * (k + 1), 0:768] = grad[0:192]
            target[192 * k : 192 * (k + 1), 768:] = grad[192:384]
            copies[k].start()

    @pl.when(core == 0)
    def _():
        for copy in for_out + for_gate:
            copy.start()
        out_rows(send_held, to_send)
        gate_rows(mine_held, to_mine)

    @pl.when(core == 1)
    def _():
        for copy in for_gate + for_out:
            copy.start()
        gate_rows(send_held, to_send)
        out_rows(mine_held, to_mine)

    for copy in to_mine + to_send:
        copy.wait()


def early_pair_kernel(mine, *rest):
    for k in range(4):
        rows = slice(192 * k, 192 * (k + 1))
        rest[4 + k][...] = (mine[rows].astype(f32) + rest[k][...].astype(f32)).astype(bf16)


def sum_blocks_kernel(a, b, c, d, total):
    for high in range(4):
        rows = slice(48 * high, 48 * (high + 1))
        value = a[rows].astype(f32) + b[rows].astype(f32) + c[rows].astype(f32) + d[rows].astype(f32)
        for low in range(4):
            total[4 * high + low] = value[:, columns(low, 384)].astype(bf16)


def late_columns(
    core, step, normed_t, halo_t, g_held, g_halo, taps, head_sums, skip_part, gather, mine, sends,
    held, sent, sems,
):
    lanes = pl.ds(pl.multiple_of(step * 512, 512), 512)
    g_mix = g_held[:, lanes]
    g_edge = jnp.concatenate([g_halo[:, lanes], jnp.zeros((LANES - 32, 512), f32)], 0).astype(bf16)
    for z in range(4):
        rows = slice(192 * z, 192 * (z + 1))
        grad = (mm(normed_t[rows], g_mix) + mm(halo_t[rows], g_edge)).astype(bf16)
        for c in range(2):
            for jj in range(4):
                held[c, jj, z] = grad[96 * c : 96 * (c + 1), columns(jj)]

    @pl.when(step == 3)
    def _():
        lane = lax.broadcasted_iota(jnp.int32, (8, LANES), 1)
        row = lax.broadcasted_iota(jnp.int32, (8, LANES), 0)
        nothing = jnp.zeros((8, LANES), f32)
        skips = sum_heads(skip_part[...], gather[...])
        head_rows = jnp.where(row == 2, jnp.sum(skips, 0, keepdims=True), head_sums[...])
        for z in range(4):
            for part in range(5):
                tile = head_rows
                if part < 4:
                    begin = 448 * z + LANES * part
                    tile = taps[:, begin // LANES * LANES : begin // LANES * LANES + LANES]
                    if begin % LANES:
                        after = min(begin // LANES + 1, XBC // LANES - 1) * LANES
                        tile = jnp.where(lane < 64, taps[:, after : after + LANES], tile)
                        tile = pltpu.roll(tile, 64, 1)
                tile = jnp.concatenate([tile, nothing], 0)
                held[0, 3, z, 16 * part : 16 * (part + 1)] = tile.astype(bf16)

    mine[...] = held[core]
    sent[pl.ds(4 * step, 4)] = held[1 - core]
    copies = [
        pltpu.make_async_copy(sent.at[pl.ds(4 * k, 4)], target, sems.at[k])
        for k, target in enumerate(sends)
    ]
    for k in range(4):

        @pl.when(step == k)
        def _(k=k):
            copies[k].start()

    @pl.when(step == 3)
    def _():
        for copy in copies:
            copy.wait()


def late_kernel(
    where, g_end, kept, given, active, mixin, mixin_halo, g_y, g_inner, g_b, g_c,
    dt, dt_arg, cumul, ending, row_part, direct, column, through, params, spread, gather, upper,
    normed_t, halo_t, skip_part,
    g_mix, g_halo, mine, send_0, send_1, send_2, send_3,
    weighted, state, extended, padded, inner_row, g_held, halo_held, taps, head_sums, held, sent,
    edge_held, sems,
):
    step = pl.program_id(0)

    @pl.when(step < 4)
    def _():
        late_rows(
            where, g_end, kept, given, active, mixin, mixin_halo, g_y, g_inner, g_b, g_c,
            dt, dt_arg, cumul, ending, row_part, direct, column, through, params, spread,
            gather, upper, g_mix, taps, head_sums,
            weighted, state, extended, padded, inner_row, edge_held,
        )
        g_held[pl.ds(pl.multiple_of(step * TOKENS, TOKENS), TOKENS)] = g_mix[0]
        rows = pl.ds(pl.multiple_of(step * EDGE, EDGE), EDGE)
        halo_held[rows, 0:XBC] = edge_held[...]
        halo_held[rows, XBC:] = jnp.zeros((EDGE, MIX_WIDE - XBC), f32)
        g_halo[0] = edge_held[...].astype(bf16)

    @pl.when(step >= 4)
    def _():
        late_columns(
            where[1], step - 4, normed_t, halo_t, g_held, halo_held, taps, head_sums, skip_part,
            gather, mine, (send_0, send_1, send_2, send_3), held, sent, sems,
        )


def both_cores(where, mine, other):
    first = where[1] == 0
    return jnp.where(first, mine, other), jnp.where(first, other, mine)


def join_kernel(where, mine, other, through, through_other, spread, total, wide):
    first = where[1] == 0
    own = jnp.where(first, through[0:2], through[2:4])
    theirs = jnp.where(first, through_other[0:2], through_other[2:4])
    through_0, through_1 = both_cores(where, own, theirs)
    everything_0, everything_1 = both_cores(where, through[...], through_other[...])
    rows = jnp.concatenate([through_0, through_1, jnp.zeros((4, LANES), f32)], 0)
    wide[...] = widen(halves(rows), spread[...])
    row = lax.broadcasted_iota(jnp.int32, (16, LANES), 0)
    piece = jnp.zeros((16, LANES), f32)
    for c, source in enumerate((everything_0, everything_1)):
        for p, value in enumerate(halves(source)):
            for a in range(4):
                piece = jnp.where(row == 4 * a + 2 * c + p, value[a : a + 1].astype(f32), piece)
    piece = piece.astype(bf16)
    for a in range(2):
        for part in range(8):
            span = slice(part * 16, (part + 1) * 16)
            state_0, state_1 = both_cores(
                where, mine[a, span].astype(f32), other[a, span].astype(f32)
            )
            value = wide[2 + a : 3 + a] * state_0 + state_1
            total[8 * a + part, :, 0:INNER] = value.astype(bf16)
            total[8 * a + part, :, INNER:] = piece


def split_kernel(where, back, mine, other, wide, kept, given):
    for a in range(2):
        for part in range(8):
            span = slice(part * 16, (part + 1) * 16)
            state_0, _ = both_cores(where, mine[a, span].astype(f32), other[a, span].astype(f32))
            in_0 = back[8 * a + part].astype(f32)
            in_1 = wide[a : a + 1] * in_0 + state_0
            keeps, gives = both_cores(where, in_0, in_1)
            kept[a, span] = keeps.astype(bf16)
            given[a, span] = gives.astype(bf16)


def scan_kernel(where, arrived, spread, before, picked, factors):
    chip = where[3] * 4 + where[4]
    forward = 2 * where[1] + chip // 8
    backward = (2 * chip + where[1]) // 8
    row = lax.broadcasted_iota(jnp.int32, (8, 16), 0)
    column = lax.broadcasted_iota(jnp.int32, (8, 16), 1)
    wanted = jnp.where(row < 2, 4 * forward + 2 * row, 4 * backward + 2 * (row - 2))
    chosen = (column >= wanted) & (column < wanted + 2) & (row < 4)
    chosen = jnp.where(chosen, 1.0, 0.0).astype(bf16)
    for i in range(16):
        picked[8 * i : 8 * (i + 1)] = mm(chosen, arrived[i, :, INNER:])
    factors[...] = widen(halves(picked[...]), spread[...])
    so_far = jnp.zeros((16, INNER), f32)
    for i in range(16):
        before[i] = so_far.astype(bf16)
        factor = factors[8 * i : 8 * i + 1] * factors[8 * i + 1 : 8 * i + 2]
        so_far = factor * so_far + arrived[i, :, :INNER].astype(f32)


def scan_back_kernel(arrived, picked, spread, after, factors):
    factors[...] = widen(halves(picked[...]), spread[...])
    so_far = jnp.zeros((16, INNER), f32)
    for i in reversed(range(32)):
        after[i] = so_far.astype(bf16)
        at = 8 * (i // 2) + 2 + i % 2
        so_far = factors[at : at + 1] * so_far + arrived[i].astype(f32)


def pair_kernel(mine, *rest):
    pair = rest[-1]
    count = rest[0].shape[0]
    for k, other in enumerate(rest[:-1]):
        rows = slice(count * k, count * (k + 1))
        pair[rows] = (mine[rows].astype(f32) + other[...].astype(f32)).astype(bf16)


def reduce_early_kernel(parts, owned):
    total = parts[0].astype(f32)
    for k in range(1, 16):
        total = total + parts[k].astype(f32)
    owned[...] = total.astype(bf16)


def reduce_kernel(early, late, owned):
    held = [early[:, columns(k)] for k in range(3)]
    total = late[0].astype(f32)
    for k in range(1, 64):
        total = total + late[k].astype(f32)
    total = total.astype(bf16)
    for copy in range(16):
        for k in range(3):
            owned[copy, 48 * k : 48 * (k + 1)] = held[k]
        owned[copy, 144:240] = total


def last_kernel(
    hidden, cotangent, mixed, g_gates, g_mix, spill, mix_weight, gate_weight, out_full, params,
    output, grad_hidden, held,
):
    x = hidden[0].astype(f32)
    output[0] = (x + mm(mixed[0], out_full[...])).astype(bf16)
    held[...] = g_mix[0, :, 0:MIX_PAD]
    end = g_mix[0, TOKENS - 16 :, 0:XBC].astype(f32)
    shift = jnp.concatenate([jnp.zeros((8, XBC), f32), spill[0].astype(f32)], 0)
    held[TOKENS - 16 :, 0:XBC] = (end + shift).astype(bf16)
    grad = mm_nt(held[...], mix_weight[...]) + mm_nt(g_gates[0], gate_weight[...])
    grad = grad * params[GAIN : GAIN + 1, 0:768]
    scale = lax.rsqrt(jnp.mean(x * x, axis=1, keepdims=True) + epsilon)
    pull = jnp.mean(grad * x, axis=1, keepdims=True)
    value = cotangent[0].astype(f32) + scale * grad - x * (scale * scale * scale * pull)
    grad_hidden[0] = value.astype(bf16)


def finish_kernel(
    where, shared, other, weight, gain, out_weight, gate_gain,
    grad, by_gain, conv_w, conv_b, grad_dt, grad_a, grad_skip, grad_out, by_gate_gain,
    sums, out_sums,
):
    up = pl.program_id(0)
    first = where[1] == 0

    def both(j, rows):
        a, b = shared[j, rows].astype(f32), other[j, rows].astype(f32)
        return jnp.where(first, a, b), jnp.where(first, b, a)

    for right in range(4):
        half, side = divmod(right, 2)
        for k in range(3):
            low, high = both(4 * up + right, slice(48 * k, 48 * (k + 1)))
            grad[:, columns(3 * right + k)] = low
            grad_out[half, :, columns(3 * side + k)] = high
    from_core = up // 2
    rows = pl.ds(pl.multiple_of(144 + 48 * lax.rem(up, 2), 16), 48)
    for j in range(15):
        begin = INNER + LANES * j
        width = min(LANES, INNER + MIX - begin)
        low, high = both(j, rows)
        grad[:, begin : begin + width] = jnp.where(from_core == 0, low, high)[:, 0:width]
    total = jnp.sum(grad[...] * weight[...].astype(f32), axis=1, keepdims=True)
    sums[pl.ds(pl.multiple_of(48 * up, 48), 48)] = jnp.broadcast_to(total, (48, LANES))
    for half in range(2):
        total = jnp.sum(grad_out[half] * out_weight[half].astype(f32), axis=1, keepdims=True)
        begin = pl.multiple_of(192 * half + 48 * up, 48)
        out_sums[pl.ds(begin, 48)] = jnp.broadcast_to(total, (48, LANES))

    @pl.when(up == 3)
    def _():
        by_gain[...] = sums[...].T[0:1].reshape(192) / gain[...]
        by_gate_gain[...] = out_sums[...].T[0:1].reshape(384) / gate_gain[...]
        rest, _ = both(15, slice(144, 240))
        for part in range(4):
            span = min(LANES, 448 - LANES * part)
            lanes = slice(LANES * part, LANES * part + span)
            conv_w[:, lanes] = rest[16 * part : 16 * part + 4, 0:span]
            conv_b[lanes] = rest[16 * part + 4 : 16 * part + 5, 0:span].reshape(span)
        for z in range(4):

            @pl.when(where[0] == z)
            def _(z=z):
                heads = pltpu.roll(rest[64:72], (LANES - 6 * z) % LANES, 1)
                for k, target in enumerate((grad_dt, grad_a, grad_skip)):
                    target[...] = heads[k : k + 1, 0:6].reshape(6)


def per_device(
    hidden,
    segments,
    norm_gain,
    in_weight,
    conv_weight,
    conv_bias,
    dt_bias,
    a_log,
    skip,
    gate_gain,
    out_weight,
    cotangent,
):
    core = lax.axis_index("seq_2")
    place = lax.axis_index("fsdp")
    chip = lax.axis_index("seq_0") * 4 + lax.axis_index("seq_1")
    where = jnp.stack(
        [
            place, core, (chip * 2 + core) * TOKENS, lax.axis_index("seq_0"),
            lax.axis_index("seq_1"),
        ]
    ).astype(jnp.int32)

    message, mix_tail = call(
        message_kernel,
        [(None, shaped((96, MIX_PAD), bf16)), (None, shaped((192, LANES), bf16))],
        [SCALARS] + [None] * 8,
        [
            where, in_weight, norm_gain, conv_weight, conv_bias, dt_bias, a_log, skip, gate_gain,
        ],
        scratch=[
            pltpu.VMEM((16, 512), f32), pltpu.VMEM((192, LANES), f32), pltpu.VMEM((96, LANES), f32)
        ],
        mib=LARGE,
    )
    mix_fetched = fetch(message)
    halo = line(hidden[:, TOKENS - EDGE :], SEQ, 1)

    head_of = np.arange(INNER) // HEADDIM
    spread = jnp.asarray((np.arange(LANES)[:, None] == head_of[None]), bf16)
    gather = jnp.asarray((head_of[:, None] == np.arange(LANES)[None]), bf16)
    lower = jnp.asarray(np.tril(np.ones((TOKENS, TOKENS))), bf16)
    upper = jnp.asarray(np.triu(np.ones((TOKENS, TOKENS))), bf16)
    low_lanes = jnp.asarray(np.ones((TOKENS, 1)) * (np.arange(LANES) < 64), bf16)
    high_lanes = jnp.asarray(np.ones((TOKENS, 1)) * (np.arange(LANES) >= 64), bf16)

    tokens = shaped((4, TOKENS, LANES))
    second, second_done = call(
        second_message_kernel,
        [(None, shaped((192, INNER), bf16))],
        [SCALARS, ANYWHERE, ANYWHERE],
        [where, in_weight, out_weight],
        scratch=[pltpu.SemaphoreType.DMA((3,))],
        marked=True,
        mib=LARGE,
    )
    same, keep, ending, passing, halo = call(
        tables_kernel,
        [
            (None, tokens), (None, tokens), (None, tokens), (None, shaped((4, LANES))),
            (None, shaped((4, EDGE, 768))),
        ],
        [SCALARS, None, None],
        [where, segments, halo],
        micros=60,
        after=[second_done],
        mib=LARGE,
    )
    half = shaped((2, STATE, INNER), bf16)
    (
        params, mixin, mixin_halo, active, dt_arg, dt, cumul, through, local_mine, local_send,
        normed, normed_t, halo_t, mix_weight,
    ) = call(
        front_kernel,
        [
            (None, shaped((16, XBC))),
            (ANYWHERE, shaped((4, TOKENS, XBC), bf16)),
            (None, shaped((4, EDGE, XBC))),
            (ANYWHERE, shaped((4, TOKENS, XBC), bf16)),
            (None, tokens),
            (None, tokens),
            (None, tokens),
            (None, shaped((4, LANES))),
            (ANYWHERE, half),
            (ANYWHERE, half),
            (ANYWHERE, shaped((512, 768), bf16)),
            (ANYWHERE, shaped((768, 512), bf16)),
            (None, shaped((768, LANES), bf16)),
            (ANYWHERE, shaped((768, MIX_PAD), bf16)),
        ],
        [SCALARS] + [None] * 6 + [ANYWHERE] * 9,
        [where, hidden, halo, ending, passing, spread, lower, message, in_weight, mix_tail]
        + mix_fetched
        + [swap(part) for part in mix_fetched],
        scratch=[
            pltpu.VMEM((768, MIX_PAD), bf16),
            pltpu.VMEM((4, 96, LANES), bf16),
            pltpu.VMEM((512, 768), bf16),
            pltpu.VMEM((768, 512), bf16),
            pltpu.VMEM((4, TOKENS, XBC), bf16),
            pltpu.VMEM((4, TOKENS, XBC), bf16),
            pltpu.VMEM((4, STATE, INNER), bf16),
            pltpu.VMEM((2, 8, EDGE + TOKENS, LANES), f32),
            pltpu.VMEM((4, STATE, TOKENS), bf16),
            pltpu.VMEM((512, LANES), bf16),
            pltpu.VMEM((2, 512, 256), f32),
            pltpu.SemaphoreType.DMA((12,)),
            pltpu.SemaphoreType.DMA((29,)),
        ],
        mib=LARGE,
        micros=10,
    )

    blocks = shaped((16, 16, INNER), bf16)
    local_other = swap(local_send)
    through_other = swap(through)
    total, wide = call(
        join_kernel,
        [(None, shaped((16, 16, INNER + LANES), bf16)), (None, shaped((8, INNER)))],
        [SCALARS] + [None] * 5,
        [where, local_mine, local_other, through, through_other, spread],
        micros=0,
    )
    fetched = fetch(second)
    inner, inner_done = call(
        inner_kernel,
        [(by_seq(TOKENS, INNER), shaped((4, TOKENS, INNER)))],
        [
            by_seq(TOKENS, XBC), by_seq(TOKENS, LANES), by_seq(TOKENS, LANES),
            by_seq(TOKENS, TOKENS), constant(LANES, INNER), constant(TOKENS, LANES),
            constant(TOKENS, LANES),
        ],
        [active, dt, cumul, same, spread, low_lanes, high_lanes],
        grid=(4,),
        scratch=[pltpu.VMEM((TOKENS, INNER), f32)],
        mib=LARGE,
        marked=True,
        micros=60,
    )
    before, picked = call(
        scan_kernel,
        [(None, blocks), (None, shaped((128, LANES)))],
        [SCALARS, None, None],
        [where, exchange(total, CHIPS), spread],
        scratch=[pltpu.VMEM((128, INNER), f32)],
        micros=0,
        after=[inner_done],
    )
    gate_weight, out_full, gates, g_mixed, projected = call(
        weights_kernel,
        [
            (ANYWHERE, shaped((768, INNER), bf16)),
            (ANYWHERE, shaped((INNER, 768), bf16)),
            (ANYWHERE, shaped((512, INNER), bf16)),
            (ANYWHERE, shaped((512, INNER), bf16)),
        ],
        [SCALARS, None, None] + [ANYWHERE] * 8,
        [where, normed, cotangent.reshape(512, 768), in_weight, out_weight]
        + fetched
        + [swap(part) for part in fetched],
        scratch=[
            pltpu.VMEM((768, INNER), bf16),
            pltpu.VMEM((INNER, 768), bf16),
            pltpu.VMEM((512, INNER), bf16),
            pltpu.VMEM((512, INNER), bf16),
            pltpu.SemaphoreType.DMA((20,)),
            pltpu.SemaphoreType.DMA((14,)),
        ],
        marked=True,
        micros=0,
        mib=LARGE,
    )
    gates = gates.reshape(4, TOKENS, INNER)
    g_mixed = g_mixed.reshape(4, TOKENS, INNER)
    kept, given = call(
        split_kernel,
        [(None, half), (None, half)],
        [SCALARS] + [None] * 4,
        [where, exchange(before, CHIPS), local_mine, local_other, wide],
        micros=0,
        after=[projected],
    )
    given = swap(given)

    mixed, g_y, g_gates, row_part, g_state = call(
        middle_kernel,
        [
            (by_seq(TOKENS, INNER), shaped((4, TOKENS, INNER), bf16)),
            (by_seq(TOKENS, INNER), shaped((4, TOKENS, INNER), bf16)),
            (by_seq(TOKENS, INNER), shaped((4, TOKENS, INNER), bf16)),
            (by_seq(TOKENS, LANES), tokens),
            (by_seq(STATE, INNER), shaped((4, STATE, INNER), bf16)),
        ],
        [
            by_seq(TOKENS, INNER), by_seq(TOKENS, XBC), own_half(STATE, INNER),
            other_half(STATE, INNER), by_seq(TOKENS, INNER), by_seq(TOKENS, INNER),
            by_seq(TOKENS, LANES), by_seq(TOKENS, LANES), constant(16, XBC),
            constant(LANES, INNER), constant(INNER, LANES),
        ],
        [inner, active, kept, given, gates, g_mixed, cumul, keep, params, spread, gather],
        scalars=where,
        grid=(4,),
        scratch=[pltpu.VMEM((TOKENS, INNER), f32)] * 6 + [pltpu.VMEM((TOKENS, INNER), bf16)],
        mib=LARGE,
        micros=11,
    )

    blocks_back = shaped((32, 16, INNER), bf16)
    arrived_back = exchange(g_state.reshape(32, 16, INNER), SEQ)

    early_shape = shaped((768, INNER), bf16)
    early_mine, *early_send, early_done = call(
        early_grads_kernel,
        [(ANYWHERE, early_shape)] + [(ANYWHERE, shaped((192, INNER), bf16))] * 4,
        [SCALARS] + [ANYWHERE] * 4,
        [
            where, mixed.reshape(512, INNER), cotangent.reshape(512, 768), normed_t,
            g_gates.reshape(512, INNER),
        ],
        scratch=[
            pltpu.VMEM((512, INNER), bf16),
            pltpu.VMEM((512, 768), bf16),
            pltpu.VMEM((768, 512), bf16),
            pltpu.VMEM((512, INNER), bf16),
            pltpu.VMEM((768, INNER), bf16),
            pltpu.VMEM((768, INNER), bf16),
            pltpu.SemaphoreType.DMA((4,)),
            pltpu.SemaphoreType.DMA((8,)),
        ],
        marked=True,
        mib=LARGE,
        micros=60,
    )
    parts = call(
        early_pair_kernel,
        [(None, shaped((192, INNER), bf16))] * 4,
        [None] * 5,
        [early_mine] + [swap(part) for part in early_send],
        micros=0,
    )
    early_parts = [parts[0]] + [ring(parts[k], "fsdp", k) for k in (1, 2, 3)]

    (after,) = call(
        scan_back_kernel,
        [(None, blocks_back)],
        [None] * 3,
        [arrived_back, picked, spread],
        scratch=[pltpu.VMEM((128, INNER), f32)],
        micros=2,
        after=[early_done],
    )

    g_inner, g_b, g_c, direct, column, skip_part, inner_back_done = call(
        inner_back_kernel,
        [
            (by_seq(TOKENS, INNER), shaped((4, TOKENS, INNER), bf16)),
            (by_seq(TOKENS, STATE), tokens),
            (by_seq(TOKENS, STATE), tokens),
            (by_seq(TOKENS, LANES), tokens),
            (by_seq(TOKENS, LANES), tokens),
            (constant(8, INNER), shaped((8, INNER))),
        ],
        [
            by_seq(TOKENS, XBC), by_seq(TOKENS, INNER), own_half(STATE, INNER),
            other_half(STATE, INNER), by_seq(TOKENS, LANES), by_seq(TOKENS, LANES),
            by_seq(TOKENS, LANES), by_seq(TOKENS, TOKENS), constant(LANES, INNER),
            constant(INNER, LANES), constant(TOKENS, LANES), constant(TOKENS, LANES),
        ],
        [
            active, g_y, kept, given, dt, cumul, keep, same, spread, gather, low_lanes, high_lanes,
        ],
        scalars=where,
        grid=(4,),
        scratch=[pltpu.VMEM((TOKENS, INNER), f32)] * 2 + [pltpu.VMEM((TOKENS, INNER), bf16)] * 4,
        mib=LARGE,
        marked=True,
        micros=60,
    )
    early_blocks, early_summed = call(
        sum_blocks_kernel,
        [(None, shaped((16, 48, 384), bf16))],
        [None] * 4,
        early_parts,
        marked=True,
        micros=0,
        after=[inner_back_done],
    )
    g_end = exchange(after, SEQ).reshape(4, STATE, INNER)
    late_spec = pl.BlockSpec((4, 4, 96, LANES), lambda s, *_: (jnp.maximum(s - 4, 0), 0, 0, 0))
    late_shape = shaped((16, 4, 96, LANES), bf16)
    piece = shaped((16 // LATE_PIECES, 4, 96, LANES), bf16)
    g_mix, g_halo, late_mine, *late_send, late_done = call(
        late_kernel,
        [
            (seq_first(TOKENS, MIX_WIDE), shaped((4, TOKENS, MIX_WIDE), bf16)),
            (seq_first(EDGE, XBC), shaped((4, EDGE, XBC), bf16)),
            (late_spec, late_shape),
        ]
        + [(ANYWHERE, piece)] * LATE_PIECES,
        [seq_first(STATE, INNER), own_half(STATE, INNER), other_half(STATE, INNER)]
        + [
            pl.BlockSpec((1, TOKENS, 256), lambda a, *_: (jnp.minimum(a, 3), 0, 6)),
            seq_first(TOKENS, XBC), seq_first(EDGE, XBC), seq_first(TOKENS, INNER),
            seq_first(TOKENS, INNER), seq_first(TOKENS, STATE), seq_first(TOKENS, STATE),
        ]
        + [seq_first(TOKENS, LANES)] * 7
        + [
            constant(4, LANES), constant(16, XBC), constant(LANES, INNER), constant(INNER, LANES),
            constant(TOKENS, TOKENS), constant(768, 512), constant(768, LANES), constant(8, INNER),
        ],
        [
            g_end, kept, given, active, mixin, mixin_halo, g_y, g_inner, g_b, g_c, dt,
            dt_arg, cumul, ending, row_part, direct, column, through, params, spread, gather, upper,
            normed_t, halo_t, skip_part,
        ],
        scalars=where,
        grid=(8,),
        scratch=[
            pltpu.VMEM((TOKENS, INNER), bf16),
            pltpu.VMEM((STATE, INNER), bf16),
            pltpu.VMEM((2, EDGE + TOKENS, LANES), f32),
            pltpu.VMEM((2, 144, LANES), f32),
            pltpu.VMEM((8, INNER), f32),
            pltpu.VMEM((512, MIX_WIDE), bf16),
            pltpu.VMEM((32, MIX_WIDE), f32),
            pltpu.VMEM((8, XBC), f32),
            pltpu.VMEM((8, LANES), f32),
            pltpu.VMEM((2, 4, 4, 96, LANES), bf16),
            pltpu.VMEM((16, 4, 96, LANES), bf16),
            pltpu.VMEM((EDGE, XBC), f32),
            pltpu.SemaphoreType.DMA((LATE_PIECES,)),
        ],
        marked=True,
        mib=LARGE,
        micros=60,
        after=[early_summed, inner_back_done],
    )
    early_owned, early_reduced = call(
        reduce_early_kernel,
        [(None, shaped((48, 384), bf16))],
        [None],
        [exchange(early_blocks, CHIPS)],
        marked=True,
        micros=0,
        after=[late_done],
    )
    spill = line(g_halo, SEQ, -1)
    (late_pair,) = call(
        pair_kernel,
        [(None, late_shape)],
        [None] * (1 + LATE_PIECES),
        [late_mine] + [swap(part) for part in late_send],
        micros=0,
        after=[spill, early_reduced],
    )
    late_parts = exchange(late_pair.reshape(64, 96, LANES), COLUMNS)

    rows = by_seq(TOKENS, 768)
    output, grad_hidden, last_done = call(
        last_kernel,
        [(rows, shaped((4, TOKENS, 768), bf16)), (rows, shaped((4, TOKENS, 768), bf16))],
        [
            rows, rows, by_seq(TOKENS, INNER), by_seq(TOKENS, INNER), by_seq(TOKENS, MIX_WIDE),
            by_seq(EDGE, XBC), constant(768, MIX_PAD), constant(768, INNER), constant(INNER, 768),
            constant(16, XBC),
        ],
        [
            hidden, cotangent, mixed, g_gates, g_mix, spill, mix_weight, gate_weight, out_full,
            params,
        ],
        grid=(4,),
        scratch=[pltpu.VMEM((TOKENS, MIX_PAD), bf16)],
        mib=LARGE,
        marked=True,
        micros=60,
    )
    (owned,) = call(
        reduce_kernel,
        [(None, shaped((16, 240, LANES), bf16))],
        [None] * 2,
        [early_owned, late_parts],
        micros=2,
        after=[last_done],
    )
    shared = exchange(owned, CHIPS)
    sum_in, by_gain, sum_conv_w, sum_conv_b, sum_dt, sum_a, sum_skip, sum_out, by_gate_gain = call(
        finish_kernel,
        [
            (pl.BlockSpec((48, INNER + MIX), lambda i, *_: (i, 0)), shaped((192, INNER + MIX))),
            (constant(192), shaped((192,))),
            (constant(4, 448), shaped((4, 448))),
            (constant(448), shaped((448,))),
            (constant(6), shaped((6,))),
            (constant(6), shaped((6,))),
            (constant(6), shaped((6,))),
            (pl.BlockSpec((2, 48, 768), lambda i, *_: (0, i, 0)), shaped((2, 192, 768))),
            (constant(384), shaped((384,))),
        ],
        [
            constant(16, 240, LANES), constant(16, 240, LANES),
            pl.BlockSpec((48, INNER + MIX), lambda i, *_: (i, 0)), constant(192),
            pl.BlockSpec((2, 48, 768), lambda i, *_: (0, i, 0)), constant(384),
        ],
        [
            shared, swap(shared), in_weight, norm_gain.astype(f32),
            out_weight.reshape(2, 192, 768), gate_gain.astype(f32),
        ],
        scalars=where,
        grid=(4,),
        scratch=[pltpu.VMEM((192, LANES), f32), pltpu.VMEM((384, LANES), f32)],
        micros=4,
    )

    return (
        output,
        grad_hidden,
        by_gain,
        sum_in,
        sum_conv_w,
        sum_conv_b,
        sum_dt,
        sum_a,
        sum_skip,
        by_gate_gain,
        sum_out.reshape(384, 768),
    )


def solution(mesh):
    finer = Mesh(
        mesh.devices.reshape(4, 4, 2, mesh.shape["fsdp"]), ("seq_0", "seq_1", "seq_2", "fsdp")
    )
    in_specs = (
        P("fsdp", SEQ, None),
        P("fsdp", SEQ),
        P("fsdp"),
        P("fsdp", None),
        P(None, "fsdp"),
        P("fsdp"),
        P("fsdp"),
        P("fsdp"),
        P("fsdp"),
        P("fsdp"),
        P("fsdp", None),
        P("fsdp", SEQ, None),
    )
    out_specs = (
        P("fsdp", SEQ, None),
        P("fsdp", SEQ, None),
        P("fsdp"),
        P("fsdp", None),
        P(None, "fsdp"),
        P("fsdp"),
        P("fsdp"),
        P("fsdp"),
        P("fsdp"),
        P("fsdp"),
        P("fsdp", None),
    )
    return jax.shard_map(
        per_device, mesh=finer, in_specs=in_specs, out_specs=out_specs, check_vma=False
    )
```

```python
import functools

import jax
import jax.numpy as jnp
import numpy as np
from jax import lax
from jax.experimental import pallas as pl
from jax.experimental.pallas import tpu as pltpu
from jax.sharding import Mesh
from jax.sharding import PartitionSpec as P

INNER = 1536
HEADS = 24
HEADDIM = 64
STATE = 128
XBC = 1792
MIX = 1816
MIX_PAD = 1920
MIX_WIDE = 2048
EDGE = 8
TOKENS = 128
LANES = 128
PAIRS = 12
SEQ = ("seq_0", "seq_1", "seq_2")
CHIPS = ("seq_0", "seq_1")
COLUMNS = ("seq_0", "seq_1", "fsdp")

epsilon = 1e-05
bf16 = jnp.bfloat16
f32 = jnp.float32
VMEM_MIB = 24
LARGE = 60
LATE_PIECES = 4
COST = 1.1e9

CONV_W, CONV_B, GATE_GAIN, GAIN, DT_BIAS, DECAY, SKIP, SKIP_WIDE = 0, 4, 5, 6, 7, 8, 9, 10


def ring(value, axis, steps):
    count = lax.axis_size(axis)
    pairs = [(source, (source + steps) % count) for source in range(count)]
    return lax.ppermute(value, axis, pairs)


def line(value, axis, steps):
    count = lax.axis_size(axis)
    initial, last = (max(0, -steps), min(count, count - steps))
    return lax.ppermute(value, axis, [(source, source + steps) for source in range(initial, last)])


def swap(value):
    return ring(value, "seq_2", 1)


def dot(pattern, left, right):
    return jnp.einsum(pattern, left, right, preferred_element_type=f32)


def exchange(blocks, axes):
    return lax.all_to_all(blocks, axes, 0, 0, tiled=False)


def split_three(value):
    high = value.astype(bf16)
    rest = value - high.astype(f32)
    middle = rest.astype(bf16)
    low = (rest - middle.astype(f32)).astype(bf16)
    return high, middle, low


def mm(left, right):
    return lax.dot_general(left, right, (((1,), (0,)), ((), ())), preferred_element_type=f32)


def mm_nt(left, right):
    return lax.dot_general(left, right, (((1,), (1,)), ((), ())), preferred_element_type=f32)


def mm_tn(left, right):
    return lax.dot_general(left, right, (((0,), (0,)), ((), ())), preferred_element_type=f32)


def exact_mm(ones, value):
    high, middle, low = split_three(value)
    return mm(ones, high) + mm(ones, middle) + mm(ones, low)


def halves(value):
    high = value.astype(bf16)
    return high, (value - high.astype(f32)).astype(bf16)


def widen(pieces, spread):
    return mm(pieces[0], spread) + mm(pieces[1], spread)


def sum_heads(value, gather):
    high, low = halves(value)
    return mm(high, gather) + mm(low, gather)


def sigmoid(value):
    return 0.5 * jnp.tanh(0.5 * value) + 0.5


HBM = pl.BlockSpec(memory_space=pltpu.HBM)


def call(
    kernel, outs, ins, operands, grid=None, scratch=(), micros=1, after=(), mib=VMEM_MIB, scalars=None,
    marked=False,
):
    whole = pl.BlockSpec(memory_space=pltpu.VMEM)
    lead = [] if scalars is None else [scalars]
    count = len(operands) + len(lead)
    if marked:
        outs = list(outs) + [(HBM, shaped((8192, 1280)))]
    first = count + len(after)
    last = first + len(outs) - marked

    def body(*refs):
        kernel(*refs[:count], *refs[first:last], *refs[last + marked :])

    return pl.pallas_call(
        body,
        grid_spec=pltpu.PrefetchScalarGridSpec(
            num_scalar_prefetch=len(lead),
            grid=grid or (),
            in_specs=[spec or whole for spec in ins]
            + [HBM] * len(after),
            out_specs=[spec or whole for spec, _ in outs],
            scratch_shapes=list(scratch),
        ),
        out_shape=[shape for _, shape in outs],
        compiler_params=pltpu.CompilerParams(vmem_limit_bytes=mib * 1024 * 1024),
        cost_estimate=pl.CostEstimate(
            flops=int(micros * COST), bytes_accessed=0, transcendentals=0
        ),
    )(*lead, *operands, *after)


def shaped(shape, dtype=f32):
    return jax.ShapeDtypeStruct(shape, dtype)


def by_seq(*shape):
    return pl.BlockSpec((1,) + shape, lambda a, *_: (a,) + (0,) * len(shape))


def constant(*shape):
    return pl.BlockSpec(shape, lambda a, *_: (0,) * len(shape))


def seq_first(*shape):
    return pl.BlockSpec(
        (1,) + shape, lambda a, *_: (jnp.minimum(a, 3),) + (0,) * len(shape)
    )


def own_half(*shape):
    return pl.BlockSpec(
        (1,) + shape,
        lambda a, where: (jnp.clip(a - 2 * where[1], 0, 1),) + (0,) * len(shape),
    )


def other_half(*shape):
    return pl.BlockSpec(
        (1,) + shape,
        lambda a, where: (jnp.clip(a - 2 + 2 * where[1], 0, 1),) + (0,) * len(shape),
    )


ANYWHERE = pl.BlockSpec(memory_space=pl.ANY)
SCALARS = pl.BlockSpec(memory_space=pltpu.SMEM)


def columns(index, width=LANES):
    return slice(index * width, (index + 1) * width)


def groups():
    listed = []
    for row, count in (
        (CONV_W, 7), (CONV_W + 1, 7), (CONV_W + 2, 7), (CONV_W + 3, 7), (CONV_B, 7), (GATE_GAIN, 6),
        (GAIN, 3),
    ):
        for j in range(count):
            listed.append((row, j, len(listed)))
    return listed


SPANS = {CONV_B: 448, GATE_GAIN: 384, GAIN: 192}
HEAD_LINE = 44


def message_kernel(
    where, in_weight, norm_gain, conv_weight, conv_bias, dt_bias, a_log, skip, gate_gain,
    message, tail, held, narrow, lines,
):
    core = where[1]
    narrow[...] = jnp.zeros_like(narrow)
    narrow[:, 0 : MIX - XBC] = in_weight[:, INNER + XBC :].astype(f32)
    tail[...] = narrow[...].astype(bf16)
    half = pl.ds(pl.multiple_of(core * 96, 96), 96)
    message[:, 0:XBC] = in_weight[half, INNER : INNER + XBC]
    held[...] = jnp.zeros_like(held)
    held[CONV_W : CONV_W + 4, 0:448] = conv_weight[...].astype(f32)
    for target, source in (
        (CONV_B, conv_bias), (GATE_GAIN, gate_gain), (GAIN, norm_gain), (DT_BIAS, dt_bias),
        (DECAY, a_log), (SKIP, skip),
    ):
        size = source.shape[0]
        held[target : target + 1, 0:size] = source[...].astype(f32).reshape(1, size)
    lane = lax.broadcasted_iota(jnp.int32, (1, LANES), 1)
    lines[...] = jnp.zeros_like(lines)
    for row, j, line in groups():
        tile = held[row : row + 1, columns(j // 2)]
        tile = tile if j % 2 else pltpu.roll(tile, 64, 1)
        lines[line : line + 1] = jnp.where(lane < 64, 0.0, tile)
    heads = pltpu.roll(held[DT_BIAS : DT_BIAS + 1, 0:LANES], 64, 1)
    heads = heads + pltpu.roll(held[DECAY : DECAY + 1, 0:LANES], 70, 1)
    lines[HEAD_LINE : HEAD_LINE + 1] = heads + pltpu.roll(held[SKIP : SKIP + 1, 0:LANES], 76, 1)
    message[:, XBC:] = (narrow[half] + lines[...]).astype(bf16)


def tables_kernel(where, segments, halo, same, keep, ending, passing, halo_held):
    start = where[2].astype(f32)
    below = lax.broadcasted_iota(jnp.int32, (TOKENS, TOKENS), 0) >= lax.broadcasted_iota(
        jnp.int32, (TOKENS, TOKENS), 1
    )
    for a in range(4):
        row = jnp.broadcast_to(segments[a : a + 1].astype(f32), (TOKENS, TOKENS))
        column = row.T
        first, last = column[0:1], column[TOKENS - 1 :]
        same[a] = jnp.where((column == row) & below, 1.0, 0.0)
        keep[a] = jnp.where((column == first) & (first < start), 1.0, 0.0)
        ending[a] = jnp.where(column == last, 1.0, 0.0)
        passing[a : a + 1] = jnp.where(last < start, 1.0, 0.0)
        halo_held[a] = halo[a].astype(f32)


def second_message_kernel(where, in_weight, out_weight, message, sems):
    core = where[1]
    low = pl.multiple_of(core * 192, 192)
    copies = [
        pltpu.make_async_copy(
            in_weight.at[pl.ds(pl.multiple_of(core * 96, 96), 96), pl.ds(0, INNER)],
            message.at[pl.ds(0, 96)],
            sems.at[0],
        )
    ]
    for k in range(2):
        copies.append(
            pltpu.make_async_copy(
                out_weight.at[pl.ds(low + 96 * k, 96)],
                message.at[pl.ds(96, 96), pl.ds(768 * k, 768)],
                sems.at[1 + k],
            )
        )
    for copy in copies:
        copy.start()
    for copy in copies:
        copy.wait()


def weights_kernel(
    where, normed, cotangent, in_weight, out_weight, m_1, m_2, m_3, o_1, o_2, o_3,
    gate_full, out_full, gates, g_mixed,
    gate_held, out_held, gates_held, g_held, in_sems, out_sems,
):
    place, core = where[0], where[1]
    gate_copies = weight_copies(
        place, core, in_weight.at[:, pl.ds(0, INNER)], (m_1, m_2, m_3), (o_1, o_2, o_3), gate_held,
        in_sems,
    )
    out_copies = [
        pltpu.make_async_copy(
            out_weight, out_held.at[pl.ds(pl.multiple_of(place * 384, 384), 384)], in_sems.at[7]
        )
    ]
    for k, (mine, other) in enumerate(((m_1, o_1), (m_2, o_2), (m_3, o_3))):
        owner = lax.rem(place + (1 + k), 4) * 384
        for which, part in ((core, mine), (1 - core, other)):
            for side in range(2):
                begin = pl.multiple_of(owner + which * 192 + 96 * side, 96)
                out_copies.append(
                    pltpu.make_async_copy(
                        part.at[pl.ds(96, 96), pl.ds(768 * side, 768)],
                        out_held.at[pl.ds(begin, 96)],
                        in_sems.at[7 + len(out_copies)],
                    )
                )
    for copy in gate_copies + out_copies:
        copy.start()
    outgoing = []

    def send(source, target):
        copy = pltpu.make_async_copy(source, target, out_sems.at[len(outgoing)])
        copy.start()
        outgoing.append(copy)

    for copy in gate_copies:
        copy.wait()
    send(gate_held, gate_full)
    for chunk in range(3):
        lanes, span = columns(chunk, 512), pl.ds(chunk * 512, 512)
        gates_held[:, lanes] = mm(normed[...], gate_held[:, lanes]).astype(bf16)
        send(gates_held.at[:, span], gates.at[:, span])
    for copy in out_copies:
        copy.wait()
    send(out_held, out_full)
    for chunk in range(3):
        lanes, span = columns(chunk, 512), pl.ds(chunk * 512, 512)
        g_held[:, lanes] = mm_nt(cotangent[...], out_held[lanes]).astype(bf16)
        send(g_held.at[:, span], g_mixed.at[:, span])
    for copy in outgoing:
        copy.wait()


def fetch(half):
    return [ring(half, "fsdp", steps) for steps in (3, 2, 1)]


def weight_copies(place, core, shard, mine, others, full, sems, own_width=None):
    rows = shard.shape[0]
    half = rows // 2
    copies = [
        pltpu.make_async_copy(
            shard,
            full.at[pl.ds(pl.multiple_of(place * rows, rows), rows), pl.ds(0, own_width or full.shape[1])],
            sems.at[0],
        )
    ]
    for k in range(3):
        owner = lax.rem(place + (1 + k), 4) * rows
        low = pl.multiple_of(owner + core * half, half)
        high = pl.multiple_of(owner + (1 - core) * half, half)
        for slot, part, begin in ((1 + 2 * k, mine[k], low), (2 + 2 * k, others[k], high)):
            copies.append(
                pltpu.make_async_copy(
                    part.at[pl.ds(0, half)], full.at[pl.ds(begin, half)], sems.at[slot]
                )
            )
    return copies


def front_kernel(
    where, hidden, halo, ending, passing, spread, lower, own, in_weight, tail,
    m_1, m_2, m_3, o_1, o_2, o_3,
    params, mixin, mixin_halo, active, dt_arg, dt, cumul, through, local_mine, local_send,
    normed, normed_t, halo_t, full,
    weight, packed, x_low, x_turned, mix_held, act_held, local_held,
    extended, state_b, scaled, wide_held, in_sems, out_sems,
):
    place, core = where[0], where[1]
    incoming = weight_copies(
        place, core, in_weight.at[:, pl.ds(INNER, XBC)], (m_1, m_2, m_3), (o_1, o_2, o_3), weight,
        in_sems, XBC,
    )
    incoming.append(
        pltpu.make_async_copy(
            tail,
            weight.at[pl.ds(pl.multiple_of(place * 192, 192), 192), pl.ds(XBC, LANES)],
            in_sems.at[11],
        )
    )
    rows_in = [
        pltpu.make_async_copy(part.at[:, pl.ds(XBC, LANES)], packed.at[k], in_sems.at[7 + k])
        for k, part in enumerate((own, m_1, m_2, m_3))
    ]
    for copy in rows_in + incoming:
        copy.start()
    outgoing = []

    def send(source, target):
        copy = pltpu.make_async_copy(source, target, out_sems.at[len(outgoing)])
        copy.start()
        outgoing.append(copy)

    for copy in rows_in:
        copy.wait()
    params[...] = jnp.zeros_like(params)
    lane = lax.broadcasted_iota(jnp.int32, (1, LANES), 1)
    for at in range(4):

        @pl.when(place == at)
        def _(at=at):
            for slot in range(4):
                z = (at + slot) % 4
                lines = packed[slot].astype(f32)
                turned = pltpu.roll(lines, 64, 1)
                for row, j, line in groups():
                    begin = SPANS.get(row, 448) * z + 64 * j
                    if begin % LANES:
                        params[row : row + 1, begin : begin + 64] = lines[line : line + 1, 64:LANES]
                    else:
                        params[row : row + 1, begin : begin + 64] = turned[line : line + 1, 0:64]
                heads = lines[HEAD_LINE : HEAD_LINE + 1]
                here = (lane >= 6 * z) & (lane < 6 * z + 6)
                for row, begin in ((DT_BIAS, 64), (DECAY, 70), (SKIP, 76)):
                    moved = pltpu.roll(heads, (LANES - begin + 6 * z) % LANES, 1)
                    params[row : row + 1, 0:LANES] += jnp.where(here, moved, 0.0)

    decay_rate = jnp.exp(params[DECAY : DECAY + 1, 0:LANES])
    params[DECAY : DECAY + 1, 0:LANES] = decay_rate
    params[SKIP_WIDE : SKIP_WIDE + 1, 0:INNER] = mm(
        params[SKIP : SKIP + 1, 0:LANES].astype(bf16), spread[...]
    )
    gain = params[GAIN : GAIN + 1, 0:768]

    def normalised(value):
        scale = lax.rsqrt(jnp.mean(value * value, axis=1, keepdims=True) + epsilon)
        return value * scale * gain

    edges = []
    for a in range(4):
        value = normalised(hidden[a].astype(f32))
        x_low[a * TOKENS : (a + 1) * TOKENS] = value.astype(bf16)
        x_turned[:, a * TOKENS : (a + 1) * TOKENS] = value.T.astype(bf16)
        edges.append(normalised(halo[a]))
    send(x_low, normed)
    send(x_turned, normed_t)
    edges = jnp.concatenate(edges, 0)
    edge_low = edges.astype(bf16)
    edges = jnp.concatenate([edges, jnp.zeros((LANES - 32, 768), f32)], 0)
    halo_t[...] = edges.T.astype(bf16)

    for copy in incoming:
        copy.wait()
    last = weight[:, XBC:].astype(f32)
    weight[:, XBC:] = jnp.where(lane < MIX - XBC, last, 0.0).astype(bf16)
    send(weight, full)
    argument = mm(x_low[...], weight[:, XBC:]) + params[DT_BIAS : DT_BIAS + 1, 0:LANES]
    steps = jnp.maximum(argument, 0.0) + jnp.log1p(jnp.exp(-jnp.abs(argument)))
    for a in range(4):
        rows = slice(a * TOKENS, (a + 1) * TOKENS)
        dt_arg[a] = argument[rows]
        dt[a] = steps[rows]
        total = exact_mm(lower[...], -steps[rows] * decay_rate)
        cumul[a] = total
        final = total[TOKENS - 1 :]
        through[a : a + 1] = jnp.exp(final) * passing[a : a + 1]
        scaled[rows] = (jnp.exp(final - total) * ending[a] * steps[rows]).astype(bf16)
    order = (6, 0, 1, 2, 3, 4, 5)

    def project(turn, a):
        chunk, slot = order[turn], turn % 2
        lanes = columns(chunk, 256)
        rows = slice(a * TOKENS, (a + 1) * TOKENS)
        if a == 0:
            edge = mm(edge_low, weight[:, lanes]).astype(bf16).astype(f32)
            for b in range(4):
                mixin_halo[b, :, lanes] = edge[b * EDGE : (b + 1) * EDGE]
                for side in range(2):
                    extended[slot, 2 * b + side, 0:EDGE] = edge[
                        b * EDGE : (b + 1) * EDGE, columns(side)
                    ]
        part = mm(x_low[rows], weight[:, lanes]).astype(bf16)
        mix_held[a, :, lanes] = part
        part = part.astype(f32)
        for side in range(2):
            extended[slot, 2 * a + side, EDGE:] = part[:, columns(side)]
        if chunk < 6:
            wide_held[slot, rows] = mm(scaled[rows], spread[:, lanes])

    def convolve(turn, a):
        chunk, slot = order[turn], turn % 2
        for side in range(2):
            lanes = columns(2 * chunk + side)
            at = 2 * a + side
            value = params[CONV_B : CONV_B + 1, lanes]
            for k in range(4):
                value = value + params[k : k + 1, lanes] * extended[
                    slot, at, EDGE - 3 + k : EDGE + 125 + k
                ]
            value = (value * sigmoid(value)).astype(bf16)
            act_held[a, :, lanes] = value
            if chunk == 6:
                if side == 0:
                    state_b[a] = value.astype(f32).T.astype(bf16)
            else:
                wide = wide_held[slot, a * TOKENS : (a + 1) * TOKENS, columns(side)]
                weighted = (wide * value.astype(f32)).astype(bf16)
                local_held[a, :, lanes] = mm(state_b[a], weighted).astype(bf16)

    for a in range(4):
        project(0, a)
    for turn, chunk in enumerate(order):
        span = pl.ds(chunk * 256, 256)
        send(mix_held.at[:, :, span], mixin.at[:, :, span])
        for a in range(4):
            if turn < 6:
                project(turn + 1, a)
            convolve(turn, a)
        send(act_held.at[:, :, span], active.at[:, :, span])
        if chunk < 6:
            own, given = pl.ds(2 * core, 2), pl.ds(2 - 2 * core, 2)
            send(local_held.at[given, :, span], local_send.at[:, :, span])
            send(local_held.at[own, :, span], local_mine.at[:, :, span])
    for copy in outgoing:
        copy.wait()


def pair_weights(p, scores, cumul, turned, same):
    made = []
    for h in (2 * p, 2 * p + 1):
        differ = cumul[:, h : h + 1] - turned[h : h + 1, :]
        decay = jnp.exp(jnp.where(same, differ, -1e30))
        made.append((decay, (scores * decay).astype(bf16)))
    return made


def inner_kernel(active, dt, cumul, same, spread, low_lanes, high_lanes, inner, dt_wide):
    b_low = active[0, :, INNER : INNER + STATE]
    c_low = active[0, :, INNER + STATE :]
    scores = mm_nt(c_low, b_low)
    total = cumul[0]
    turned = total.T
    allowed = same[0] > 0
    dt_wide[...] = mm(dt[0].astype(bf16), spread[...])
    for p in range(PAIRS):
        lanes = columns(p)
        (_, first), (_, second) = pair_weights(p, scores, total, turned, allowed)
        xdt = (dt_wide[:, lanes] * active[0, :, lanes].astype(f32)).astype(bf16)
        stacked = jnp.concatenate([xdt * low_lanes[...], xdt * high_lanes[...]], 0)
        inner[0, :, lanes] = mm(jnp.concatenate([first, second], 1), stacked)


def pick(where, kept, given, use):
    own = where[1] == pl.program_id(0) // 2

    @pl.when(own)
    def _():
        use(kept)

    @pl.when(jnp.logical_not(own))
    def _():
        use(given)


def pick_lanes(where, kept, given, lanes):
    own = where[1] == pl.program_id(0) // 2
    return jnp.where(own, kept[0, :, lanes].astype(f32), given[0, :, lanes].astype(f32)).astype(bf16)


def middle_kernel(
    where, inner, active, kept, given, gates, g_mixed, cumul, keep, params, spread, gather,
    mixed, g_y, g_gates, row_part, g_state,
    gated_held, recur_held, act_held, slope_held, unit_held, enter_held, entered,
):
    enter = (jnp.exp(cumul[0]) * keep[0]).astype(bf16)
    c_low = active[0, :, INNER + STATE :]
    squares = jnp.zeros((TOKENS, LANES), f32)
    products = jnp.zeros((TOKENS, LANES), f32)
    for p in range(PAIRS):
        lanes = columns(p)
        carried = mm(c_low, pick_lanes(where, kept, given, lanes))
        wide = mm(enter, spread[:, lanes])
        enter_held[:, lanes] = wide
        recur = inner[0, :, lanes] + wide * carried
        y = recur + params[SKIP_WIDE : SKIP_WIDE + 1, lanes] * active[0, :, lanes].astype(f32)
        gate = gates[0, :, lanes].astype(f32)
        unit_grad = g_mixed[0, :, lanes].astype(f32) * params[GATE_GAIN : GATE_GAIN + 1, lanes]
        sig = sigmoid(gate)
        act = gate * sig
        gated = y * act
        squares = squares + gated * gated
        products = products + unit_grad * gated
        gated_held[:, lanes] = gated
        recur_held[:, lanes] = recur
        act_held[:, lanes] = act
        slope_held[:, lanes] = y * (sig + act * (1.0 - sig))
        unit_held[:, lanes] = unit_grad
    scale = lax.rsqrt(jnp.sum(squares, 1, keepdims=True) * (1.0 / INNER) + epsilon)
    slant = scale * jnp.sum(products, 1, keepdims=True) * (1.0 / INNER)
    rows = jnp.zeros((TOKENS, LANES), f32)
    for p in range(PAIRS):
        lanes = columns(p)
        unit = gated_held[:, lanes] * scale
        mixed[0, :, lanes] = (unit * params[GATE_GAIN : GATE_GAIN + 1, lanes]).astype(bf16)
        g_gated = scale * (unit_held[:, lanes] - unit * slant)
        grad = g_gated * act_held[:, lanes]
        g_gates[0, :, lanes] = (g_gated * slope_held[:, lanes]).astype(bf16)
        low = grad.astype(bf16)
        g_y[0, :, lanes] = low
        low = low.astype(f32)
        rows = rows + sum_heads(low * recur_held[:, lanes], gather[lanes])
        entered[:, lanes] = (enter_held[:, lanes] * low).astype(bf16)
    row_part[0] = rows
    g_state[0] = mm_tn(c_low, entered[...]).astype(bf16)


def inner_back_kernel(
    where, active, g_y, kept, given, dt, cumul, keep, same, spread, gather, low_lanes, high_lanes,
    g_inner, g_b, g_c, direct, column, skip_part,
    dt_wide, enter_wide, entered, by_x, column_high, column_low,
):
    b_low = active[0, :, INNER : INNER + STATE]
    c_low = active[0, :, INNER + STATE :]
    scores = mm_nt(c_low, b_low)
    total = cumul[0]
    turned = total.T
    allowed = same[0] > 0
    dt_wide[...] = mm(dt[0].astype(bf16), spread[...])
    enter_wide[...] = mm((jnp.exp(total) * keep[0]).astype(bf16), spread[...])
    g_scores = jnp.zeros((TOKENS, TOKENS), f32)

    @pl.when(pl.program_id(0) == 0)
    def _():
        skip_part[...] = jnp.zeros_like(skip_part)

    for p in range(PAIRS):
        lanes = columns(p)
        (decay_1, first), (decay_2, second) = pair_weights(p, scores, total, turned, allowed)
        x = active[0, :, lanes].astype(f32)
        xdt = (dt_wide[:, lanes] * x).astype(bf16)
        grad = g_y[0, :, lanes]
        wide = grad.astype(f32)
        entered[:, lanes] = (enter_wide[:, lanes] * wide).astype(bf16)
        skip_part[:, lanes] += jnp.sum((wide * x).reshape(16, 8, LANES), 0)
        stacked = jnp.concatenate([grad * low_lanes[...], grad * high_lanes[...]], 0)
        g_weights = mm_nt(stacked, xdt)
        g_scores = g_scores + g_weights[:TOKENS] * decay_1 + g_weights[TOKENS:] * decay_2
        own = mm_tn(jnp.concatenate([first, second], 0), stacked)
        g_inner[0, :, lanes] = own.astype(bf16)
        by_x[:, lanes] = (x * own).astype(bf16)
        column_high[:, lanes], column_low[:, lanes] = halves(xdt.astype(f32) * own)
    direct[0] = mm(by_x[...], gather[...])
    column[0] = mm(column_high[...], gather[...]) + mm(column_low[...], gather[...])
    g_scores = g_scores.astype(bf16)
    from_scores = mm(g_scores, b_low)

    def add_state(state):
        g_c[0] = from_scores + mm_nt(entered[...], state[0])

    pick(where, kept, given, add_state)
    g_b[0] = mm_tn(g_scores, c_low)


def late_rows(
    where, g_end, kept, given, active, mixin, mixin_halo, g_y, g_inner, g_b, g_c,
    dt, dt_arg, cumul, ending, row_part, direct, column, through, params, spread, gather, upper,
    g_mix, taps, head_sums,
    weighted, state, extended, padded, inner_row, halo_held,
):
    a = pl.program_id(0)

    @pl.when(a == 0)
    def _():
        taps[...] = jnp.zeros_like(taps)
        head_sums[...] = jnp.zeros_like(head_sums)

    b_low = active[0, :, 0:STATE]
    decay_rate = params[DECAY : DECAY + 1, 0:LANES]
    total = cumul[0]
    steps = dt[0]
    to_end = jnp.exp(total[TOKENS - 1 :] - total) * ending[0]
    scaled = to_end * steps
    to_end_low = to_end.astype(bf16)
    scaled_low = scaled.astype(bf16)
    dt_low = steps.astype(bf16)
    through_state = jnp.zeros((TOKENS, LANES), f32)
    padded[:, 0:8] = jnp.zeros((2, 8, LANES), f32)
    padded[:, 136:144] = jnp.zeros((2, 8, LANES), f32)

    def convolved(chunk):
        lanes = columns(chunk)
        slot = chunk % 2
        extended[slot, 0:EDGE] = mixin_halo[0, :, lanes]
        extended[slot, EDGE:] = mixin[0, :, lanes].astype(f32)
        shifted = [extended[slot, EDGE - 3 + k : EDGE + 125 + k] for k in range(4)]
        value = params[CONV_B : CONV_B + 1, lanes]
        for k in range(4):
            value = value + params[k : k + 1, lanes] * shifted[k]
        return value, sigmoid(value), shifted

    def back(chunk, grad, value, sig, shifted):
        lanes = columns(chunk)
        slot = chunk % 2
        grad = grad * (sig + value * sig * (1.0 - sig))
        padded[slot, 8:136] = grad
        main = params[0:1, lanes] * padded[slot, 11:139]
        edge = params[0:1, lanes] * padded[slot, 3:11]
        for k in range(4):
            if k:
                tap = params[k : k + 1, lanes]
                main = main + tap * padded[slot, 11 - k : 139 - k]
                edge = edge + tap * padded[slot, 3 - k : 11 - k]
            taps[k : k + 1, lanes] += jnp.sum(grad * shifted[k], 0, keepdims=True)
        taps[4:5, lanes] += jnp.sum(grad, 0, keepdims=True)
        g_mix[0, :, lanes] = main.astype(bf16)
        halo_held[:, lanes] = edge

    for p in range(PAIRS):
        lanes = columns(p)
        end = g_end[0, :, lanes]
        begin = pick_lanes(where, kept, given, lanes)
        inner_row[0:1, lanes] = jnp.sum(begin.astype(f32) * end.astype(f32), 0, keepdims=True)
        state[:, lanes] = end
        from_state = mm(b_low, end)
        value, sig, shifted = convolved(p)
        x = (value * sig).astype(bf16).astype(f32)
        weighted[:, lanes] = (mm(scaled_low, spread[:, lanes]) * x).astype(bf16)
        grad = mm(dt_low, spread[:, lanes]) * (
            g_inner[0, :, lanes].astype(f32) + mm(to_end_low, spread[:, lanes]) * from_state
        ) + params[SKIP_WIDE : SKIP_WIDE + 1, lanes] * g_y[0, :, lanes].astype(f32)
        through_state = through_state + mm((x * from_state).astype(bf16), gather[lanes])
        back(p, grad, value, sig, shifted)
    state_part = scaled * through_state
    inner_sum = jnp.zeros((8, LANES), f32)
    for p in range(PAIRS):
        lanes = columns(p)
        inner_sum = inner_sum + sum_heads(inner_row[:, lanes], gather[lanes])
    mask = lax.broadcasted_iota(jnp.int32, (4, LANES), 0) == a
    flow = jnp.sum(jnp.where(mask, through[...], 0.0), 0, keepdims=True)
    at_end = jnp.sum(state_part, 0, keepdims=True) + flow * inner_sum[0:1]
    g_rate = exact_mm(upper[...], row_part[0] - column[0] - state_part) + at_end
    g_raw = direct[0] + to_end * through_state - decay_rate * g_rate
    g_raw = g_raw * sigmoid(dt_arg[0])
    head_sums[0:1] += jnp.sum(g_raw, 0, keepdims=True)
    head_sums[1:2] -= decay_rate * jnp.sum(steps * g_rate, 0, keepdims=True)
    g_mix[0, :, XBC:MIX_PAD] = g_raw.astype(bf16)
    g_mix[0, :, MIX_PAD:] = jnp.zeros((TOKENS, MIX_WIDE - MIX_PAD), bf16)
    back(PAIRS, g_b[0] + mm_nt(weighted[...], state[...]), *convolved(PAIRS))
    back(PAIRS + 1, g_c[0], *convolved(PAIRS + 1))


def early_grads_kernel(
    where, mixed, cotangent, normed_t, g_gates, mine, send_0, send_1, send_2, send_3,
    mixed_held, cot_held, normed_held, gates_held, mine_held, send_held, in_sems, out_sems,
):
    place, core = where[0], where[1]
    for_out = [
        pltpu.make_async_copy(mixed, mixed_held, in_sems.at[0]),
        pltpu.make_async_copy(cotangent, cot_held, in_sems.at[1]),
    ]
    for_gate = [
        pltpu.make_async_copy(normed_t, normed_held, in_sems.at[2]),
        pltpu.make_async_copy(g_gates, gates_held, in_sems.at[3]),
    ]
    to_mine = [
        pltpu.make_async_copy(
            mine_held.at[pl.ds(192 * k, 192)], mine.at[pl.ds(192 * k, 192)], out_sems.at[k]
        )
        for k in range(4)
    ]
    to_send = [
        pltpu.make_async_copy(send_held.at[pl.ds(192 * k, 192)], target, out_sems.at[4 + k])
        for k, target in enumerate((send_0, send_1, send_2, send_3))
    ]

    def gate_rows(target, copies):
        for copy in for_gate:
            copy.wait()
        for k in range(4):
            rows = pl.ds(pl.multiple_of(lax.rem(place + k, 4) * 192, 192), 192)
            target[192 * k : 192 * (k + 1)] = mm(normed_held[rows], gates_held[...]).astype(bf16)
            copies[k].start()

    def out_rows(target, copies):
        for copy in for_out:
            copy.wait()
        for k in range(4):
            lanes = pl.ds(pl.multiple_of(lax.rem(place + k, 4) * 384, 384), 384)
            grad = mm_tn(mixed_held[:, lanes], cot_held[...]).astype(bf16)
            target[192 * k : 192 * (k + 1), 0:768] = grad[0:192]
            target[192 * k : 192 * (k + 1), 768:] = grad[192:384]
            copies[k].start()

    @pl.when(core == 0)
    def _():
        for copy in for_out + for_gate:
            copy.start()
        out_rows(send_held, to_send)
        gate_rows(mine_held, to_mine)

    @pl.when(core == 1)
    def _():
        for copy in for_gate + for_out:
            copy.start()
        gate_rows(send_held, to_send)
        out_rows(mine_held, to_mine)

    for copy in to_mine + to_send:
        copy.wait()


def early_pair_kernel(mine, *rest):
    for k in range(4):
        rows = slice(192 * k, 192 * (k + 1))
        rest[4 + k][...] = (mine[rows].astype(f32) + rest[k][...].astype(f32)).astype(bf16)


def sum_blocks_kernel(a, b, c, d, total):
    for high in range(4):
        rows = slice(48 * high, 48 * (high + 1))
        value = a[rows].astype(f32) + b[rows].astype(f32) + c[rows].astype(f32) + d[rows].astype(f32)
        for low in range(4):
            total[4 * high + low] = value[:, columns(low, 384)].astype(bf16)


def late_columns(
    core, step, normed_t, halo_t, g_held, g_halo, taps, head_sums, skip_part, gather, mine, sends,
    held, sent, sems,
):
    lanes = pl.ds(pl.multiple_of(step * 512, 512), 512)
    g_mix = g_held[:, lanes]
    g_edge = jnp.concatenate([g_halo[:, lanes], jnp.zeros((LANES - 32, 512), f32)], 0).astype(bf16)
    for z in range(4):
        rows = slice(192 * z, 192 * (z + 1))
        grad = (mm(normed_t[rows], g_mix) + mm(halo_t[rows], g_edge)).astype(bf16)
        for c in range(2):
            for jj in range(4):
                held[c, jj, z] = grad[96 * c : 96 * (c + 1), columns(jj)]

    @pl.when(step == 3)
    def _():
        lane = lax.broadcasted_iota(jnp.int32, (8, LANES), 1)
        row = lax.broadcasted_iota(jnp.int32, (8, LANES), 0)
        nothing = jnp.zeros((8, LANES), f32)
        skips = sum_heads(skip_part[...], gather[...])
        head_rows = jnp.where(row == 2, jnp.sum(skips, 0, keepdims=True), head_sums[...])
        for z in range(4):
            for part in range(5):
                tile = head_rows
                if part < 4:
                    begin = 448 * z + LANES * part
                    tile = taps[:, begin // LANES * LANES : begin // LANES * LANES + LANES]
                    if begin % LANES:
                        after = min(begin // LANES + 1, XBC // LANES - 1) * LANES
                        tile = jnp.where(lane < 64, taps[:, after : after + LANES], tile)
                        tile = pltpu.roll(tile, 64, 1)
                tile = jnp.concatenate([tile, nothing], 0)
                held[0, 3, z, 16 * part : 16 * (part + 1)] = tile.astype(bf16)

    mine[...] = held[core]
    sent[pl.ds(4 * step, 4)] = held[1 - core]
    copies = [
        pltpu.make_async_copy(sent.at[pl.ds(4 * k, 4)], target, sems.at[k])
        for k, target in enumerate(sends)
    ]
    for k in range(4):

        @pl.when(step == k)
        def _(k=k):
            copies[k].start()

    @pl.when(step == 3)
    def _():
        for copy in copies:
            copy.wait()


def late_kernel(
    where, g_end, kept, given, active, mixin, mixin_halo, g_y, g_inner, g_b, g_c,
    dt, dt_arg, cumul, ending, row_part, direct, column, through, params, spread, gather, upper,
    normed_t, halo_t, skip_part,
    g_mix, g_halo, mine, send_0, send_1, send_2, send_3,
    weighted, state, extended, padded, inner_row, g_held, halo_held, taps, head_sums, held, sent,
    edge_held, sems,
):
    step = pl.program_id(0)

    @pl.when(step < 4)
    def _():
        late_rows(
            where, g_end, kept, given, active, mixin, mixin_halo, g_y, g_inner, g_b, g_c,
            dt, dt_arg, cumul, ending, row_part, direct, column, through, params, spread,
            gather, upper, g_mix, taps, head_sums,
            weighted, state, extended, padded, inner_row, edge_held,
        )
        g_held[pl.ds(pl.multiple_of(step * TOKENS, TOKENS), TOKENS)] = g_mix[0]
        rows = pl.ds(pl.multiple_of(step * EDGE, EDGE), EDGE)
        halo_held[rows, 0:XBC] = edge_held[...]
        halo_held[rows, XBC:] = jnp.zeros((EDGE, MIX_WIDE - XBC), f32)
        g_halo[0] = edge_held[...].astype(bf16)

    @pl.when(step >= 4)
    def _():
        late_columns(
            where[1], step - 4, normed_t, halo_t, g_held, halo_held, taps, head_sums, skip_part,
            gather, mine, (send_0, send_1, send_2, send_3), held, sent, sems,
        )


def both_cores(where, mine, other):
    first = where[1] == 0
    return jnp.where(first, mine, other), jnp.where(first, other, mine)


def join_kernel(where, mine, other, through, through_other, spread, total, wide):
    first = where[1] == 0
    own = jnp.where(first, through[0:2], through[2:4])
    theirs = jnp.where(first, through_other[0:2], through_other[2:4])
    through_0, through_1 = both_cores(where, own, theirs)
    everything_0, everything_1 = both_cores(where, through[...], through_other[...])
    rows = jnp.concatenate([through_0, through_1, jnp.zeros((4, LANES), f32)], 0)
    wide[...] = widen(halves(rows), spread[...])
    row = lax.broadcasted_iota(jnp.int32, (16, LANES), 0)
    piece = jnp.zeros((16, LANES), f32)
    for c, source in enumerate((everything_0, everything_1)):
        for p, value in enumerate(halves(source)):
            for a in range(4):
                piece = jnp.where(row == 4 * a + 2 * c + p, value[a : a + 1].astype(f32), piece)
    piece = piece.astype(bf16)
    for a in range(2):
        for part in range(8):
            span = slice(part * 16, (part + 1) * 16)
            state_0, state_1 = both_cores(
                where, mine[a, span].astype(f32), other[a, span].astype(f32)
            )
            value = wide[2 + a : 3 + a] * state_0 + state_1
            total[8 * a + part, :, 0:INNER] = value.astype(bf16)
            total[8 * a + part, :, INNER:] = piece


def split_kernel(where, back, mine, other, wide, kept, given):
    for a in range(2):
        for part in range(8):
            span = slice(part * 16, (part + 1) * 16)
            state_0, _ = both_cores(where, mine[a, span].astype(f32), other[a, span].astype(f32))
            in_0 = back[8 * a + part].astype(f32)
            in_1 = wide[a : a + 1] * in_0 + state_0
            keeps, gives = both_cores(where, in_0, in_1)
            kept[a, span] = keeps.astype(bf16)
            given[a, span] = gives.astype(bf16)


def scan_kernel(where, arrived, spread, before, picked, factors):
    chip = where[3] * 4 + where[4]
    forward = 2 * where[1] + chip // 8
    backward = (2 * chip + where[1]) // 8
    row = lax.broadcasted_iota(jnp.int32, (8, 16), 0)
    column = lax.broadcasted_iota(jnp.int32, (8, 16), 1)
    wanted = jnp.where(row < 2, 4 * forward + 2 * row, 4 * backward + 2 * (row - 2))
    chosen = (column >= wanted) & (column < wanted + 2) & (row < 4)
    chosen = jnp.where(chosen, 1.0, 0.0).astype(bf16)
    for i in range(16):
        picked[8 * i : 8 * (i + 1)] = mm(chosen, arrived[i, :, INNER:])
    factors[...] = widen(halves(picked[...]), spread[...])
    so_far = jnp.zeros((16, INNER), f32)
    for i in range(16):
        before[i] = so_far.astype(bf16)
        factor = factors[8 * i : 8 * i + 1] * factors[8 * i + 1 : 8 * i + 2]
        so_far = factor * so_far + arrived[i, :, :INNER].astype(f32)


def scan_back_kernel(arrived, picked, spread, after, factors):
    factors[...] = widen(halves(picked[...]), spread[...])
    so_far = jnp.zeros((16, INNER), f32)
    for i in reversed(range(32)):
        after[i] = so_far.astype(bf16)
        at = 8 * (i // 2) + 2 + i % 2
        so_far = factors[at : at + 1] * so_far + arrived[i].astype(f32)


def pair_kernel(mine, *rest):
    pair = rest[-1]
    count = rest[0].shape[0]
    for k, other in enumerate(rest[:-1]):
        rows = slice(count * k, count * (k + 1))
        pair[rows] = (mine[rows].astype(f32) + other[...].astype(f32)).astype(bf16)


def reduce_early_kernel(parts, owned):
    total = parts[0].astype(f32)
    for k in range(1, 16):
        total = total + parts[k].astype(f32)
    owned[...] = total.astype(bf16)


def reduce_kernel(early, late, owned):
    held = [early[:, columns(k)] for k in range(3)]
    total = late[0].astype(f32)
    for k in range(1, 64):
        total = total + late[k].astype(f32)
    total = total.astype(bf16)
    for copy in range(16):
        for k in range(3):
            owned[copy, 48 * k : 48 * (k + 1)] = held[k]
        owned[copy, 144:240] = total


def last_kernel(
    hidden, cotangent, mixed, g_gates, g_mix, spill, mix_weight, gate_weight, out_full, params,
    output, grad_hidden, held,
):
    x = hidden[0].astype(f32)
    output[0] = (x + mm(mixed[0], out_full[...])).astype(bf16)
    held[...] = g_mix[0, :, 0:MIX_PAD]
    end = g_mix[0, TOKENS - 16 :, 0:XBC].astype(f32)
    shift = jnp.concatenate([jnp.zeros((8, XBC), f32), spill[0].astype(f32)], 0)
    held[TOKENS - 16 :, 0:XBC] = (end + shift).astype(bf16)
    grad = mm_nt(held[...], mix_weight[...]) + mm_nt(g_gates[0], gate_weight[...])
    grad = grad * params[GAIN : GAIN + 1, 0:768]
    scale = lax.rsqrt(jnp.mean(x * x, axis=1, keepdims=True) + epsilon)
    pull = jnp.mean(grad * x, axis=1, keepdims=True)
    value = cotangent[0].astype(f32) + scale * grad - x * (scale * scale * scale * pull)
    grad_hidden[0] = value.astype(bf16)


def finish_kernel(
    where, shared, other, weight, gain, out_weight, gate_gain,
    grad, by_gain, conv_w, conv_b, grad_dt, grad_a, grad_skip, grad_out, by_gate_gain,
    sums, out_sums,
):
    up = pl.program_id(0)
    first = where[1] == 0

    def both(j, rows):
        a, b = shared[j, rows].astype(f32), other[j, rows].astype(f32)
        return jnp.where(first, a, b), jnp.where(first, b, a)

    for right in range(4):
        half, side = divmod(right, 2)
        for k in range(3):
            low, high = both(4 * up + right, slice(48 * k, 48 * (k + 1)))
            grad[:, columns(3 * right + k)] = low
            grad_out[half, :, columns(3 * side + k)] = high
    from_core = up // 2
    rows = pl.ds(pl.multiple_of(144 + 48 * lax.rem(up, 2), 16), 48)
    for j in range(15):
        begin = INNER + LANES * j
        width = min(LANES, INNER + MIX - begin)
        low, high = both(j, rows)
        grad[:, begin : begin + width] = jnp.where(from_core == 0, low, high)[:, 0:width]
    total = jnp.sum(grad[...] * weight[...].astype(f32), axis=1, keepdims=True)
    sums[pl.ds(pl.multiple_of(48 * up, 48), 48)] = jnp.broadcast_to(total, (48, LANES))
    for half in range(2):
        total = jnp.sum(grad_out[half] * out_weight[half].astype(f32), axis=1, keepdims=True)
        begin = pl.multiple_of(192 * half + 48 * up, 48)
        out_sums[pl.ds(begin, 48)] = jnp.broadcast_to(total, (48, LANES))

    @pl.when(up == 3)
    def _():
        by_gain[...] = sums[...].T[0:1].reshape(192) / gain[...]
        by_gate_gain[...] = out_sums[...].T[0:1].reshape(384) / gate_gain[...]
        rest, _ = both(15, slice(144, 240))
        for part in range(4):
            span = min(LANES, 448 - LANES * part)
            lanes = slice(LANES * part, LANES * part + span)
            conv_w[:, lanes] = rest[16 * part : 16 * part + 4, 0:span]
            conv_b[lanes] = rest[16 * part + 4 : 16 * part + 5, 0:span].reshape(span)
        for z in range(4):

            @pl.when(where[0] == z)
            def _(z=z):
                heads = pltpu.roll(rest[64:72], (LANES - 6 * z) % LANES, 1)
                for k, target in enumerate((grad_dt, grad_a, grad_skip)):
                    target[...] = heads[k : k + 1, 0:6].reshape(6)


def per_device(
    hidden,
    segments,
    norm_gain,
    in_weight,
    conv_weight,
    conv_bias,
    dt_bias,
    a_log,
    skip,
    gate_gain,
    out_weight,
    cotangent,
):
    core = lax.axis_index("seq_2")
    place = lax.axis_index("fsdp")
    chip = lax.axis_index("seq_0") * 4 + lax.axis_index("seq_1")
    where = jnp.stack(
        [
            place, core, (chip * 2 + core) * TOKENS, lax.axis_index("seq_0"),
            lax.axis_index("seq_1"),
        ]
    ).astype(jnp.int32)

    message, mix_tail = call(
        message_kernel,
        [(None, shaped((96, MIX_PAD), bf16)), (None, shaped((192, LANES), bf16))],
        [SCALARS] + [None] * 8,
        [
            where, in_weight, norm_gain, conv_weight, conv_bias, dt_bias, a_log, skip, gate_gain,
        ],
        scratch=[
            pltpu.VMEM((16, 512), f32), pltpu.VMEM((192, LANES), f32), pltpu.VMEM((96, LANES), f32)
        ],
        mib=LARGE,
    )
    mix_fetched = fetch(message)
    halo = line(hidden[:, TOKENS - EDGE :], SEQ, 1)

    head_of = np.arange(INNER) // HEADDIM
    spread = jnp.asarray((np.arange(LANES)[:, None] == head_of[None]), bf16)
    gather = jnp.asarray((head_of[:, None] == np.arange(LANES)[None]), bf16)
    lower = jnp.asarray(np.tril(np.ones((TOKENS, TOKENS))), bf16)
    upper = jnp.asarray(np.triu(np.ones((TOKENS, TOKENS))), bf16)
    low_lanes = jnp.asarray(np.ones((TOKENS, 1)) * (np.arange(LANES) < 64), bf16)
    high_lanes = jnp.asarray(np.ones((TOKENS, 1)) * (np.arange(LANES) >= 64), bf16)

    tokens = shaped((4, TOKENS, LANES))
    second, second_done = call(
        second_message_kernel,
        [(None, shaped((192, INNER), bf16))],
        [SCALARS, ANYWHERE, ANYWHERE],
        [where, in_weight, out_weight],
        scratch=[pltpu.SemaphoreType.DMA((3,))],
        marked=True,
        mib=LARGE,
    )
    same, keep, ending, passing, halo = call(
        tables_kernel,
        [
            (None, tokens), (None, tokens), (None, tokens), (None, shaped((4, LANES))),
            (None, shaped((4, EDGE, 768))),
        ],
        [SCALARS, None, None],
        [where, segments, halo],
        micros=60,
        after=[second_done],
        mib=LARGE,
    )
    half = shaped((2, STATE, INNER), bf16)
    (
        params, mixin, mixin_halo, active, dt_arg, dt, cumul, through, local_mine, local_send,
        normed, normed_t, halo_t, mix_weight,
    ) = call(
        front_kernel,
        [
            (None, shaped((16, XBC))),
            (ANYWHERE, shaped((4, TOKENS, XBC), bf16)),
            (None, shaped((4, EDGE, XBC))),
            (ANYWHERE, shaped((4, TOKENS, XBC), bf16)),
            (None, tokens),
            (None, tokens),
            (None, tokens),
            (None, shaped((4, LANES))),
            (ANYWHERE, half),
            (ANYWHERE, half),
            (ANYWHERE, shaped((512, 768), bf16)),
            (ANYWHERE, shaped((768, 512), bf16)),
            (None, shaped((768, LANES), bf16)),
            (ANYWHERE, shaped((768, MIX_PAD), bf16)),
        ],
        [SCALARS] + [None] * 6 + [ANYWHERE] * 9,
        [where, hidden, halo, ending, passing, spread, lower, message, in_weight, mix_tail]
        + mix_fetched
        + [swap(part) for part in mix_fetched],
        scratch=[
            pltpu.VMEM((768, MIX_PAD), bf16),
            pltpu.VMEM((4, 96, LANES), bf16),
            pltpu.VMEM((512, 768), bf16),
            pltpu.VMEM((768, 512), bf16),
            pltpu.VMEM((4, TOKENS, XBC), bf16),
            pltpu.VMEM((4, TOKENS, XBC), bf16),
            pltpu.VMEM((4, STATE, INNER), bf16),
            pltpu.VMEM((2, 8, EDGE + TOKENS, LANES), f32),
            pltpu.VMEM((4, STATE, TOKENS), bf16),
            pltpu.VMEM((512, LANES), bf16),
            pltpu.VMEM((2, 512, 256), f32),
            pltpu.SemaphoreType.DMA((12,)),
            pltpu.SemaphoreType.DMA((29,)),
        ],
        mib=LARGE,
        micros=10,
    )

    blocks = shaped((16, 16, INNER), bf16)
    local_other = swap(local_send)
    through_other = swap(through)
    total, wide = call(
        join_kernel,
        [(None, shaped((16, 16, INNER + LANES), bf16)), (None, shaped((8, INNER)))],
        [SCALARS] + [None] * 5,
        [where, local_mine, local_other, through, through_other, spread],
        micros=0,
    )
    fetched = fetch(second)
    inner, inner_done = call(
        inner_kernel,
        [(by_seq(TOKENS, INNER), shaped((4, TOKENS, INNER)))],
        [
            by_seq(TOKENS, XBC), by_seq(TOKENS, LANES), by_seq(TOKENS, LANES),
            by_seq(TOKENS, TOKENS), constant(LANES, INNER), constant(TOKENS, LANES),
            constant(TOKENS, LANES),
        ],
        [active, dt, cumul, same, spread, low_lanes, high_lanes],
        grid=(4,),
        scratch=[pltpu.VMEM((TOKENS, INNER), f32)],
        mib=LARGE,
        marked=True,
        micros=60,
    )
    before, picked = call(
        scan_kernel,
        [(None, blocks), (None, shaped((128, LANES)))],
        [SCALARS, None, None],
        [where, exchange(total, CHIPS), spread],
        scratch=[pltpu.VMEM((128, INNER), f32)],
        micros=0,
        after=[inner_done],
    )
    gate_weight, out_full, gates, g_mixed, projected = call(
        weights_kernel,
        [
            (ANYWHERE, shaped((768, INNER), bf16)),
            (ANYWHERE, shaped((INNER, 768), bf16)),
            (ANYWHERE, shaped((512, INNER), bf16)),
            (ANYWHERE, shaped((512, INNER), bf16)),
        ],
        [SCALARS, None, None] + [ANYWHERE] * 8,
        [where, normed, cotangent.reshape(512, 768), in_weight, out_weight]
        + fetched
        + [swap(part) for part in fetched],
        scratch=[
            pltpu.VMEM((768, INNER), bf16),
            pltpu.VMEM((INNER, 768), bf16),
            pltpu.VMEM((512, INNER), bf16),
            pltpu.VMEM((512, INNER), bf16),
            pltpu.SemaphoreType.DMA((20,)),
            pltpu.SemaphoreType.DMA((14,)),
        ],
        marked=True,
        micros=0,
        mib=LARGE,
    )
    gates = gates.reshape(4, TOKENS, INNER)
    g_mixed = g_mixed.reshape(4, TOKENS, INNER)
    kept, given = call(
        split_kernel,
        [(None, half), (None, half)],
        [SCALARS] + [None] * 4,
        [where, exchange(before, CHIPS), local_mine, local_other, wide],
        micros=0,
        after=[projected],
    )
    given = swap(given)

    mixed, g_y, g_gates, row_part, g_state = call(
        middle_kernel,
        [
            (by_seq(TOKENS, INNER), shaped((4, TOKENS, INNER), bf16)),
            (by_seq(TOKENS, INNER), shaped((4, TOKENS, INNER), bf16)),
            (by_seq(TOKENS, INNER), shaped((4, TOKENS, INNER), bf16)),
            (by_seq(TOKENS, LANES), tokens),
            (by_seq(STATE, INNER), shaped((4, STATE, INNER), bf16)),
        ],
        [
            by_seq(TOKENS, INNER), by_seq(TOKENS, XBC), own_half(STATE, INNER),
            other_half(STATE, INNER), by_seq(TOKENS, INNER), by_seq(TOKENS, INNER),
            by_seq(TOKENS, LANES), by_seq(TOKENS, LANES), constant(16, XBC),
            constant(LANES, INNER), constant(INNER, LANES),
        ],
        [inner, active, kept, given, gates, g_mixed, cumul, keep, params, spread, gather],
        scalars=where,
        grid=(4,),
        scratch=[pltpu.VMEM((TOKENS, INNER), f32)] * 6 + [pltpu.VMEM((TOKENS, INNER), bf16)],
        mib=LARGE,
        micros=11,
    )

    blocks_back = shaped((32, 16, INNER), bf16)
    arrived_back = exchange(g_state.reshape(32, 16, INNER), SEQ)

    early_shape = shaped((768, INNER), bf16)
    early_mine, *early_send, early_done = call(
        early_grads_kernel,
        [(ANYWHERE, early_shape)] + [(ANYWHERE, shaped((192, INNER), bf16))] * 4,
        [SCALARS] + [ANYWHERE] * 4,
        [
            where, mixed.reshape(512, INNER), cotangent.reshape(512, 768), normed_t,
            g_gates.reshape(512, INNER),
        ],
        scratch=[
            pltpu.VMEM((512, INNER), bf16),
            pltpu.VMEM((512, 768), bf16),
            pltpu.VMEM((768, 512), bf16),
            pltpu.VMEM((512, INNER), bf16),
            pltpu.VMEM((768, INNER), bf16),
            pltpu.VMEM((768, INNER), bf16),
            pltpu.SemaphoreType.DMA((4,)),
            pltpu.SemaphoreType.DMA((8,)),
        ],
        marked=True,
        mib=LARGE,
        micros=60,
    )
    parts = call(
        early_pair_kernel,
        [(None, shaped((192, INNER), bf16))] * 4,
        [None] * 5,
        [early_mine] + [swap(part) for part in early_send],
        micros=0,
    )
    early_parts = [parts[0]] + [ring(parts[k], "fsdp", k) for k in (1, 2, 3)]

    (after,) = call(
        scan_back_kernel,
        [(None, blocks_back)],
        [None] * 3,
        [arrived_back, picked, spread],
        scratch=[pltpu.VMEM((128, INNER), f32)],
        micros=2,
        after=[early_done],
    )

    g_inner, g_b, g_c, direct, column, skip_part, inner_back_done = call(
        inner_back_kernel,
        [
            (by_seq(TOKENS, INNER), shaped((4, TOKENS, INNER), bf16)),
            (by_seq(TOKENS, STATE), tokens),
            (by_seq(TOKENS, STATE), tokens),
            (by_seq(TOKENS, LANES), tokens),
            (by_seq(TOKENS, LANES), tokens),
            (constant(8, INNER), shaped((8, INNER))),
        ],
        [
            by_seq(TOKENS, XBC), by_seq(TOKENS, INNER), own_half(STATE, INNER),
            other_half(STATE, INNER), by_seq(TOKENS, LANES), by_seq(TOKENS, LANES),
            by_seq(TOKENS, LANES), by_seq(TOKENS, TOKENS), constant(LANES, INNER),
            constant(INNER, LANES), constant(TOKENS, LANES), constant(TOKENS, LANES),
        ],
        [
            active, g_y, kept, given, dt, cumul, keep, same, spread, gather, low_lanes, high_lanes,
        ],
        scalars=where,
        grid=(4,),
        scratch=[pltpu.VMEM((TOKENS, INNER), f32)] * 2 + [pltpu.VMEM((TOKENS, INNER), bf16)] * 4,
        mib=LARGE,
        marked=True,
        micros=60,
    )
    early_blocks, early_summed = call(
        sum_blocks_kernel,
        [(None, shaped((16, 48, 384), bf16))],
        [None] * 4,
        early_parts,
        marked=True,
        micros=0,
        after=[inner_back_done],
    )
    g_end = exchange(after, SEQ).reshape(4, STATE, INNER)
    late_spec = pl.BlockSpec((4, 4, 96, LANES), lambda s, *_: (jnp.maximum(s - 4, 0), 0, 0, 0))
    late_shape = shaped((16, 4, 96, LANES), bf16)
    piece = shaped((16 // LATE_PIECES, 4, 96, LANES), bf16)
    g_mix, g_halo, late_mine, *late_send, late_done = call(
        late_kernel,
        [
            (seq_first(TOKENS, MIX_WIDE), shaped((4, TOKENS, MIX_WIDE), bf16)),
            (seq_first(EDGE, XBC), shaped((4, EDGE, XBC), bf16)),
            (late_spec, late_shape),
        ]
        + [(ANYWHERE, piece)] * LATE_PIECES,
        [seq_first(STATE, INNER), own_half(STATE, INNER), other_half(STATE, INNER)]
        + [
            pl.BlockSpec((1, TOKENS, 256), lambda a, *_: (jnp.minimum(a, 3), 0, 6)),
            seq_first(TOKENS, XBC), seq_first(EDGE, XBC), seq_first(TOKENS, INNER),
            seq_first(TOKENS, INNER), seq_first(TOKENS, STATE), seq_first(TOKENS, STATE),
        ]
        + [seq_first(TOKENS, LANES)] * 7
        + [
            constant(4, LANES), constant(16, XBC), constant(LANES, INNER), constant(INNER, LANES),
            constant(TOKENS, TOKENS), constant(768, 512), constant(768, LANES), constant(8, INNER),
        ],
        [
            g_end, kept, given, active, mixin, mixin_halo, g_y, g_inner, g_b, g_c, dt,
            dt_arg, cumul, ending, row_part, direct, column, through, params, spread, gather, upper,
            normed_t, halo_t, skip_part,
        ],
        scalars=where,
        grid=(8,),
        scratch=[
            pltpu.VMEM((TOKENS, INNER), bf16),
            pltpu.VMEM((STATE, INNER), bf16),
            pltpu.VMEM((2, EDGE + TOKENS, LANES), f32),
            pltpu.VMEM((2, 144, LANES), f32),
            pltpu.VMEM((8, INNER), f32),
            pltpu.VMEM((512, MIX_WIDE), bf16),
            pltpu.VMEM((32, MIX_WIDE), f32),
            pltpu.VMEM((8, XBC), f32),
            pltpu.VMEM((8, LANES), f32),
            pltpu.VMEM((2, 4, 4, 96, LANES), bf16),
            pltpu.VMEM((16, 4, 96, LANES), bf16),
            pltpu.VMEM((EDGE, XBC), f32),
            pltpu.SemaphoreType.DMA((LATE_PIECES,)),
        ],
        marked=True,
        mib=LARGE,
        micros=60,
        after=[early_summed, inner_back_done],
    )
    early_owned, early_reduced = call(
        reduce_early_kernel,
        [(None, shaped((48, 384), bf16))],
        [None],
        [exchange(early_blocks, CHIPS)],
        marked=True,
        micros=0,
        after=[late_done],
    )
    spill = line(g_halo, SEQ, -1)
    (late_pair,) = call(
        pair_kernel,
        [(None, late_shape)],
        [None] * (1 + LATE_PIECES),
        [late_mine] + [swap(part) for part in late_send],
        micros=0,
        after=[spill, early_reduced],
    )
    late_parts = exchange(late_pair.reshape(64, 96, LANES), COLUMNS)

    rows = by_seq(TOKENS, 768)
    output, grad_hidden, last_done = call(
        last_kernel,
        [(rows, shaped((4, TOKENS, 768), bf16)), (rows, shaped((4, TOKENS, 768), bf16))],
        [
            rows, rows, by_seq(TOKENS, INNER), by_seq(TOKENS, INNER), by_seq(TOKENS, MIX_WIDE),
            by_seq(EDGE, XBC), constant(768, MIX_PAD), constant(768, INNER), constant(INNER, 768),
            constant(16, XBC),
        ],
        [
            hidden, cotangent, mixed, g_gates, g_mix, spill, mix_weight, gate_weight, out_full,
            params,
        ],
        grid=(4,),
        scratch=[pltpu.VMEM((TOKENS, MIX_PAD), bf16)],
        mib=LARGE,
        marked=True,
        micros=60,
    )
    (owned,) = call(
        reduce_kernel,
        [(None, shaped((16, 240, LANES), bf16))],
        [None] * 2,
        [early_owned, late_parts],
        micros=2,
        after=[last_done],
    )
    shared = exchange(owned, CHIPS)
    sum_in, by_gain, sum_conv_w, sum_conv_b, sum_dt, sum_a, sum_skip, sum_out, by_gate_gain = call(
        finish_kernel,
        [
            (pl.BlockSpec((48, INNER + MIX), lambda i, *_: (i, 0)), shaped((192, INNER + MIX))),
            (constant(192), shaped((192,))),
            (constant(4, 448), shaped((4, 448))),
            (constant(448), shaped((448,))),
            (constant(6), shaped((6,))),
            (constant(6), shaped((6,))),
            (constant(6), shaped((6,))),
            (pl.BlockSpec((2, 48, 768), lambda i, *_: (0, i, 0)), shaped((2, 192, 768))),
            (constant(384), shaped((384,))),
        ],
        [
            constant(16, 240, LANES), constant(16, 240, LANES),
            pl.BlockSpec((48, INNER + MIX), lambda i, *_: (i, 0)), constant(192),
            pl.BlockSpec((2, 48, 768), lambda i, *_: (0, i, 0)), constant(384),
        ],
        [
            shared, swap(shared), in_weight, norm_gain.astype(f32),
            out_weight.reshape(2, 192, 768), gate_gain.astype(f32),
        ],
        scalars=where,
        grid=(4,),
        scratch=[pltpu.VMEM((192, LANES), f32), pltpu.VMEM((384, LANES), f32)],
        micros=4,
    )

    return (
        output,
        grad_hidden,
        by_gain,
        sum_in,
        sum_conv_w,
        sum_conv_b,
        sum_dt,
        sum_a,
        sum_skip,
        by_gate_gain,
        sum_out.reshape(384, 768),
    )


def solution(mesh):
    finer = Mesh(
        mesh.devices.reshape(4, 4, 2, mesh.shape["fsdp"]), ("seq_0", "seq_1", "seq_2", "fsdp")
    )
    in_specs = (
        P("fsdp", SEQ, None),
        P("fsdp", SEQ),
        P("fsdp"),
        P("fsdp", None),
        P(None, "fsdp"),
        P("fsdp"),
        P("fsdp"),
        P("fsdp"),
        P("fsdp"),
        P("fsdp"),
        P("fsdp", None),
        P("fsdp", SEQ, None),
    )
    out_specs = (
        P("fsdp", SEQ, None),
        P("fsdp", SEQ, None),
        P("fsdp"),
        P("fsdp", None),
        P(None, "fsdp"),
        P("fsdp"),
        P("fsdp"),
        P("fsdp"),
        P("fsdp"),
        P("fsdp"),
        P("fsdp", None),
    )
    return jax.shard_map(
        per_device, mesh=finer, in_specs=in_specs, out_specs=out_specs, check_vma=False
    )
```

```python
import functools

import jax
import jax.numpy as jnp
import numpy as np
from jax import lax
from jax.experimental import pallas as pl
from jax.experimental.pallas import tpu as pltpu
from jax.sharding import Mesh
from jax.sharding import PartitionSpec as P

INNER = 1536
HEADS = 24
HEADDIM = 64
STATE = 128
XBC = 1792
MIX = 1816
MIX_PAD = 1920
MIX_WIDE = 2048
EDGE = 8
TOKENS = 128
LANES = 128
PAIRS = 12
SEQ = ("seq_0", "seq_1", "seq_2")
CHIPS = ("seq_0", "seq_1")
COLUMNS = ("seq_0", "seq_1", "fsdp")

epsilon = 1e-05
bf16 = jnp.bfloat16
f32 = jnp.float32
VMEM_MIB = 24
LARGE = 60
LATE_PIECES = 4
COST = 1.1e9

CONV_W, CONV_B, GATE_GAIN, GAIN, DT_BIAS, DECAY, SKIP, SKIP_WIDE = 0, 4, 5, 6, 7, 8, 9, 10


def ring(value, axis, steps):
    count = lax.axis_size(axis)
    pairs = [(source, (source + steps) % count) for source in range(count)]
    return lax.ppermute(value, axis, pairs)


def line(value, axis, steps):
    count = lax.axis_size(axis)
    initial, last = (max(0, -steps), min(count, count - steps))
    return lax.ppermute(value, axis, [(source, source + steps) for source in range(initial, last)])


def swap(value):
    return ring(value, "seq_2", 1)


def dot(pattern, left, right):
    return jnp.einsum(pattern, left, right, preferred_element_type=f32)


def exchange(blocks, axes):
    return lax.all_to_all(blocks, axes, 0, 0, tiled=False)


def split_three(value):
    high = value.astype(bf16)
    rest = value - high.astype(f32)
    middle = rest.astype(bf16)
    low = (rest - middle.astype(f32)).astype(bf16)
    return high, middle, low


def mm(left, right):
    return lax.dot_general(left, right, (((1,), (0,)), ((), ())), preferred_element_type=f32)


def mm_nt(left, right):
    return lax.dot_general(left, right, (((1,), (1,)), ((), ())), preferred_element_type=f32)


def mm_tn(left, right):
    return lax.dot_general(left, right, (((0,), (0,)), ((), ())), preferred_element_type=f32)


def exact_mm(ones, value):
    high, middle, low = split_three(value)
    return mm(ones, high) + mm(ones, middle) + mm(ones, low)


def halves(value):
    high = value.astype(bf16)
    return high, (value - high.astype(f32)).astype(bf16)


def widen(pieces, spread):
    return mm(pieces[0], spread) + mm(pieces[1], spread)


def sum_heads(value, gather):
    high, low = halves(value)
    return mm(high, gather) + mm(low, gather)


def sigmoid(value):
    return 0.5 * jnp.tanh(0.5 * value) + 0.5


HBM = pl.BlockSpec(memory_space=pltpu.HBM)


def call(
    kernel, outs, ins, operands, grid=None, scratch=(), micros=1, after=(), mib=VMEM_MIB, scalars=None,
    marked=False,
):
    whole = pl.BlockSpec(memory_space=pltpu.VMEM)
    lead = [] if scalars is None else [scalars]
    count = len(operands) + len(lead)
    if marked:
        outs = list(outs) + [(HBM, shaped((8192, 1280)))]
    first = count + len(after)
    last = first + len(outs) - marked

    def body(*refs):
        kernel(*refs[:count], *refs[first:last], *refs[last + marked :])

    return pl.pallas_call(
        body,
        grid_spec=pltpu.PrefetchScalarGridSpec(
            num_scalar_prefetch=len(lead),
            grid=grid or (),
            in_specs=[spec or whole for spec in ins]
            + [HBM] * len(after),
            out_specs=[spec or whole for spec, _ in outs],
            scratch_shapes=list(scratch),
        ),
        out_shape=[shape for _, shape in outs],
        compiler_params=pltpu.CompilerParams(vmem_limit_bytes=mib * 1024 * 1024),
        cost_estimate=pl.CostEstimate(
            flops=int(micros * COST), bytes_accessed=0, transcendentals=0
        ),
    )(*lead, *operands, *after)


def shaped(shape, dtype=f32):
    return jax.ShapeDtypeStruct(shape, dtype)


def by_seq(*shape):
    return pl.BlockSpec((1,) + shape, lambda a, *_: (a,) + (0,) * len(shape))


def constant(*shape):
    return pl.BlockSpec(shape, lambda a, *_: (0,) * len(shape))


def seq_first(*shape):
    return pl.BlockSpec(
        (1,) + shape, lambda a, *_: (jnp.minimum(a, 3),) + (0,) * len(shape)
    )


def own_half(*shape):
    return pl.BlockSpec(
        (1,) + shape,
        lambda a, where: (jnp.clip(a - 2 * where[1], 0, 1),) + (0,) * len(shape),
    )


def other_half(*shape):
    return pl.BlockSpec(
        (1,) + shape,
        lambda a, where: (jnp.clip(a - 2 + 2 * where[1], 0, 1),) + (0,) * len(shape),
    )


ANYWHERE = pl.BlockSpec(memory_space=pl.ANY)
SCALARS = pl.BlockSpec(memory_space=pltpu.SMEM)


def columns(index, width=LANES):
    return slice(index * width, (index + 1) * width)


def groups():
    listed = []
    for row, count in (
        (CONV_W, 7), (CONV_W + 1, 7), (CONV_W + 2, 7), (CONV_W + 3, 7), (CONV_B, 7), (GATE_GAIN, 6),
        (GAIN, 3),
    ):
        for j in range(count):
            listed.append((row, j, len(listed)))
    return listed


SPANS = {CONV_B: 448, GATE_GAIN: 384, GAIN: 192}
HEAD_LINE = 44


def message_kernel(
    where, in_weight, norm_gain, conv_weight, conv_bias, dt_bias, a_log, skip, gate_gain,
    message, tail, held, narrow, lines,
):
    core = where[1]
    narrow[...] = jnp.zeros_like(narrow)
    narrow[:, 0 : MIX - XBC] = in_weight[:, INNER + XBC :].astype(f32)
    tail[...] = narrow[...].astype(bf16)
    half = pl.ds(pl.multiple_of(core * 96, 96), 96)
    message[:, 0:XBC] = in_weight[half, INNER : INNER + XBC]
    held[...] = jnp.zeros_like(held)
    held[CONV_W : CONV_W + 4, 0:448] = conv_weight[...].astype(f32)
    for target, source in (
        (CONV_B, conv_bias), (GATE_GAIN, gate_gain), (GAIN, norm_gain), (DT_BIAS, dt_bias),
        (DECAY, a_log), (SKIP, skip),
    ):
        size = source.shape[0]
        held[target : target + 1, 0:size] = source[...].astype(f32).reshape(1, size)
    lane = lax.broadcasted_iota(jnp.int32, (1, LANES), 1)
    lines[...] = jnp.zeros_like(lines)
    for row, j, line in groups():
        tile = held[row : row + 1, columns(j // 2)]
        tile = tile if j % 2 else pltpu.roll(tile, 64, 1)
        lines[line : line + 1] = jnp.where(lane < 64, 0.0, tile)
    heads = pltpu.roll(held[DT_BIAS : DT_BIAS + 1, 0:LANES], 64, 1)
    heads = heads + pltpu.roll(held[DECAY : DECAY + 1, 0:LANES], 70, 1)
    lines[HEAD_LINE : HEAD_LINE + 1] = heads + pltpu.roll(held[SKIP : SKIP + 1, 0:LANES], 76, 1)
    message[:, XBC:] = (narrow[half] + lines[...]).astype(bf16)


def tables_kernel(where, segments, halo, same, keep, ending, passing, halo_held):
    start = where[2].astype(f32)
    below = lax.broadcasted_iota(jnp.int32, (TOKENS, TOKENS), 0) >= lax.broadcasted_iota(
        jnp.int32, (TOKENS, TOKENS), 1
    )
    for a in range(4):
        row = jnp.broadcast_to(segments[a : a + 1].astype(f32), (TOKENS, TOKENS))
        column = row.T
        first, last = column[0:1], column[TOKENS - 1 :]
        same[a] = jnp.where((column == row) & below, 1.0, 0.0)
        keep[a] = jnp.where((column == first) & (first < start), 1.0, 0.0)
        ending[a] = jnp.where(column == last, 1.0, 0.0)
        passing[a : a + 1] = jnp.where(last < start, 1.0, 0.0)
        halo_held[a] = halo[a].astype(f32)


def second_message_kernel(where, in_weight, out_weight, message, sems):
    core = where[1]
    low = pl.multiple_of(core * 192, 192)
    copies = [
        pltpu.make_async_copy(
            in_weight.at[pl.ds(pl.multiple_of(core * 96, 96), 96), pl.ds(0, INNER)],
            message.at[pl.ds(0, 96)],
            sems.at[0],
        )
    ]
    for k in range(2):
        copies.append(
            pltpu.make_async_copy(
                out_weight.at[pl.ds(low + 96 * k, 96)],
                message.at[pl.ds(96, 96), pl.ds(768 * k, 768)],
                sems.at[1 + k],
            )
        )
    for copy in copies:
        copy.start()
    for copy in copies:
        copy.wait()


def weights_kernel(
    where, normed, cotangent, in_weight, out_weight, m_1, m_2, m_3, o_1, o_2, o_3,
    gate_full, out_full, gates, g_mixed,
    gate_held, out_held, gates_held, g_held, in_sems, out_sems,
):
    place, core = where[0], where[1]
    gate_copies = weight_copies(
        place, core, in_weight.at[:, pl.ds(0, INNER)], (m_1, m_2, m_3), (o_1, o_2, o_3), gate_held,
        in_sems,
    )
    out_copies = [
        pltpu.make_async_copy(
            out_weight, out_held.at[pl.ds(pl.multiple_of(place * 384, 384), 384)], in_sems.at[7]
        )
    ]
    for k, (mine, other) in enumerate(((m_1, o_1), (m_2, o_2), (m_3, o_3))):
        owner = lax.rem(place + (1 + k), 4) * 384
        for which, part in ((core, mine), (1 - core, other)):
            for side in range(2):
                begin = pl.multiple_of(owner + which * 192 + 96 * side, 96)
                out_copies.append(
                    pltpu.make_async_copy(
                        part.at[pl.ds(96, 96), pl.ds(768 * side, 768)],
                        out_held.at[pl.ds(begin, 96)],
                        in_sems.at[7 + len(out_copies)],
                    )
                )
    for copy in gate_copies + out_copies:
        copy.start()
    outgoing = []

    def send(source, target):
        copy = pltpu.make_async_copy(source, target, out_sems.at[len(outgoing)])
        copy.start()
        outgoing.append(copy)

    for copy in gate_copies:
        copy.wait()
    send(gate_held, gate_full)
    for chunk in range(3):
        lanes, span = columns(chunk, 512), pl.ds(chunk * 512, 512)
        gates_held[:, lanes] = mm(normed[...], gate_held[:, lanes]).astype(bf16)
        send(gates_held.at[:, span], gates.at[:, span])
    for copy in out_copies:
        copy.wait()
    send(out_held, out_full)
    for chunk in range(3):
        lanes, span = columns(chunk, 512), pl.ds(chunk * 512, 512)
        g_held[:, lanes] = mm_nt(cotangent[...], out_held[lanes]).astype(bf16)
        send(g_held.at[:, span], g_mixed.at[:, span])
    for copy in outgoing:
        copy.wait()


def fetch(half):
    return [ring(half, "fsdp", steps) for steps in (3, 2, 1)]


def weight_copies(place, core, shard, mine, others, full, sems, own_width=None):
    rows = shard.shape[0]
    half = rows // 2
    copies = [
        pltpu.make_async_copy(
            shard,
            full.at[pl.ds(pl.multiple_of(place * rows, rows), rows), pl.ds(0, own_width or full.shape[1])],
            sems.at[0],
        )
    ]
    for k in range(3):
        owner = lax.rem(place + (1 + k), 4) * rows
        low = pl.multiple_of(owner + core * half, half)
        high = pl.multiple_of(owner + (1 - core) * half, half)
        for slot, part, begin in ((1 + 2 * k, mine[k], low), (2 + 2 * k, others[k], high)):
            copies.append(
                pltpu.make_async_copy(
                    part.at[pl.ds(0, half)], full.at[pl.ds(begin, half)], sems.at[slot]
                )
            )
    return copies


def front_kernel(
    where, hidden, halo, ending, passing, spread, lower, own, in_weight, tail,
    m_1, m_2, m_3, o_1, o_2, o_3,
    params, mixin, mixin_halo, active, dt_arg, dt, cumul, through, local_mine, local_send,
    normed, normed_t, halo_t, full,
    weight, packed, x_low, x_turned, mix_held, act_held, local_held,
    extended, state_b, scaled, wide_held, in_sems, out_sems,
):
    place, core = where[0], where[1]
    incoming = weight_copies(
        place, core, in_weight.at[:, pl.ds(INNER, XBC)], (m_1, m_2, m_3), (o_1, o_2, o_3), weight,
        in_sems, XBC,
    )
    incoming.append(
        pltpu.make_async_copy(
            tail,
            weight.at[pl.ds(pl.multiple_of(place * 192, 192), 192), pl.ds(XBC, LANES)],
            in_sems.at[11],
        )
    )
    rows_in = [
        pltpu.make_async_copy(part.at[:, pl.ds(XBC, LANES)], packed.at[k], in_sems.at[7 + k])
        for k, part in enumerate((own, m_1, m_2, m_3))
    ]
    for copy in rows_in + incoming:
        copy.start()
    outgoing = []

    def send(source, target):
        copy = pltpu.make_async_copy(source, target, out_sems.at[len(outgoing)])
        copy.start()
        outgoing.append(copy)

    for copy in rows_in:
        copy.wait()
    params[...] = jnp.zeros_like(params)
    lane = lax.broadcasted_iota(jnp.int32, (1, LANES), 1)
    for at in range(4):

        @pl.when(place == at)
        def _(at=at):
            for slot in range(4):
                z = (at + slot) % 4
                lines = packed[slot].astype(f32)
                turned = pltpu.roll(lines, 64, 1)
                for row, j, line in groups():
                    begin = SPANS.get(row, 448) * z + 64 * j
                    if begin % LANES:
                        params[row : row + 1, begin : begin + 64] = lines[line : line + 1, 64:LANES]
                    else:
                        params[row : row + 1, begin : begin + 64] = turned[line : line + 1, 0:64]
                heads = lines[HEAD_LINE : HEAD_LINE + 1]
                here = (lane >= 6 * z) & (lane < 6 * z + 6)
                for row, begin in ((DT_BIAS, 64), (DECAY, 70), (SKIP, 76)):
                    moved = pltpu.roll(heads, (LANES - begin + 6 * z) % LANES, 1)
                    params[row : row + 1, 0:LANES] += jnp.where(here, moved, 0.0)

    decay_rate = jnp.exp(params[DECAY : DECAY + 1, 0:LANES])
    params[DECAY : DECAY + 1, 0:LANES] = decay_rate
    params[SKIP_WIDE : SKIP_WIDE + 1, 0:INNER] = mm(
        params[SKIP : SKIP + 1, 0:LANES].astype(bf16), spread[...]
    )
    gain = params[GAIN : GAIN + 1, 0:768]

    def normalised(value):
        scale = lax.rsqrt(jnp.mean(value * value, axis=1, keepdims=True) + epsilon)
        return value * scale * gain

    edges = []
    for a in range(4):
        value = normalised(hidden[a].astype(f32))
        x_low[a * TOKENS : (a + 1) * TOKENS] = value.astype(bf16)
        x_turned[:, a * TOKENS : (a + 1) * TOKENS] = value.T.astype(bf16)
        edges.append(normalised(halo[a]))
    send(x_low, normed)
    send(x_turned, normed_t)
    edges = jnp.concatenate(edges, 0)
    edge_low = edges.astype(bf16)
    edges = jnp.concatenate([edges, jnp.zeros((LANES - 32, 768), f32)], 0)
    halo_t[...] = edges.T.astype(bf16)

    for copy in incoming:
        copy.wait()
    last = weight[:, XBC:].astype(f32)
    weight[:, XBC:] = jnp.where(lane < MIX - XBC, last, 0.0).astype(bf16)
    send(weight, full)
    argument = mm(x_low[...], weight[:, XBC:]) + params[DT_BIAS : DT_BIAS + 1, 0:LANES]
    steps = jnp.maximum(argument, 0.0) + jnp.log1p(jnp.exp(-jnp.abs(argument)))
    for a in range(4):
        rows = slice(a * TOKENS, (a + 1) * TOKENS)
        dt_arg[a] = argument[rows]
        dt[a] = steps[rows]
        total = exact_mm(lower[...], -steps[rows] * decay_rate)
        cumul[a] = total
        final = total[TOKENS - 1 :]
        through[a : a + 1] = jnp.exp(final) * passing[a : a + 1]
        scaled[rows] = (jnp.exp(final - total) * ending[a] * steps[rows]).astype(bf16)
    order = (6, 0, 1, 2, 3, 4, 5)

    def project(turn, a):
        chunk, slot = order[turn], turn % 2
        lanes = columns(chunk, 256)
        rows = slice(a * TOKENS, (a + 1) * TOKENS)
        if a == 0:
            edge = mm(edge_low, weight[:, lanes]).astype(bf16).astype(f32)
            for b in range(4):
                mixin_halo[b, :, lanes] = edge[b * EDGE : (b + 1) * EDGE]
                for side in range(2):
                    extended[slot, 2 * b + side, 0:EDGE] = edge[
                        b * EDGE : (b + 1) * EDGE, columns(side)
                    ]
        part = mm(x_low[rows], weight[:, lanes]).astype(bf16)
        mix_held[a, :, lanes] = part
        part = part.astype(f32)
        for side in range(2):
            extended[slot, 2 * a + side, EDGE:] = part[:, columns(side)]
        if chunk < 6:
            wide_held[slot, rows] = mm(scaled[rows], spread[:, lanes])

    def convolve(turn, a):
        chunk, slot = order[turn], turn % 2
        for side in range(2):
            lanes = columns(2 * chunk + side)
            at = 2 * a + side
            value = params[CONV_B : CONV_B + 1, lanes]
            for k in range(4):
                value = value + params[k : k + 1, lanes] * extended[
                    slot, at, EDGE - 3 + k : EDGE + 125 + k
                ]
            value = (value * sigmoid(value)).astype(bf16)
            act_held[a, :, lanes] = value
            if chunk == 6:
                if side == 0:
                    state_b[a] = value.astype(f32).T.astype(bf16)
            else:
                wide = wide_held[slot, a * TOKENS : (a + 1) * TOKENS, columns(side)]
                weighted = (wide * value.astype(f32)).astype(bf16)
                local_held[a, :, lanes] = mm(state_b[a], weighted).astype(bf16)

    for a in range(4):
        project(0, a)
    for turn, chunk in enumerate(order):
        span = pl.ds(chunk * 256, 256)
        send(mix_held.at[:, :, span], mixin.at[:, :, span])
        for a in range(4):
            if turn < 6:
                project(turn + 1, a)
            convolve(turn, a)
        send(act_held.at[:, :, span], active.at[:, :, span])
        if chunk < 6:
            own, given = pl.ds(2 * core, 2), pl.ds(2 - 2 * core, 2)
            send(local_held.at[given, :, span], local_send.at[:, :, span])
            send(local_held.at[own, :, span], local_mine.at[:, :, span])
    for copy in outgoing:
        copy.wait()


def pair_weights(p, scores, cumul, turned, same):
    made = []
    for h in (2 * p, 2 * p + 1):
        differ = cumul[:, h : h + 1] - turned[h : h + 1, :]
        decay = jnp.exp(jnp.where(same, differ, -1e30))
        made.append((decay, (scores * decay).astype(bf16)))
    return made


def inner_kernel(active, dt, cumul, same, spread, low_lanes, high_lanes, inner, dt_wide):
    b_low = active[0, :, INNER : INNER + STATE]
    c_low = active[0, :, INNER + STATE :]
    scores = mm_nt(c_low, b_low)
    total = cumul[0]
    turned = total.T
    allowed = same[0] > 0
    dt_wide[...] = mm(dt[0].astype(bf16), spread[...])
    for p in range(PAIRS):
        lanes = columns(p)
        (_, first), (_, second) = pair_weights(p, scores, total, turned, allowed)
        xdt = (dt_wide[:, lanes] * active[0, :, lanes].astype(f32)).astype(bf16)
        stacked = jnp.concatenate([xdt * low_lanes[...], xdt * high_lanes[...]], 0)
        inner[0, :, lanes] = mm(jnp.concatenate([first, second], 1), stacked)


def pick(where, kept, given, use):
    own = where[1] == pl.program_id(0) // 2

    @pl.when(own)
    def _():
        use(kept)

    @pl.when(jnp.logical_not(own))
    def _():
        use(given)


def pick_lanes(where, kept, given, lanes):
    own = where[1] == pl.program_id(0) // 2
    return jnp.where(own, kept[0, :, lanes].astype(f32), given[0, :, lanes].astype(f32)).astype(bf16)


def middle_kernel(
    where, inner, active, kept, given, gates, g_mixed, cumul, keep, params, spread, gather,
    mixed, g_y, g_gates, row_part, g_state,
    gated_held, recur_held, act_held, slope_held, unit_held, enter_held, entered,
):
    enter = (jnp.exp(cumul[0]) * keep[0]).astype(bf16)
    c_low = active[0, :, INNER + STATE :]
    squares = jnp.zeros((TOKENS, LANES), f32)
    products = jnp.zeros((TOKENS, LANES), f32)
    for p in range(PAIRS):
        lanes = columns(p)
        carried = mm(c_low, pick_lanes(where, kept, given, lanes))
        wide = mm(enter, spread[:, lanes])
        enter_held[:, lanes] = wide
        recur = inner[0, :, lanes] + wide * carried
        y = recur + params[SKIP_WIDE : SKIP_WIDE + 1, lanes] * active[0, :, lanes].astype(f32)
        gate = gates[0, :, lanes].astype(f32)
        unit_grad = g_mixed[0, :, lanes].astype(f32) * params[GATE_GAIN : GATE_GAIN + 1, lanes]
        sig = sigmoid(gate)
        act = gate * sig
        gated = y * act
        squares = squares + gated * gated
        products = products + unit_grad * gated
        gated_held[:, lanes] = gated
        recur_held[:, lanes] = recur
        act_held[:, lanes] = act
        slope_held[:, lanes] = y * (sig + act * (1.0 - sig))
        unit_held[:, lanes] = unit_grad
    scale = lax.rsqrt(jnp.sum(squares, 1, keepdims=True) * (1.0 / INNER) + epsilon)
    slant = scale * jnp.sum(products, 1, keepdims=True) * (1.0 / INNER)
    rows = jnp.zeros((TOKENS, LANES), f32)
    for p in range(PAIRS):
        lanes = columns(p)
        unit = gated_held[:, lanes] * scale
        mixed[0, :, lanes] = (unit * params[GATE_GAIN : GATE_GAIN + 1, lanes]).astype(bf16)
        g_gated = scale * (unit_held[:, lanes] - unit * slant)
        grad = g_gated * act_held[:, lanes]
        g_gates[0, :, lanes] = (g_gated * slope_held[:, lanes]).astype(bf16)
        low = grad.astype(bf16)
        g_y[0, :, lanes] = low
        low = low.astype(f32)
        rows = rows + sum_heads(low * recur_held[:, lanes], gather[lanes])
        entered[:, lanes] = (enter_held[:, lanes] * low).astype(bf16)
    row_part[0] = rows
    g_state[0] = mm_tn(c_low, entered[...]).astype(bf16)


def inner_back_kernel(
    where, active, g_y, kept, given, dt, cumul, keep, same, spread, gather, low_lanes, high_lanes,
    g_inner, g_b, g_c, direct, column, skip_part,
    dt_wide, enter_wide, entered, by_x, column_high, column_low,
):
    b_low = active[0, :, INNER : INNER + STATE]
    c_low = active[0, :, INNER + STATE :]
    scores = mm_nt(c_low, b_low)
    total = cumul[0]
    turned = total.T
    allowed = same[0] > 0
    dt_wide[...] = mm(dt[0].astype(bf16), spread[...])
    enter_wide[...] = mm((jnp.exp(total) * keep[0]).astype(bf16), spread[...])
    g_scores = jnp.zeros((TOKENS, TOKENS), f32)

    @pl.when(pl.program_id(0) == 0)
    def _():
        skip_part[...] = jnp.zeros_like(skip_part)

    for p in range(PAIRS):
        lanes = columns(p)
        (decay_1, first), (decay_2, second) = pair_weights(p, scores, total, turned, allowed)
        x = active[0, :, lanes].astype(f32)
        xdt = (dt_wide[:, lanes] * x).astype(bf16)
        grad = g_y[0, :, lanes]
        wide = grad.astype(f32)
        entered[:, lanes] = (enter_wide[:, lanes] * wide).astype(bf16)
        skip_part[:, lanes] += jnp.sum((wide * x).reshape(16, 8, LANES), 0)
        stacked = jnp.concatenate([grad * low_lanes[...], grad * high_lanes[...]], 0)
        g_weights = mm_nt(stacked, xdt)
        g_scores = g_scores + g_weights[:TOKENS] * decay_1 + g_weights[TOKENS:] * decay_2
        own = mm_tn(jnp.concatenate([first, second], 0), stacked)
        g_inner[0, :, lanes] = own.astype(bf16)
        by_x[:, lanes] = (x * own).astype(bf16)
        column_high[:, lanes], column_low[:, lanes] = halves(xdt.astype(f32) * own)
    direct[0] = mm(by_x[...], gather[...])
    column[0] = mm(column_high[...], gather[...]) + mm(column_low[...], gather[...])
    g_scores = g_scores.astype(bf16)
    from_scores = mm(g_scores, b_low)

    def add_state(state):
        g_c[0] = from_scores + mm_nt(entered[...], state[0])

    pick(where, kept, given, add_state)
    g_b[0] = mm_tn(g_scores, c_low)


def late_rows(
    where, g_end, kept, given, active, mixin, mixin_halo, g_y, g_inner, g_b, g_c,
    dt, dt_arg, cumul, ending, row_part, direct, column, through, params, spread, gather, upper,
    g_mix, taps, head_sums,
    weighted, state, extended, padded, inner_row, halo_held,
):
    a = pl.program_id(0)

    @pl.when(a == 0)
    def _():
        taps[...] = jnp.zeros_like(taps)
        head_sums[...] = jnp.zeros_like(head_sums)

    b_low = active[0, :, 0:STATE]
    decay_rate = params[DECAY : DECAY + 1, 0:LANES]
    total = cumul[0]
    steps = dt[0]
    to_end = jnp.exp(total[TOKENS - 1 :] - total) * ending[0]
    scaled = to_end * steps
    to_end_low = to_end.astype(bf16)
    scaled_low = scaled.astype(bf16)
    dt_low = steps.astype(bf16)
    through_state = jnp.zeros((TOKENS, LANES), f32)
    padded[:, 0:8] = jnp.zeros((2, 8, LANES), f32)
    padded[:, 136:144] = jnp.zeros((2, 8, LANES), f32)

    def convolved(chunk):
        lanes = columns(chunk)
        slot = chunk % 2
        extended[slot, 0:EDGE] = mixin_halo[0, :, lanes]
        extended[slot, EDGE:] = mixin[0, :, lanes].astype(f32)
        shifted = [extended[slot, EDGE - 3 + k : EDGE + 125 + k] for k in range(4)]
        value = params[CONV_B : CONV_B + 1, lanes]
        for k in range(4):
            value = value + params[k : k + 1, lanes] * shifted[k]
        return value, sigmoid(value), shifted

    def back(chunk, grad, value, sig, shifted):
        lanes = columns(chunk)
        slot = chunk % 2
        grad = grad * (sig + value * sig * (1.0 - sig))
        padded[slot, 8:136] = grad
        main = params[0:1, lanes] * padded[slot, 11:139]
        edge = params[0:1, lanes] * padded[slot, 3:11]
        for k in range(4):
            if k:
                tap = params[k : k + 1, lanes]
                main = main + tap * padded[slot, 11 - k : 139 - k]
                edge = edge + tap * padded[slot, 3 - k : 11 - k]
            taps[k : k + 1, lanes] += jnp.sum(grad * shifted[k], 0, keepdims=True)
        taps[4:5, lanes] += jnp.sum(grad, 0, keepdims=True)
        g_mix[0, :, lanes] = main.astype(bf16)
        halo_held[:, lanes] = edge

    for p in range(PAIRS):
        lanes = columns(p)
        end = g_end[0, :, lanes]
        begin = pick_lanes(where, kept, given, lanes)
        inner_row[0:1, lanes] = jnp.sum(begin.astype(f32) * end.astype(f32), 0, keepdims=True)
        state[:, lanes] = end
        from_state = mm(b_low, end)
        value, sig, shifted = convolved(p)
        x = (value * sig).astype(bf16).astype(f32)
        weighted[:, lanes] = (mm(scaled_low, spread[:, lanes]) * x).astype(bf16)
        grad = mm(dt_low, spread[:, lanes]) * (
            g_inner[0, :, lanes].astype(f32) + mm(to_end_low, spread[:, lanes]) * from_state
        ) + params[SKIP_WIDE : SKIP_WIDE + 1, lanes] * g_y[0, :, lanes].astype(f32)
        through_state = through_state + mm((x * from_state).astype(bf16), gather[lanes])
        back(p, grad, value, sig, shifted)
    state_part = scaled * through_state
    inner_sum = jnp.zeros((8, LANES), f32)
    for p in range(PAIRS):
        lanes = columns(p)
        inner_sum = inner_sum + sum_heads(inner_row[:, lanes], gather[lanes])
    mask = lax.broadcasted_iota(jnp.int32, (4, LANES), 0) == a
    flow = jnp.sum(jnp.where(mask, through[...], 0.0), 0, keepdims=True)
    at_end = jnp.sum(state_part, 0, keepdims=True) + flow * inner_sum[0:1]
    g_rate = exact_mm(upper[...], row_part[0] - column[0] - state_part) + at_end
    g_raw = direct[0] + to_end * through_state - decay_rate * g_rate
    g_raw = g_raw * sigmoid(dt_arg[0])
    head_sums[0:1] += jnp.sum(g_raw, 0, keepdims=True)
    head_sums[1:2] -= decay_rate * jnp.sum(steps * g_rate, 0, keepdims=True)
    g_mix[0, :, XBC:MIX_PAD] = g_raw.astype(bf16)
    g_mix[0, :, MIX_PAD:] = jnp.zeros((TOKENS, MIX_WIDE - MIX_PAD), bf16)
    back(PAIRS, g_b[0] + mm_nt(weighted[...], state[...]), *convolved(PAIRS))
    back(PAIRS + 1, g_c[0], *convolved(PAIRS + 1))


def early_grads_kernel(
    where, mixed, cotangent, normed_t, g_gates, mine, send_0, send_1, send_2, send_3,
    mixed_held, cot_held, normed_held, gates_held, mine_held, send_held, in_sems, out_sems,
):
    place, core = where[0], where[1]
    for_out = [
        pltpu.make_async_copy(mixed, mixed_held, in_sems.at[0]),
        pltpu.make_async_copy(cotangent, cot_held, in_sems.at[1]),
    ]
    for_gate = [
        pltpu.make_async_copy(normed_t, normed_held, in_sems.at[2]),
        pltpu.make_async_copy(g_gates, gates_held, in_sems.at[3]),
    ]
    to_mine = [
        pltpu.make_async_copy(
            mine_held.at[pl.ds(192 * k, 192)], mine.at[pl.ds(192 * k, 192)], out_sems.at[k]
        )
        for k in range(4)
    ]
    to_send = [
        pltpu.make_async_copy(send_held.at[pl.ds(192 * k, 192)], target, out_sems.at[4 + k])
        for k, target in enumerate((send_0, send_1, send_2, send_3))
    ]

    def gate_rows(target, copies):
        for copy in for_gate:
            copy.wait()
        for k in range(4):
            rows = pl.ds(pl.multiple_of(lax.rem(place + k, 4) * 192, 192), 192)
            target[192 * k : 192 * (k + 1)] = mm(normed_held[rows], gates_held[...]).astype(bf16)
            copies[k].start()

    def out_rows(target, copies):
        for copy in for_out:
            copy.wait()
        for k in range(4):
            lanes = pl.ds(pl.multiple_of(lax.rem(place + k, 4) * 384, 384), 384)
            grad = mm_tn(mixed_held[:, lanes], cot_held[...]).astype(bf16)
            target[192 * k : 192 * (k + 1), 0:768] = grad[0:192]
            target[192 * k : 192 * (k + 1), 768:] = grad[192:384]
            copies[k].start()

    @pl.when(core == 0)
    def _():
        for copy in for_out + for_gate:
            copy.start()
        out_rows(send_held, to_send)
        gate_rows(mine_held, to_mine)

    @pl.when(core == 1)
    def _():
        for copy in for_gate + for_out:
            copy.start()
        gate_rows(send_held, to_send)
        out_rows(mine_held, to_mine)

    for copy in to_mine + to_send:
        copy.wait()


def early_pair_kernel(mine, *rest):
    for k in range(4):
        rows = slice(192 * k, 192 * (k + 1))
        rest[4 + k][...] = (mine[rows].astype(f32) + rest[k][...].astype(f32)).astype(bf16)


def sum_blocks_kernel(a, b, c, d, total):
    for high in range(4):
        rows = slice(48 * high, 48 * (high + 1))
        value = a[rows].astype(f32) + b[rows].astype(f32) + c[rows].astype(f32) + d[rows].astype(f32)
        for low in range(4):
            total[4 * high + low] = value[:, columns(low, 384)].astype(bf16)


def late_columns(
    core, step, normed_t, halo_t, g_held, g_halo, taps, head_sums, skip_part, gather, mine, sends,
    held, sent, sems,
):
    lanes = pl.ds(pl.multiple_of(step * 512, 512), 512)
    g_mix = g_held[:, lanes]
    g_edge = jnp.concatenate([g_halo[:, lanes], jnp.zeros((LANES - 32, 512), f32)], 0).astype(bf16)
    for pair in range(2):
        rows = slice(384 * pair, 384 * (pair + 1))
        grad = (mm(normed_t[rows], g_mix) + mm(halo_t[rows], g_edge)).astype(bf16)
        for part in range(4):
            for jj in range(4):
                held[part % 2, jj, 2 * pair + part // 2] = grad[
                    96 * part : 96 * (part + 1), columns(jj)
                ]

    @pl.when(step == 3)
    def _():
        lane = lax.broadcasted_iota(jnp.int32, (8, LANES), 1)
        row = lax.broadcasted_iota(jnp.int32, (8, LANES), 0)
        nothing = jnp.zeros((8, LANES), f32)
        skips = sum_heads(skip_part[...], gather[...])
        head_rows = jnp.where(row == 2, jnp.sum(skips, 0, keepdims=True), head_sums[...])
        for z in range(4):
            for part in range(5):
                tile = head_rows
                if part < 4:
                    begin = 448 * z + LANES * part
                    tile = taps[:, begin // LANES * LANES : begin // LANES * LANES + LANES]
                    if begin % LANES:
                        after = min(begin // LANES + 1, XBC // LANES - 1) * LANES
                        tile = jnp.where(lane < 64, taps[:, after : after + LANES], tile)
                        tile = pltpu.roll(tile, 64, 1)
                tile = jnp.concatenate([tile, nothing], 0)
                held[0, 3, z, 16 * part : 16 * (part + 1)] = tile.astype(bf16)

    mine[...] = held[core]
    sent[pl.ds(4 * step, 4)] = held[1 - core]
    copies = [
        pltpu.make_async_copy(sent.at[pl.ds(4 * k, 4)], target, sems.at[k])
        for k, target in enumerate(sends)
    ]
    for k in range(4):

        @pl.when(step == k)
        def _(k=k):
            copies[k].start()

    @pl.when(step == 3)
    def _():
        for copy in copies:
            copy.wait()


def late_kernel(
    where, g_end, kept, given, active, mixin, mixin_halo, g_y, g_inner, g_b, g_c,
    dt, dt_arg, cumul, ending, row_part, direct, column, through, params, spread, gather, upper,
    normed_t, halo_t, skip_part,
    g_mix, g_halo, mine, send_0, send_1, send_2, send_3,
    weighted, state, extended, padded, inner_row, g_held, halo_held, taps, head_sums, held, sent,
    edge_held, sems,
):
    step = pl.program_id(0)

    @pl.when(step < 4)
    def _():
        late_rows(
            where, g_end, kept, given, active, mixin, mixin_halo, g_y, g_inner, g_b, g_c,
            dt, dt_arg, cumul, ending, row_part, direct, column, through, params, spread,
            gather, upper, g_mix, taps, head_sums,
            weighted, state, extended, padded, inner_row, edge_held,
        )
        g_held[pl.ds(pl.multiple_of(step * TOKENS, TOKENS), TOKENS)] = g_mix[0]
        rows = pl.ds(pl.multiple_of(step * EDGE, EDGE), EDGE)
        halo_held[rows, 0:XBC] = edge_held[...]
        halo_held[rows, XBC:] = jnp.zeros((EDGE, MIX_WIDE - XBC), f32)
        g_halo[0] = edge_held[...].astype(bf16)

    @pl.when(step >= 4)
    def _():
        late_columns(
            where[1], step - 4, normed_t, halo_t, g_held, halo_held, taps, head_sums, skip_part,
            gather, mine, (send_0, send_1, send_2, send_3), held, sent, sems,
        )


def both_cores(where, mine, other):
    first = where[1] == 0
    return jnp.where(first, mine, other), jnp.where(first, other, mine)


def join_kernel(where, mine, other, through, through_other, spread, total, wide):
    first = where[1] == 0
    own = jnp.where(first, through[0:2], through[2:4])
    theirs = jnp.where(first, through_other[0:2], through_other[2:4])
    through_0, through_1 = both_cores(where, own, theirs)
    everything_0, everything_1 = both_cores(where, through[...], through_other[...])
    rows = jnp.concatenate([through_0, through_1, jnp.zeros((4, LANES), f32)], 0)
    wide[...] = widen(halves(rows), spread[...])
    row = lax.broadcasted_iota(jnp.int32, (16, LANES), 0)
    piece = jnp.zeros((16, LANES), f32)
    for c, source in enumerate((everything_0, everything_1)):
        for p, value in enumerate(halves(source)):
            for a in range(4):
                piece = jnp.where(row == 4 * a + 2 * c + p, value[a : a + 1].astype(f32), piece)
    piece = piece.astype(bf16)
    for a in range(2):
        for part in range(8):
            span = slice(part * 16, (part + 1) * 16)
            state_0, state_1 = both_cores(
                where, mine[a, span].astype(f32), other[a, span].astype(f32)
            )
            value = wide[2 + a : 3 + a] * state_0 + state_1
            total[8 * a + part, :, 0:INNER] = value.astype(bf16)
            total[8 * a + part, :, INNER:] = piece


def split_kernel(where, back, mine, other, wide, kept, given):
    for a in range(2):
        for part in range(8):
            span = slice(part * 16, (part + 1) * 16)
            state_0, _ = both_cores(where, mine[a, span].astype(f32), other[a, span].astype(f32))
            in_0 = back[8 * a + part].astype(f32)
            in_1 = wide[a : a + 1] * in_0 + state_0
            keeps, gives = both_cores(where, in_0, in_1)
            kept[a, span] = keeps.astype(bf16)
            given[a, span] = gives.astype(bf16)


def scan_kernel(where, arrived, spread, before, picked, factors):
    chip = where[3] * 4 + where[4]
    forward = 2 * where[1] + chip // 8
    backward = (2 * chip + where[1]) // 8
    row = lax.broadcasted_iota(jnp.int32, (8, 16), 0)
    column = lax.broadcasted_iota(jnp.int32, (8, 16), 1)
    wanted = jnp.where(row < 2, 4 * forward + 2 * row, 4 * backward + 2 * (row - 2))
    chosen = (column >= wanted) & (column < wanted + 2) & (row < 4)
    chosen = jnp.where(chosen, 1.0, 0.0).astype(bf16)
    for i in range(16):
        picked[8 * i : 8 * (i + 1)] = mm(chosen, arrived[i, :, INNER:])
    factors[...] = widen(halves(picked[...]), spread[...])
    so_far = jnp.zeros((16, INNER), f32)
    for i in range(16):
        before[i] = so_far.astype(bf16)
        factor = factors[8 * i : 8 * i + 1] * factors[8 * i + 1 : 8 * i + 2]
        so_far = factor * so_far + arrived[i, :, :INNER].astype(f32)


def scan_back_kernel(arrived, picked, spread, after, factors):
    factors[...] = widen(halves(picked[...]), spread[...])
    so_far = jnp.zeros((16, INNER), f32)
    for i in reversed(range(32)):
        after[i] = so_far.astype(bf16)
        at = 8 * (i // 2) + 2 + i % 2
        so_far = factors[at : at + 1] * so_far + arrived[i].astype(f32)


def pair_kernel(mine, *rest):
    pair = rest[-1]
    count = rest[0].shape[0]
    for k, other in enumerate(rest[:-1]):
        rows = slice(count * k, count * (k + 1))
        pair[rows] = (mine[rows].astype(f32) + other[...].astype(f32)).astype(bf16)


def reduce_early_kernel(parts, owned):
    total = parts[0].astype(f32)
    for k in range(1, 16):
        total = total + parts[k].astype(f32)
    owned[...] = total.astype(bf16)


def reduce_kernel(early, late, owned):
    held = [early[:, columns(k)] for k in range(3)]
    total = late[0].astype(f32)
    for k in range(1, 64):
        total = total + late[k].astype(f32)
    total = total.astype(bf16)
    for copy in range(16):
        for k in range(3):
            owned[copy, 48 * k : 48 * (k + 1)] = held[k]
        owned[copy, 144:240] = total


def last_kernel(
    hidden, cotangent, mixed, g_gates, g_mix, spill, mix_weight, gate_weight, out_full, params,
    output, grad_hidden, held,
):
    x = hidden[0].astype(f32)
    output[0] = (x + mm(mixed[0], out_full[...])).astype(bf16)
    held[...] = g_mix[0, :, 0:MIX_PAD]
    end = g_mix[0, TOKENS - 16 :, 0:XBC].astype(f32)
    shift = jnp.concatenate([jnp.zeros((8, XBC), f32), spill[0].astype(f32)], 0)
    held[TOKENS - 16 :, 0:XBC] = (end + shift).astype(bf16)
    grad = mm_nt(held[...], mix_weight[...]) + mm_nt(g_gates[0], gate_weight[...])
    grad = grad * params[GAIN : GAIN + 1, 0:768]
    scale = lax.rsqrt(jnp.mean(x * x, axis=1, keepdims=True) + epsilon)
    pull = jnp.mean(grad * x, axis=1, keepdims=True)
    value = cotangent[0].astype(f32) + scale * grad - x * (scale * scale * scale * pull)
    grad_hidden[0] = value.astype(bf16)


def finish_kernel(
    where, shared, other, weight, gain, out_weight, gate_gain,
    grad, by_gain, conv_w, conv_b, grad_dt, grad_a, grad_skip, grad_out, by_gate_gain,
    sums, out_sums,
):
    up = pl.program_id(0)
    first = where[1] == 0

    def both(j, rows):
        a, b = shared[j, rows].astype(f32), other[j, rows].astype(f32)
        return jnp.where(first, a, b), jnp.where(first, b, a)

    for right in range(4):
        half, side = divmod(right, 2)
        for k in range(3):
            low, high = both(4 * up + right, slice(48 * k, 48 * (k + 1)))
            grad[:, columns(3 * right + k)] = low
            grad_out[half, :, columns(3 * side + k)] = high
    from_core = up // 2
    rows = pl.ds(pl.multiple_of(144 + 48 * lax.rem(up, 2), 16), 48)
    for j in range(15):
        begin = INNER + LANES * j
        width = min(LANES, INNER + MIX - begin)
        low, high = both(j, rows)
        grad[:, begin : begin + width] = jnp.where(from_core == 0, low, high)[:, 0:width]
    total = jnp.sum(grad[...] * weight[...].astype(f32), axis=1, keepdims=True)
    sums[pl.ds(pl.multiple_of(48 * up, 48), 48)] = jnp.broadcast_to(total, (48, LANES))
    for half in range(2):
        total = jnp.sum(grad_out[half] * out_weight[half].astype(f32), axis=1, keepdims=True)
        begin = pl.multiple_of(192 * half + 48 * up, 48)
        out_sums[pl.ds(begin, 48)] = jnp.broadcast_to(total, (48, LANES))

    @pl.when(up == 3)
    def _():
        by_gain[...] = sums[...].T[0:1].reshape(192) / gain[...]
        by_gate_gain[...] = out_sums[...].T[0:1].reshape(384) / gate_gain[...]
        rest, _ = both(15, slice(144, 240))
        for part in range(4):
            span = min(LANES, 448 - LANES * part)
            lanes = slice(LANES * part, LANES * part + span)
            conv_w[:, lanes] = rest[16 * part : 16 * part + 4, 0:span]
            conv_b[lanes] = rest[16 * part + 4 : 16 * part + 5, 0:span].reshape(span)
        for z in range(4):

            @pl.when(where[0] == z)
            def _(z=z):
                heads = pltpu.roll(rest[64:72], (LANES - 6 * z) % LANES, 1)
                for k, target in enumerate((grad_dt, grad_a, grad_skip)):
                    target[...] = heads[k : k + 1, 0:6].reshape(6)


def per_device(
    hidden,
    segments,
    norm_gain,
    in_weight,
    conv_weight,
    conv_bias,
    dt_bias,
    a_log,
    skip,
    gate_gain,
    out_weight,
    cotangent,
):
    core = lax.axis_index("seq_2")
    place = lax.axis_index("fsdp")
    chip = lax.axis_index("seq_0") * 4 + lax.axis_index("seq_1")
    where = jnp.stack(
        [
            place, core, (chip * 2 + core) * TOKENS, lax.axis_index("seq_0"),
            lax.axis_index("seq_1"),
        ]
    ).astype(jnp.int32)

    message, mix_tail = call(
        message_kernel,
        [(None, shaped((96, MIX_PAD), bf16)), (None, shaped((192, LANES), bf16))],
        [SCALARS] + [None] * 8,
        [
            where, in_weight, norm_gain, conv_weight, conv_bias, dt_bias, a_log, skip, gate_gain,
        ],
        scratch=[
            pltpu.VMEM((16, 512), f32), pltpu.VMEM((192, LANES), f32), pltpu.VMEM((96, LANES), f32)
        ],
        mib=LARGE,
    )
    mix_fetched = fetch(message)
    halo = line(hidden[:, TOKENS - EDGE :], SEQ, 1)

    head_of = np.arange(INNER) // HEADDIM
    spread = jnp.asarray((np.arange(LANES)[:, None] == head_of[None]), bf16)
    gather = jnp.asarray((head_of[:, None] == np.arange(LANES)[None]), bf16)
    lower = jnp.asarray(np.tril(np.ones((TOKENS, TOKENS))), bf16)
    upper = jnp.asarray(np.triu(np.ones((TOKENS, TOKENS))), bf16)
    low_lanes = jnp.asarray(np.ones((TOKENS, 1)) * (np.arange(LANES) < 64), bf16)
    high_lanes = jnp.asarray(np.ones((TOKENS, 1)) * (np.arange(LANES) >= 64), bf16)

    tokens = shaped((4, TOKENS, LANES))
    second, second_done = call(
        second_message_kernel,
        [(None, shaped((192, INNER), bf16))],
        [SCALARS, ANYWHERE, ANYWHERE],
        [where, in_weight, out_weight],
        scratch=[pltpu.SemaphoreType.DMA((3,))],
        marked=True,
        mib=LARGE,
    )
    same, keep, ending, passing, halo = call(
        tables_kernel,
        [
            (None, tokens), (None, tokens), (None, tokens), (None, shaped((4, LANES))),
            (None, shaped((4, EDGE, 768))),
        ],
        [SCALARS, None, None],
        [where, segments, halo],
        micros=60,
        after=[second_done],
        mib=LARGE,
    )
    half = shaped((2, STATE, INNER), bf16)
    (
        params, mixin, mixin_halo, active, dt_arg, dt, cumul, through, local_mine, local_send,
        normed, normed_t, halo_t, mix_weight,
    ) = call(
        front_kernel,
        [
            (None, shaped((16, XBC))),
            (ANYWHERE, shaped((4, TOKENS, XBC), bf16)),
            (None, shaped((4, EDGE, XBC))),
            (ANYWHERE, shaped((4, TOKENS, XBC), bf16)),
            (None, tokens),
            (None, tokens),
            (None, tokens),
            (None, shaped((4, LANES))),
            (ANYWHERE, half),
            (ANYWHERE, half),
            (ANYWHERE, shaped((512, 768), bf16)),
            (ANYWHERE, shaped((768, 512), bf16)),
            (None, shaped((768, LANES), bf16)),
            (ANYWHERE, shaped((768, MIX_PAD), bf16)),
        ],
        [SCALARS] + [None] * 6 + [ANYWHERE] * 9,
        [where, hidden, halo, ending, passing, spread, lower, message, in_weight, mix_tail]
        + mix_fetched
        + [swap(part) for part in mix_fetched],
        scratch=[
            pltpu.VMEM((768, MIX_PAD), bf16),
            pltpu.VMEM((4, 96, LANES), bf16),
            pltpu.VMEM((512, 768), bf16),
            pltpu.VMEM((768, 512), bf16),
            pltpu.VMEM((4, TOKENS, XBC), bf16),
            pltpu.VMEM((4, TOKENS, XBC), bf16),
            pltpu.VMEM((4, STATE, INNER), bf16),
            pltpu.VMEM((2, 8, EDGE + TOKENS, LANES), f32),
            pltpu.VMEM((4, STATE, TOKENS), bf16),
            pltpu.VMEM((512, LANES), bf16),
            pltpu.VMEM((2, 512, 256), f32),
            pltpu.SemaphoreType.DMA((12,)),
            pltpu.SemaphoreType.DMA((29,)),
        ],
        mib=LARGE,
        micros=10,
    )

    blocks = shaped((16, 16, INNER), bf16)
    local_other = swap(local_send)
    through_other = swap(through)
    total, wide = call(
        join_kernel,
        [(None, shaped((16, 16, INNER + LANES), bf16)), (None, shaped((8, INNER)))],
        [SCALARS] + [None] * 5,
        [where, local_mine, local_other, through, through_other, spread],
        micros=0,
    )
    fetched = fetch(second)
    inner, inner_done = call(
        inner_kernel,
        [(by_seq(TOKENS, INNER), shaped((4, TOKENS, INNER)))],
        [
            by_seq(TOKENS, XBC), by_seq(TOKENS, LANES), by_seq(TOKENS, LANES),
            by_seq(TOKENS, TOKENS), constant(LANES, INNER), constant(TOKENS, LANES),
            constant(TOKENS, LANES),
        ],
        [active, dt, cumul, same, spread, low_lanes, high_lanes],
        grid=(4,),
        scratch=[pltpu.VMEM((TOKENS, INNER), f32)],
        mib=LARGE,
        marked=True,
        micros=60,
    )
    before, picked = call(
        scan_kernel,
        [(None, blocks), (None, shaped((128, LANES)))],
        [SCALARS, None, None],
        [where, exchange(total, CHIPS), spread],
        scratch=[pltpu.VMEM((128, INNER), f32)],
        micros=0,
        after=[inner_done],
    )
    gate_weight, out_full, gates, g_mixed, projected = call(
        weights_kernel,
        [
            (ANYWHERE, shaped((768, INNER), bf16)),
            (ANYWHERE, shaped((INNER, 768), bf16)),
            (ANYWHERE, shaped((512, INNER), bf16)),
            (ANYWHERE, shaped((512, INNER), bf16)),
        ],
        [SCALARS, None, None] + [ANYWHERE] * 8,
        [where, normed, cotangent.reshape(512, 768), in_weight, out_weight]
        + fetched
        + [swap(part) for part in fetched],
        scratch=[
            pltpu.VMEM((768, INNER), bf16),
            pltpu.VMEM((INNER, 768), bf16),
            pltpu.VMEM((512, INNER), bf16),
            pltpu.VMEM((512, INNER), bf16),
            pltpu.SemaphoreType.DMA((20,)),
            pltpu.SemaphoreType.DMA((14,)),
        ],
        marked=True,
        micros=0,
        mib=LARGE,
    )
    gates = gates.reshape(4, TOKENS, INNER)
    g_mixed = g_mixed.reshape(4, TOKENS, INNER)
    kept, given = call(
        split_kernel,
        [(None, half), (None, half)],
        [SCALARS] + [None] * 4,
        [where, exchange(before, CHIPS), local_mine, local_other, wide],
        micros=0,
        after=[projected],
    )
    given = swap(given)

    mixed, g_y, g_gates, row_part, g_state = call(
        middle_kernel,
        [
            (by_seq(TOKENS, INNER), shaped((4, TOKENS, INNER), bf16)),
            (by_seq(TOKENS, INNER), shaped((4, TOKENS, INNER), bf16)),
            (by_seq(TOKENS, INNER), shaped((4, TOKENS, INNER), bf16)),
            (by_seq(TOKENS, LANES), tokens),
            (by_seq(STATE, INNER), shaped((4, STATE, INNER), bf16)),
        ],
        [
            by_seq(TOKENS, INNER), by_seq(TOKENS, XBC), own_half(STATE, INNER),
            other_half(STATE, INNER), by_seq(TOKENS, INNER), by_seq(TOKENS, INNER),
            by_seq(TOKENS, LANES), by_seq(TOKENS, LANES), constant(16, XBC),
            constant(LANES, INNER), constant(INNER, LANES),
        ],
        [inner, active, kept, given, gates, g_mixed, cumul, keep, params, spread, gather],
        scalars=where,
        grid=(4,),
        scratch=[pltpu.VMEM((TOKENS, INNER), f32)] * 6 + [pltpu.VMEM((TOKENS, INNER), bf16)],
        mib=LARGE,
        micros=11,
    )

    blocks_back = shaped((32, 16, INNER), bf16)
    arrived_back = exchange(g_state.reshape(32, 16, INNER), SEQ)

    early_shape = shaped((768, INNER), bf16)
    early_mine, *early_send, early_done = call(
        early_grads_kernel,
        [(ANYWHERE, early_shape)] + [(ANYWHERE, shaped((192, INNER), bf16))] * 4,
        [SCALARS] + [ANYWHERE] * 4,
        [
            where, mixed.reshape(512, INNER), cotangent.reshape(512, 768), normed_t,
            g_gates.reshape(512, INNER),
        ],
        scratch=[
            pltpu.VMEM((512, INNER), bf16),
            pltpu.VMEM((512, 768), bf16),
            pltpu.VMEM((768, 512), bf16),
            pltpu.VMEM((512, INNER), bf16),
            pltpu.VMEM((768, INNER), bf16),
            pltpu.VMEM((768, INNER), bf16),
            pltpu.SemaphoreType.DMA((4,)),
            pltpu.SemaphoreType.DMA((8,)),
        ],
        marked=True,
        mib=LARGE,
        micros=60,
    )
    parts = call(
        early_pair_kernel,
        [(None, shaped((192, INNER), bf16))] * 4,
        [None] * 5,
        [early_mine] + [swap(part) for part in early_send],
        micros=0,
    )
    early_parts = [parts[0]] + [ring(parts[k], "fsdp", k) for k in (1, 2, 3)]

    (after,) = call(
        scan_back_kernel,
        [(None, blocks_back)],
        [None] * 3,
        [arrived_back, picked, spread],
        scratch=[pltpu.VMEM((128, INNER), f32)],
        micros=2,
        after=[early_done],
    )

    g_inner, g_b, g_c, direct, column, skip_part, inner_back_done = call(
        inner_back_kernel,
        [
            (by_seq(TOKENS, INNER), shaped((4, TOKENS, INNER), bf16)),
            (by_seq(TOKENS, STATE), tokens),
            (by_seq(TOKENS, STATE), tokens),
            (by_seq(TOKENS, LANES), tokens),
            (by_seq(TOKENS, LANES), tokens),
            (constant(8, INNER), shaped((8, INNER))),
        ],
        [
            by_seq(TOKENS, XBC), by_seq(TOKENS, INNER), own_half(STATE, INNER),
            other_half(STATE, INNER), by_seq(TOKENS, LANES), by_seq(TOKENS, LANES),
            by_seq(TOKENS, LANES), by_seq(TOKENS, TOKENS), constant(LANES, INNER),
            constant(INNER, LANES), constant(TOKENS, LANES), constant(TOKENS, LANES),
        ],
        [
            active, g_y, kept, given, dt, cumul, keep, same, spread, gather, low_lanes, high_lanes,
        ],
        scalars=where,
        grid=(4,),
        scratch=[pltpu.VMEM((TOKENS, INNER), f32)] * 2 + [pltpu.VMEM((TOKENS, INNER), bf16)] * 4,
        mib=LARGE,
        marked=True,
        micros=60,
    )
    early_blocks, early_summed = call(
        sum_blocks_kernel,
        [(None, shaped((16, 48, 384), bf16))],
        [None] * 4,
        early_parts,
        marked=True,
        micros=0,
        after=[inner_back_done],
    )
    g_end = exchange(after, SEQ).reshape(4, STATE, INNER)
    late_spec = pl.BlockSpec((4, 4, 96, LANES), lambda s, *_: (jnp.maximum(s - 4, 0), 0, 0, 0))
    late_shape = shaped((16, 4, 96, LANES), bf16)
    piece = shaped((16 // LATE_PIECES, 4, 96, LANES), bf16)
    g_mix, g_halo, late_mine, *late_send, late_done = call(
        late_kernel,
        [
            (seq_first(TOKENS, MIX_WIDE), shaped((4, TOKENS, MIX_WIDE), bf16)),
            (seq_first(EDGE, XBC), shaped((4, EDGE, XBC), bf16)),
            (late_spec, late_shape),
        ]
        + [(ANYWHERE, piece)] * LATE_PIECES,
        [seq_first(STATE, INNER), own_half(STATE, INNER), other_half(STATE, INNER)]
        + [
            pl.BlockSpec((1, TOKENS, 256), lambda a, *_: (jnp.minimum(a, 3), 0, 6)),
            seq_first(TOKENS, XBC), seq_first(EDGE, XBC), seq_first(TOKENS, INNER),
            seq_first(TOKENS, INNER), seq_first(TOKENS, STATE), seq_first(TOKENS, STATE),
        ]
        + [seq_first(TOKENS, LANES)] * 7
        + [
            constant(4, LANES), constant(16, XBC), constant(LANES, INNER), constant(INNER, LANES),
            constant(TOKENS, TOKENS), constant(768, 512), constant(768, LANES), constant(8, INNER),
        ],
        [
            g_end, kept, given, active, mixin, mixin_halo, g_y, g_inner, g_b, g_c, dt,
            dt_arg, cumul, ending, row_part, direct, column, through, params, spread, gather, upper,
            normed_t, halo_t, skip_part,
        ],
        scalars=where,
        grid=(8,),
        scratch=[
            pltpu.VMEM((TOKENS, INNER), bf16),
            pltpu.VMEM((STATE, INNER), bf16),
            pltpu.VMEM((2, EDGE + TOKENS, LANES), f32),
            pltpu.VMEM((2, 144, LANES), f32),
            pltpu.VMEM((8, INNER), f32),
            pltpu.VMEM((512, MIX_WIDE), bf16),
            pltpu.VMEM((32, MIX_WIDE), f32),
            pltpu.VMEM((8, XBC), f32),
            pltpu.VMEM((8, LANES), f32),
            pltpu.VMEM((2, 4, 4, 96, LANES), bf16),
            pltpu.VMEM((16, 4, 96, LANES), bf16),
            pltpu.VMEM((EDGE, XBC), f32),
            pltpu.SemaphoreType.DMA((LATE_PIECES,)),
        ],
        marked=True,
        mib=LARGE,
        micros=60,
        after=[early_summed, inner_back_done],
    )
    early_owned, early_reduced = call(
        reduce_early_kernel,
        [(None, shaped((48, 384), bf16))],
        [None],
        [exchange(early_blocks, CHIPS)],
        marked=True,
        micros=0,
        after=[late_done],
    )
    spill = line(g_halo, SEQ, -1)
    (late_pair,) = call(
        pair_kernel,
        [(None, late_shape)],
        [None] * (1 + LATE_PIECES),
        [late_mine] + [swap(part) for part in late_send],
        micros=0,
        after=[spill, early_reduced],
    )
    late_parts = exchange(late_pair.reshape(64, 96, LANES), COLUMNS)

    rows = by_seq(TOKENS, 768)
    output, grad_hidden, last_done = call(
        last_kernel,
        [(rows, shaped((4, TOKENS, 768), bf16)), (rows, shaped((4, TOKENS, 768), bf16))],
        [
            rows, rows, by_seq(TOKENS, INNER), by_seq(TOKENS, INNER), by_seq(TOKENS, MIX_WIDE),
            by_seq(EDGE, XBC), constant(768, MIX_PAD), constant(768, INNER), constant(INNER, 768),
            constant(16, XBC),
        ],
        [
            hidden, cotangent, mixed, g_gates, g_mix, spill, mix_weight, gate_weight, out_full,
            params,
        ],
        grid=(4,),
        scratch=[pltpu.VMEM((TOKENS, MIX_PAD), bf16)],
        mib=LARGE,
        marked=True,
        micros=60,
    )
    (owned,) = call(
        reduce_kernel,
        [(None, shaped((16, 240, LANES), bf16))],
        [None] * 2,
        [early_owned, late_parts],
        micros=2,
        after=[last_done],
    )
    shared = exchange(owned, CHIPS)
    sum_in, by_gain, sum_conv_w, sum_conv_b, sum_dt, sum_a, sum_skip, sum_out, by_gate_gain = call(
        finish_kernel,
        [
            (pl.BlockSpec((48, INNER + MIX), lambda i, *_: (i, 0)), shaped((192, INNER + MIX))),
            (constant(192), shaped((192,))),
            (constant(4, 448), shaped((4, 448))),
            (constant(448), shaped((448,))),
            (constant(6), shaped((6,))),
            (constant(6), shaped((6,))),
            (constant(6), shaped((6,))),
            (pl.BlockSpec((2, 48, 768), lambda i, *_: (0, i, 0)), shaped((2, 192, 768))),
            (constant(384), shaped((384,))),
        ],
        [
            constant(16, 240, LANES), constant(16, 240, LANES),
            pl.BlockSpec((48, INNER + MIX), lambda i, *_: (i, 0)), constant(192),
            pl.BlockSpec((2, 48, 768), lambda i, *_: (0, i, 0)), constant(384),
        ],
        [
            shared, swap(shared), in_weight, norm_gain.astype(f32),
            out_weight.reshape(2, 192, 768), gate_gain.astype(f32),
        ],
        scalars=where,
        grid=(4,),
        scratch=[pltpu.VMEM((192, LANES), f32), pltpu.VMEM((384, LANES), f32)],
        micros=4,
    )

    return (
        output,
        grad_hidden,
        by_gain,
        sum_in,
        sum_conv_w,
        sum_conv_b,
        sum_dt,
        sum_a,
        sum_skip,
        by_gate_gain,
        sum_out.reshape(384, 768),
    )


def solution(mesh):
    finer = Mesh(
        mesh.devices.reshape(4, 4, 2, mesh.shape["fsdp"]), ("seq_0", "seq_1", "seq_2", "fsdp")
    )
    in_specs = (
        P("fsdp", SEQ, None),
        P("fsdp", SEQ),
        P("fsdp"),
        P("fsdp", None),
        P(None, "fsdp"),
        P("fsdp"),
        P("fsdp"),
        P("fsdp"),
        P("fsdp"),
        P("fsdp"),
        P("fsdp", None),
        P("fsdp", SEQ, None),
    )
    out_specs = (
        P("fsdp", SEQ, None),
        P("fsdp", SEQ, None),
        P("fsdp"),
        P("fsdp", None),
        P(None, "fsdp"),
        P("fsdp"),
        P("fsdp"),
        P("fsdp"),
        P("fsdp"),
        P("fsdp"),
        P("fsdp", None),
    )
    return jax.shard_map(
        per_device, mesh=finer, in_specs=in_specs, out_specs=out_specs, check_vma=False
    )
```
